32 devices in a mesh: rows: 16 (over z, y, core), seq: 2 (over x).
Axes of the slice: x: 2, y: 2, z: 4, core: 2. Of those that a mesh axis runs over, the one named last changes fastest.
Arguments:
- enc_ids: int32 [16, 1024], P('rows', 'seq'), may hold values from 0 to 32127
- enc_segs: int32 [16, 1024], P('rows'), may hold values from 0 to 3, as said below
- sentinel: int32 [16, 1024], P('rows', 'seq'), may hold values 0 or 1
- mode: int32 [16, 4], P('rows'), may hold values from 0 to 2
- dec_ids: int32 [16, 512], P('rows', 'seq'), may hold values from 0 to 32127
- dec_segs: int32 [16, 512], P('rows'), may hold values from 0 to 3
- target_ids: int32 [16, 512], P('rows', 'seq'), may hold values from 0 to 32127
- target_mask: int32 [16, 512], P('rows', 'seq'), may hold values 0 or 1
- buckets: int32 [2, 2048], replicated, may hold values from 0 to 31
- embed: float32 [32128, 768], P(('rows', 'seq')), may hold values from -9 to 9
- attn_in: float32 [3, 768, 2304], P(None, ('rows', 'seq')), may hold values from -0.21875 to 0.21875
- attn_out: float32 [3, 768, 768], P(None, ('rows', 'seq')), may hold values from -0.875 to 0.875
- ffn_in: float32 [2, 768, 4096], P(None, ('rows', 'seq')), may hold values from -0.21875 to 0.21875
- ffn_out: float32 [2, 2048, 768], P(None, ('rows', 'seq')), may hold values from -0.25 to 0.25
- rel_table: float32 [2, 384], P(None, ('rows', 'seq')), may hold values from -6 to 6
- gains: float32 [7, 768], P(None, ('rows', 'seq')), may hold values from 0.5 to 1.5
- m_embed: float32 [32128, 768], P(('rows', 'seq')), may hold values from -2.3841858e-06 to 2.3841858e-06
- v_embed: float32 [32128, 768], P(('rows', 'seq')), may hold values from 2.4274484e-15 to 9.709794e-15
- m_attn_in: float32 [3, 768, 2304], P(None, ('rows', 'seq')), may hold values from -2.3841858e-06 to 2.3841858e-06
- v_attn_in: float32 [3, 768, 2304], P(None, ('rows', 'seq')), may hold values from 2.4274484e-15 to 9.709794e-15
- m_attn_out: float32 [3, 768, 768], P(None, ('rows', 'seq')), may hold values from -2.3841858e-06 to 2.3841858e-06
- v_attn_out: float32 [3, 768, 768], P(None, ('rows', 'seq')), may hold values from 2.4274484e-15 to 9.709794e-15
- m_ffn_in: float32 [2, 768, 4096], P(None, ('rows', 'seq')), may hold values from -2.3841858e-06 to 2.3841858e-06
- v_ffn_in: float32 [2, 768, 4096], P(None, ('rows', 'seq')), may hold values from 2.4274484e-15 to 9.709794e-15
- m_ffn_out: float32 [2, 2048, 768], P(None, ('rows', 'seq')), may hold values from -2.3841858e-06 to 2.3841858e-06
- v_ffn_out: float32 [2, 2048, 768], P(None, ('rows', 'seq')), may hold values from 2.4274484e-15 to 9.709794e-15
- m_rel: float32 [2, 384], P(None, ('rows', 'seq')), may hold values from -9.536743e-06 to 9.536743e-06
- v_rel: float32 [2, 384], P(None, ('rows', 'seq')), may hold values from 3.8839175e-14 to 1.553567e-13
- m_gains: float32 [7, 768], P(None, ('rows', 'seq')), may hold values from -9.536743e-06 to 9.536743e-06
- v_gains: float32 [7, 768], P(None, ('rows', 'seq')), may hold values from 3.8839175e-14 to 1.553567e-13
Outputs:
- loss: float32 [], replicated
- grad_norm: float32 [], replicated
- clipped_embed_grad: float32 [32128, 768], P(('rows', 'seq'))
- new_v_embed: float32 [32128, 768], P(('rows', 'seq'))
- new_embed: float32 [32128, 768], P(('rows', 'seq'))
- new_m_attn_in: float32 [3, 768, 2304], P(None, ('rows', 'seq'))
- new_v_attn_in: float32 [3, 768, 2304], P(None, ('rows', 'seq'))
- new_attn_in: float32 [3, 768, 2304], P(None, ('rows', 'seq'))
- new_m_attn_out: float32 [3, 768, 768], P(None, ('rows', 'seq'))
- new_v_attn_out: float32 [3, 768, 768], P(None, ('rows', 'seq'))
- new_attn_out: float32 [3, 768, 768], P(None, ('rows', 'seq'))
- new_m_ffn_in: float32 [2, 768, 4096], P(None, ('rows', 'seq'))
- new_v_ffn_in: float32 [2, 768, 4096], P(None, ('rows', 'seq'))
- new_ffn_in: float32 [2, 768, 4096], P(None, ('rows', 'seq'))
- new_m_ffn_out: float32 [2, 2048, 768], P(None, ('rows', 'seq'))
- new_v_ffn_out: float32 [2, 2048, 768], P(None, ('rows', 'seq'))
- new_ffn_out: float32 [2, 2048, 768], P(None, ('rows', 'seq'))
- new_m_rel: float32 [2, 384], P(None, ('rows', 'seq'))
- new_v_rel: float32 [2, 384], P(None, ('rows', 'seq'))
- new_rel_table: float32 [2, 384], P(None, ('rows', 'seq'))
- new_m_gains: float32 [7, 768], P(None, ('rows', 'seq'))
- new_v_gains: float32 [7, 768], P(None, ('rows', 'seq'))
- new_gains: float32 [7, 768], P(None, ('rows', 'seq'))
The draws below stay inside these ranges and needn't reach their ends.
Inputs may be any that keep to these rules, and one draw needn't show every extreme that they name: Every row holds all 4 examples in enc_segs and in dec_segs, numbered alike and never falling along the row; decoder example s reads encoder example s.
All inputs are finite; a program needn't handle non-finite values. No bound on the sum of `sentinel` or of `target_mask` on one device may be relied on, other than what follows from the above.
Results may differ from the reference program's by a relative error of at most 0.012.
The reference program's roundings to bfloat16 on the way count: a program that leaves them out, or rounds other values in their place, can miss the bound.
Values may be sent and summed in bfloat16 or wider, within the bound.
A program may use at most 448 MiB of HBM per device.

```python
import math
import jax
import jax.numpy as jnp
import numpy as np
from jax import lax

D = 768
HEADS = 12
HEAD_DIM = 64
FF = 2048
V = 32128
BUCKETS = 32
SEGS = 4
STEP = 10
ENC_DEV = 512
DEC_DEV = 256
ENC_LEN = 1024
DEC_LEN = 512
ROWS = 16
PARAMS = 41195520


def segment_numbers(key, length, per_device):
    keys = jax.random.split(key, ROWS)
    span = per_device - 1
    positions = jnp.arange(length, dtype=jnp.int32)

    def one_row(row_key):
        order = jax.random.permutation(row_key, 2 * span)[:SEGS - 1]
        cuts = jnp.where(order < span, order + 1, length - per_device + 1 + order - span)
        return jnp.sum((positions[:, None] >= cuts[None, :]).astype(jnp.int32), axis=1)
    return jax.vmap(one_row)(keys).astype(jnp.int32)


def draw_enc_segs(key, part):
    key = jax.random.fold_in(key, 11)
    return segment_numbers(key, ENC_LEN, ENC_DEV)


def draw_dec_segs(key, part):
    key = jax.random.fold_in(key, 12)
    return segment_numbers(key, DEC_LEN, DEC_DEV)


def touch_ends(array, own_key, least, largest):
    place = [jax.random.randint(jax.random.fold_in(own_key, axis), (), 0, length) for axis, length in enumerate(array.shape)]
    main_axis = array.shape.index(max(array.shape))
    neighbour = place[:main_axis] + [(place[main_axis] + 1) % array.shape[main_axis]] + place[main_axis + 1:]
    return array.at[tuple(place)].set(least).at[tuple(neighbour)].set(largest)


def shard_levels(own_key, shape, cuts, low, high):
    level = 1.0
    for axis_at, shards_of in cuts:
        draws = jax.random.uniform(jax.random.fold_in(jax.random.fold_in(own_key, 6), axis_at), (shards_of,), jnp.float32, low / len(cuts), high / len(cuts))
        level = level * jnp.repeat(jnp.exp(draws), shape[axis_at] // shards_of).reshape((-1,) + (1,) * (len(shape) - 1 - axis_at))
    return level


def rank_table(amount, lean):
    portions = [(1 << 20) // math.isqrt(standing ** lean) + 1 for standing in range(1, amount + 1)]
    deviation = 1 + sum(portions) // (1 << 30)
    return np.cumsum(np.array([max(1, weight // deviation) for weight in portions]))


def ranked_ids(rng, extent, number_of, skew):
    grid = rank_table(number_of, skew)
    lot = jax.random.randint(jax.random.fold_in(rng, 1), extent, 0, int(grid[number_of - 1]))
    rank = jnp.searchsorted(jnp.asarray(grid, jnp.int32), lot, side="right")
    return jax.random.permutation(jax.random.fold_in(rng, 2), number_of)[rank].astype(jnp.int32)


def scatter_about(stream_key, dims, width, most, cuts=(), kind=jnp.bfloat16):
    entries = jax.random.normal(stream_key, dims, jnp.float32) * width
    if len(cuts) > 0:
        entries = shard_levels(stream_key, dims, cuts, -0.22, 0.18) * entries
    return jnp.clip(entries, min=-most, max=most).astype(kind)


def setup_inputs(seed: int = 0) -> dict:
    arg_keys = jax.random.split(jax.random.key(seed), 31)
    return {
        "enc_ids": touch_ends(ranked_ids(arg_keys[0], (ROWS, ENC_LEN), V, 2), jax.random.fold_in(arg_keys[0], 3), 0, V - 1).astype(jnp.int32),
        "enc_segs": draw_enc_segs(jax.random.fold_in(arg_keys[30], 71), 0),
        "sentinel": touch_ends((jax.random.randint(arg_keys[2], (ROWS, ENC_LEN), 0, 8) < 1).astype(jnp.int32), jax.random.fold_in(arg_keys[2], 1), 0, 1),
        "mode": touch_ends(jax.random.randint(arg_keys[3], (ROWS, SEGS), 0, 3), jax.random.fold_in(arg_keys[3], 1), 0, 2).astype(jnp.int32),
        "dec_ids": touch_ends(ranked_ids(arg_keys[4], (ROWS, DEC_LEN), V, 2), jax.random.fold_in(arg_keys[4], 3), 0, V - 1).astype(jnp.int32),
        "dec_segs": draw_dec_segs(jax.random.fold_in(arg_keys[30], 71), 0),
        "target_ids": touch_ends(ranked_ids(arg_keys[6], (ROWS, DEC_LEN), V, 2), jax.random.fold_in(arg_keys[6], 3), 0, V - 1).astype(jnp.int32),
        "target_mask": touch_ends((jax.random.randint(arg_keys[7], (ROWS, DEC_LEN), 0, 4) < 3).astype(jnp.int32), jax.random.fold_in(arg_keys[7], 1), 0, 1),
        "buckets": touch_ends(jax.random.randint(arg_keys[8], (2, 2 * ENC_LEN), 0, BUCKETS), jax.random.fold_in(arg_keys[8], 1), 0, BUCKETS - 1).astype(jnp.int32),
        "embed": scatter_about(arg_keys[9], (V, D), 1.5, 9.0, ((0, 32),), jnp.float32),
        "attn_in": scatter_about(arg_keys[10], (3, D, 3 * D), D ** -0.5, 0.21875, ((1, 32),), jnp.float32),
        "attn_out": scatter_about(arg_keys[11], (3, D, D), (D // 16) ** -0.5, 0.875, ((1, 32),), jnp.float32),
        "ffn_in": scatter_about(arg_keys[12], (2, D, 2 * FF), D ** -0.5, 0.21875, ((1, 32),), jnp.float32),
        "ffn_out": scatter_about(arg_keys[13], (2, FF, D), (FF // 4) ** -0.5, 0.25, ((1, 32),), jnp.float32),
        "rel_table": scatter_about(arg_keys[14], (2, BUCKETS * HEADS), 1.0, 6.0, ((1, 32),), jnp.float32),
        "gains": jnp.clip(1.0 + 0.1 * jax.random.normal(arg_keys[15], (7, D), jnp.float32), 0.5, 1.5),
        "m_embed": scatter_about(arg_keys[16], (V, D), (0.00111 * PARAMS ** -0.5), 2.384185791015625e-06, ((0, 32),), jnp.float32),
        "v_embed": jnp.clip(jnp.exp(math.log(9.709793631293168e-15) - 1.3862944 * jax.random.uniform(arg_keys[17], (V, D), jnp.float32) ** shard_levels(arg_keys[17], (V, D), ((0, 32),), -0.2, 0.2)), 2.427448407823292e-15, 9.709793631293168e-15),
        "m_attn_in": scatter_about(arg_keys[18], (3, D, 3 * D), (0.00111 * PARAMS ** -0.5), 2.384185791015625e-06, ((1, 32),), jnp.float32),
        "v_attn_in": jnp.clip(jnp.exp(math.log(9.709793631293168e-15) - 1.3862944 * jax.random.uniform(arg_keys[19], (3, D, 3 * D), jnp.float32) ** shard_levels(arg_keys[19], (3, D, 3 * D), ((1, 32),), -0.2, 0.2)), 2.427448407823292e-15, 9.709793631293168e-15),
        "m_attn_out": scatter_about(arg_keys[20], (3, D, D), (0.00111 * PARAMS ** -0.5), 2.384185791015625e-06, ((1, 32),), jnp.float32),
        "v_attn_out": jnp.clip(jnp.exp(math.log(9.709793631293168e-15) - 1.3862944 * jax.random.uniform(arg_keys[21], (3, D, D), jnp.float32) ** shard_levels(arg_keys[21], (3, D, D), ((1, 32),), -0.2, 0.2)), 2.427448407823292e-15, 9.709793631293168e-15),
        "m_ffn_in": scatter_about(arg_keys[22], (2, D, 2 * FF), (0.00111 * PARAMS ** -0.5), 2.384185791015625e-06, ((1, 32),), jnp.float32),
        "v_ffn_in": jnp.clip(jnp.exp(math.log(9.709793631293168e-15) - 1.3862944 * jax.random.uniform(arg_keys[23], (2, D, 2 * FF), jnp.float32) ** shard_levels(arg_keys[23], (2, D, 2 * FF), ((1, 32),), -0.2, 0.2)), 2.427448407823292e-15, 9.709793631293168e-15),
        "m_ffn_out": scatter_about(arg_keys[24], (2, FF, D), (0.00111 * PARAMS ** -0.5), 2.384185791015625e-06, ((1, 32),), jnp.float32),
        "v_ffn_out": jnp.clip(jnp.exp(math.log(9.709793631293168e-15) - 1.3862944 * jax.random.uniform(arg_keys[25], (2, FF, D), jnp.float32) ** shard_levels(arg_keys[25], (2, FF, D), ((1, 32),), -0.2, 0.2)), 2.427448407823292e-15, 9.709793631293168e-15),
        "m_rel": scatter_about(arg_keys[26], (2, BUCKETS * HEADS), (0.00444 * PARAMS ** -0.5), 9.5367431640625e-06, ((1, 32),), jnp.float32),
        "v_rel": jnp.clip(jnp.exp(math.log(1.553566981006907e-13) - 1.3862944 * jax.random.uniform(arg_keys[27], (2, BUCKETS * HEADS), jnp.float32) ** shard_levels(arg_keys[27], (2, BUCKETS * HEADS), ((1, 32),), -0.2, 0.2)), 3.8839174525172673e-14, 1.553566981006907e-13),
        "m_gains": scatter_about(arg_keys[28], (7, D), (0.00444 * PARAMS ** -0.5), 9.5367431640625e-06, ((1, 32),), jnp.float32),
        "v_gains": jnp.clip(jnp.exp(math.log(1.553566981006907e-13) - 1.3862944 * jax.random.uniform(arg_keys[29], (7, D), jnp.float32) ** shard_levels(arg_keys[29], (7, D), ((1, 32),), -0.2, 0.2)), 3.8839174525172673e-14, 1.553566981006907e-13),
    }


highest = lax.Precision.HIGHEST
clip_limit = 0.01

@jax.custom_vjp
def low(v):
    return lax.optimization_barrier(v.astype(jnp.bfloat16)).astype(jnp.float32)

@jax.custom_vjp
def low_back(v):
    return v

def low_keep(v):
    return (low(v), None)

def low_pass(kept, grad):
    return (grad,)

def back_keep(v):
    return (v, None)

def back_low(kept, grad):
    return (low(grad),)
low.defvjp(low_keep, low_pass)
low_back.defvjp(back_keep, back_low)

def matmul_high(left, right):
    return jnp.dot(left, right, precision=highest)

def rms_norm(values, gain):
    return values * lax.rsqrt(lax.optimization_barrier(jnp.mean(values * values, axis=-1, keepdims=True)) + 1e-06) * gain

def relative_bias(table_row, bucket_row, q_pos, k_pos):
    index = bucket_row[k_pos[None, :] - q_pos[:, None] + ENC_LEN]
    lookup_matrix = table_row.reshape(BUCKETS, HEADS)
    return jnp.transpose(lookup_matrix[index], (2, 0, 1))

def attention(query, keyval, bias, allowed):
    count_q = query.shape[0]
    key_count_total = keyval.shape[0]
    query3 = query.reshape(count_q, HEADS, HEAD_DIM)
    keys3 = keyval[:, :D].reshape(key_count_total, HEADS, HEAD_DIM)
    vals3 = keyval[:, D:].reshape(key_count_total, HEADS, HEAD_DIM)
    scores = jnp.einsum('qhd,khd->hqk', query3, keys3, precision=highest) * HEAD_DIM ** (-0.5) + bias
    scores = low_back(scores)
    scores = jnp.where(allowed[None], scores, -1e+30)
    probs = jax.nn.softmax(scores, axis=-1)
    out = jnp.einsum('hqk,khd->qhd', low(probs), vals3, precision=highest)
    return low_back(low(out.reshape(count_q, D)))

def self_branch(resid, gain, w_in, w_out, bias, allowed):
    normed = low(rms_norm(resid, gain))
    proj_qkv = low_back(low(matmul_high(normed, w_in)))
    out = attention(proj_qkv[:, :D], proj_qkv[:, D:], bias, allowed)
    return low_back(matmul_high(out, w_out))

def feed_forward(resid, gain, w_in, w_out):
    normed = low(rms_norm(resid, gain))
    both = low_back(matmul_high(normed, w_in))
    hidden = low(jax.nn.gelu(both[:, :FF], approximate=True) * both[:, FF:])
    return low_back(matmul_high(hidden, w_out))

def per_row_loss(weights, row, buckets):
    embed, attn_in, attn_out, ffn_in, ffn_out, rel_table, gains = [low(item) for item in weights]
    enc_tok, enc_seg, dec_tok, dec_seg, targets, weight = row
    enc_pos = jnp.arange(ENC_LEN, dtype=jnp.int32)
    dec_pos = jnp.arange(DEC_LEN, dtype=jnp.int32)
    enc_x = embed[enc_tok]
    enc_bias = relative_bias(rel_table[0], buckets[0], enc_pos, enc_pos)
    enc_same = enc_seg[:, None] == enc_seg[None, :]
    enc_x = enc_x + self_branch(enc_x, gains[0], attn_in[0], attn_out[0], enc_bias, enc_same)
    enc_x = enc_x + feed_forward(enc_x, gains[1], ffn_in[0], ffn_out[0])
    enc_out = low(rms_norm(enc_x, gains[2]))
    dec_y = embed[dec_tok]
    dec_bias = relative_bias(rel_table[1], buckets[1], dec_pos, dec_pos)
    causal = (dec_seg[:, None] == dec_seg[None, :]) & (dec_pos[None, :] <= dec_pos[:, None])
    dec_y = dec_y + self_branch(dec_y, gains[3], attn_in[1], attn_out[1], dec_bias, causal)
    normed = low(rms_norm(dec_y, gains[4]))
    cross_q = low_back(low(matmul_high(normed, attn_in[2][:, :D])))
    cross_kv = low_back(low(matmul_high(enc_out, attn_in[2][:, D:])))
    cross = attention(cross_q, cross_kv, 0.0, dec_seg[:, None] == enc_seg[None, :])
    dec_y = dec_y + low_back(matmul_high(cross, attn_out[2]))
    dec_y = dec_y + feed_forward(dec_y, gains[5], ffn_in[1], ffn_out[1])
    hidden = low(rms_norm(dec_y, gains[6]) * D ** (-0.5))
    logits = low_back(matmul_high(hidden, embed.T))
    lse = jax.nn.logsumexp(logits, axis=-1)
    picked = jnp.take_along_axis(logits, targets[:, None], axis=1)[:, 0]
    return jnp.sum(weight * (lse - picked))

def encoder_tokens(enc_ids, enc_segs, sentinel, mode):
    prior = jnp.concatenate([enc_segs[:, :1] - 1, enc_segs[:, :-1]], axis=1)
    first = enc_segs != prior
    mode_of = lax.optimization_barrier(jnp.sum(jnp.where(enc_segs[:, :, None] == jnp.arange(SEGS, dtype=jnp.int32)[None, None], mode[:, None, :], 0), axis=2))
    tokens = jnp.where(sentinel == 1, V - 1 - enc_segs, enc_ids)
    return jnp.where(first, V - 101 - mode_of, tokens)

def adamw(weight, grad, first_m, second_m, count, rate, decay):
    first_new = 0.9 * first_m + 0.1 * grad
    second_new = 0.999 * second_m + 0.001 * grad * grad
    first_hat = first_new / (1.0 - 0.9 ** count)
    second_hat = second_new / (1.0 - 0.999 ** count)
    return (first_new, second_new, weight - rate * (first_hat / (jnp.sqrt(second_hat) + 1e-08) + decay * weight))

def reference(enc_ids, enc_segs, sentinel, mode, dec_ids, dec_segs, target_ids, target_mask, buckets, embed, attn_in, attn_out, ffn_in, ffn_out, rel_table, gains, m_embed, v_embed, m_attn_in, v_attn_in, m_attn_out, v_attn_out, m_ffn_in, v_ffn_in, m_ffn_out, v_ffn_out, m_rel, v_rel, m_gains, v_gains):
    enc_tok = encoder_tokens(enc_ids, enc_segs, sentinel, mode)
    weights = (embed, attn_in, attn_out, ffn_in, ffn_out, rel_table, gains)
    rows = (enc_tok, enc_segs, dec_ids, dec_segs, target_ids, target_mask.astype(jnp.float32))

    def one_row(carry, row):
        total, grads = carry
        value, pull = jax.vjp(lambda params: per_row_loss(params, row, buckets), weights)
        got, = pull(jnp.ones_like(value))
        return ((total + value, jax.tree.map(jnp.add, grads, got)), None)
    start = (jnp.zeros((), jnp.float32), jax.tree.map(jnp.zeros_like, weights))
    (loss_sum, grads), _ = lax.scan(one_row, start, rows)
    count = jnp.sum(target_mask.astype(jnp.float32))
    grads = [item / count for item in grads]
    grad_norm = jnp.sqrt(sum((jnp.sum(item * item) for item in grads)))
    factor = jnp.minimum(1.0, clip_limit / grad_norm)
    moments = [(m_embed, v_embed), (m_attn_in, v_attn_in), (m_attn_out, v_attn_out), (m_ffn_in, v_ffn_in), (m_ffn_out, v_ffn_out), (m_rel, v_rel), (m_gains, v_gains)]
    settings = [(1.0, 0.01), (0.05, 0.01), (0.05, 0.01), (0.05, 0.01), (0.05, 0.01), (0.3, 0.0), (0.3, 0.0)]
    results = [loss_sum / count, grad_norm]
    for slot_number, (weight, grad, pair, setting) in enumerate(zip(weights, grads, moments, settings)):
        clipped = grad * factor
        first_new, second_new, new_weight = adamw(weight, clipped, pair[0], pair[1], float(STEP), setting[0], setting[1])
        results.extend((clipped if slot_number == 0 else first_new, second_new, new_weight))
    return tuple(results)
```

```python
import functools

import jax
import jax.numpy as jnp
from jax import lax
from jax.experimental import pallas as pl
from jax.experimental.pallas import tpu as pltpu
from jax.sharding import Mesh
from jax.sharding import PartitionSpec as P

D = 768
HEADS = 12
HEAD_DIM = 64
FF = 2048
V = 32128
BUCKETS = 32
STEP = 10

masked_out = -1e30
clip_limit = 0.01
ALL = ("z", "p", "core", "seq")
PLANE = ("p", "core", "seq")
bf16 = jnp.bfloat16
f32 = jnp.float32
VMEM_LIMIT = 56 * 1024 * 1024


def rms_scale(values, gain):
    return values * lax.rsqrt(jnp.mean(values * values, axis=-1, keepdims=True) + 1e-06) * gain


def norm_pull(values, gain, factor, upstream):
    _, pull = jax.vjp(lambda left, right: rms_scale(left, right) * factor, values, gain)
    return pull(upstream)


def gate_up(both):
    return jax.nn.gelu(both[:, :FF], approximate=True) * both[:, FF:]


def project(left, right):
    return jnp.dot(left, right, preferred_element_type=f32)


def weight_grad(inputs, grads):
    return jnp.einsum("td,te->de", inputs, grads, preferred_element_type=f32)


def input_grad(grads, weight):
    return jnp.einsum("te,de->td", grads, weight, preferred_element_type=f32)


def dot_nt(a, b):
    return lax.dot_general(a, b, (((1,), (1,)), ((), ())), preferred_element_type=f32)


def dot_tn(a, b):
    return lax.dot_general(a, b, (((0,), (0,)), ((), ())), preferred_element_type=f32)


def dot_nn(a, b):
    return lax.dot_general(a, b, (((1,), (0,)), ((), ())), preferred_element_type=f32)


def spread(eight, rows, width):
    total = eight.shape[-1]
    grid = eight
    have = 8
    while have < rows:
        grid = jnp.concatenate([pltpu.roll(grid, total - have, 1), grid], axis=0)
        have *= 2
    return grid[:, :width]


def collect(grid, total):
    rows, width = grid.shape
    have = jnp.concatenate([grid, jnp.zeros((rows, total - width), f32)], axis=1)
    while rows > 8:
        rows //= 2
        have = pltpu.roll(have[:rows], rows, 1) + have[rows:]
    return have


def probs_of(cfg, refs, block, head):
    bq, has_bias, causal = cfg
    rows = slice(block * bq, (block + 1) * bq)
    cols = slice(head * HEAD_DIM, (head + 1) * HEAD_DIM)
    query = refs["q"][rows, cols]
    scores = []
    for part in range(2):
        keys = refs["k"][part][:, cols]
        s = dot_nt(query, keys) * HEAD_DIM ** (-0.5)
        if has_bias:
            s = s + spread(refs["x8"][block, part, head], bq, keys.shape[0])
        allowed = refs["qseg"][rows, :] == refs["kseg"][part]
        if causal:
            allowed = allowed & (refs["kpos"][part] <= refs["qpos"][rows, :])
        scores.append(jnp.where(allowed, s, masked_out))
    top = jnp.maximum(
        jnp.max(scores[0], axis=1, keepdims=True), jnp.max(scores[1], axis=1, keepdims=True)
    )
    exps = [jnp.exp(s - top) for s in scores]
    total = jnp.sum(exps[0], axis=1, keepdims=True) + jnp.sum(exps[1], axis=1, keepdims=True)
    scale = 1.0 / total
    return query, [e * scale for e in exps]


def name_refs(cfg, refs):
    bq, has_bias, causal = cfg
    it = iter(refs)
    named = {"q": next(it)}
    k0, v0, k1, v1 = next(it), next(it), next(it), next(it)
    named["k"], named["v"] = (k0, k1), (v0, v1)
    ids = next(it), next(it), next(it), next(it), next(it), next(it)
    named["qseg"], named["kseg"] = ids[0], (ids[1][...], ids[2][...])
    named["qpos"], named["kpos"] = ids[3], (ids[4][...], ids[5][...])
    if has_bias:
        named["x8"] = next(it)
    return named, list(it)


def attend_forward_kernel(cfg, *refs):
    named, (out,) = name_refs(cfg, refs)
    bq = cfg[0]
    for block in range(named["q"].shape[0] // bq):
        for head in range(2):
            cols = slice(head * HEAD_DIM, (head + 1) * HEAD_DIM)
            _, probs = probs_of(cfg, named, block, head)
            acc = dot_nn(probs[0].astype(bf16), named["v"][0][:, cols])
            acc = acc + dot_nn(probs[1].astype(bf16), named["v"][1][:, cols])
            out[block * bq : (block + 1) * bq, cols] = acc.astype(bf16)


def attend_backward_kernel(cfg, *refs):
    named, rest = name_refs(cfg, refs)
    bq, has_bias, causal = cfg
    if has_bias:
        grad, dq, own, other, y8 = rest
    else:
        grad, dq, own, other = rest
    blocks = named["q"].shape[0] // bq
    for head in range(2):
        cols = slice(head * HEAD_DIM, (head + 1) * HEAD_DIM)
        dk, dv = [None, None], [None, None]
        for block in range(blocks):
            rows = slice(block * bq, (block + 1) * bq)
            query, probs = probs_of(cfg, named, block, head)
            do = grad[rows, cols]
            dp = [dot_nt(do, named["v"][part][:, cols]) for part in range(2)]
            delta = jnp.sum(probs[0] * dp[0], axis=1, keepdims=True) + jnp.sum(
                probs[1] * dp[1], axis=1, keepdims=True
            )
            acc = None
            for part in range(2):
                ds = (probs[part] * (dp[part] - delta)).astype(bf16)
                term = dot_nn(ds, named["k"][part][:, cols])
                acc = term if acc is None else acc + term
                k_term = dot_tn(query, ds)
                v_term = dot_tn(do, probs[part].astype(bf16))
                dk[part] = k_term if dk[part] is None else dk[part] + k_term
                dv[part] = v_term if dv[part] is None else dv[part] + v_term
                if has_bias:
                    y8[block, part, head] = collect(ds.astype(f32), y8.shape[-1])
            dq[rows, cols] = (acc * HEAD_DIM ** (-0.5)).astype(bf16)
        for part, target in enumerate((own, other)):
            target[0, :, cols] = (dk[part] * HEAD_DIM ** (-0.5)).T.astype(target.dtype)
            target[1, :, cols] = dv[part].T.astype(target.dtype)


def attend_specs(q_len, k_len, has_bias, x8):
    whole = lambda shape: pl.BlockSpec(shape, lambda i: (0,) * len(shape))
    kv = [
        pl.BlockSpec((k_len, 128), lambda i: (0, i)),
        pl.BlockSpec((k_len, 128), lambda i: (0, i + 6)),
    ]
    specs = [pl.BlockSpec((q_len, 128), lambda i: (0, i))] + kv + kv
    specs += [whole((q_len, 1)), whole((1, k_len)), whole((1, k_len))] * 2
    if has_bias:
        specs.append(
            pl.BlockSpec((x8.shape[0], 2, 2, 8, x8.shape[-1]), lambda i: (0, 0, i, 0, 0))
        )
    return specs


def attend_args(q, kv_own, kv_other, ids, x8):
    args = [q, kv_own, kv_own, kv_other, kv_other] + list(ids)
    if x8 is not None:
        args.append(x8)
    return args


def attend_cost(q_len, k_len, products):
    size = HEADS * q_len * 2 * k_len
    return pl.CostEstimate(
        flops=2 * products * size * HEAD_DIM, bytes_accessed=8 * D * (q_len + 4 * k_len),
        transcendentals=size,
    )


def attend_forward(q, kv_own, kv_other, ids, x8, causal):
    q_len, k_len = q.shape[0], kv_own.shape[0]
    cfg = (256, x8 is not None, causal)
    return pl.pallas_call(
        functools.partial(attend_forward_kernel, cfg),
        grid=(HEADS // 2,),
        in_specs=attend_specs(q_len, k_len, x8 is not None, x8),
        out_specs=pl.BlockSpec((q_len, 128), lambda i: (0, i)),
        out_shape=jax.ShapeDtypeStruct((q_len, D), bf16),
        compiler_params=pltpu.CompilerParams(vmem_limit_bytes=VMEM_LIMIT),
        cost_estimate=attend_cost(q_len, k_len, 2),
    )(*attend_args(q, kv_own, kv_other, ids, x8))


def attend_backward(grad, q, kv_own, kv_other, ids, x8, causal):
    q_len, k_len = q.shape[0], kv_own.shape[0]
    cfg = (256, x8 is not None, causal)
    kv_spec = pl.BlockSpec((2, k_len, 128), lambda i: (0, 0, i))
    out_specs = [pl.BlockSpec((q_len, 128), lambda i: (0, i)), kv_spec, kv_spec]
    out_shape = [
        jax.ShapeDtypeStruct((q_len, D), bf16),
        jax.ShapeDtypeStruct((2, k_len, D), f32),
        jax.ShapeDtypeStruct((2, k_len, D), bf16),
    ]
    if x8 is not None:
        out_specs.append(
            pl.BlockSpec((x8.shape[0], 2, 2, 8, x8.shape[-1]), lambda i: (0, 0, i, 0, 0))
        )
        out_shape.append(jax.ShapeDtypeStruct(x8.shape, f32))
    return pl.pallas_call(
        functools.partial(attend_backward_kernel, cfg),
        grid=(HEADS // 2,),
        in_specs=attend_specs(q_len, k_len, x8 is not None, x8)
        + [pl.BlockSpec((q_len, 128), lambda i: (0, i))],
        out_specs=out_specs,
        out_shape=out_shape,
        compiler_params=pltpu.CompilerParams(vmem_limit_bytes=VMEM_LIMIT),
        cost_estimate=attend_cost(q_len, k_len, 5),
    )(*attend_args(q, kv_own, kv_other, ids, x8), grad)


def bias_bases(core, q_len, k_len, offset):
    bases = []
    for block in range(q_len // 256):
        for part in range(2):
            k_start = (core if part == 0 else 1 - core) * k_len
            q_start = core * q_len + block * 256
            bases.append(k_start - q_start - 255 + offset)
    return bases


def bias_eights(table, bucket_row, core, q_len, k_len):
    size = bucket_row.shape[0]
    picks = (bucket_row[None, :] == jnp.arange(BUCKETS, dtype=jnp.int32)[:, None]).astype(bf16)
    per_offset = jnp.einsum("bh,bn->hn", table, picks, preferred_element_type=f32)
    per_offset = jnp.pad(per_offset, ((0, 0), (0, 16)))
    width = k_len + 256
    found = []
    for base in bias_bases(core, q_len, k_len, size // 2):
        window = lax.dynamic_slice_in_dim(per_offset, base, width + 7, axis=1)
        found.append(jnp.stack([window[:, 7 - r : 7 - r + width] for r in range(8)], axis=1))
    return jnp.stack(found).reshape(q_len // 256, 2, HEADS, 8, width), picks


def bias_gradient(y8, picks, core, q_len, k_len):
    size = picks.shape[1]
    width = k_len + 256
    total = jnp.zeros((HEADS, size + 16), f32)
    flat = y8.reshape(-1, HEADS, 8, width)
    for number, base in enumerate(bias_bases(core, q_len, k_len, size // 2)):
        window = sum(
            jnp.pad(flat[number, :, r], ((0, 0), (7 - r, r))) for r in range(8)
        )
        old = lax.dynamic_slice_in_dim(total, base, width + 7, axis=1)
        total = lax.dynamic_update_slice_in_dim(total, old + window, base, axis=1)
    return jnp.einsum(
        "bn,hn->bh", picks.astype(f32), total[:, :size], precision=lax.Precision.HIGHEST
    )


def head_stats_kernel(count, hid, tab, tgt, lse_out, pick_out):
    logits = dot_nt(tab[...], hid[...])
    row = lax.broadcasted_iota(jnp.int32, logits.shape, 0)
    pick_out[...] = jnp.sum(jnp.where(row == tgt[...], logits, 0.0), axis=0, keepdims=True)
    logits = jnp.where(row < count, logits, masked_out)
    top = jnp.max(logits, axis=0, keepdims=True)
    lse_out[...] = top + jnp.log(jnp.sum(jnp.exp(logits - top), axis=0, keepdims=True))


def head_grad_kernel(count, hid, tab, tgt, msk, lse, dhid, dtab):
    logits = dot_nt(tab[...], hid[...])
    row = lax.broadcasted_iota(jnp.int32, logits.shape, 0)
    soft = jnp.exp(jnp.where(row < count, logits, masked_out) - lse[...])
    grad = ((soft - jnp.where(row == tgt[...], 1.0, 0.0)) * msk[...]).astype(bf16)
    dhid[...] = dot_tn(grad, tab[...]).astype(bf16)
    term = dot_nn(grad, hid[...])

    @pl.when(pl.program_id(0) == 0)
    def _():
        dtab[...] = term

    @pl.when(pl.program_id(0) != 0)
    def _():
        dtab[...] += term


def head_stats(hidden, table, targets, count):
    tokens, rows = hidden.shape[0], table.shape[0]
    block = 512
    line = pl.BlockSpec((1, block), lambda i: (0, i))
    return pl.pallas_call(
        functools.partial(head_stats_kernel, count),
        grid=(tokens // block,),
        in_specs=[
            pl.BlockSpec((block, D), lambda i: (i, 0)),
            pl.BlockSpec((rows, D), lambda i: (0, 0)),
            line,
        ],
        out_specs=[line, line],
        out_shape=[jax.ShapeDtypeStruct((1, tokens), f32)] * 2,
        compiler_params=pltpu.CompilerParams(vmem_limit_bytes=VMEM_LIMIT),
        cost_estimate=pl.CostEstimate(
            flops=2 * tokens * rows * D, bytes_accessed=2 * tokens * D, transcendentals=tokens * rows
        ),
    )(hidden, table, targets)


def head_grad(hidden, table, targets, mask, lse, count):
    tokens, rows = hidden.shape[0], table.shape[0]
    block = 512
    line = pl.BlockSpec((1, block), lambda i: (0, i))
    return pl.pallas_call(
        functools.partial(head_grad_kernel, count),
        grid=(tokens // block,),
        in_specs=[
            pl.BlockSpec((block, D), lambda i: (i, 0)),
            pl.BlockSpec((rows, D), lambda i: (0, 0)),
            line,
            line,
            line,
        ],
        out_specs=[
            pl.BlockSpec((block, D), lambda i: (i, 0)),
            pl.BlockSpec((rows, D), lambda i: (0, 0)),
        ],
        out_shape=[
            jax.ShapeDtypeStruct((tokens, D), bf16),
            jax.ShapeDtypeStruct((rows, D), f32),
        ],
        compiler_params=pltpu.CompilerParams(vmem_limit_bytes=VMEM_LIMIT),
        cost_estimate=pl.CostEstimate(
            flops=6 * tokens * rows * D, bytes_accessed=4 * tokens * D, transcendentals=tokens * rows
        ),
    )(hidden, table, targets, mask, lse)


def place_kernel(ids, grads, out):
    rows = out.shape[0]
    row = lax.broadcasted_iota(jnp.int32, (rows, ids.shape[1]), 0) + pl.program_id(0) * rows
    hot = jnp.where(row == ids[...], 1.0, 0.0).astype(bf16)
    out[...] = dot_nn(hot, grads[...]).astype(bf16)


def place_rows(ids, grads, parts, rows):
    tokens = grads.shape[0]
    return pl.pallas_call(
        place_kernel,
        grid=(parts,),
        in_specs=[
            pl.BlockSpec((1, tokens), lambda i: (0, 0)),
            pl.BlockSpec((tokens, D), lambda i: (0, 0)),
        ],
        out_specs=pl.BlockSpec((rows, D), lambda i: (i, 0)),
        out_shape=jax.ShapeDtypeStruct((parts * rows, D), bf16),
        compiler_params=pltpu.CompilerParams(vmem_limit_bytes=VMEM_LIMIT),
        cost_estimate=pl.CostEstimate(
            flops=2 * tokens * parts * rows * D, bytes_accessed=2 * parts * rows * D, transcendentals=0
        ),
    )(ids, grads)


def gather_axis(value, axis):
    size = lax.axis_size(axis)
    me = lax.axis_index(axis)
    got = [value]
    for step in range(1, size):
        got.append(lax.ppermute(value, axis, [(i, (i + step) % size) for i in range(size)]))
    stacked = jnp.stack(got)
    return jnp.take(stacked, (me - jnp.arange(size, dtype=jnp.int32)) % size, axis=0)


def gather_small(value, axes):
    shape = value.shape
    for axis in reversed(axes):
        value = gather_axis(value, axis)
        value = value.reshape((-1,) + shape)
    return value


def fold_all(value, combine):
    for axis in reversed(ALL):
        size = lax.axis_size(axis)
        hop = 1
        while hop < size:
            other = lax.ppermute(value, axis, [(i, i ^ hop) for i in range(size)])
            value = combine(value, other)
            hop *= 2
    return value


def swap_core(value):
    return lax.ppermute(value, "core", [(0, 1), (1, 0)])


def add_logs(left, right):
    top = jnp.maximum(left, right)
    return top + jnp.log(jnp.exp(left - top) + jnp.exp(right - top))


def ffn_forward(resid, gain, w_in, w_out):
    normed = rms_scale(resid, gain).astype(bf16)
    both = project(normed, w_in)
    hidden = gate_up(both).astype(bf16)
    return (resid + project(hidden, w_out), (normed, both, hidden))


def ffn_backward(upstream, resid, gain, w_in, w_out, saved):
    normed, both, hidden = saved
    grad_b = upstream.astype(bf16)
    d_out = weight_grad(hidden, grad_b).astype(bf16)
    _, pull = jax.vjp(gate_up, both)
    (d_both,) = pull(input_grad(grad_b, w_out))
    d_both_b = d_both.astype(bf16)
    d_in = weight_grad(normed, d_both_b).astype(bf16)
    d_resid, d_gain = norm_pull(resid, gain, 1.0, input_grad(d_both_b, w_in))
    return (upstream + d_resid, d_gain, d_in, d_out)


def branch_backward(upstream, out_b, w_out):
    grad_b = upstream.astype(bf16)
    return (weight_grad(out_b, grad_b).astype(bf16), input_grad(grad_b, w_out).astype(bf16))


def adamw(weight, grad, first_m, second_m, count, rate, decay):
    first_new = 0.9 * first_m + 0.1 * grad
    second_new = 0.999 * second_m + 0.001 * grad * grad
    first_hat = first_new / (1.0 - 0.9**count)
    second_hat = second_new / (1.0 - 0.999**count)
    return (
        first_new,
        second_new,
        weight - rate * (first_hat / (jnp.sqrt(second_hat) + 1e-08) + decay * weight),
    )


def body(
    enc_ids,
    enc_segs,
    sentinel,
    mode,
    dec_ids,
    dec_segs,
    target_ids,
    target_mask,
    buckets,
    embed,
    attn_in,
    attn_out,
    ffn_in,
    ffn_out,
    rel_table,
    gains,
    m_embed,
    v_embed,
    m_attn_in,
    v_attn_in,
    m_attn_out,
    v_attn_out,
    m_ffn_in,
    v_ffn_in,
    m_ffn_out,
    v_ffn_out,
    m_rel,
    v_rel,
    m_gains,
    v_gains,
):
    core = lax.axis_index("core")
    z_at = lax.axis_index("z")
    z_size = lax.axis_size("z")
    plane_size = lax.axis_size(PLANE)
    device = lax.axis_index(ALL)
    shard = embed.shape[0]
    padded = -(-shard // 16) * 16
    enc_count, dec_count = enc_ids.shape[1], dec_ids.shape[1]
    enc_len, dec_len = enc_segs.shape[1], dec_segs.shape[1]

    table_b = jnp.pad(embed.astype(bf16), ((0, padded - shard), (0, 0)))
    plane_table = lax.all_gather(table_b, PLANE, axis=0, tiled=True)
    misc = jnp.concatenate([gains.T, rel_table.reshape(-1, 1)], axis=1)
    misc = jnp.pad(misc, ((0, 0), (0, 120)))
    shard_in = attn_in.shape[1]
    enc_pack = lax.all_gather(
        jnp.concatenate([attn_in[0], ffn_in[0], attn_out[0], misc], axis=1).astype(bf16),
        ALL,
        axis=0,
        tiled=True,
    )
    fo_pack = lax.all_gather(ffn_out.astype(bf16), ALL, axis=1, tiled=True)
    dec_pack = lax.all_gather(
        jnp.concatenate(
            [attn_in[1], attn_in[2], ffn_in[1], attn_out[1], attn_out[2]], axis=1
        ).astype(bf16),
        ALL,
        axis=0,
        tiled=True,
    )
    cut = lambda pack, start, width: lax.slice_in_dim(pack, start, start + width, axis=1)
    enc_wi, enc_fi = cut(enc_pack, 0, 3 * D), cut(enc_pack, 3 * D, 2 * FF)
    enc_wo, misc_all = cut(enc_pack, 3 * D + 2 * FF, D), cut(enc_pack, 4 * D + 2 * FF, 128)
    dec_wi, cross_wi = cut(dec_pack, 0, 3 * D), cut(dec_pack, 3 * D, 3 * D)
    dec_fi = cut(dec_pack, 6 * D, 2 * FF)
    dec_wo, cross_wo = cut(dec_pack, 6 * D + 2 * FF, D), cut(dec_pack, 7 * D + 2 * FF, D)
    enc_fo, dec_fo = fo_pack[0], fo_pack[1]
    gain = misc_all[:, :7].T.astype(f32)
    rel_all = jnp.transpose(misc_all[:, 7].reshape(-1, 2, rel_table.shape[1]), (1, 0, 2))
    rel_all = rel_all.reshape(2, BUCKETS, HEADS)

    flat = jnp.concatenate(
        [
            enc_ids[0],
            sentinel[0],
            dec_ids[0],
            target_ids[0],
            target_mask[0],
            enc_segs[0],
            dec_segs[0],
            jnp.pad(mode[0], (0, 128 - mode.shape[1])),
        ]
    )
    flat = lax.ppermute(flat, ("core", "seq"), [(0, 0), (1, 2), (2, 1), (3, 3)])
    sizes = [enc_count, enc_count, dec_count, dec_count, dec_count, enc_len, dec_len]
    pieces, start = [], 0
    for size in sizes:
        pieces.append(flat[start : start + size])
        start += size
    enc_id, sent, dec_id, targets, mask_i, enc_seg_all, dec_seg_all = pieces
    mode_row = flat[start : start + mode.shape[1]]
    mask = mask_i.astype(f32)

    enc_seg = lax.dynamic_slice_in_dim(enc_seg_all, core * enc_count, enc_count)
    enc_seg_other = lax.dynamic_slice_in_dim(enc_seg_all, (1 - core) * enc_count, enc_count)
    dec_seg = lax.dynamic_slice_in_dim(dec_seg_all, core * dec_count, dec_count)
    dec_seg_other = lax.dynamic_slice_in_dim(dec_seg_all, (1 - core) * dec_count, dec_count)
    enc_range = jnp.arange(enc_count, dtype=jnp.int32)
    dec_range = jnp.arange(dec_count, dtype=jnp.int32)
    enc_pos, enc_pos_other = core * enc_count + enc_range, (1 - core) * enc_count + enc_range
    dec_pos, dec_pos_other = core * dec_count + dec_range, (1 - core) * dec_count + dec_range
    prior_all = jnp.concatenate([enc_seg_all[:1], enc_seg_all[:-1]])
    prior = lax.dynamic_slice_in_dim(prior_all, core * enc_count, enc_count)
    first = (enc_pos == 0) | (enc_seg != prior)
    mode_of = jnp.sum(
        jnp.where(
            enc_seg[:, None] == jnp.arange(mode.shape[1], dtype=jnp.int32)[None], mode_row[None], 0
        ),
        axis=1,
    )
    enc_tok = jnp.where(sent == 1, V - 1 - enc_seg, enc_id)
    enc_tok = jnp.where(first, V - 101 - mode_of, enc_tok)
    local_ids = jnp.concatenate([enc_tok, dec_id])

    line_ids = gather_small(local_ids, ("z",))
    line_flat = line_ids.reshape(-1)
    plane_rows = plane_size * shard
    rel_id = line_flat - z_at * plane_rows
    inside = (rel_id >= 0) & (rel_id < plane_rows)
    place = jnp.where(inside, (rel_id // shard) * padded + rel_id % shard, -1)
    got = jnp.take(plane_table, jnp.maximum(place, 0), axis=0)
    got = jnp.where(inside[:, None], got, jnp.zeros((), bf16))
    looked = lax.psum_scatter(got, "z", scatter_dimension=0, tiled=True).astype(f32)
    enc_x0, dec_y0 = looked[:enc_count], looked[enc_count:]

    enc_x8, enc_picks = bias_eights(rel_all[0], buckets[0], core, enc_count, enc_count)
    dec_x8, dec_picks = bias_eights(rel_all[1], buckets[1], core, dec_count, dec_count)
    col, line = (lambda v: v[:, None]), (lambda v: v[None, :])
    enc_info = (
        col(enc_seg), line(enc_seg), line(enc_seg_other),
        col(enc_pos), line(enc_pos), line(enc_pos_other),
    )
    dec_info = (
        col(dec_seg), line(dec_seg), line(dec_seg_other),
        col(dec_pos), line(dec_pos), line(dec_pos_other),
    )
    cross_info = (
        col(dec_seg), line(enc_seg), line(enc_seg_other),
        col(dec_pos), line(enc_pos), line(enc_pos_other),
    )

    enc_n1 = rms_scale(enc_x0, gain[0]).astype(bf16)
    enc_q = project(enc_n1, enc_wi[:, :D]).astype(bf16)
    enc_kv = project(enc_n1, enc_wi[:, D:]).astype(bf16)
    enc_kv2 = swap_core(enc_kv)
    enc_ob = attend_forward(enc_q, enc_kv, enc_kv2, enc_info, enc_x8, False)
    enc_x1 = enc_x0 + project(enc_ob, enc_wo)
    enc_x2, enc_saved = ffn_forward(enc_x1, gain[1], enc_fi, enc_fo)
    enc_out = rms_scale(enc_x2, gain[2]).astype(bf16)

    dec_n1 = rms_scale(dec_y0, gain[3]).astype(bf16)
    dec_q = project(dec_n1, dec_wi[:, :D]).astype(bf16)
    dec_kv = project(dec_n1, dec_wi[:, D:]).astype(bf16)
    dec_kv2 = swap_core(dec_kv)
    dec_ob = attend_forward(dec_q, dec_kv, dec_kv2, dec_info, dec_x8, True)
    dec_y1 = dec_y0 + project(dec_ob, dec_wo)
    cross_kv = project(enc_out, cross_wi[:, D:]).astype(bf16)
    cross_kv2 = swap_core(cross_kv)
    cross_n = rms_scale(dec_y1, gain[4]).astype(bf16)
    cross_q = project(cross_n, cross_wi[:, :D]).astype(bf16)
    cross_ob = attend_forward(cross_q, cross_kv, cross_kv2, cross_info, None, False)
    dec_y2 = dec_y1 + project(cross_ob, cross_wo)
    dec_y3, dec_saved = ffn_forward(dec_y2, gain[5], dec_fi, dec_fo)
    head_scale = D ** (-0.5)
    hidden_b = (rms_scale(dec_y3, gain[6]) * head_scale).astype(bf16)

    hidden_all = lax.all_gather(hidden_b, ALL, axis=0, tiled=True)
    info = gather_small(jnp.stack([targets, mask_i]), ALL)
    targets_all = info[:, 0].reshape(1, -1) - device * shard
    mask_all = info[:, 1].reshape(1, -1).astype(f32)
    lse_part, picked = head_stats(hidden_all, table_b, targets_all, shard)
    lse = fold_all(lse_part, add_logs)
    d_hidden_all, head_embed = head_grad(
        hidden_all, table_b, targets_all, mask_all, lse, shard
    )
    d_hidden = lax.psum_scatter(d_hidden_all, ALL, scatter_dimension=0, tiled=True).astype(f32)
    lse_mine = lax.dynamic_slice_in_dim(lse[0], device * dec_count, dec_count)
    loss_local = jnp.sum(mask * lse_mine) - jnp.sum(mask_all * picked)

    d_y3, d_gain_final = norm_pull(dec_y3, gain[6], head_scale, d_hidden)
    d_y2, d_gain_dffn, d_dec_fi, d_dec_fo = ffn_backward(
        d_y3, dec_y2, gain[5], dec_fi, dec_fo, dec_saved
    )
    d_cross_wo, d_cross_ob = branch_backward(d_y2, cross_ob, cross_wo)
    d_cross_q, own, other = attend_backward(
        d_cross_ob, cross_q, cross_kv, cross_kv2, cross_info, None, False
    )
    got = (own + swap_core(other).astype(f32)).astype(bf16)
    d_cross_kv = jnp.concatenate([got[0], got[1]], axis=1)
    d_cross_wq = weight_grad(cross_n, d_cross_q)
    d_y1_norm, d_gain_cross = norm_pull(
        dec_y1, gain[4], 1.0, input_grad(d_cross_q, cross_wi[:, :D])
    )
    d_y1 = d_y2 + d_y1_norm
    d_cross_wkv = weight_grad(enc_out, d_cross_kv)
    d_dec_wo, d_dec_ob = branch_backward(d_y1, dec_ob, dec_wo)
    d_dec_q, own, other, dec_y8 = attend_backward(
        d_dec_ob, dec_q, dec_kv, dec_kv2, dec_info, dec_x8, True
    )
    got = (own + swap_core(other).astype(f32)).astype(bf16)
    d_dec_qkv = jnp.concatenate([d_dec_q, got[0], got[1]], axis=1)
    d_dec_table = bias_gradient(dec_y8, dec_picks, core, dec_count, dec_count)
    d_dec_wi = weight_grad(dec_n1, d_dec_qkv)
    d_y0_norm, d_gain_datt = norm_pull(dec_y0, gain[3], 1.0, input_grad(d_dec_qkv, dec_wi))
    d_y0 = d_y1 + d_y0_norm
    dec_grads = lax.psum_scatter(
        jnp.concatenate(
            [
                d_dec_wi.astype(bf16),
                d_cross_wq.astype(bf16),
                d_cross_wkv.astype(bf16),
                d_dec_fi,
                d_dec_wo,
                d_cross_wo,
            ],
            axis=1,
        ),
        ALL,
        scatter_dimension=0,
        tiled=True,
    ).astype(f32)

    d_x2, d_gain_efin = norm_pull(
        enc_x2, gain[2], 1.0, input_grad(d_cross_kv, cross_wi[:, D:])
    )
    d_x1, d_gain_effn, d_enc_fi, d_enc_fo = ffn_backward(
        d_x2, enc_x1, gain[1], enc_fi, enc_fo, enc_saved
    )
    fo_grads = lax.psum_scatter(
        jnp.stack([d_enc_fo, d_dec_fo]), ALL, scatter_dimension=1, tiled=True
    ).astype(f32)
    d_enc_wo, d_enc_ob = branch_backward(d_x1, enc_ob, enc_wo)
    d_enc_q, own, other, enc_y8 = attend_backward(
        d_enc_ob, enc_q, enc_kv, enc_kv2, enc_info, enc_x8, False
    )
    got = (own + swap_core(other).astype(f32)).astype(bf16)
    d_enc_qkv = jnp.concatenate([d_enc_q, got[0], got[1]], axis=1)
    d_enc_table = bias_gradient(enc_y8, enc_picks, core, enc_count, enc_count)
    d_enc_wi = weight_grad(enc_n1, d_enc_qkv)
    d_x0_norm, d_gain_eatt = norm_pull(enc_x0, gain[0], 1.0, input_grad(d_enc_qkv, enc_wi))
    d_x0 = d_x1 + d_x0_norm

    d_inputs = jnp.concatenate([d_x0, d_y0]).astype(bf16)
    d_line = lax.all_gather(d_inputs, "z", axis=0, tiled=True)
    placed = place_rows(place[None, :], d_line, plane_size, padded)
    input_embed = lax.psum_scatter(placed, PLANE, scatter_dimension=0, tiled=True)
    grad_embed = head_embed[:shard] + input_embed[:shard].astype(f32)

    d_gains = jnp.stack(
        [
            d_gain_eatt,
            d_gain_effn,
            d_gain_efin,
            d_gain_datt,
            d_gain_cross,
            d_gain_dffn,
            d_gain_final,
        ]
    )
    d_rel = jnp.stack([d_enc_table.reshape(-1), d_dec_table.reshape(-1)])
    d_rel = jnp.transpose(d_rel.reshape(2, -1, rel_table.shape[1]), (1, 0, 2)).reshape(D, 1)
    d_misc = jnp.pad(jnp.concatenate([d_gains.T, d_rel], axis=1), ((0, 0), (0, 120)))
    enc_grads = lax.psum_scatter(
        jnp.concatenate([d_enc_wi.astype(bf16), d_enc_fi, d_enc_wo, d_misc.astype(bf16)], axis=1),
        ALL,
        scatter_dimension=0,
        tiled=True,
    ).astype(f32)
    owned = (
        jnp.stack(
            [cut(enc_grads, 0, 3 * D), cut(dec_grads, 0, 3 * D), cut(dec_grads, 3 * D, 3 * D)]
        ),
        jnp.stack(
            [
                cut(enc_grads, 3 * D + 2 * FF, D),
                cut(dec_grads, 6 * D + 2 * FF, D),
                cut(dec_grads, 7 * D + 2 * FF, D),
            ]
        ),
        jnp.stack([cut(enc_grads, 3 * D, 2 * FF), cut(dec_grads, 6 * D, 2 * FF)]),
        fo_grads,
        enc_grads[:, 4 * D + 2 * FF + 7].reshape(2, -1),
        enc_grads[:, 4 * D + 2 * FF : 4 * D + 2 * FF + 7].T,
    )
    grads = (grad_embed,) + owned
    squares = sum((jnp.sum(item * item) for item in grads))
    sums = fold_all(jnp.stack([jnp.sum(mask), loss_local, squares]), jnp.add)
    count_all, loss_all, squares_all = sums[0], sums[1], sums[2]
    grad_norm = jnp.sqrt(squares_all) / count_all
    factor = jnp.minimum(1.0, clip_limit / grad_norm) / count_all
    weights = (embed, attn_in, attn_out, ffn_in, ffn_out, rel_table, gains)
    moments = [
        (m_embed, v_embed),
        (m_attn_in, v_attn_in),
        (m_attn_out, v_attn_out),
        (m_ffn_in, v_ffn_in),
        (m_ffn_out, v_ffn_out),
        (m_rel, v_rel),
        (m_gains, v_gains),
    ]
    settings = [
        (1.0, 0.01),
        (0.05, 0.01),
        (0.05, 0.01),
        (0.05, 0.01),
        (0.05, 0.01),
        (0.3, 0.0),
        (0.3, 0.0),
    ]
    results = [loss_all / count_all, grad_norm]
    for slot_number, (param, grad, pair, setting) in enumerate(
        zip(weights, grads, moments, settings)
    ):
        clipped = grad * factor
        first_new, second_new, new_param = adamw(
            param, clipped, pair[0], pair[1], float(STEP), setting[0], setting[1]
        )
        results.extend((clipped if slot_number == 0 else first_new, second_new, new_param))
    return tuple(results)


def solution(mesh):
    rows = ("z", "p", "core")
    every = ALL
    inner = Mesh(mesh.devices.reshape(4, -1, 2, mesh.devices.shape[1]), ALL)
    mat = P(None, every, None)
    vec = P(None, every)
    emb = P(every, None)
    in_specs = (
        P(rows, "seq"),
        P(rows, None),
        P(rows, "seq"),
        P(rows, None),
        P(rows, "seq"),
        P(rows, None),
        P(rows, "seq"),
        P(rows, "seq"),
        P(),
        emb,
        mat,
        mat,
        mat,
        mat,
        vec,
        vec,
        emb,
        emb,
    ) + (mat,) * 8 + (vec,) * 4
    out_specs = (P(), P()) + (emb,) * 3 + (mat,) * 12 + (vec,) * 6
    return jax.shard_map(body, mesh=inner, in_specs=in_specs, out_specs=out_specs, check_vma=False)
```

```python
import functools

import jax
import jax.numpy as jnp
from jax import lax
from jax.experimental import pallas as pl
from jax.experimental.pallas import tpu as pltpu
from jax.sharding import Mesh
from jax.sharding import PartitionSpec as P

D = 768
HEADS = 12
HEAD_DIM = 64
FF = 2048
V = 32128
BUCKETS = 32
STEP = 10

masked_out = -1e30
clip_limit = 0.01
ALL = ("z", "p", "core", "seq")
PLANE = ("p", "core", "seq")
bf16 = jnp.bfloat16
f32 = jnp.float32
VMEM_LIMIT = 56 * 1024 * 1024


def rms_scale(values, gain):
    return values * lax.rsqrt(jnp.mean(values * values, axis=-1, keepdims=True) + 1e-06) * gain


def norm_pull(values, gain, factor, upstream):
    _, pull = jax.vjp(lambda left, right: rms_scale(left, right) * factor, values, gain)
    return pull(upstream)


def gate_up(both):
    return jax.nn.gelu(both[:, :FF], approximate=True) * both[:, FF:]


def project(left, right):
    return jnp.dot(left, right, preferred_element_type=f32)


def weight_grad(inputs, grads):
    return jnp.einsum("td,te->de", inputs, grads, preferred_element_type=f32)


def input_grad(grads, weight):
    return jnp.einsum("te,de->td", grads, weight, preferred_element_type=f32)


def dot_nt(a, b):
    return lax.dot_general(a, b, (((1,), (1,)), ((), ())), preferred_element_type=f32)


def dot_tn(a, b):
    return lax.dot_general(a, b, (((0,), (0,)), ((), ())), preferred_element_type=f32)


def dot_nn(a, b):
    return lax.dot_general(a, b, (((1,), (0,)), ((), ())), preferred_element_type=f32)


def spread(eight, rows, width):
    total = eight.shape[-1]
    grid = eight
    have = 8
    while have < rows:
        grid = jnp.concatenate([pltpu.roll(grid, total - have, 1), grid], axis=0)
        have *= 2
    return grid[:, :width]


def collect(grid, total):
    rows, width = grid.shape
    have = jnp.concatenate([grid, jnp.zeros((rows, total - width), f32)], axis=1)
    while rows > 8:
        rows //= 2
        have = pltpu.roll(have[:rows], rows, 1) + have[rows:]
    return have


def probs_of(cfg, refs, block, head):
    bq, has_bias, causal = cfg
    rows = slice(block * bq, (block + 1) * bq)
    cols = slice(head * HEAD_DIM, (head + 1) * HEAD_DIM)
    query = refs["q"][rows, cols]
    scores = []
    for part in range(2):
        keys = refs["k"][part][:, cols]
        s = dot_nt(query, keys) * HEAD_DIM ** (-0.5)
        if has_bias:
            s = s + spread(refs["x8"][block, part, head], bq, keys.shape[0])
        allowed = refs["qseg"][rows, :] == refs["kseg"][part]
        if causal:
            allowed = allowed & (refs["kpos"][part] <= refs["qpos"][rows, :])
        scores.append(jnp.where(allowed, s, masked_out))
    top = jnp.maximum(
        jnp.max(scores[0], axis=1, keepdims=True), jnp.max(scores[1], axis=1, keepdims=True)
    )
    exps = [jnp.exp(s - top) for s in scores]
    total = jnp.sum(exps[0], axis=1, keepdims=True) + jnp.sum(exps[1], axis=1, keepdims=True)
    scale = 1.0 / total
    return query, [e * scale for e in exps]


def name_refs(cfg, refs):
    bq, has_bias, causal = cfg
    it = iter(refs)
    named = {"q": next(it)}
    k0, v0, k1, v1 = next(it), next(it), next(it), next(it)
    named["k"], named["v"] = (k0, k1), (v0, v1)
    ids = next(it), next(it), next(it), next(it), next(it), next(it)
    named["qseg"], named["kseg"] = ids[0], (ids[1][...], ids[2][...])
    named["qpos"], named["kpos"] = ids[3], (ids[4][...], ids[5][...])
    if has_bias:
        named["x8"] = next(it)
    return named, list(it)


def attend_forward_kernel(cfg, *refs):
    named, (out,) = name_refs(cfg, refs)
    bq = cfg[0]
    for block in range(named["q"].shape[0] // bq):
        for head in range(2):
            cols = slice(head * HEAD_DIM, (head + 1) * HEAD_DIM)
            _, probs = probs_of(cfg, named, block, head)
            acc = dot_nn(probs[0].astype(bf16), named["v"][0][:, cols])
            acc = acc + dot_nn(probs[1].astype(bf16), named["v"][1][:, cols])
            out[block * bq : (block + 1) * bq, cols] = acc.astype(bf16)


def attend_backward_kernel(cfg, *refs):
    named, rest = name_refs(cfg, refs)
    bq, has_bias, causal = cfg
    if has_bias:
        grad, dq, own, other, y8 = rest
    else:
        grad, dq, own, other = rest
    blocks = named["q"].shape[0] // bq
    for head in range(2):
        cols = slice(head * HEAD_DIM, (head + 1) * HEAD_DIM)
        dk, dv = [None, None], [None, None]
        for block in range(blocks):
            rows = slice(block * bq, (block + 1) * bq)
            query, probs = probs_of(cfg, named, block, head)
            do = grad[rows, cols]
            dp = [dot_nt(do, named["v"][part][:, cols]) for part in range(2)]
            delta = jnp.sum(probs[0] * dp[0], axis=1, keepdims=True) + jnp.sum(
                probs[1] * dp[1], axis=1, keepdims=True
            )
            acc = None
            for part in range(2):
                ds = (probs[part] * (dp[part] - delta)).astype(bf16)
                term = dot_nn(ds, named["k"][part][:, cols])
                acc = term if acc is None else acc + term
                k_term = dot_tn(query, ds)
                v_term = dot_tn(do, probs[part].astype(bf16))
                dk[part] = k_term if dk[part] is None else dk[part] + k_term
                dv[part] = v_term if dv[part] is None else dv[part] + v_term
                if has_bias:
                    y8[block, part, head] = collect(ds.astype(f32), y8.shape[-1])
            dq[rows, cols] = (acc * HEAD_DIM ** (-0.5)).astype(bf16)
        for part, target in enumerate((own, other)):
            target[0, :, cols] = (dk[part] * HEAD_DIM ** (-0.5)).T.astype(target.dtype)
            target[1, :, cols] = dv[part].T.astype(target.dtype)


def attend_specs(q_len, k_len, has_bias, x8):
    whole = lambda shape: pl.BlockSpec(shape, lambda i: (0,) * len(shape))
    kv = [
        pl.BlockSpec((k_len, 128), lambda i: (0, i)),
        pl.BlockSpec((k_len, 128), lambda i: (0, i + 6)),
    ]
    specs = [pl.BlockSpec((q_len, 128), lambda i: (0, i))] + kv + kv
    specs += [whole((q_len, 1)), whole((1, k_len)), whole((1, k_len))] * 2
    if has_bias:
        specs.append(
            pl.BlockSpec((x8.shape[0], 2, 2, 8, x8.shape[-1]), lambda i: (0, 0, i, 0, 0))
        )
    return specs


def attend_args(q, kv_own, kv_other, ids, x8):
    args = [q, kv_own, kv_own, kv_other, kv_other] + list(ids)
    if x8 is not None:
        args.append(x8)
    return args


def attend_cost(q_len, k_len, products):
    size = HEADS * q_len * 2 * k_len
    return pl.CostEstimate(
        flops=2 * products * size * HEAD_DIM, bytes_accessed=8 * D * (q_len + 4 * k_len),
        transcendentals=size,
    )


def attend_forward(q, kv_own, kv_other, ids, x8, causal):
    q_len, k_len = q.shape[0], kv_own.shape[0]
    cfg = (256, x8 is not None, causal)
    return pl.pallas_call(
        functools.partial(attend_forward_kernel, cfg),
        grid=(HEADS // 2,),
        in_specs=attend_specs(q_len, k_len, x8 is not None, x8),
        out_specs=pl.BlockSpec((q_len, 128), lambda i: (0, i)),
        out_shape=jax.ShapeDtypeStruct((q_len, D), bf16),
        compiler_params=pltpu.CompilerParams(vmem_limit_bytes=VMEM_LIMIT),
        cost_estimate=attend_cost(q_len, k_len, 2),
    )(*attend_args(q, kv_own, kv_other, ids, x8))


def attend_backward(grad, q, kv_own, kv_other, ids, x8, causal):
    q_len, k_len = q.shape[0], kv_own.shape[0]
    cfg = (256, x8 is not None, causal)
    kv_spec = pl.BlockSpec((2, k_len, 128), lambda i: (0, 0, i))
    out_specs = [pl.BlockSpec((q_len, 128), lambda i: (0, i)), kv_spec, kv_spec]
    out_shape = [
        jax.ShapeDtypeStruct((q_len, D), bf16),
        jax.ShapeDtypeStruct((2, k_len, D), f32),
        jax.ShapeDtypeStruct((2, k_len, D), bf16),
    ]
    if x8 is not None:
        out_specs.append(
            pl.BlockSpec((x8.shape[0], 2, 2, 8, x8.shape[-1]), lambda i: (0, 0, i, 0, 0))
        )
        out_shape.append(jax.ShapeDtypeStruct(x8.shape, f32))
    return pl.pallas_call(
        functools.partial(attend_backward_kernel, cfg),
        grid=(HEADS // 2,),
        in_specs=attend_specs(q_len, k_len, x8 is not None, x8)
        + [pl.BlockSpec((q_len, 128), lambda i: (0, i))],
        out_specs=out_specs,
        out_shape=out_shape,
        compiler_params=pltpu.CompilerParams(vmem_limit_bytes=VMEM_LIMIT),
        cost_estimate=attend_cost(q_len, k_len, 5),
    )(*attend_args(q, kv_own, kv_other, ids, x8), grad)


def bias_bases(core, q_len, k_len, offset):
    bases = []
    for block in range(q_len // 256):
        for part in range(2):
            k_start = (core if part == 0 else 1 - core) * k_len
            q_start = core * q_len + block * 256
            bases.append(k_start - q_start - 255 + offset)
    return bases


def bias_eights(table, bucket_row, core, q_len, k_len):
    size = bucket_row.shape[0]
    picks = (bucket_row[None, :] == jnp.arange(BUCKETS, dtype=jnp.int32)[:, None]).astype(bf16)
    per_offset = jnp.einsum("bh,bn->hn", table, picks, preferred_element_type=f32)
    per_offset = jnp.pad(per_offset, ((0, 0), (0, 16)))
    width = k_len + 256
    found = []
    for base in bias_bases(core, q_len, k_len, size // 2):
        window = lax.dynamic_slice_in_dim(per_offset, base, width + 7, axis=1)
        found.append(jnp.stack([window[:, 7 - r : 7 - r + width] for r in range(8)], axis=1))
    return jnp.stack(found).reshape(q_len // 256, 2, HEADS, 8, width), picks


def bias_gradient(y8, picks, core, q_len, k_len):
    size = picks.shape[1]
    width = k_len + 256
    total = jnp.zeros((HEADS, size + 16), f32)
    flat = y8.reshape(-1, HEADS, 8, width)
    for number, base in enumerate(bias_bases(core, q_len, k_len, size // 2)):
        window = sum(
            jnp.pad(flat[number, :, r], ((0, 0), (7 - r, r))) for r in range(8)
        )
        old = lax.dynamic_slice_in_dim(total, base, width + 7, axis=1)
        total = lax.dynamic_update_slice_in_dim(total, old + window, base, axis=1)
    return jnp.einsum(
        "bn,hn->bh", picks.astype(f32), total[:, :size], precision=lax.Precision.HIGHEST
    )


def head_stats_kernel(count, hid, tab, tgt, lse_out, pick_out):
    logits = dot_nt(tab[...], hid[...].reshape(-1, D))
    row = lax.broadcasted_iota(jnp.int32, logits.shape, 0)
    pick_out[...] = jnp.sum(jnp.where(row == tgt[...], logits, 0.0), axis=0, keepdims=True)
    logits = jnp.where(row < count, logits, masked_out)
    top = jnp.max(logits, axis=0, keepdims=True)
    lse_out[...] = top + jnp.log(jnp.sum(jnp.exp(logits - top), axis=0, keepdims=True))


def head_grad_kernel(count, hid, tab, tgt, msk, lse, dhid, dtab):
    tokens = hid[...].reshape(-1, D)
    logits = dot_nt(tab[...], tokens)
    row = lax.broadcasted_iota(jnp.int32, logits.shape, 0)
    soft = jnp.exp(jnp.where(row < count, logits, masked_out) - lse[...])
    grad = ((soft - jnp.where(row == tgt[...], 1.0, 0.0)) * msk[...]).astype(bf16)
    dhid[...] = dot_tn(grad, tab[...]).astype(bf16).reshape(dhid.shape)
    term = dot_nn(grad, tokens)

    @pl.when(pl.program_id(0) == 0)
    def _():
        dtab[...] = term

    @pl.when(pl.program_id(0) != 0)
    def _():
        dtab[...] += term


def head_stats(hidden, table, targets, count):
    devices, each, _ = hidden.shape
    tokens, rows = devices * each, table.shape[0]
    steps = devices // 4
    line = pl.BlockSpec((1, 2 * each), lambda h, i: (0, h * steps + i))
    return pl.pallas_call(
        functools.partial(head_stats_kernel, count),
        grid=(2, steps),
        in_specs=[
            pl.BlockSpec((4, each // 2, D), lambda h, i: (i, h, 0)),
            pl.BlockSpec((rows, D), lambda h, i: (0, 0)),
            line,
        ],
        out_specs=[line, line],
        out_shape=[jax.ShapeDtypeStruct((1, tokens), f32)] * 2,
        compiler_params=pltpu.CompilerParams(vmem_limit_bytes=VMEM_LIMIT),
        cost_estimate=pl.CostEstimate(
            flops=2 * tokens * rows * D, bytes_accessed=2 * tokens * D, transcendentals=tokens * rows
        ),
    )(hidden, table, targets)


def head_grad(hidden, table, targets, mask, lse, count, half):
    devices, each, _ = hidden.shape
    tokens, rows = devices * each // 2, table.shape[0]
    steps = devices // 4
    line = pl.BlockSpec((1, 2 * each), lambda i: (0, half * steps + i))
    return pl.pallas_call(
        functools.partial(head_grad_kernel, count),
        grid=(steps,),
        in_specs=[
            pl.BlockSpec((4, each // 2, D), lambda i: (i, half, 0)),
            pl.BlockSpec((rows, D), lambda i: (0, 0)),
            line,
            line,
            line,
        ],
        out_specs=[
            pl.BlockSpec((4, each // 2, D), lambda i: (i, 0, 0)),
            pl.BlockSpec((rows, D), lambda i: (0, 0)),
        ],
        out_shape=[
            jax.ShapeDtypeStruct((devices, each // 2, D), bf16),
            jax.ShapeDtypeStruct((rows, D), f32),
        ],
        compiler_params=pltpu.CompilerParams(vmem_limit_bytes=VMEM_LIMIT),
        cost_estimate=pl.CostEstimate(
            flops=6 * tokens * rows * D, bytes_accessed=4 * tokens * D, transcendentals=tokens * rows
        ),
    )(hidden, table, targets, mask, lse)


def place_kernel(first, *refs):
    out = refs[-1]
    rows = out.shape[0]
    base = (pl.program_id(0) + first) * rows
    total = None
    for ids, grads in zip(refs[:-1:2], refs[1:-1:2]):
        row = lax.broadcasted_iota(jnp.int32, (rows, ids.shape[1]), 0) + base
        hot = jnp.where(row == ids[...], 1.0, 0.0).astype(bf16)
        term = dot_nn(hot, grads[...])
        total = term if total is None else total + term
    out[...] = total.astype(bf16)


def place_rows(pairs, first, parts, rows):
    tokens = sum(grads.shape[0] for _, grads in pairs)
    specs, args = [], []
    for ids, grads in pairs:
        specs.append(pl.BlockSpec(ids.shape, lambda i: (0, 0)))
        specs.append(pl.BlockSpec(grads.shape, lambda i: (0, 0)))
        args += [ids, grads]
    return pl.pallas_call(
        functools.partial(place_kernel, first),
        grid=(parts,),
        in_specs=specs,
        out_specs=pl.BlockSpec((rows, D), lambda i: (i, 0)),
        out_shape=jax.ShapeDtypeStruct((parts * rows, D), bf16),
        compiler_params=pltpu.CompilerParams(vmem_limit_bytes=VMEM_LIMIT),
        cost_estimate=pl.CostEstimate(
            flops=2 * tokens * parts * rows * D, bytes_accessed=2 * parts * rows * D, transcendentals=0
        ),
    )(*args)


def gather_axis(value, axis):
    size = lax.axis_size(axis)
    me = lax.axis_index(axis)
    got = [value]
    for step in range(1, size):
        got.append(lax.ppermute(value, axis, [(i, (i + step) % size) for i in range(size)]))
    stacked = jnp.stack(got)
    return jnp.take(stacked, (me - jnp.arange(size, dtype=jnp.int32)) % size, axis=0)


def gather_small(value, axes):
    shape = value.shape
    for axis in reversed(axes):
        value = gather_axis(value, axis)
        value = value.reshape((-1,) + shape)
    return value


def fold_all(value, combine):
    for axis in reversed(ALL):
        size = lax.axis_size(axis)
        hop = 1
        while hop < size:
            other = lax.ppermute(value, axis, [(i, i ^ hop) for i in range(size)])
            value = combine(value, other)
            hop *= 2
    return value


def swap(value, axis):
    return lax.ppermute(value, axis, [(0, 1), (1, 0)])


def swap_core(value):
    return swap(value, "core")


def add16(left, right):
    return (left.astype(f32) + right.astype(f32)).astype(bf16)


def pick(value, index, dim):
    return lax.dynamic_index_in_dim(value, index, dim, keepdims=False)


def scatter_pair(value, axis, dim):
    if lax.axis_size(axis) != 2:
        return lax.psum_scatter(value, axis, scatter_dimension=dim, tiled=False)
    me = lax.axis_index(axis)
    got = swap(pick(value, 1 - me, dim), axis)
    return add16(pick(value, me, dim), got)


def scatter_chain(value, seq_first):
    sizes = tuple(lax.axis_size(axis) for axis in ALL)
    value = value.reshape(sizes + (-1, value.shape[-1]))
    value = scatter_pair(value, "core", 2)
    if seq_first:
        value = scatter_pair(scatter_pair(value, "seq", 2), "p", 1)
    else:
        value = scatter_pair(scatter_pair(value, "p", 1), "seq", 1)
    size, me = sizes[0], lax.axis_index("z")
    total = pick(value, me, 0).astype(f32)
    for hop in range(1, size):
        send = pick(value, (me + hop) % size, 0)
        got = lax.ppermute(send, "z", [(i, (i + hop) % size) for i in range(size)])
        total = total + got.astype(f32)
    return total


def line_gather(value, axis):
    size = lax.axis_size(axis)
    ups, downs = [value], [value]
    for _ in range(1, size):
        ups.append(lax.ppermute(ups[-1], axis, [(i, i + 1) for i in range(size - 1)]))
        downs.append(lax.ppermute(downs[-1], axis, [(i + 1, i) for i in range(size - 1)]))
    return [value] + [ups[k] + downs[size - k] for k in range(1, size)]


def line_scatter(parts, axis):
    size = lax.axis_size(axis)
    up, down = None, None
    for step in range(1, size):
        far = size - step
        send_up, send_down = parts[size - far], parts[far]
        if up is not None:
            send_up, send_down = send_up + up, send_down + down
        up = lax.ppermute(send_up, axis, [(i, i + 1) for i in range(step)])
        down = lax.ppermute(send_down, axis, [(size - 1 - i, size - 2 - i) for i in range(step)])
    return parts[0].astype(f32) + up.astype(f32) + down.astype(f32)


def plane_gather(table):
    if lax.axis_size("p") != 2:
        return lax.all_gather(table, PLANE, axis=0, tiled=True)
    half = table.shape[0] // 2
    by_seq, by_p = swap(table, "seq"), swap(table, "p")
    far = [swap(by_p[:half], "seq"), swap(by_seq[half:], "p")]
    mine = [table, by_seq, by_p] + far
    return jnp.concatenate(mine + [swap_core(item) for item in mine])


def plane_slot(owner):
    if lax.axis_size("p") != 2:
        return owner
    other = owner ^ lax.axis_index(PLANE)
    return ((other >> 1) & 1) * 4 + (other >> 2) * 2 + (other & 1)


def plane_scatter(pairs, rows):
    count = lax.axis_size(PLANE)
    if lax.axis_size("p") != 2:
        placed = place_rows(pairs, 0, count, rows)
        return lax.psum_scatter(placed, PLANE, scatter_dimension=0, tiled=True).astype(f32)
    away = swap_core(place_rows(pairs, 4, 4, rows))
    home = place_rows(pairs, 0, 4, rows)
    half = rows // 2
    part = lambda first, last: add16(home[first:last], away[first:last])
    got_low = swap(part(3 * rows, 3 * rows + half), "seq")
    got_high = swap(part(3 * rows + half, 4 * rows), "p")
    seq_high = add16(part(rows + half, 2 * rows), got_high)
    p_low = add16(part(2 * rows, 2 * rows + half), got_low)
    from_seq = swap(jnp.concatenate([part(rows, rows + half), seq_high]), "seq")
    from_p = swap(jnp.concatenate([p_low, part(2 * rows + half, 3 * rows)]), "p")
    return part(0, rows).astype(f32) + from_seq.astype(f32) + from_p.astype(f32)


def add_logs(left, right):
    top = jnp.maximum(left, right)
    return top + jnp.log(jnp.exp(left - top) + jnp.exp(right - top))


def ffn_forward(resid, gain, w_in, w_out):
    normed = rms_scale(resid, gain).astype(bf16)
    both = project(normed, w_in)
    hidden = gate_up(both).astype(bf16)
    return (resid + project(hidden, w_out), (normed, both, hidden))


def ffn_backward(upstream, resid, gain, w_in, w_out, saved):
    normed, both, hidden = saved
    grad_b = upstream.astype(bf16)
    d_out = weight_grad(hidden, grad_b).astype(bf16)
    _, pull = jax.vjp(gate_up, both)
    (d_both,) = pull(input_grad(grad_b, w_out))
    d_both_b = d_both.astype(bf16)
    d_in = weight_grad(normed, d_both_b).astype(bf16)
    d_resid, d_gain = norm_pull(resid, gain, 1.0, input_grad(d_both_b, w_in))
    return (upstream + d_resid, d_gain, d_in, d_out)


def branch_backward(upstream, out_b, w_out):
    grad_b = upstream.astype(bf16)
    return (weight_grad(out_b, grad_b).astype(bf16), input_grad(grad_b, w_out).astype(bf16))


def adamw(weight, grad, first_m, second_m, count, rate, decay):
    first_new = 0.9 * first_m + 0.1 * grad
    second_new = 0.999 * second_m + 0.001 * grad * grad
    first_hat = first_new / (1.0 - 0.9**count)
    second_hat = second_new / (1.0 - 0.999**count)
    return (
        first_new,
        second_new,
        weight - rate * (first_hat / (jnp.sqrt(second_hat) + 1e-08) + decay * weight),
    )


def body(
    enc_ids,
    enc_segs,
    sentinel,
    mode,
    dec_ids,
    dec_segs,
    target_ids,
    target_mask,
    buckets,
    embed,
    attn_in,
    attn_out,
    ffn_in,
    ffn_out,
    rel_table,
    gains,
    m_embed,
    v_embed,
    m_attn_in,
    v_attn_in,
    m_attn_out,
    v_attn_out,
    m_ffn_in,
    v_ffn_in,
    m_ffn_out,
    v_ffn_out,
    m_rel,
    v_rel,
    m_gains,
    v_gains,
):
    core = lax.axis_index("core")
    z_at = lax.axis_index("z")
    z_size = lax.axis_size("z")
    plane_size = lax.axis_size(PLANE)
    device = lax.axis_index(ALL)
    shard = embed.shape[0]
    padded = (shard // 16 + 1) * 16
    enc_count, dec_count = enc_ids.shape[1], dec_ids.shape[1]
    enc_len, dec_len = enc_segs.shape[1], dec_segs.shape[1]

    table_b = jnp.pad(embed.astype(bf16), ((0, padded - shard), (0, 0)))
    misc = jnp.concatenate([gains.T, rel_table.reshape(-1, 1)], axis=1)
    misc = jnp.pad(misc, ((0, 0), (0, 120)))
    shard_in = attn_in.shape[1]
    flat_out = ffn_out.astype(bf16).reshape(2, shard_in, -1)
    enc_cast = jnp.concatenate([attn_in[0], ffn_in[0], attn_out[0], misc], axis=1).astype(bf16)
    enc_pack = lax.all_gather(
        jnp.concatenate([enc_cast, flat_out[0]], axis=1), ALL, axis=0, tiled=True
    )
    dec_cast = jnp.concatenate(
        [attn_in[1], attn_in[2], ffn_in[1], attn_out[1], attn_out[2]], axis=1
    ).astype(bf16)
    dec_cast = jnp.concatenate([dec_cast, flat_out[1]], axis=1)
    dec_cast, _ = lax.optimization_barrier((dec_cast, enc_pack[0, 0]))
    dec_pack = lax.all_gather(dec_cast, ALL, axis=0, tiled=True)
    cut = lambda pack, start, width: lax.slice_in_dim(pack, start, start + width, axis=1)
    enc_wi, enc_fi = cut(enc_pack, 0, 3 * D), cut(enc_pack, 3 * D, 2 * FF)
    enc_wo, misc_all = cut(enc_pack, 3 * D + 2 * FF, D), cut(enc_pack, 4 * D + 2 * FF, 128)
    dec_wi, cross_wi = cut(dec_pack, 0, 3 * D), cut(dec_pack, 3 * D, 3 * D)
    dec_fi = cut(dec_pack, 6 * D, 2 * FF)
    dec_wo, cross_wo = cut(dec_pack, 6 * D + 2 * FF, D), cut(dec_pack, 7 * D + 2 * FF, D)
    enc_fo = cut(enc_pack, 4 * D + 2 * FF + 128, FF).reshape(FF, D)
    dec_fo = cut(dec_pack, 8 * D + 2 * FF, FF).reshape(FF, D)
    gain = misc_all[:, :7].T.astype(f32)
    rel_all = jnp.transpose(misc_all[:, 7].reshape(-1, 2, rel_table.shape[1]), (1, 0, 2))
    rel_all = rel_all.reshape(2, BUCKETS, HEADS)

    flat = jnp.concatenate(
        [
            enc_ids[0],
            sentinel[0],
            dec_ids[0],
            target_ids[0],
            target_mask[0],
            enc_segs[0],
            dec_segs[0],
            jnp.pad(mode[0], (0, 128 - mode.shape[1])),
        ]
    )
    flat = lax.ppermute(flat, ("core", "seq"), [(0, 0), (1, 2), (2, 1), (3, 3)])
    sizes = [enc_count, enc_count, dec_count, dec_count, dec_count, enc_len, dec_len]
    pieces, start = [], 0
    for size in sizes:
        pieces.append(flat[start : start + size])
        start += size
    enc_id, sent, dec_id, targets, mask_i, enc_seg_all, dec_seg_all = pieces
    mode_row = flat[start : start + mode.shape[1]]
    mask = mask_i.astype(f32)

    enc_seg = lax.dynamic_slice_in_dim(enc_seg_all, core * enc_count, enc_count)
    enc_seg_other = lax.dynamic_slice_in_dim(enc_seg_all, (1 - core) * enc_count, enc_count)
    dec_seg = lax.dynamic_slice_in_dim(dec_seg_all, core * dec_count, dec_count)
    dec_seg_other = lax.dynamic_slice_in_dim(dec_seg_all, (1 - core) * dec_count, dec_count)
    enc_range = jnp.arange(enc_count, dtype=jnp.int32)
    dec_range = jnp.arange(dec_count, dtype=jnp.int32)
    enc_pos, enc_pos_other = core * enc_count + enc_range, (1 - core) * enc_count + enc_range
    dec_pos, dec_pos_other = core * dec_count + dec_range, (1 - core) * dec_count + dec_range
    prior_all = jnp.concatenate([enc_seg_all[:1], enc_seg_all[:-1]])
    prior = lax.dynamic_slice_in_dim(prior_all, core * enc_count, enc_count)
    first = (enc_pos == 0) | (enc_seg != prior)
    mode_of = jnp.sum(
        jnp.where(
            enc_seg[:, None] == jnp.arange(mode.shape[1], dtype=jnp.int32)[None], mode_row[None], 0
        ),
        axis=1,
    )
    enc_tok = jnp.where(sent == 1, V - 1 - enc_seg, enc_id)
    enc_tok = jnp.where(first, V - 101 - mode_of, enc_tok)
    local_ids = jnp.concatenate([enc_tok, dec_id])

    plane_table = plane_gather(table_b)
    line_ids = line_gather(local_ids, "z")
    plane_rows = plane_size * shard
    places = []
    for ids in line_ids:
        rel_id = ids - z_at * plane_rows
        inside = (rel_id >= 0) & (rel_id < plane_rows)
        places.append(
            jnp.where(inside, plane_slot(rel_id // shard) * padded + rel_id % shard, shard)
        )
    enc_places = [item[:enc_count] for item in places]
    dec_places = [item[enc_count:] for item in places]
    look = lambda item: jnp.take(plane_table, item, axis=0, mode="clip")
    enc_x0 = line_scatter([look(item) for item in enc_places], "z")
    dec_y0 = line_scatter([look(item) for item in dec_places], "z")

    enc_x8, enc_picks = bias_eights(rel_all[0], buckets[0], core, enc_count, enc_count)
    dec_x8, dec_picks = bias_eights(rel_all[1], buckets[1], core, dec_count, dec_count)
    col, line = (lambda v: v[:, None]), (lambda v: v[None, :])
    enc_info = (
        col(enc_seg), line(enc_seg), line(enc_seg_other),
        col(enc_pos), line(enc_pos), line(enc_pos_other),
    )
    dec_info = (
        col(dec_seg), line(dec_seg), line(dec_seg_other),
        col(dec_pos), line(dec_pos), line(dec_pos_other),
    )
    cross_info = (
        col(dec_seg), line(enc_seg), line(enc_seg_other),
        col(dec_pos), line(enc_pos), line(enc_pos_other),
    )

    enc_n1 = rms_scale(enc_x0, gain[0]).astype(bf16)
    enc_q = project(enc_n1, enc_wi[:, :D]).astype(bf16)
    enc_kv = project(enc_n1, enc_wi[:, D:]).astype(bf16)
    enc_kv2 = swap_core(enc_kv)
    enc_ob = attend_forward(enc_q, enc_kv, enc_kv2, enc_info, enc_x8, False)
    enc_x1 = enc_x0 + project(enc_ob, enc_wo)
    enc_x2, enc_saved = ffn_forward(enc_x1, gain[1], enc_fi, enc_fo)
    enc_out = rms_scale(enc_x2, gain[2]).astype(bf16)

    dec_n1 = rms_scale(dec_y0, gain[3]).astype(bf16)
    dec_q = project(dec_n1, dec_wi[:, :D]).astype(bf16)
    dec_kv = project(dec_n1, dec_wi[:, D:]).astype(bf16)
    dec_kv2 = swap_core(dec_kv)
    dec_ob = attend_forward(dec_q, dec_kv, dec_kv2, dec_info, dec_x8, True)
    dec_y1 = dec_y0 + project(dec_ob, dec_wo)
    cross_kv = project(enc_out, cross_wi[:, D:]).astype(bf16)
    cross_kv2 = swap_core(cross_kv)
    cross_n = rms_scale(dec_y1, gain[4]).astype(bf16)
    cross_q = project(cross_n, cross_wi[:, :D]).astype(bf16)
    cross_ob = attend_forward(cross_q, cross_kv, cross_kv2, cross_info, None, False)
    dec_y2 = dec_y1 + project(cross_ob, cross_wo)
    dec_y3, dec_saved = ffn_forward(dec_y2, gain[5], dec_fi, dec_fo)
    head_scale = D ** (-0.5)
    hidden_b = (rms_scale(dec_y3, gain[6]) * head_scale).astype(bf16)

    hidden_all = lax.all_gather(hidden_b, ALL, axis=0, tiled=True)
    hidden_all = hidden_all.reshape(-1, dec_count, D)
    info = gather_small(jnp.stack([targets, mask_i]), ALL)
    info = jnp.transpose(info.reshape(-1, 2, 2, dec_count // 2), (1, 2, 0, 3)).reshape(2, 1, -1)
    targets_all = info[0] - device * shard
    mask_all = info[1].astype(f32)
    lse_part, picked = head_stats(hidden_all, table_b, targets_all, shard)
    lse = fold_all(lse_part, add_logs)
    halves = [
        head_grad(hidden_all, table_b, targets_all, mask_all, lse, shard, half) for half in range(2)
    ]
    head_embed = halves[0][1] + halves[1][1]
    d_hidden = jnp.concatenate(
        [scatter_chain(item[0], number == 0) for number, item in enumerate(halves)]
    )
    lse_mine = lax.dynamic_slice_in_dim(
        lse.reshape(2, -1), device * (dec_count // 2), dec_count // 2, axis=1
    )
    loss_local = jnp.sum(mask * lse_mine.reshape(-1)) - jnp.sum(mask_all * picked)

    d_y3, d_gain_final = norm_pull(dec_y3, gain[6], head_scale, d_hidden)
    d_y2, d_gain_dffn, d_dec_fi, d_dec_fo = ffn_backward(
        d_y3, dec_y2, gain[5], dec_fi, dec_fo, dec_saved
    )
    d_cross_wo, d_cross_ob = branch_backward(d_y2, cross_ob, cross_wo)
    d_cross_q, own, other = attend_backward(
        d_cross_ob, cross_q, cross_kv, cross_kv2, cross_info, None, False
    )
    got = (own + swap_core(other).astype(f32)).astype(bf16)
    d_cross_kv = jnp.concatenate([got[0], got[1]], axis=1)
    d_cross_wq = weight_grad(cross_n, d_cross_q)
    d_y1_norm, d_gain_cross = norm_pull(
        dec_y1, gain[4], 1.0, input_grad(d_cross_q, cross_wi[:, :D])
    )
    d_y1 = d_y2 + d_y1_norm
    d_cross_wkv = weight_grad(enc_out, d_cross_kv)
    d_dec_wo, d_dec_ob = branch_backward(d_y1, dec_ob, dec_wo)
    d_dec_q, own, other, dec_y8 = attend_backward(
        d_dec_ob, dec_q, dec_kv, dec_kv2, dec_info, dec_x8, True
    )
    got = (own + swap_core(other).astype(f32)).astype(bf16)
    d_dec_qkv = jnp.concatenate([d_dec_q, got[0], got[1]], axis=1)
    d_dec_table = bias_gradient(dec_y8, dec_picks, core, dec_count, dec_count)
    d_dec_wi = weight_grad(dec_n1, d_dec_qkv)
    d_y0_norm, d_gain_datt = norm_pull(dec_y0, gain[3], 1.0, input_grad(d_dec_qkv, dec_wi))
    d_y0 = d_y1 + d_y0_norm
    d_dec_rest = jnp.concatenate(
        [
            d_dec_wi.astype(bf16),
            d_cross_wq.astype(bf16),
            d_cross_wkv.astype(bf16),
            d_dec_wo,
            d_cross_wo,
        ],
        axis=1,
    )
    g_dec_fi = scatter_chain(d_dec_fi, True)
    g_dec_fo = scatter_chain(d_dec_fo, False)
    g_dec_rest = scatter_chain(d_dec_rest, False)
    dec_lines = line_gather(d_y0.astype(bf16), "z")

    d_x2, d_gain_efin = norm_pull(
        enc_x2, gain[2], 1.0, input_grad(d_cross_kv, cross_wi[:, D:])
    )
    d_x1, d_gain_effn, d_enc_fi, d_enc_fo = ffn_backward(
        d_x2, enc_x1, gain[1], enc_fi, enc_fo, enc_saved
    )
    g_enc_fi = scatter_chain(d_enc_fi, True)
    g_enc_fo = scatter_chain(d_enc_fo, False)
    d_enc_wo, d_enc_ob = branch_backward(d_x1, enc_ob, enc_wo)
    d_enc_q, own, other, enc_y8 = attend_backward(
        d_enc_ob, enc_q, enc_kv, enc_kv2, enc_info, enc_x8, False
    )
    got = (own + swap_core(other).astype(f32)).astype(bf16)
    d_enc_qkv = jnp.concatenate([d_enc_q, got[0], got[1]], axis=1)
    d_enc_table = bias_gradient(enc_y8, enc_picks, core, enc_count, enc_count)
    d_enc_wi = weight_grad(enc_n1, d_enc_qkv)
    d_x0_norm, d_gain_eatt = norm_pull(enc_x0, gain[0], 1.0, input_grad(d_enc_qkv, enc_wi))
    d_x0 = d_x1 + d_x0_norm

    enc_lines = line_gather(d_x0.astype(bf16), "z")
    far_place = lambda item: jnp.where(item == shard, -1, item)[None, :]
    pairs = [
        (far_place(item), grads)
        for item, grads in zip(enc_places + dec_places, enc_lines + dec_lines)
    ]
    input_embed = plane_scatter(pairs, padded)
    grad_embed = head_embed[:shard] + input_embed[:shard]

    d_gains = jnp.stack(
        [
            d_gain_eatt,
            d_gain_effn,
            d_gain_efin,
            d_gain_datt,
            d_gain_cross,
            d_gain_dffn,
            d_gain_final,
        ]
    )
    d_rel = jnp.stack([d_enc_table.reshape(-1), d_dec_table.reshape(-1)])
    d_rel = jnp.transpose(d_rel.reshape(2, -1, rel_table.shape[1]), (1, 0, 2)).reshape(D, 1)
    d_misc = jnp.pad(jnp.concatenate([d_gains.T, d_rel], axis=1), ((0, 0), (0, 120)))
    g_enc_wi = scatter_chain(d_enc_wi.astype(bf16), True)
    g_enc_rest = scatter_chain(
        jnp.concatenate([d_enc_wo, d_misc.astype(bf16)], axis=1), False
    )
    owned = (
        jnp.stack([g_enc_wi, cut(g_dec_rest, 0, 3 * D), cut(g_dec_rest, 3 * D, 3 * D)]),
        jnp.stack(
            [cut(g_enc_rest, 0, D), cut(g_dec_rest, 6 * D, D), cut(g_dec_rest, 7 * D, D)]
        ),
        jnp.stack([g_enc_fi, g_dec_fi]),
        jnp.stack([g_enc_fo, g_dec_fo]),
        g_enc_rest[:, D + 7].reshape(2, -1),
        g_enc_rest[:, D : D + 7].T,
    )
    grads = (grad_embed,) + owned
    squares = sum((jnp.sum(item * item) for item in grads))
    sums = fold_all(jnp.stack([jnp.sum(mask), loss_local, squares]), jnp.add)
    count_all, loss_all, squares_all = sums[0], sums[1], sums[2]
    grad_norm = jnp.sqrt(squares_all) / count_all
    factor = jnp.minimum(1.0, clip_limit / grad_norm) / count_all
    weights = (embed, attn_in, attn_out, ffn_in, ffn_out, rel_table, gains)
    moments = [
        (m_embed, v_embed),
        (m_attn_in, v_attn_in),
        (m_attn_out, v_attn_out),
        (m_ffn_in, v_ffn_in),
        (m_ffn_out, v_ffn_out),
        (m_rel, v_rel),
        (m_gains, v_gains),
    ]
    settings = [
        (1.0, 0.01),
        (0.05, 0.01),
        (0.05, 0.01),
        (0.05, 0.01),
        (0.05, 0.01),
        (0.3, 0.0),
        (0.3, 0.0),
    ]
    results = [loss_all / count_all, grad_norm]
    for slot_number, (param, grad, pair, setting) in enumerate(
        zip(weights, grads, moments, settings)
    ):
        clipped = grad * factor
        first_new, second_new, new_param = adamw(
            param, clipped, pair[0], pair[1], float(STEP), setting[0], setting[1]
        )
        results.extend((clipped if slot_number == 0 else first_new, second_new, new_param))
    return tuple(results)


def solution(mesh):
    rows = ("z", "p", "core")
    every = ALL
    inner = Mesh(mesh.devices.reshape(4, -1, 2, mesh.devices.shape[1]), ALL)
    mat = P(None, every, None)
    vec = P(None, every)
    emb = P(every, None)
    in_specs = (
        P(rows, "seq"),
        P(rows, None),
        P(rows, "seq"),
        P(rows, None),
        P(rows, "seq"),
        P(rows, None),
        P(rows, "seq"),
        P(rows, "seq"),
        P(),
        emb,
        mat,
        mat,
        mat,
        mat,
        vec,
        vec,
        emb,
        emb,
    ) + (mat,) * 8 + (vec,) * 4
    out_specs = (P(), P()) + (emb,) * 3 + (mat,) * 12 + (vec,) * 6
    return jax.shard_map(body, mesh=inner, in_specs=in_specs, out_specs=out_specs, check_vma=False)
```

```python
import functools

import jax
import jax.numpy as jnp
from jax import lax
from jax.experimental import pallas as pl
from jax.experimental.pallas import tpu as pltpu
from jax.sharding import Mesh
from jax.sharding import PartitionSpec as P

D = 768
HEADS = 12
HEAD_DIM = 64
FF = 2048
V = 32128
BUCKETS = 32
STEP = 10

masked_out = -1e30
clip_limit = 0.01
ALL = ("z", "p", "core", "seq")
PLANE = ("p", "core", "seq")
bf16 = jnp.bfloat16
f32 = jnp.float32
VMEM_LIMIT = 56 * 1024 * 1024


def rms_scale(values, gain):
    return values * lax.rsqrt(jnp.mean(values * values, axis=-1, keepdims=True) + 1e-06) * gain


def norm_pull(values, gain, factor, upstream):
    _, pull = jax.vjp(lambda left, right: rms_scale(left, right) * factor, values, gain)
    return pull(upstream)


def gate_up(both):
    return jax.nn.gelu(both[:, :FF], approximate=True) * both[:, FF:]


def project(left, right):
    return jnp.dot(left, right, preferred_element_type=f32)


def weight_grad(inputs, grads):
    return jnp.einsum("td,te->de", inputs, grads, preferred_element_type=f32)


def input_grad(grads, weight):
    return jnp.einsum("te,de->td", grads, weight, preferred_element_type=f32)


def dot_nt(a, b):
    return lax.dot_general(a, b, (((1,), (1,)), ((), ())), preferred_element_type=f32)


def dot_tn(a, b):
    return lax.dot_general(a, b, (((0,), (0,)), ((), ())), preferred_element_type=f32)


def dot_nn(a, b):
    return lax.dot_general(a, b, (((1,), (0,)), ((), ())), preferred_element_type=f32)


def spread(eight, rows, width):
    total = eight.shape[-1]
    grid = eight
    have = 8
    while have < rows:
        grid = jnp.concatenate([pltpu.roll(grid, total - have, 1), grid], axis=0)
        have *= 2
    return grid[:, :width]


def collect(grid, total):
    rows, width = grid.shape
    have = jnp.concatenate([grid, jnp.zeros((rows, total - width), f32)], axis=1)
    while rows > 8:
        rows //= 2
        have = pltpu.roll(have[:rows], rows, 1) + have[rows:]
    return have


def probs_of(cfg, refs, block, head):
    bq, has_bias, causal = cfg
    rows = slice(block * bq, (block + 1) * bq)
    cols = slice(head * HEAD_DIM, (head + 1) * HEAD_DIM)
    query = refs["q"][rows, cols]
    scores = []
    for part in range(2):
        keys = refs["k"][part][:, cols]
        s = dot_nt(query, keys) * HEAD_DIM ** (-0.5)
        if has_bias:
            s = s + spread(refs["x8"][block, part, head], bq, keys.shape[0])
        allowed = refs["qseg"][rows, :] == refs["kseg"][part]
        if causal:
            allowed = allowed & (refs["kpos"][part] <= refs["qpos"][rows, :])
        scores.append(jnp.where(allowed, s, masked_out))
    top = jnp.maximum(
        jnp.max(scores[0], axis=1, keepdims=True), jnp.max(scores[1], axis=1, keepdims=True)
    )
    exps = [jnp.exp(s - top) for s in scores]
    total = jnp.sum(exps[0], axis=1, keepdims=True) + jnp.sum(exps[1], axis=1, keepdims=True)
    scale = 1.0 / total
    return query, [e * scale for e in exps]


def name_refs(cfg, refs):
    bq, has_bias, causal = cfg
    it = iter(refs)
    named = {"q": next(it)}
    k0, v0, k1, v1 = next(it), next(it), next(it), next(it)
    named["k"], named["v"] = (k0, k1), (v0, v1)
    ids = next(it), next(it), next(it), next(it), next(it), next(it)
    named["qseg"], named["kseg"] = ids[0], (ids[1][...], ids[2][...])
    named["qpos"], named["kpos"] = ids[3], (ids[4][...], ids[5][...])
    if has_bias:
        named["x8"] = next(it)
    return named, list(it)


def attend_forward_kernel(cfg, *refs):
    named, (out,) = name_refs(cfg, refs)
    bq = cfg[0]
    for block in range(named["q"].shape[0] // bq):
        for head in range(2):
            cols = slice(head * HEAD_DIM, (head + 1) * HEAD_DIM)
            _, probs = probs_of(cfg, named, block, head)
            acc = dot_nn(probs[0].astype(bf16), named["v"][0][:, cols])
            acc = acc + dot_nn(probs[1].astype(bf16), named["v"][1][:, cols])
            out[block * bq : (block + 1) * bq, cols] = acc.astype(bf16)


def attend_backward_kernel(cfg, *refs):
    named, rest = name_refs(cfg, refs)
    bq, has_bias, causal = cfg
    if has_bias:
        grad, dq, own, other, y8 = rest
    else:
        grad, dq, own, other = rest
    blocks = named["q"].shape[0] // bq
    for head in range(2):
        cols = slice(head * HEAD_DIM, (head + 1) * HEAD_DIM)
        dk, dv = [None, None], [None, None]
        for block in range(blocks):
            rows = slice(block * bq, (block + 1) * bq)
            query, probs = probs_of(cfg, named, block, head)
            do = grad[rows, cols]
            dp = [dot_nt(do, named["v"][part][:, cols]) for part in range(2)]
            delta = jnp.sum(probs[0] * dp[0], axis=1, keepdims=True) + jnp.sum(
                probs[1] * dp[1], axis=1, keepdims=True
            )
            acc = None
            for part in range(2):
                ds = (probs[part] * (dp[part] - delta)).astype(bf16)
                term = dot_nn(ds, named["k"][part][:, cols])
                acc = term if acc is None else acc + term
                k_term = dot_tn(query, ds)
                v_term = dot_tn(do, probs[part].astype(bf16))
                dk[part] = k_term if dk[part] is None else dk[part] + k_term
                dv[part] = v_term if dv[part] is None else dv[part] + v_term
                if has_bias:
                    y8[block, part, head] = collect(ds.astype(f32), y8.shape[-1])
            dq[rows, cols] = (acc * HEAD_DIM ** (-0.5)).astype(bf16)
        for part, target in enumerate((own, other)):
            target[0, :, cols] = (dk[part] * HEAD_DIM ** (-0.5)).T.astype(target.dtype)
            target[1, :, cols] = dv[part].T.astype(target.dtype)


def attend_specs(q_len, k_len, has_bias, x8):
    whole = lambda shape: pl.BlockSpec(shape, lambda i: (0,) * len(shape))
    kv = [
        pl.BlockSpec((k_len, 128), lambda i: (0, i)),
        pl.BlockSpec((k_len, 128), lambda i: (0, i + 6)),
    ]
    specs = [pl.BlockSpec((q_len, 128), lambda i: (0, i))] + kv + kv
    specs += [whole((q_len, 1)), whole((1, k_len)), whole((1, k_len))] * 2
    if has_bias:
        specs.append(
            pl.BlockSpec((x8.shape[0], 2, 2, 8, x8.shape[-1]), lambda i: (0, 0, i, 0, 0))
        )
    return specs


def attend_args(q, kv_own, kv_other, ids, x8):
    args = [q, kv_own, kv_own, kv_other, kv_other] + list(ids)
    if x8 is not None:
        args.append(x8)
    return args


def attend_cost(q_len, k_len, products):
    return pl.CostEstimate(flops=products, bytes_accessed=q_len, transcendentals=0)


def attend_forward(q, kv_own, kv_other, ids, x8, causal):
    q_len, k_len = q.shape[0], kv_own.shape[0]
    cfg = (256, x8 is not None, causal)
    return pl.pallas_call(
        functools.partial(attend_forward_kernel, cfg),
        grid=(HEADS // 2,),
        in_specs=attend_specs(q_len, k_len, x8 is not None, x8),
        out_specs=pl.BlockSpec((q_len, 128), lambda i: (0, i)),
        out_shape=jax.ShapeDtypeStruct((q_len, D), bf16),
        compiler_params=pltpu.CompilerParams(vmem_limit_bytes=VMEM_LIMIT),
        cost_estimate=attend_cost(q_len, k_len, 2),
    )(*attend_args(q, kv_own, kv_other, ids, x8))


def attend_backward(grad, q, kv_own, kv_other, ids, x8, causal):
    q_len, k_len = q.shape[0], kv_own.shape[0]
    cfg = (256, x8 is not None, causal)
    kv_spec = pl.BlockSpec((2, k_len, 128), lambda i: (0, 0, i))
    out_specs = [pl.BlockSpec((q_len, 128), lambda i: (0, i)), kv_spec, kv_spec]
    out_shape = [
        jax.ShapeDtypeStruct((q_len, D), bf16),
        jax.ShapeDtypeStruct((2, k_len, D), f32),
        jax.ShapeDtypeStruct((2, k_len, D), bf16),
    ]
    if x8 is not None:
        out_specs.append(
            pl.BlockSpec((x8.shape[0], 2, 2, 8, x8.shape[-1]), lambda i: (0, 0, i, 0, 0))
        )
        out_shape.append(jax.ShapeDtypeStruct(x8.shape, f32))
    return pl.pallas_call(
        functools.partial(attend_backward_kernel, cfg),
        grid=(HEADS // 2,),
        in_specs=attend_specs(q_len, k_len, x8 is not None, x8)
        + [pl.BlockSpec((q_len, 128), lambda i: (0, i))],
        out_specs=out_specs,
        out_shape=out_shape,
        compiler_params=pltpu.CompilerParams(vmem_limit_bytes=VMEM_LIMIT),
        cost_estimate=attend_cost(q_len, k_len, 5),
    )(*attend_args(q, kv_own, kv_other, ids, x8), grad)


def bias_bases(core, q_len, k_len, offset):
    bases = []
    for block in range(q_len // 256):
        for part in range(2):
            k_start = (core if part == 0 else 1 - core) * k_len
            q_start = core * q_len + block * 256
            bases.append(k_start - q_start - 255 + offset)
    return bases


def bias_eights(table, bucket_row, core, q_len, k_len):
    size = bucket_row.shape[0]
    picks = (bucket_row[None, :] == jnp.arange(BUCKETS, dtype=jnp.int32)[:, None]).astype(bf16)
    per_offset = jnp.einsum("bh,bn->hn", table, picks, preferred_element_type=f32)
    per_offset = jnp.pad(per_offset, ((0, 0), (0, 16)))
    width = k_len + 256
    found = []
    for base in bias_bases(core, q_len, k_len, size // 2):
        window = lax.dynamic_slice_in_dim(per_offset, base, width + 7, axis=1)
        found.append(jnp.stack([window[:, 7 - r : 7 - r + width] for r in range(8)], axis=1))
    return jnp.stack(found).reshape(q_len // 256, 2, HEADS, 8, width), picks


def bias_gradient(y8, picks, core, q_len, k_len):
    size = picks.shape[1]
    width = k_len + 256
    total = jnp.zeros((HEADS, size + 16), f32)
    flat = y8.reshape(-1, HEADS, 8, width)
    for number, base in enumerate(bias_bases(core, q_len, k_len, size // 2)):
        window = sum(
            jnp.pad(flat[number, :, r], ((0, 0), (7 - r, r))) for r in range(8)
        )
        old = lax.dynamic_slice_in_dim(total, base, width + 7, axis=1)
        total = lax.dynamic_update_slice_in_dim(total, old + window, base, axis=1)
    return jnp.einsum(
        "bn,hn->bh", picks.astype(f32), total[:, :size], precision=lax.Precision.HIGHEST
    )


def head_stats_kernel(count, hid, tab, tgt, lse_out, pick_out):
    logits = dot_nt(tab[...], hid[...].reshape(-1, D))
    row = lax.broadcasted_iota(jnp.int32, logits.shape, 0)
    pick_out[...] = jnp.sum(jnp.where(row == tgt[...], logits, 0.0), axis=0, keepdims=True)
    logits = jnp.where(row < count, logits, masked_out)
    top = jnp.max(logits, axis=0, keepdims=True)
    lse_out[...] = top + jnp.log(jnp.sum(jnp.exp(logits - top), axis=0, keepdims=True))


def head_grad_kernel(count, core, hid, tab, tgt, msk, lse, dhid_a, dhid_b, dtab):
    tokens = hid[...].reshape(-1, D)
    logits = dot_nt(tab[...], tokens)
    row = lax.broadcasted_iota(jnp.int32, logits.shape, 0)
    soft = jnp.exp(jnp.where(row < count, logits, masked_out) - lse[...])
    grad = ((soft - jnp.where(row == tgt[...], 1.0, 0.0)) * msk[...]).astype(bf16)
    dhid = dot_tn(grad, tab[...]).astype(bf16).reshape(hid.shape)
    cut = hid.shape[3] // 2
    dhid_a[...] = dhid[:, 0, :, :cut]
    dhid_b[...] = dhid[:, 0, :, cut:]
    term = dot_nn(grad, tokens)

    @pl.when(pl.program_id(0) == 0)
    def _():
        dtab[...] = term

    @pl.when(pl.program_id(0) != 0)
    def _():
        dtab[...] += term


def head_stats(hidden, table, targets, count):
    places, each = hidden.shape[0], hidden.shape[3]
    tokens, rows = places * 4 * each, table.shape[0]
    steps = places // 2
    line = pl.BlockSpec((1, 2 * each), lambda h, c, i: (0, (h * 2 + c) * steps + i))
    return pl.pallas_call(
        functools.partial(head_stats_kernel, count),
        grid=(2, 2, steps),
        in_specs=[
            pl.BlockSpec((2, 1, 2, each // 2, D), lambda h, c, i: (i, c, 0, h, 0)),
            pl.BlockSpec((rows, D), lambda h, c, i: (0, 0)),
            line,
        ],
        out_specs=[line, line],
        out_shape=[jax.ShapeDtypeStruct((1, tokens), f32)] * 2,
        compiler_params=pltpu.CompilerParams(vmem_limit_bytes=VMEM_LIMIT),
        cost_estimate=pl.CostEstimate(
            flops=2 * tokens * rows * D, bytes_accessed=2 * tokens * D, transcendentals=tokens * rows
        ),
    )(hidden, table, targets)


def head_grad(core, hidden, table, targets, mask, lse, count, half):
    places, each = hidden.shape[0], hidden.shape[3]
    tokens, rows = places * each, table.shape[0]
    steps = places // 2
    line = pl.BlockSpec((1, 2 * each), lambda i, c: (0, (half * 2 + c[0]) * steps + i))
    piece = pl.BlockSpec((2, 2, each // 4, D), lambda i, c: (i, 0, 0, 0))
    return pl.pallas_call(
        functools.partial(head_grad_kernel, count),
        grid_spec=pltpu.PrefetchScalarGridSpec(
            num_scalar_prefetch=1,
            grid=(steps,),
            in_specs=[
                pl.BlockSpec((2, 1, 2, each // 2, D), lambda i, c: (i, c[0], 0, half, 0)),
                pl.BlockSpec((rows, D), lambda i, c: (0, 0)),
                line,
                line,
                line,
            ],
            out_specs=[piece, piece, pl.BlockSpec((rows, D), lambda i, c: (0, 0))],
        ),
        out_shape=[
            jax.ShapeDtypeStruct((places, 2, each // 4, D), bf16),
            jax.ShapeDtypeStruct((places, 2, each // 4, D), bf16),
            jax.ShapeDtypeStruct((rows, D), f32),
        ],
        compiler_params=pltpu.CompilerParams(vmem_limit_bytes=VMEM_LIMIT),
        cost_estimate=pl.CostEstimate(
            flops=6 * tokens * rows * D, bytes_accessed=4 * tokens * D, transcendentals=tokens * rows
        ),
    )(core.reshape(1), hidden, table, targets, mask, lse)


def place_kernel(first, *refs):
    out = refs[-1]
    rows = out.shape[0]
    base = (pl.program_id(0) + first) * rows
    total = None
    for ids, grads in zip(refs[:-1:2], refs[1:-1:2]):
        row = lax.broadcasted_iota(jnp.int32, (rows, ids.shape[1]), 0) + base
        hot = jnp.where(row == ids[...], 1.0, 0.0).astype(bf16)
        term = dot_nn(hot, grads[...])
        total = term if total is None else total + term
    out[...] = total.astype(bf16)


def place_rows(pairs, first, parts, rows):
    tokens = sum(grads.shape[0] for _, grads in pairs)
    specs, args = [], []
    for ids, grads in pairs:
        specs.append(pl.BlockSpec(ids.shape, lambda i: (0, 0)))
        specs.append(pl.BlockSpec(grads.shape, lambda i: (0, 0)))
        args += [ids, grads]
    return pl.pallas_call(
        functools.partial(place_kernel, first),
        grid=(parts,),
        in_specs=specs,
        out_specs=pl.BlockSpec((rows, D), lambda i: (i, 0)),
        out_shape=jax.ShapeDtypeStruct((parts * rows, D), bf16),
        compiler_params=pltpu.CompilerParams(vmem_limit_bytes=VMEM_LIMIT),
        cost_estimate=pl.CostEstimate(
            flops=2 * tokens * parts * rows * D, bytes_accessed=2 * parts * rows * D, transcendentals=0
        ),
    )(*args)


def gather_axis(value, axis):
    size = lax.axis_size(axis)
    me = lax.axis_index(axis)
    got = [value]
    for step in range(1, size):
        got.append(lax.ppermute(value, axis, [(i, (i + step) % size) for i in range(size)]))
    stacked = jnp.stack(got)
    return jnp.take(stacked, (me - jnp.arange(size, dtype=jnp.int32)) % size, axis=0)


def gather_small(value, axes):
    shape = value.shape
    for axis in reversed(axes):
        value = gather_axis(value, axis)
        value = value.reshape((-1,) + shape)
    return value


def fold_all(value, combine):
    for axis in reversed(ALL):
        size = lax.axis_size(axis)
        hop = 1
        while hop < size:
            other = lax.ppermute(value, axis, [(i, i ^ hop) for i in range(size)])
            value = combine(value, other)
            hop *= 2
    return value


def swap(value, axis):
    return lax.ppermute(value, axis, [(0, 1), (1, 0)])


def swap_core(value):
    return swap(value, "core")


def add16(left, right):
    return (left.astype(f32) + right.astype(f32)).astype(bf16)


def pick(value, index, dim):
    return lax.dynamic_index_in_dim(value, index, dim, keepdims=False)


def scatter_pair(value, axis, dim):
    if lax.axis_size(axis) != 2:
        return lax.psum_scatter(value, axis, scatter_dimension=dim, tiled=False)
    me = lax.axis_index(axis)
    got = swap(pick(value, 1 - me, dim), axis)
    return add16(pick(value, me, dim), got)


def scatter_rest(value, seq_first):
    if seq_first:
        value = scatter_pair(scatter_pair(value, "seq", 2), "p", 1)
    else:
        value = scatter_pair(scatter_pair(value, "p", 1), "seq", 1)
    size, me = value.shape[0], lax.axis_index("z")
    total = pick(value, me, 0).astype(f32)
    for hop in range(1, size):
        send = pick(value, (me + hop) % size, 0)
        got = lax.ppermute(send, "z", [(i, (i + hop) % size) for i in range(size)])
        total = total + got.astype(f32)
    return total


def scatter_chain(value, seq_first):
    sizes = tuple(lax.axis_size(axis) for axis in ALL)
    value = value.reshape(sizes + (-1, value.shape[-1]))
    return scatter_rest(scatter_pair(value, "core", 2), seq_first)


def line_gather(value, axis):
    size = lax.axis_size(axis)
    ups, downs = [value], [value]
    for _ in range(1, size):
        ups.append(lax.ppermute(ups[-1], axis, [(i, i + 1) for i in range(size - 1)]))
        downs.append(lax.ppermute(downs[-1], axis, [(i + 1, i) for i in range(size - 1)]))
    return [value] + [ups[k] + downs[size - k] for k in range(1, size)]


def line_scatter(parts, axis):
    size = lax.axis_size(axis)
    up, down = None, None
    for step in range(1, size):
        far = size - step
        send_up, send_down = parts[size - far], parts[far]
        if up is not None:
            send_up, send_down = send_up + up, send_down + down
        up = lax.ppermute(send_up, axis, [(i, i + 1) for i in range(step)])
        down = lax.ppermute(send_down, axis, [(size - 1 - i, size - 2 - i) for i in range(step)])
    return parts[0].astype(f32) + up.astype(f32) + down.astype(f32)


def plane_gather(table):
    if lax.axis_size("p") != 2:
        return lax.all_gather(table, PLANE, axis=0, tiled=True)
    half = table.shape[0] // 2
    by_seq, by_p = swap(table, "seq"), swap(table, "p")
    far = [swap(by_p[:half], "seq"), swap(by_seq[half:], "p")]
    mine = [table, by_seq, by_p] + far
    return jnp.concatenate(mine + [swap_core(item) for item in mine])


def plane_slot(owner):
    if lax.axis_size("p") != 2:
        return owner
    other = owner ^ lax.axis_index(PLANE)
    return ((other >> 1) & 1) * 4 + (other >> 2) * 2 + (other & 1)


def plane_scatter(pairs, rows):
    count = lax.axis_size(PLANE)
    if lax.axis_size("p") != 2:
        placed = place_rows(pairs, 0, count, rows)
        return lax.psum_scatter(placed, PLANE, scatter_dimension=0, tiled=True).astype(f32)
    away = swap_core(place_rows(pairs, 4, 4, rows))
    home = place_rows(pairs, 0, 4, rows)
    half = rows // 2
    part = lambda first, last: add16(home[first:last], away[first:last])
    got_low = swap(part(3 * rows, 3 * rows + half), "seq")
    got_high = swap(part(3 * rows + half, 4 * rows), "p")
    seq_high = add16(part(rows + half, 2 * rows), got_high)
    p_low = add16(part(2 * rows, 2 * rows + half), got_low)
    from_seq = swap(jnp.concatenate([part(rows, rows + half), seq_high]), "seq")
    from_p = swap(jnp.concatenate([p_low, part(2 * rows + half, 3 * rows)]), "p")
    return part(0, rows).astype(f32) + from_seq.astype(f32) + from_p.astype(f32)


def add_logs(left, right):
    top = jnp.maximum(left, right)
    return top + jnp.log(jnp.exp(left - top) + jnp.exp(right - top))


def ffn_forward(resid, gain, w_in, w_out):
    normed = rms_scale(resid, gain).astype(bf16)
    both = project(normed, w_in)
    hidden = gate_up(both).astype(bf16)
    return (resid + project(hidden, w_out), (normed, both, hidden))


def ffn_backward(upstream, resid, gain, w_in, w_out, saved):
    normed, both, hidden = saved
    grad_b = upstream.astype(bf16)
    d_out = weight_grad(hidden, grad_b).astype(bf16)
    _, pull = jax.vjp(gate_up, both)
    (d_both,) = pull(input_grad(grad_b, w_out))
    d_both_b = d_both.astype(bf16)
    d_in = weight_grad(normed, d_both_b).astype(bf16)
    d_resid, d_gain = norm_pull(resid, gain, 1.0, input_grad(d_both_b, w_in))
    return (upstream + d_resid, d_gain, d_in, d_out)


def branch_backward(upstream, out_b, w_out):
    grad_b = upstream.astype(bf16)
    return (weight_grad(out_b, grad_b).astype(bf16), input_grad(grad_b, w_out).astype(bf16))


def adamw(weight, grad, first_m, second_m, count, rate, decay):
    first_new = 0.9 * first_m + 0.1 * grad
    second_new = 0.999 * second_m + 0.001 * grad * grad
    first_hat = first_new / (1.0 - 0.9**count)
    second_hat = second_new / (1.0 - 0.999**count)
    return (
        first_new,
        second_new,
        weight - rate * (first_hat / (jnp.sqrt(second_hat) + 1e-08) + decay * weight),
    )


def body(
    enc_ids,
    enc_segs,
    sentinel,
    mode,
    dec_ids,
    dec_segs,
    target_ids,
    target_mask,
    buckets,
    embed,
    attn_in,
    attn_out,
    ffn_in,
    ffn_out,
    rel_table,
    gains,
    m_embed,
    v_embed,
    m_attn_in,
    v_attn_in,
    m_attn_out,
    v_attn_out,
    m_ffn_in,
    v_ffn_in,
    m_ffn_out,
    v_ffn_out,
    m_rel,
    v_rel,
    m_gains,
    v_gains,
):
    core = lax.axis_index("core")
    z_at = lax.axis_index("z")
    z_size = lax.axis_size("z")
    plane_size = lax.axis_size(PLANE)
    device = lax.axis_index(ALL)
    shard = embed.shape[0]
    padded = (shard // 16 + 1) * 16
    enc_count, dec_count = enc_ids.shape[1], dec_ids.shape[1]
    enc_len, dec_len = enc_segs.shape[1], dec_segs.shape[1]

    table_b = jnp.pad(embed.astype(bf16), ((0, padded - shard), (0, 0)))
    misc = jnp.concatenate([gains.T, rel_table.reshape(-1, 1)], axis=1)
    misc = jnp.pad(misc, ((0, 0), (0, 120)))
    shard_in = attn_in.shape[1]
    flat_out = ffn_out.astype(bf16).reshape(2, shard_in, -1)
    enc_cast = jnp.concatenate([attn_in[0], ffn_in[0], attn_out[0], misc], axis=1).astype(bf16)
    enc_pack = lax.all_gather(
        jnp.concatenate([enc_cast, flat_out[0]], axis=1), ALL, axis=0, tiled=True
    )
    dec_cast = jnp.concatenate(
        [attn_in[1], attn_in[2], attn_out[1], attn_out[2]], axis=1
    ).astype(bf16)
    ffn_cast = jnp.concatenate([ffn_in[1].astype(bf16), flat_out[1]], axis=1)
    plane_table = plane_gather(table_b)
    flat = jnp.concatenate(
        [
            enc_ids[0],
            sentinel[0],
            dec_ids[0],
            target_ids[0],
            target_mask[0],
            enc_segs[0],
            dec_segs[0],
            jnp.pad(mode[0], (0, 128 - mode.shape[1])),
        ]
    )
    flat = lax.ppermute(flat, ("core", "seq"), [(0, 0), (1, 2), (2, 1), (3, 3)])
    sizes = [enc_count, enc_count, dec_count, dec_count, dec_count, enc_len, dec_len]
    pieces, start = [], 0
    for size in sizes:
        pieces.append(flat[start : start + size])
        start += size
    enc_id, sent, dec_id, targets, mask_i, enc_seg_all, dec_seg_all = pieces
    mode_row = flat[start : start + mode.shape[1]]
    mask = mask_i.astype(f32)

    enc_seg = lax.dynamic_slice_in_dim(enc_seg_all, core * enc_count, enc_count)
    enc_seg_other = lax.dynamic_slice_in_dim(enc_seg_all, (1 - core) * enc_count, enc_count)
    dec_seg = lax.dynamic_slice_in_dim(dec_seg_all, core * dec_count, dec_count)
    dec_seg_other = lax.dynamic_slice_in_dim(dec_seg_all, (1 - core) * dec_count, dec_count)
    enc_range = jnp.arange(enc_count, dtype=jnp.int32)
    dec_range = jnp.arange(dec_count, dtype=jnp.int32)
    enc_pos, enc_pos_other = core * enc_count + enc_range, (1 - core) * enc_count + enc_range
    dec_pos, dec_pos_other = core * dec_count + dec_range, (1 - core) * dec_count + dec_range
    prior_all = jnp.concatenate([enc_seg_all[:1], enc_seg_all[:-1]])
    prior = lax.dynamic_slice_in_dim(prior_all, core * enc_count, enc_count)
    first = (enc_pos == 0) | (enc_seg != prior)
    mode_of = jnp.sum(
        jnp.where(
            enc_seg[:, None] == jnp.arange(mode.shape[1], dtype=jnp.int32)[None], mode_row[None], 0
        ),
        axis=1,
    )
    enc_tok = jnp.where(sent == 1, V - 1 - enc_seg, enc_id)
    enc_tok = jnp.where(first, V - 101 - mode_of, enc_tok)
    local_ids = jnp.concatenate([enc_tok, dec_id])

    line_ids = line_gather(local_ids, "z")
    plane_rows = plane_size * shard
    places = []
    for ids in line_ids:
        rel_id = ids - z_at * plane_rows
        inside = (rel_id >= 0) & (rel_id < plane_rows)
        places.append(
            jnp.where(inside, plane_slot(rel_id // shard) * padded + rel_id % shard, shard)
        )
    dec_cast, enc_pack, plane_table, places = lax.optimization_barrier(
        (dec_cast, enc_pack, plane_table, places)
    )
    dec_pack = lax.all_gather(dec_cast, ALL, axis=0, tiled=True)
    enc_places = [item[:enc_count] for item in places]
    dec_places = [item[enc_count:] for item in places]

    def look(items):
        got = jnp.take(plane_table, jnp.concatenate(items), axis=0, mode="clip")
        return line_scatter(jnp.split(got, len(items)), "z")

    enc_x0 = look(enc_places)
    dec_y0 = look(dec_places)

    cut = lambda pack, start, width: lax.slice_in_dim(pack, start, start + width, axis=1)
    enc_wi, enc_fi = cut(enc_pack, 0, 3 * D), cut(enc_pack, 3 * D, 2 * FF)
    enc_wo, misc_all = cut(enc_pack, 3 * D + 2 * FF, D), cut(enc_pack, 4 * D + 2 * FF, 128)
    enc_fo = cut(enc_pack, 4 * D + 2 * FF + 128, FF).reshape(FF, D)
    gain = misc_all[:, :7].T.astype(f32)
    rel_all = jnp.transpose(misc_all[:, 7].reshape(-1, 2, rel_table.shape[1]), (1, 0, 2))
    rel_all = rel_all.reshape(2, BUCKETS, HEADS)

    enc_x8, enc_picks = bias_eights(rel_all[0], buckets[0], core, enc_count, enc_count)
    dec_x8, dec_picks = bias_eights(rel_all[1], buckets[1], core, dec_count, dec_count)
    col, line = (lambda v: v[:, None]), (lambda v: v[None, :])
    enc_info = (
        col(enc_seg), line(enc_seg), line(enc_seg_other),
        col(enc_pos), line(enc_pos), line(enc_pos_other),
    )
    dec_info = (
        col(dec_seg), line(dec_seg), line(dec_seg_other),
        col(dec_pos), line(dec_pos), line(dec_pos_other),
    )
    cross_info = (
        col(dec_seg), line(enc_seg), line(enc_seg_other),
        col(dec_pos), line(enc_pos), line(enc_pos_other),
    )

    enc_n1 = rms_scale(enc_x0, gain[0]).astype(bf16)
    enc_q = project(enc_n1, enc_wi[:, :D]).astype(bf16)
    enc_kv = project(enc_n1, enc_wi[:, D:]).astype(bf16)
    enc_kv2 = swap_core(enc_kv)
    enc_ob = attend_forward(enc_q, enc_kv, enc_kv2, enc_info, enc_x8, False)
    ffn_cast, dec_pack, enc_ob = lax.optimization_barrier((ffn_cast, dec_pack, enc_ob))
    ffn_pack = lax.all_gather(ffn_cast, ALL, axis=0, tiled=True)
    dec_wi, cross_wi = cut(dec_pack, 0, 3 * D), cut(dec_pack, 3 * D, 3 * D)
    dec_wo, cross_wo = cut(dec_pack, 6 * D, D), cut(dec_pack, 7 * D, D)
    dec_fi = cut(ffn_pack, 0, 2 * FF)
    dec_fo = cut(ffn_pack, 2 * FF, FF).reshape(FF, D)
    enc_x1 = enc_x0 + project(enc_ob, enc_wo)
    enc_x2, enc_saved = ffn_forward(enc_x1, gain[1], enc_fi, enc_fo)
    enc_out = rms_scale(enc_x2, gain[2]).astype(bf16)

    dec_n1 = rms_scale(dec_y0, gain[3]).astype(bf16)
    dec_q = project(dec_n1, dec_wi[:, :D]).astype(bf16)
    dec_kv = project(dec_n1, dec_wi[:, D:]).astype(bf16)
    dec_kv2 = swap_core(dec_kv)
    dec_ob = attend_forward(dec_q, dec_kv, dec_kv2, dec_info, dec_x8, True)
    dec_y1 = dec_y0 + project(dec_ob, dec_wo)
    cross_kv = project(enc_out, cross_wi[:, D:]).astype(bf16)
    cross_kv2 = swap_core(cross_kv)
    cross_n = rms_scale(dec_y1, gain[4]).astype(bf16)
    cross_q = project(cross_n, cross_wi[:, :D]).astype(bf16)
    cross_ob = attend_forward(cross_q, cross_kv, cross_kv2, cross_info, None, False)
    dec_y2 = dec_y1 + project(cross_ob, cross_wo)
    dec_y3, dec_saved = ffn_forward(dec_y2, gain[5], dec_fi, dec_fo)
    head_scale = D ** (-0.5)
    hidden_b = (rms_scale(dec_y3, gain[6]) * head_scale).astype(bf16)

    hidden_all = lax.all_gather(hidden_b, ALL, axis=0, tiled=True)
    sizes = tuple(lax.axis_size(axis) for axis in ALL)
    hidden_all = hidden_all.reshape(-1, 2, 2, dec_count, D)
    info = gather_small(jnp.stack([targets, mask_i]), ALL)
    info = info.reshape(-1, 2, 2, 2, 2, dec_count // 2)
    info = jnp.transpose(info, (3, 4, 1, 0, 2, 5)).reshape(2, 1, -1)
    targets_all = info[0] - device * shard
    mask_all = info[1].astype(f32)
    lse_part, picked = head_stats(hidden_all, table_b, targets_all, shard)
    lse = fold_all(lse_part, add_logs)
    d_hidden, head_embed = [], None
    for half in range(2):
        *away, term = head_grad(
            1 - core, hidden_all, table_b, targets_all, mask_all, lse, shard, half
        )
        head_embed = term if head_embed is None else head_embed + term
        away = [swap_core(item) for item in away]
        *home, term = head_grad(
            core, hidden_all, table_b, targets_all, mask_all, lse, shard, half
        )
        head_embed = head_embed + term
        for number in range(2):
            item = add16(home[number], away[number])
            item = item.reshape(sizes[:2] + (2,) + item.shape[2:])
            d_hidden.append(scatter_rest(item, number == 0))
    d_hidden = jnp.concatenate(d_hidden)
    mine = (core * sizes[0] * sizes[1] + device // 4) * 2 + lax.axis_index("seq")
    lse_mine = lax.dynamic_slice_in_dim(
        lse.reshape(2, -1), mine * (dec_count // 2), dec_count // 2, axis=1
    )
    loss_local = jnp.sum(mask * lse_mine.reshape(-1)) - jnp.sum(mask_all * picked)

    d_y3, d_gain_final = norm_pull(dec_y3, gain[6], head_scale, d_hidden)
    d_y2, d_gain_dffn, d_dec_fi, d_dec_fo = ffn_backward(
        d_y3, dec_y2, gain[5], dec_fi, dec_fo, dec_saved
    )
    d_cross_wo, d_cross_ob = branch_backward(d_y2, cross_ob, cross_wo)
    rows_in = lambda out: out.reshape(-1, ffn_out.shape[1], D).reshape(D, FF)
    early, d_cross_ob = lax.optimization_barrier(
        (jnp.concatenate([d_dec_fi, rows_in(d_dec_fo)], axis=1), d_cross_ob)
    )
    early = lax.psum_scatter(early, ALL, scatter_dimension=0, tiled=True)
    d_cross_q, own, other = attend_backward(
        d_cross_ob, cross_q, cross_kv, cross_kv2, cross_info, None, False
    )
    got = (own + swap_core(other).astype(f32)).astype(bf16)
    d_cross_kv = jnp.concatenate([got[0], got[1]], axis=1)
    d_cross_wq = weight_grad(cross_n, d_cross_q)
    d_y1_norm, d_gain_cross = norm_pull(
        dec_y1, gain[4], 1.0, input_grad(d_cross_q, cross_wi[:, :D])
    )
    d_y1 = d_y2 + d_y1_norm
    d_cross_wkv = weight_grad(enc_out, d_cross_kv)
    d_dec_wo, d_dec_ob = branch_backward(d_y1, dec_ob, dec_wo)
    d_dec_q, own, other, dec_y8 = attend_backward(
        d_dec_ob, dec_q, dec_kv, dec_kv2, dec_info, dec_x8, True
    )
    got = (own + swap_core(other).astype(f32)).astype(bf16)
    d_dec_qkv = jnp.concatenate([d_dec_q, got[0], got[1]], axis=1)
    d_dec_table = bias_gradient(dec_y8, dec_picks, core, dec_count, dec_count)
    d_dec_wi = weight_grad(dec_n1, d_dec_qkv)
    d_y0_norm, d_gain_datt = norm_pull(dec_y0, gain[3], 1.0, input_grad(d_dec_qkv, dec_wi))
    d_y0 = d_y1 + d_y0_norm
    d_dec_rest = jnp.concatenate(
        [
            d_dec_wi.astype(bf16),
            d_cross_wq.astype(bf16),
            d_cross_wkv.astype(bf16),
            d_dec_wo,
            d_cross_wo,
        ],
        axis=1,
    )
    dec_lines = line_gather(d_y0.astype(bf16), "z")

    d_x2, d_gain_efin = norm_pull(
        enc_x2, gain[2], 1.0, input_grad(d_cross_kv, cross_wi[:, D:])
    )
    d_x1, d_gain_effn, d_enc_fi, d_enc_fo = ffn_backward(
        d_x2, enc_x1, gain[1], enc_fi, enc_fo, enc_saved
    )
    d_enc_wo, d_enc_ob = branch_backward(d_x1, enc_ob, enc_wo)
    late, early, dec_lines, d_enc_ob = lax.optimization_barrier(
        (
            jnp.concatenate([d_dec_rest, d_enc_fi, rows_in(d_enc_fo)], axis=1),
            early,
            dec_lines,
            d_enc_ob,
        )
    )
    late = lax.psum_scatter(late, ALL, scatter_dimension=0, tiled=True).astype(f32)
    early = early.astype(f32)
    d_enc_q, own, other, enc_y8 = attend_backward(
        d_enc_ob, enc_q, enc_kv, enc_kv2, enc_info, enc_x8, False
    )
    got = (own + swap_core(other).astype(f32)).astype(bf16)
    d_enc_qkv = jnp.concatenate([d_enc_q, got[0], got[1]], axis=1)
    d_enc_table = bias_gradient(enc_y8, enc_picks, core, enc_count, enc_count)
    d_enc_wi = weight_grad(enc_n1, d_enc_qkv)
    d_x0_norm, d_gain_eatt = norm_pull(enc_x0, gain[0], 1.0, input_grad(d_enc_qkv, enc_wi))
    d_x0 = d_x1 + d_x0_norm

    enc_lines = line_gather(d_x0.astype(bf16), "z")
    far_place = lambda item: jnp.where(item == shard, -1, item)[None, :]
    pairs = [
        (far_place(item), grads)
        for item, grads in zip(enc_places + dec_places, enc_lines + dec_lines)
    ]
    input_embed = plane_scatter(pairs, padded)
    grad_embed = head_embed[:shard] + input_embed[:shard]

    d_gains = jnp.stack(
        [
            d_gain_eatt,
            d_gain_effn,
            d_gain_efin,
            d_gain_datt,
            d_gain_cross,
            d_gain_dffn,
            d_gain_final,
        ]
    )
    d_rel = jnp.stack([d_enc_table.reshape(-1), d_dec_table.reshape(-1)])
    d_rel = jnp.transpose(d_rel.reshape(2, -1, rel_table.shape[1]), (1, 0, 2)).reshape(D, 1)
    d_misc = jnp.pad(jnp.concatenate([d_gains.T, d_rel], axis=1), ((0, 0), (0, 120)))
    d_last = jnp.concatenate([d_enc_wi.astype(bf16), d_enc_wo, d_misc.astype(bf16)], axis=1)
    last = jnp.concatenate(
        [scatter_chain(d_last[:, : 2 * D], True), scatter_chain(d_last[:, 2 * D :], False)], axis=1
    )
    rows_out = lambda out: out.reshape(-1, D)
    owned = (
        jnp.stack([cut(last, 0, 3 * D), cut(late, 0, 3 * D), cut(late, 3 * D, 3 * D)]),
        jnp.stack([cut(last, 3 * D, D), cut(late, 6 * D, D), cut(late, 7 * D, D)]),
        jnp.stack([cut(late, 8 * D, 2 * FF), cut(early, 0, 2 * FF)]),
        jnp.stack([rows_out(cut(late, 8 * D + 2 * FF, FF)), rows_out(cut(early, 2 * FF, FF))]),
        last[:, 4 * D + 7].reshape(2, -1),
        last[:, 4 * D : 4 * D + 7].T,
    )
    grads = (grad_embed,) + owned
    squares = sum((jnp.sum(item * item) for item in grads))
    sums = fold_all(jnp.stack([jnp.sum(mask), loss_local, squares]), jnp.add)
    count_all, loss_all, squares_all = sums[0], sums[1], sums[2]
    grad_norm = jnp.sqrt(squares_all) / count_all
    factor = jnp.minimum(1.0, clip_limit / grad_norm) / count_all
    weights = (embed, attn_in, attn_out, ffn_in, ffn_out, rel_table, gains)
    moments = [
        (m_embed, v_embed),
        (m_attn_in, v_attn_in),
        (m_attn_out, v_attn_out),
        (m_ffn_in, v_ffn_in),
        (m_ffn_out, v_ffn_out),
        (m_rel, v_rel),
        (m_gains, v_gains),
    ]
    settings = [
        (1.0, 0.01),
        (0.05, 0.01),
        (0.05, 0.01),
        (0.05, 0.01),
        (0.05, 0.01),
        (0.3, 0.0),
        (0.3, 0.0),
    ]
    results = [loss_all / count_all, grad_norm]
    for slot_number, (param, grad, pair, setting) in enumerate(
        zip(weights, grads, moments, settings)
    ):
        clipped = grad * factor
        first_new, second_new, new_param = adamw(
            param, clipped, pair[0], pair[1], float(STEP), setting[0], setting[1]
        )
        results.extend((clipped if slot_number == 0 else first_new, second_new, new_param))
    return tuple(results)


def solution(mesh):
    rows = ("z", "p", "core")
    every = ALL
    inner = Mesh(mesh.devices.reshape(4, -1, 2, mesh.devices.shape[1]), ALL)
    mat = P(None, every, None)
    vec = P(None, every)
    emb = P(every, None)
    in_specs = (
        P(rows, "seq"),
        P(rows, None),
        P(rows, "seq"),
        P(rows, None),
        P(rows, "seq"),
        P(rows, None),
        P(rows, "seq"),
        P(rows, "seq"),
        P(),
        emb,
        mat,
        mat,
        mat,
        mat,
        vec,
        vec,
        emb,
        emb,
    ) + (mat,) * 8 + (vec,) * 4
    out_specs = (P(), P()) + (emb,) * 3 + (mat,) * 12 + (vec,) * 6
    return jax.shard_map(body, mesh=inner, in_specs=in_specs, out_specs=out_specs, check_vma=False)
```

```python
import functools

import jax
import jax.numpy as jnp
from jax import lax
from jax.experimental import pallas as pl
from jax.experimental.pallas import tpu as pltpu
from jax.sharding import Mesh
from jax.sharding import PartitionSpec as P

D = 768
HEADS = 12
HEAD_DIM = 64
FF = 2048
V = 32128
BUCKETS = 32
STEP = 10

masked_out = -1e30
clip_limit = 0.01
ALL = ("z", "p", "core", "seq")
PLANE = ("p", "core", "seq")
bf16 = jnp.bfloat16
f32 = jnp.float32
VMEM_LIMIT = 56 * 1024 * 1024


def rms_scale(values, gain):
    return values * lax.rsqrt(jnp.mean(values * values, axis=-1, keepdims=True) + 1e-06) * gain


def norm_pull(values, gain, factor, upstream):
    _, pull = jax.vjp(lambda left, right: rms_scale(left, right) * factor, values, gain)
    return pull(upstream)


def gate_up(both):
    return jax.nn.gelu(both[:, :FF], approximate=True) * both[:, FF:]


def project(left, right):
    return jnp.dot(left, right, preferred_element_type=f32)


def weight_grad(inputs, grads):
    return jnp.einsum("td,te->de", inputs, grads, preferred_element_type=f32)


def input_grad(grads, weight):
    return jnp.einsum("te,de->td", grads, weight, preferred_element_type=f32)


def dot_nt(a, b):
    return lax.dot_general(a, b, (((1,), (1,)), ((), ())), preferred_element_type=f32)


def dot_tn(a, b):
    return lax.dot_general(a, b, (((0,), (0,)), ((), ())), preferred_element_type=f32)


def dot_nn(a, b):
    return lax.dot_general(a, b, (((1,), (0,)), ((), ())), preferred_element_type=f32)


def shifted_rows(grid, back):
    total = grid.shape[-1]
    row = 7 - lax.broadcasted_iota(jnp.int32, grid.shape, 0)
    for bit in (1, 2, 4):
        moved = pltpu.roll(grid, bit if back else total - bit, 1)
        grid = jnp.where((row & bit) != 0, moved, grid)
    return grid


def spread(line, rows, width):
    total = line.shape[-1]
    grid = shifted_rows(jnp.broadcast_to(line, (8, total)), False)
    have = 8
    while have < rows:
        grid = jnp.concatenate([pltpu.roll(grid, total - have, 1), grid], axis=0)
        have *= 2
    return grid[:, :width]


def collect(grid, total):
    rows, width = grid.shape
    have = jnp.concatenate([grid, jnp.zeros((rows, total - width), f32)], axis=1)
    while rows > 8:
        rows //= 2
        have = pltpu.roll(have[:rows], rows, 1) + have[rows:]
    return jnp.sum(shifted_rows(have, True), axis=0, keepdims=True)


def probs_of(cfg, refs, block, head):
    bq, has_bias, causal = cfg
    rows = slice(block * bq, (block + 1) * bq)
    cols = slice(head * HEAD_DIM, (head + 1) * HEAD_DIM)
    query = refs["q"][rows, cols]
    scores = []
    for part in range(2):
        keys = refs["k"][part][:, cols]
        s = dot_nt(query, keys) * HEAD_DIM ** (-0.5)
        if has_bias:
            s = s + spread(refs["x8"][head, pl.ds(block * 2 + part, 1), :], bq, keys.shape[0])
        allowed = refs["qseg"][rows, :] == refs["kseg"][part]
        if causal:
            allowed = allowed & (refs["kpos"][part] <= refs["qpos"][rows, :])
        scores.append(jnp.where(allowed, s, masked_out))
    top = jnp.maximum(
        jnp.max(scores[0], axis=1, keepdims=True), jnp.max(scores[1], axis=1, keepdims=True)
    )
    exps = [jnp.exp(s - top) for s in scores]
    total = jnp.sum(exps[0], axis=1, keepdims=True) + jnp.sum(exps[1], axis=1, keepdims=True)
    scale = 1.0 / total
    return query, [e * scale for e in exps]


def name_refs(cfg, refs):
    bq, has_bias, causal = cfg
    it = iter(refs)
    named = {"q": next(it)}
    k0, v0, k1, v1 = next(it), next(it), next(it), next(it)
    named["k"], named["v"] = (k0, k1), (v0, v1)
    ids = next(it), next(it), next(it), next(it), next(it), next(it)
    named["qseg"], named["kseg"] = ids[0], (ids[1][...], ids[2][...])
    named["qpos"], named["kpos"] = ids[3], (ids[4][...], ids[5][...])
    if has_bias:
        named["x8"] = next(it)
    return named, list(it)


def attend_forward_kernel(cfg, *refs):
    named, (out,) = name_refs(cfg, refs)
    bq = cfg[0]
    for block in range(named["q"].shape[0] // bq):
        for head in range(2):
            cols = slice(head * HEAD_DIM, (head + 1) * HEAD_DIM)
            _, probs = probs_of(cfg, named, block, head)
            acc = dot_nn(probs[0].astype(bf16), named["v"][0][:, cols])
            acc = acc + dot_nn(probs[1].astype(bf16), named["v"][1][:, cols])
            out[block * bq : (block + 1) * bq, cols] = acc.astype(bf16)


def attend_backward_kernel(cfg, *refs):
    named, rest = name_refs(cfg, refs)
    bq, has_bias, causal = cfg
    if has_bias:
        grad, dq, own, other, y8 = rest
    else:
        grad, dq, own, other = rest
    blocks = named["q"].shape[0] // bq
    for head in range(2):
        cols = slice(head * HEAD_DIM, (head + 1) * HEAD_DIM)
        dk, dv = [None, None], [None, None]
        for block in range(blocks):
            rows = slice(block * bq, (block + 1) * bq)
            query, probs = probs_of(cfg, named, block, head)
            do = grad[rows, cols]
            dp = [dot_nt(do, named["v"][part][:, cols]) for part in range(2)]
            delta = jnp.sum(probs[0] * dp[0], axis=1, keepdims=True) + jnp.sum(
                probs[1] * dp[1], axis=1, keepdims=True
            )
            acc = None
            for part in range(2):
                ds = (probs[part] * (dp[part] - delta)).astype(bf16)
                term = dot_nn(ds, named["k"][part][:, cols])
                acc = term if acc is None else acc + term
                k_term = dot_tn(query, ds)
                v_term = dot_tn(do, probs[part].astype(bf16))
                dk[part] = k_term if dk[part] is None else dk[part] + k_term
                dv[part] = v_term if dv[part] is None else dv[part] + v_term
                if has_bias:
                    line = collect(ds.astype(f32), y8.shape[-1])
                    y8[head, pl.ds(block * 2 + part, 1), :] = line
            dq[rows, cols] = (acc * HEAD_DIM ** (-0.5)).astype(bf16)
        for part, target in enumerate((own, other)):
            target[0, :, cols] = (dk[part] * HEAD_DIM ** (-0.5)).T.astype(target.dtype)
            target[1, :, cols] = dv[part].T.astype(target.dtype)


def attend_specs(q_len, k_len, has_bias, x8):
    whole = lambda shape: pl.BlockSpec(shape, lambda i: (0,) * len(shape))
    kv = [
        pl.BlockSpec((k_len, 128), lambda i: (0, i)),
        pl.BlockSpec((k_len, 128), lambda i: (0, i + 6)),
    ]
    specs = [pl.BlockSpec((q_len, 128), lambda i: (0, i))] + kv + kv
    specs += [whole((q_len, 1)), whole((1, k_len)), whole((1, k_len))] * 2
    if has_bias:
        specs.append(pl.BlockSpec((2,) + x8.shape[1:], lambda i: (i, 0, 0)))
    return specs


def attend_args(q, kv_own, kv_other, ids, x8):
    args = [q, kv_own, kv_own, kv_other, kv_other] + list(ids)
    if x8 is not None:
        args.append(x8)
    return args


def attend_cost(q_len, k_len, products):
    return pl.CostEstimate(flops=products, bytes_accessed=q_len, transcendentals=0)


def attend_forward(q, kv_own, kv_other, ids, x8, causal):
    q_len, k_len = q.shape[0], kv_own.shape[0]
    cfg = (256, x8 is not None, causal)
    return pl.pallas_call(
        functools.partial(attend_forward_kernel, cfg),
        grid=(HEADS // 2,),
        in_specs=attend_specs(q_len, k_len, x8 is not None, x8),
        out_specs=pl.BlockSpec((q_len, 128), lambda i: (0, i)),
        out_shape=jax.ShapeDtypeStruct((q_len, D), bf16),
        compiler_params=pltpu.CompilerParams(vmem_limit_bytes=VMEM_LIMIT),
        cost_estimate=attend_cost(q_len, k_len, 2),
    )(*attend_args(q, kv_own, kv_other, ids, x8))


def attend_backward(grad, q, kv_own, kv_other, ids, x8, causal):
    q_len, k_len = q.shape[0], kv_own.shape[0]
    cfg = (256, x8 is not None, causal)
    kv_spec = pl.BlockSpec((2, k_len, 128), lambda i: (0, 0, i))
    out_specs = [pl.BlockSpec((q_len, 128), lambda i: (0, i)), kv_spec, kv_spec]
    out_shape = [
        jax.ShapeDtypeStruct((q_len, D), bf16),
        jax.ShapeDtypeStruct((2, k_len, D), f32),
        jax.ShapeDtypeStruct((2, k_len, D), bf16),
    ]
    if x8 is not None:
        out_specs.append(pl.BlockSpec((2,) + x8.shape[1:], lambda i: (i, 0, 0)))
        out_shape.append(jax.ShapeDtypeStruct(x8.shape, f32))
    return pl.pallas_call(
        functools.partial(attend_backward_kernel, cfg),
        grid=(HEADS // 2,),
        in_specs=attend_specs(q_len, k_len, x8 is not None, x8)
        + [pl.BlockSpec((q_len, 128), lambda i: (0, i))],
        out_specs=out_specs,
        out_shape=out_shape,
        compiler_params=pltpu.CompilerParams(vmem_limit_bytes=VMEM_LIMIT),
        cost_estimate=attend_cost(q_len, k_len, 5),
    )(*attend_args(q, kv_own, kv_other, ids, x8), grad)


def bias_bases(core, q_len, k_len, offset):
    bases = []
    for block in range(q_len // 256):
        for part in range(2):
            k_start = (core if part == 0 else 1 - core) * k_len
            q_start = core * q_len + block * 256
            bases.append(k_start - q_start - 255 + offset)
    return bases


def bias_windows(array, core, q_len, k_len):
    size = array.shape[1]
    array = jnp.pad(array, ((0, 0), (0, 16)))
    bases = bias_bases(core, q_len, k_len, size // 2)
    cut = lambda base: lax.dynamic_slice_in_dim(array, base, k_len + 256, axis=1)
    return jnp.stack([cut(base) for base in bases], axis=1)


def bias_lines(table, bucket_row, core, q_len, k_len):
    picks = (bucket_row[None, :] == jnp.arange(BUCKETS, dtype=jnp.int32)[:, None]).astype(bf16)
    per_offset = jnp.einsum("bh,bn->hn", table, picks, preferred_element_type=f32)
    return (
        bias_windows(per_offset, core, q_len, k_len),
        bias_windows(picks.astype(f32), core, q_len, k_len),
    )


def bias_gradient(y8, picks):
    return jnp.einsum("bnw,hnw->bh", picks, y8, precision=lax.Precision.HIGHEST)


def head_stats_kernel(count, hid, tab, tgt, lse_out, pick_out):
    logits = dot_nt(tab[...], hid[...].reshape(-1, D))
    row = lax.broadcasted_iota(jnp.int32, logits.shape, 0)
    pick_out[...] = jnp.sum(jnp.where(row == tgt[...], logits, 0.0), axis=0, keepdims=True)
    logits = jnp.where(row < count, logits, masked_out)
    top = jnp.max(logits, axis=0, keepdims=True)
    lse_out[...] = top + jnp.log(jnp.sum(jnp.exp(logits - top), axis=0, keepdims=True))


def head_grad_kernel(count, core, hid, tab, tgt, msk, lse, dhid_a, dhid_b, dtab):
    tokens = hid[...].reshape(-1, D)
    logits = dot_nt(tab[...], tokens)
    row = lax.broadcasted_iota(jnp.int32, logits.shape, 0)
    soft = jnp.exp(jnp.where(row < count, logits, masked_out) - lse[...])
    grad = ((soft - jnp.where(row == tgt[...], 1.0, 0.0)) * msk[...]).astype(bf16)
    dhid = dot_tn(grad, tab[...]).astype(bf16).reshape(hid.shape)
    cut = hid.shape[3] // 2
    dhid_a[...] = dhid[:, 0, :, :cut]
    dhid_b[...] = dhid[:, 0, :, cut:]
    term = dot_nn(grad, tokens)

    @pl.when(pl.program_id(0) == 0)
    def _():
        dtab[...] = term

    @pl.when(pl.program_id(0) != 0)
    def _():
        dtab[...] += term


def head_stats(hidden, table, targets, count):
    places, each = hidden.shape[0], hidden.shape[3]
    tokens, rows = places * 4 * each, table.shape[0]
    steps = places // 2
    line = pl.BlockSpec((1, 2 * each), lambda h, c, i: (0, (h * 2 + c) * steps + i))
    return pl.pallas_call(
        functools.partial(head_stats_kernel, count),
        grid=(2, 2, steps),
        in_specs=[
            pl.BlockSpec((2, 1, 2, each // 2, D), lambda h, c, i: (i, c, 0, h, 0)),
            pl.BlockSpec((rows, D), lambda h, c, i: (0, 0)),
            line,
        ],
        out_specs=[line, line],
        out_shape=[jax.ShapeDtypeStruct((1, tokens), f32)] * 2,
        compiler_params=pltpu.CompilerParams(vmem_limit_bytes=VMEM_LIMIT),
        cost_estimate=pl.CostEstimate(
            flops=2 * tokens * rows * D, bytes_accessed=2 * tokens * D, transcendentals=tokens * rows
        ),
    )(hidden, table, targets)


def head_grad(core, hidden, table, targets, mask, lse, count, half):
    places, each = hidden.shape[0], hidden.shape[3]
    tokens, rows = places * each, table.shape[0]
    steps = places // 2
    line = pl.BlockSpec((1, 2 * each), lambda i, c: (0, (half * 2 + c[0]) * steps + i))
    piece = pl.BlockSpec((2, 2, each // 4, D), lambda i, c: (i, 0, 0, 0))
    return pl.pallas_call(
        functools.partial(head_grad_kernel, count),
        grid_spec=pltpu.PrefetchScalarGridSpec(
            num_scalar_prefetch=1,
            grid=(steps,),
            in_specs=[
                pl.BlockSpec((2, 1, 2, each // 2, D), lambda i, c: (i, c[0], 0, half, 0)),
                pl.BlockSpec((rows, D), lambda i, c: (0, 0)),
                line,
                line,
                line,
            ],
            out_specs=[piece, piece, pl.BlockSpec((rows, D), lambda i, c: (0, 0))],
        ),
        out_shape=[
            jax.ShapeDtypeStruct((places, 2, each // 4, D), bf16),
            jax.ShapeDtypeStruct((places, 2, each // 4, D), bf16),
            jax.ShapeDtypeStruct((rows, D), f32),
        ],
        compiler_params=pltpu.CompilerParams(vmem_limit_bytes=VMEM_LIMIT),
        cost_estimate=pl.CostEstimate(
            flops=6 * tokens * rows * D, bytes_accessed=4 * tokens * D, transcendentals=tokens * rows
        ),
    )(core.reshape(1), hidden, table, targets, mask, lse)


def place_kernel(first, *refs):
    out = refs[-1]
    rows = out.shape[0]
    base = (pl.program_id(0) + first) * rows
    total = None
    for ids, grads in zip(refs[:-1:2], refs[1:-1:2]):
        row = lax.broadcasted_iota(jnp.int32, (rows, ids.shape[1]), 0) + base
        hot = jnp.where(row == ids[...], 1.0, 0.0).astype(bf16)
        term = dot_nn(hot, grads[...])
        total = term if total is None else total + term
    out[...] = total.astype(bf16)


def place_rows(pairs, first, parts, rows):
    specs, args = [], []
    for ids, grads in pairs:
        specs.append(pl.BlockSpec(ids.shape, lambda i: (0, 0)))
        specs.append(pl.BlockSpec(grads.shape, lambda i: (0, 0)))
        args += [ids, grads]
    return pl.pallas_call(
        functools.partial(place_kernel, first),
        grid=(parts,),
        in_specs=specs,
        out_specs=pl.BlockSpec((rows, D), lambda i: (i, 0)),
        out_shape=jax.ShapeDtypeStruct((parts * rows, D), bf16),
        compiler_params=pltpu.CompilerParams(vmem_limit_bytes=VMEM_LIMIT),
        cost_estimate=pl.CostEstimate(flops=1, bytes_accessed=rows, transcendentals=0),
    )(*args)


def gather_axis(value, axis):
    size = lax.axis_size(axis)
    me = lax.axis_index(axis)
    got = [value]
    for step in range(1, size):
        got.append(lax.ppermute(value, axis, [(i, (i + step) % size) for i in range(size)]))
    stacked = jnp.stack(got)
    return jnp.take(stacked, (me - jnp.arange(size, dtype=jnp.int32)) % size, axis=0)


def gather_small(value, axes):
    shape = value.shape
    for axis in reversed(axes):
        value = gather_axis(value, axis)
        value = value.reshape((-1,) + shape)
    return value


def fold_all(value, combine):
    for axis in reversed(ALL):
        size = lax.axis_size(axis)
        hop = 1
        while hop < size:
            other = lax.ppermute(value, axis, [(i, i ^ hop) for i in range(size)])
            value = combine(value, other)
            hop *= 2
    return value


def swap(value, axis):
    return lax.ppermute(value, axis, [(0, 1), (1, 0)])


def swap_core(value):
    return swap(value, "core")


def add16(left, right):
    return (left.astype(f32) + right.astype(f32)).astype(bf16)


def pick(value, index, dim):
    return lax.dynamic_index_in_dim(value, index, dim, keepdims=False)


def scatter_pair(value, axis, dim):
    if lax.axis_size(axis) != 2:
        return lax.psum_scatter(value, axis, scatter_dimension=dim, tiled=False)
    me = lax.axis_index(axis)
    got = swap(pick(value, 1 - me, dim), axis)
    return add16(pick(value, me, dim), got)


def scatter_rest(value, seq_first):
    if seq_first:
        value = scatter_pair(scatter_pair(value, "seq", 2), "p", 1)
    else:
        value = scatter_pair(scatter_pair(value, "p", 1), "seq", 1)
    size, me = value.shape[0], lax.axis_index("z")
    total = pick(value, me, 0).astype(f32)
    for hop in range(1, size):
        send = pick(value, (me + hop) % size, 0)
        got = lax.ppermute(send, "z", [(i, (i + hop) % size) for i in range(size)])
        total = total + got.astype(f32)
    return total


def scatter_core(value):
    sizes = tuple(lax.axis_size(axis) for axis in ALL)
    return scatter_pair(value.reshape(sizes + (-1, value.shape[-1])), "core", 2)


def scatter_chain(value, seq_first):
    return scatter_rest(scatter_core(value), seq_first)


def line_gather(value, axis):
    size = lax.axis_size(axis)
    ups, downs = [value], [value]
    for _ in range(1, size):
        ups.append(lax.ppermute(ups[-1], axis, [(i, i + 1) for i in range(size - 1)]))
        downs.append(lax.ppermute(downs[-1], axis, [(i + 1, i) for i in range(size - 1)]))
    return [value] + [ups[k] + downs[size - k] for k in range(1, size)]


def line_scatter(parts, axis):
    size = lax.axis_size(axis)
    up, down = None, None
    for step in range(1, size):
        far = size - step
        send_up, send_down = parts[size - far], parts[far]
        if up is not None:
            send_up, send_down = send_up + up, send_down + down
        up = lax.ppermute(send_up, axis, [(i, i + 1) for i in range(step)])
        down = lax.ppermute(send_down, axis, [(size - 1 - i, size - 2 - i) for i in range(step)])
    return parts[0].astype(f32) + up.astype(f32) + down.astype(f32)


def plane_gather(table):
    if lax.axis_size("p") != 2:
        return lax.all_gather(table, PLANE, axis=0, tiled=True)
    half = table.shape[0] // 2
    by_seq, by_p = swap(table, "seq"), swap(table, "p")
    far = [swap(by_p[:half], "seq"), swap(by_seq[half:], "p")]
    mine = [table, by_seq, by_p] + far
    return jnp.concatenate(mine + [swap_core(item) for item in mine])


def plane_slot(owner):
    if lax.axis_size("p") != 2:
        return owner
    other = owner ^ lax.axis_index(PLANE)
    return ((other >> 1) & 1) * 4 + (other >> 2) * 2 + (other & 1)


def plane_scatter(pairs, rows, before):
    pairs, before = lax.optimization_barrier((pairs, before))
    count = lax.axis_size(PLANE)
    if lax.axis_size("p") != 2:
        placed = place_rows(pairs, 0, count, rows)
        placed = lax.psum_scatter(placed, PLANE, scatter_dimension=0, tiled=True)
        return placed.astype(f32), before
    away = swap_core(place_rows(pairs, 4, 4, rows))
    home = place_rows(pairs, 0, 4, rows)
    half = rows // 2
    part = lambda first, last: add16(home[first:last], away[first:last])
    got_low = swap(part(3 * rows, 3 * rows + half), "seq")
    got_high = swap(part(3 * rows + half, 4 * rows), "p")
    seq_high = add16(part(rows + half, 2 * rows), got_high)
    p_low = add16(part(2 * rows, 2 * rows + half), got_low)
    from_seq = swap(jnp.concatenate([part(rows, rows + half), seq_high]), "seq")
    from_p = swap(jnp.concatenate([p_low, part(2 * rows + half, 3 * rows)]), "p")
    return part(0, rows).astype(f32) + from_seq.astype(f32) + from_p.astype(f32), before


def add_logs(left, right):
    top = jnp.maximum(left, right)
    return top + jnp.log(jnp.exp(left - top) + jnp.exp(right - top))


def ffn_forward(resid, gain, w_in, w_out):
    normed = rms_scale(resid, gain).astype(bf16)
    both = project(normed, w_in)
    hidden = gate_up(both).astype(bf16)
    return (resid + project(hidden, w_out), (normed, both, hidden))


def ffn_backward(upstream, resid, gain, w_in, w_out, saved):
    normed, both, hidden = saved
    grad_b = upstream.astype(bf16)
    d_out = weight_grad(hidden, grad_b).astype(bf16)
    _, pull = jax.vjp(gate_up, both)
    (d_both,) = pull(input_grad(grad_b, w_out))
    d_both_b = d_both.astype(bf16)
    d_in = weight_grad(normed, d_both_b).astype(bf16)
    d_resid, d_gain = norm_pull(resid, gain, 1.0, input_grad(d_both_b, w_in))
    return (upstream + d_resid, d_gain, d_in, d_out)


def branch_backward(upstream, out_b, w_out):
    grad_b = upstream.astype(bf16)
    return (weight_grad(out_b, grad_b).astype(bf16), input_grad(grad_b, w_out).astype(bf16))


def adamw(weight, grad, first_m, second_m, count, rate, decay):
    first_new = 0.9 * first_m + 0.1 * grad
    second_new = 0.999 * second_m + 0.001 * grad * grad
    first_hat = first_new / (1.0 - 0.9**count)
    second_hat = second_new / (1.0 - 0.999**count)
    return (
        first_new,
        second_new,
        weight - rate * (first_hat / (jnp.sqrt(second_hat) + 1e-08) + decay * weight),
    )


def body(
    enc_ids,
    enc_segs,
    sentinel,
    mode,
    dec_ids,
    dec_segs,
    target_ids,
    target_mask,
    buckets,
    embed,
    attn_in,
    attn_out,
    ffn_in,
    ffn_out,
    rel_table,
    gains,
    m_embed,
    v_embed,
    m_attn_in,
    v_attn_in,
    m_attn_out,
    v_attn_out,
    m_ffn_in,
    v_ffn_in,
    m_ffn_out,
    v_ffn_out,
    m_rel,
    v_rel,
    m_gains,
    v_gains,
):
    core = lax.axis_index("core")
    z_at = lax.axis_index("z")
    z_size = lax.axis_size("z")
    plane_size = lax.axis_size(PLANE)
    device = lax.axis_index(ALL)
    shard = embed.shape[0]
    padded = (shard // 16 + 1) * 16
    enc_count, dec_count = enc_ids.shape[1], dec_ids.shape[1]
    enc_len, dec_len = enc_segs.shape[1], dec_segs.shape[1]

    table_b = jnp.pad(embed.astype(bf16), ((0, padded - shard), (0, 0)))
    misc = jnp.concatenate([gains.T, rel_table.reshape(-1, 1)], axis=1)
    misc = jnp.pad(misc, ((0, 0), (0, 120)))
    shard_in = attn_in.shape[1]
    flat_out = ffn_out.astype(bf16).reshape(2, shard_in, -1)
    enc_cast = jnp.concatenate([attn_in[0], ffn_in[0], attn_out[0], misc], axis=1).astype(bf16)
    enc_pack = lax.all_gather(
        jnp.concatenate([enc_cast, flat_out[0]], axis=1), ALL, axis=0, tiled=True
    )
    dec_cast = jnp.concatenate(
        [attn_in[1], attn_in[2], attn_out[1], attn_out[2]], axis=1
    ).astype(bf16)
    ffn_cast = jnp.concatenate([ffn_in[1].astype(bf16), flat_out[1]], axis=1)
    plane_table = plane_gather(table_b)
    flat = jnp.concatenate(
        [
            enc_ids[0],
            sentinel[0],
            dec_ids[0],
            target_ids[0],
            target_mask[0],
            enc_segs[0],
            dec_segs[0],
            jnp.pad(mode[0], (0, 128 - mode.shape[1])),
        ]
    )
    flat = lax.ppermute(flat, ("core", "seq"), [(0, 0), (1, 2), (2, 1), (3, 3)])
    sizes = [enc_count, enc_count, dec_count, dec_count, dec_count, enc_len, dec_len]
    pieces, start = [], 0
    for size in sizes:
        pieces.append(flat[start : start + size])
        start += size
    enc_id, sent, dec_id, targets, mask_i, enc_seg_all, dec_seg_all = pieces
    mode_row = flat[start : start + mode.shape[1]]
    mask = mask_i.astype(f32)

    enc_seg = lax.dynamic_slice_in_dim(enc_seg_all, core * enc_count, enc_count)
    enc_seg_other = lax.dynamic_slice_in_dim(enc_seg_all, (1 - core) * enc_count, enc_count)
    dec_seg = lax.dynamic_slice_in_dim(dec_seg_all, core * dec_count, dec_count)
    dec_seg_other = lax.dynamic_slice_in_dim(dec_seg_all, (1 - core) * dec_count, dec_count)
    enc_range = jnp.arange(enc_count, dtype=jnp.int32)
    dec_range = jnp.arange(dec_count, dtype=jnp.int32)
    enc_pos, enc_pos_other = core * enc_count + enc_range, (1 - core) * enc_count + enc_range
    dec_pos, dec_pos_other = core * dec_count + dec_range, (1 - core) * dec_count + dec_range
    prior_all = jnp.concatenate([enc_seg_all[:1], enc_seg_all[:-1]])
    prior = lax.dynamic_slice_in_dim(prior_all, core * enc_count, enc_count)
    first = (enc_pos == 0) | (enc_seg != prior)
    mode_of = jnp.sum(
        jnp.where(
            enc_seg[:, None] == jnp.arange(mode.shape[1], dtype=jnp.int32)[None], mode_row[None], 0
        ),
        axis=1,
    )
    enc_tok = jnp.where(sent == 1, V - 1 - enc_seg, enc_id)
    enc_tok = jnp.where(first, V - 101 - mode_of, enc_tok)
    local_ids = jnp.concatenate([enc_tok, dec_id])

    line_ids = line_gather(local_ids, "z")
    plane_rows = plane_size * shard
    places = []
    for ids in line_ids:
        rel_id = ids - z_at * plane_rows
        inside = (rel_id >= 0) & (rel_id < plane_rows)
        places.append(
            jnp.where(inside, plane_slot(rel_id // shard) * padded + rel_id % shard, shard)
        )
    dec_cast, enc_pack, plane_table, places = lax.optimization_barrier(
        (dec_cast, enc_pack, plane_table, places)
    )
    dec_pack = lax.all_gather(dec_cast, ALL, axis=0, tiled=True)
    enc_places = [item[:enc_count] for item in places]
    dec_places = [item[enc_count:] for item in places]

    def look(items):
        got = jnp.take(plane_table, jnp.concatenate(items), axis=0, mode="clip")
        return line_scatter(jnp.split(got, len(items)), "z")

    looked = look(places)
    enc_x0, dec_y0 = looked[:enc_count], looked[enc_count:]

    cut = lambda pack, start, width: lax.slice_in_dim(pack, start, start + width, axis=1)
    enc_wi, enc_fi = cut(enc_pack, 0, 3 * D), cut(enc_pack, 3 * D, 2 * FF)
    enc_wo, misc_all = cut(enc_pack, 3 * D + 2 * FF, D), cut(enc_pack, 4 * D + 2 * FF, 128)
    enc_fo = cut(enc_pack, 4 * D + 2 * FF + 128, FF).reshape(FF, D)
    gain = misc_all[:, :7].T.astype(f32)
    rel_all = jnp.transpose(misc_all[:, 7].reshape(-1, 2, rel_table.shape[1]), (1, 0, 2))
    rel_all = rel_all.reshape(2, BUCKETS, HEADS)

    enc_x8, enc_picks = bias_lines(rel_all[0], buckets[0], core, enc_count, enc_count)
    dec_x8, dec_picks = bias_lines(rel_all[1], buckets[1], core, dec_count, dec_count)
    col, line = (lambda v: v[:, None]), (lambda v: v[None, :])
    enc_info = (
        col(enc_seg), line(enc_seg), line(enc_seg_other),
        col(enc_pos), line(enc_pos), line(enc_pos_other),
    )
    dec_info = (
        col(dec_seg), line(dec_seg), line(dec_seg_other),
        col(dec_pos), line(dec_pos), line(dec_pos_other),
    )
    cross_info = (
        col(dec_seg), line(enc_seg), line(enc_seg_other),
        col(dec_pos), line(enc_pos), line(enc_pos_other),
    )

    enc_n1 = rms_scale(enc_x0, gain[0]).astype(bf16)
    enc_q = project(enc_n1, enc_wi[:, :D]).astype(bf16)
    enc_kv = project(enc_n1, enc_wi[:, D:]).astype(bf16)
    enc_kv2 = swap_core(enc_kv)
    enc_ob = attend_forward(enc_q, enc_kv, enc_kv2, enc_info, enc_x8, False)
    ffn_cast, dec_pack, enc_ob = lax.optimization_barrier((ffn_cast, dec_pack, enc_ob))
    ffn_pack = lax.all_gather(ffn_cast, ALL, axis=0, tiled=True)
    dec_wi, cross_wi = cut(dec_pack, 0, 3 * D), cut(dec_pack, 3 * D, 3 * D)
    dec_wo, cross_wo = cut(dec_pack, 6 * D, D), cut(dec_pack, 7 * D, D)
    dec_fi = cut(ffn_pack, 0, 2 * FF)
    dec_fo = cut(ffn_pack, 2 * FF, FF).reshape(FF, D)
    enc_x1 = enc_x0 + project(enc_ob, enc_wo)
    enc_x2, enc_saved = ffn_forward(enc_x1, gain[1], enc_fi, enc_fo)
    enc_out = rms_scale(enc_x2, gain[2]).astype(bf16)

    dec_n1 = rms_scale(dec_y0, gain[3]).astype(bf16)
    dec_q = project(dec_n1, dec_wi[:, :D]).astype(bf16)
    dec_kv = project(dec_n1, dec_wi[:, D:]).astype(bf16)
    dec_kv2 = swap_core(dec_kv)
    dec_ob = attend_forward(dec_q, dec_kv, dec_kv2, dec_info, dec_x8, True)
    dec_y1 = dec_y0 + project(dec_ob, dec_wo)
    cross_kv = project(enc_out, cross_wi[:, D:]).astype(bf16)
    cross_kv2 = swap_core(cross_kv)
    cross_n = rms_scale(dec_y1, gain[4]).astype(bf16)
    cross_q = project(cross_n, cross_wi[:, :D]).astype(bf16)
    cross_ob = attend_forward(cross_q, cross_kv, cross_kv2, cross_info, None, False)
    dec_y2 = dec_y1 + project(cross_ob, cross_wo)
    dec_y3, dec_saved = ffn_forward(dec_y2, gain[5], dec_fi, dec_fo)
    head_scale = D ** (-0.5)
    hidden_b = (rms_scale(dec_y3, gain[6]) * head_scale).astype(bf16)

    hidden_all = lax.all_gather(hidden_b, ALL, axis=0, tiled=True)
    sizes = tuple(lax.axis_size(axis) for axis in ALL)
    hidden_all = hidden_all.reshape(-1, 2, 2, dec_count, D)
    info = gather_small(jnp.stack([targets, mask_i]), ALL)
    info = info.reshape(-1, 2, 2, 2, 2, dec_count // 2)
    info = jnp.transpose(info, (3, 4, 1, 0, 2, 5)).reshape(2, 1, -1)
    targets_all = info[0] - device * shard
    mask_all = info[1].astype(f32)
    lse_part, picked = head_stats(hidden_all, table_b, targets_all, shard)
    lse = fold_all(lse_part, add_logs)
    d_hidden, head_embed = [], None
    for half in range(2):
        *away, term = head_grad(
            1 - core, hidden_all, table_b, targets_all, mask_all, lse, shard, half
        )
        head_embed = term if head_embed is None else head_embed + term
        away = [swap_core(item) for item in away]
        *home, term = head_grad(
            core, hidden_all, table_b, targets_all, mask_all, lse, shard, half
        )
        head_embed = head_embed + term
        for number in range(2):
            item = add16(home[number], away[number])
            item = item.reshape(sizes[:2] + (2,) + item.shape[2:])
            d_hidden.append(scatter_rest(item, number == 0))
    d_hidden = jnp.concatenate(d_hidden)
    mine = (core * sizes[0] * sizes[1] + device // 4) * 2 + lax.axis_index("seq")
    lse_mine = lax.dynamic_slice_in_dim(
        lse.reshape(2, -1), mine * (dec_count // 2), dec_count // 2, axis=1
    )
    loss_local = jnp.sum(mask * lse_mine.reshape(-1)) - jnp.sum(mask_all * picked)

    d_y3, d_gain_final = norm_pull(dec_y3, gain[6], head_scale, d_hidden)
    d_y2, d_gain_dffn, d_dec_fi, d_dec_fo = ffn_backward(
        d_y3, dec_y2, gain[5], dec_fi, dec_fo, dec_saved
    )
    d_cross_wo, d_cross_ob = branch_backward(d_y2, cross_ob, cross_wo)
    rows_in = lambda out: out.reshape(-1, ffn_out.shape[1], D).reshape(D, FF)
    early, d_cross_ob = lax.optimization_barrier(
        (jnp.concatenate([d_dec_fi, rows_in(d_dec_fo)], axis=1), d_cross_ob)
    )
    early = lax.psum_scatter(early, ALL, scatter_dimension=0, tiled=True)
    d_cross_q, own, other = attend_backward(
        d_cross_ob, cross_q, cross_kv, cross_kv2, cross_info, None, False
    )
    got = (own + swap_core(other).astype(f32)).astype(bf16)
    d_cross_kv = jnp.concatenate([got[0], got[1]], axis=1)
    d_cross_wq = weight_grad(cross_n, d_cross_q)
    d_y1_norm, d_gain_cross = norm_pull(
        dec_y1, gain[4], 1.0, input_grad(d_cross_q, cross_wi[:, :D])
    )
    d_y1 = d_y2 + d_y1_norm
    d_cross_wkv = weight_grad(enc_out, d_cross_kv)
    d_dec_wo, d_dec_ob = branch_backward(d_y1, dec_ob, dec_wo)
    d_dec_q, own, other, dec_y8 = attend_backward(
        d_dec_ob, dec_q, dec_kv, dec_kv2, dec_info, dec_x8, True
    )
    got = (own + swap_core(other).astype(f32)).astype(bf16)
    d_dec_qkv = jnp.concatenate([d_dec_q, got[0], got[1]], axis=1)
    d_dec_table = bias_gradient(dec_y8, dec_picks)
    d_dec_wi = weight_grad(dec_n1, d_dec_qkv)
    d_y0_norm, d_gain_datt = norm_pull(dec_y0, gain[3], 1.0, input_grad(d_dec_qkv, dec_wi))
    d_y0 = d_y1 + d_y0_norm
    d_dec_rest = jnp.concatenate(
        [
            d_dec_wi.astype(bf16),
            d_cross_wq.astype(bf16),
            d_cross_wkv.astype(bf16),
            d_dec_wo,
            d_cross_wo,
        ],
        axis=1,
    )
    dec_lines = line_gather(d_y0.astype(bf16), "z")

    d_x2, d_gain_efin = norm_pull(
        enc_x2, gain[2], 1.0, input_grad(d_cross_kv, cross_wi[:, D:])
    )
    d_x1, d_gain_effn, d_enc_fi, d_enc_fo = ffn_backward(
        d_x2, enc_x1, gain[1], enc_fi, enc_fo, enc_saved
    )
    early, d_x1 = lax.optimization_barrier((early, d_x1))
    d_enc_wo, d_enc_ob = branch_backward(d_x1, enc_ob, enc_wo)
    d_enc_low, d_enc_high = d_enc_fi[:, :3456], jnp.concatenate([d_enc_fi[:, 3456:], d_enc_wo], 1)
    enc_sums = [scatter_core(item) for item in (d_enc_low, d_enc_high, d_enc_fo)]
    late, dec_lines, enc_sums, d_enc_ob = lax.optimization_barrier(
        (d_dec_rest, dec_lines, enc_sums, d_enc_ob)
    )
    late = lax.psum_scatter(late, ALL, scatter_dimension=0, tiled=True)
    early = early.astype(f32)
    g_low, g_high, g_fo = [
        scatter_rest(item, number == 0) for number, item in enumerate(enc_sums)
    ]
    d_enc_q, own, other, enc_y8 = attend_backward(
        d_enc_ob, enc_q, enc_kv, enc_kv2, enc_info, enc_x8, False
    )
    got = (own + swap_core(other).astype(f32)).astype(bf16)
    d_enc_qkv = jnp.concatenate([d_enc_q, got[0], got[1]], axis=1)
    d_enc_table = bias_gradient(enc_y8, enc_picks)
    d_enc_wi = weight_grad(enc_n1, d_enc_qkv)
    d_x0_norm, d_gain_eatt = norm_pull(enc_x0, gain[0], 1.0, input_grad(d_enc_qkv, enc_wi))
    d_x0 = d_x1 + d_x0_norm

    enc_lines = line_gather(d_x0.astype(bf16), "z")
    far_place = lambda item: jnp.where(item == shard, -1, item)[None, :]
    pairs = [
        (far_place(item), grads)
        for item, grads in zip(enc_places + dec_places, enc_lines + dec_lines)
    ]
    input_embed, late = plane_scatter(pairs, padded, late)
    late = late.astype(f32)
    grad_embed = head_embed[:shard] + input_embed[:shard]

    d_gains = jnp.stack(
        [
            d_gain_eatt,
            d_gain_effn,
            d_gain_efin,
            d_gain_datt,
            d_gain_cross,
            d_gain_dffn,
            d_gain_final,
        ]
    )
    d_rel = jnp.stack([d_enc_table.reshape(-1), d_dec_table.reshape(-1)])
    d_rel = jnp.transpose(d_rel.reshape(2, -1, rel_table.shape[1]), (1, 0, 2)).reshape(D, 1)
    d_misc = jnp.pad(jnp.concatenate([d_gains.T, d_rel], axis=1), ((0, 0), (0, 120)))
    d_last = jnp.concatenate([d_enc_wi.astype(bf16), d_misc.astype(bf16)], axis=1)
    last = [scatter_chain(d_last[:, :1152], True), scatter_chain(d_last[:, 1152:], False)]
    squares = sum(
        (jnp.sum(item * item) for item in (grad_embed, early, late, g_low, g_high, g_fo, *last))
    )
    sums = fold_all(jnp.stack([jnp.sum(mask), loss_local, squares]), jnp.add)
    last = jnp.concatenate(last, axis=1)
    rows_out = lambda out: out.reshape(-1, D)
    owned = (
        jnp.stack([cut(last, 0, 3 * D), cut(late, 0, 3 * D), cut(late, 3 * D, 3 * D)]),
        jnp.stack([cut(g_high, 640, D), cut(late, 6 * D, D), cut(late, 7 * D, D)]),
        jnp.stack(
            [jnp.concatenate([g_low, cut(g_high, 0, 640)], axis=1), cut(early, 0, 2 * FF)]
        ),
        jnp.stack([g_fo, rows_out(cut(early, 2 * FF, FF))]),
        last[:, 3 * D + 7].reshape(2, -1),
        last[:, 3 * D : 3 * D + 7].T,
    )
    grads = (grad_embed,) + owned
    count_all, loss_all, squares_all = sums[0], sums[1], sums[2]
    grad_norm = jnp.sqrt(squares_all) / count_all
    factor = jnp.minimum(1.0, clip_limit / grad_norm) / count_all
    weights = (embed, attn_in, attn_out, ffn_in, ffn_out, rel_table, gains)
    moments = [
        (m_embed, v_embed),
        (m_attn_in, v_attn_in),
        (m_attn_out, v_attn_out),
        (m_ffn_in, v_ffn_in),
        (m_ffn_out, v_ffn_out),
        (m_rel, v_rel),
        (m_gains, v_gains),
    ]
    settings = [
        (1.0, 0.01),
        (0.05, 0.01),
        (0.05, 0.01),
        (0.05, 0.01),
        (0.05, 0.01),
        (0.3, 0.0),
        (0.3, 0.0),
    ]
    results = [loss_all / count_all, grad_norm]
    for slot_number, (param, grad, pair, setting) in enumerate(
        zip(weights, grads, moments, settings)
    ):
        clipped = grad * factor
        first_new, second_new, new_param = adamw(
            param, clipped, pair[0], pair[1], float(STEP), setting[0], setting[1]
        )
        results.extend((clipped if slot_number == 0 else first_new, second_new, new_param))
    return tuple(results)


def solution(mesh):
    rows = ("z", "p", "core")
    every = ALL
    inner = Mesh(mesh.devices.reshape(4, -1, 2, mesh.devices.shape[1]), ALL)
    mat = P(None, every, None)
    vec = P(None, every)
    emb = P(every, None)
    in_specs = (
        P(rows, "seq"),
        P(rows, None),
        P(rows, "seq"),
        P(rows, None),
        P(rows, "seq"),
        P(rows, None),
        P(rows, "seq"),
        P(rows, "seq"),
        P(),
        emb,
        mat,
        mat,
        mat,
        mat,
        vec,
        vec,
        emb,
        emb,
    ) + (mat,) * 8 + (vec,) * 4
    out_specs = (P(), P()) + (emb,) * 3 + (mat,) * 12 + (vec,) * 6
    return jax.shard_map(body, mesh=inner, in_specs=in_specs, out_specs=out_specs, check_vma=False)
```

```python
import functools

import jax
import jax.numpy as jnp
from jax import lax
from jax.experimental import pallas as pl
from jax.experimental.pallas import tpu as pltpu
from jax.sharding import Mesh
from jax.sharding import PartitionSpec as P

D = 768
HEADS = 12
HEAD_DIM = 64
FF = 2048
V = 32128
BUCKETS = 32
STEP = 10

masked_out = -1e30
clip_limit = 0.01
ALL = ("z", "p", "core", "seq")
PLANE = ("p", "core", "seq")
bf16 = jnp.bfloat16
f32 = jnp.float32
VMEM_LIMIT = 56 * 1024 * 1024


def rms_scale(values, gain):
    return values * lax.rsqrt(jnp.mean(values * values, axis=-1, keepdims=True) + 1e-06) * gain


def norm_pull(values, gain, factor, upstream):
    _, pull = jax.vjp(lambda left, right: rms_scale(left, right) * factor, values, gain)
    return pull(upstream)


def gate_up(both):
    return jax.nn.gelu(both[:, :FF], approximate=True) * both[:, FF:]


def project(left, right):
    return jnp.dot(left, right, preferred_element_type=f32)


def weight_grad(inputs, grads):
    return jnp.einsum("td,te->de", inputs, grads, preferred_element_type=f32)


def input_grad(grads, weight):
    return jnp.einsum("te,de->td", grads, weight, preferred_element_type=f32)


def dot_nt(a, b):
    return lax.dot_general(a, b, (((1,), (1,)), ((), ())), preferred_element_type=f32)


def dot_tn(a, b):
    return lax.dot_general(a, b, (((0,), (0,)), ((), ())), preferred_element_type=f32)


def dot_nn(a, b):
    return lax.dot_general(a, b, (((1,), (0,)), ((), ())), preferred_element_type=f32)


def spread(eight, rows, width):
    total = eight.shape[-1]
    grid = eight
    have = 8
    while have < rows:
        grid = jnp.concatenate([pltpu.roll(grid, total - have, 1), grid], axis=0)
        have *= 2
    return grid[:, :width]


def collect(grid, total):
    rows, width = grid.shape
    have = jnp.concatenate([grid, jnp.zeros((rows, total - width), f32)], axis=1)
    while rows > 8:
        rows //= 2
        have = pltpu.roll(have[:rows], rows, 1) + have[rows:]
    return have


def probs_of(cfg, refs, block, head):
    bq, has_bias, causal = cfg
    rows = slice(block * bq, (block + 1) * bq)
    cols = slice(head * HEAD_DIM, (head + 1) * HEAD_DIM)
    query = refs["q"][rows, cols]
    scores = []
    for part in range(2):
        keys = refs["k"][part][:, cols]
        s = dot_nt(query, keys) * HEAD_DIM ** (-0.5)
        if has_bias:
            s = s + spread(refs["x8"][head, block * 2 + part], bq, keys.shape[0])
        allowed = refs["qseg"][rows, :] == refs["kseg"][part]
        if causal:
            allowed = allowed & (refs["kpos"][part] <= refs["qpos"][rows, :])
        scores.append(jnp.where(allowed, s, masked_out))
    top = jnp.maximum(
        jnp.max(scores[0], axis=1, keepdims=True), jnp.max(scores[1], axis=1, keepdims=True)
    )
    exps = [jnp.exp(s - top) for s in scores]
    total = jnp.sum(exps[0], axis=1, keepdims=True) + jnp.sum(exps[1], axis=1, keepdims=True)
    scale = 1.0 / total
    return query, [e * scale for e in exps]


def name_refs(cfg, refs):
    bq, has_bias, causal = cfg
    it = iter(refs)
    named = {"q": next(it)}
    k0, v0, k1, v1 = next(it), next(it), next(it), next(it)
    named["k"], named["v"] = (k0, k1), (v0, v1)
    ids = next(it), next(it), next(it), next(it), next(it), next(it)
    named["qseg"], named["kseg"] = ids[0], (ids[1][...], ids[2][...])
    named["qpos"], named["kpos"] = ids[3], (ids[4][...], ids[5][...])
    if has_bias:
        named["x8"] = next(it)
    return named, list(it)


def attend_forward_kernel(cfg, *refs):
    named, (out,) = name_refs(cfg, refs)
    bq = cfg[0]
    for block in range(named["q"].shape[0] // bq):
        for head in range(2):
            cols = slice(head * HEAD_DIM, (head + 1) * HEAD_DIM)
            _, probs = probs_of(cfg, named, block, head)
            acc = dot_nn(probs[0].astype(bf16), named["v"][0][:, cols])
            acc = acc + dot_nn(probs[1].astype(bf16), named["v"][1][:, cols])
            out[block * bq : (block + 1) * bq, cols] = acc.astype(bf16)


def attend_backward_kernel(cfg, *refs):
    named, rest = name_refs(cfg, refs)
    bq, has_bias, causal = cfg
    if has_bias:
        grad, dq, own, other, y8 = rest
    else:
        grad, dq, own, other = rest
    blocks = named["q"].shape[0] // bq
    for head in range(2):
        cols = slice(head * HEAD_DIM, (head + 1) * HEAD_DIM)
        dk, dv = [None, None], [None, None]
        for block in range(blocks):
            rows = slice(block * bq, (block + 1) * bq)
            query, probs = probs_of(cfg, named, block, head)
            do = grad[rows, cols]
            dp = [dot_nt(do, named["v"][part][:, cols]) for part in range(2)]
            delta = jnp.sum(probs[0] * dp[0], axis=1, keepdims=True) + jnp.sum(
                probs[1] * dp[1], axis=1, keepdims=True
            )
            acc = None
            for part in range(2):
                ds = (probs[part] * (dp[part] - delta)).astype(bf16)
                term = dot_nn(ds, named["k"][part][:, cols])
                acc = term if acc is None else acc + term
                k_term = dot_tn(query, ds)
                v_term = dot_tn(do, probs[part].astype(bf16))
                dk[part] = k_term if dk[part] is None else dk[part] + k_term
                dv[part] = v_term if dv[part] is None else dv[part] + v_term
                if has_bias:
                    y8[head, block * 2 + part] = collect(ds.astype(f32), y8.shape[-1])
            dq[rows, cols] = (acc * HEAD_DIM ** (-0.5)).astype(bf16)
        for part, target in enumerate((own, other)):
            target[0, :, cols] = (dk[part] * HEAD_DIM ** (-0.5)).T.astype(target.dtype)
            target[1, :, cols] = dv[part].T.astype(target.dtype)


def attend_specs(q_len, k_len, has_bias, x8):
    whole = lambda shape: pl.BlockSpec(shape, lambda i: (0,) * len(shape))
    kv = [
        pl.BlockSpec((k_len, 128), lambda i: (0, i)),
        pl.BlockSpec((k_len, 128), lambda i: (0, i + 6)),
    ]
    specs = [pl.BlockSpec((q_len, 128), lambda i: (0, i))] + kv + kv
    specs += [whole((q_len, 1)), whole((1, k_len)), whole((1, k_len))] * 2
    if has_bias:
        specs.append(pl.BlockSpec((2,) + x8.shape[1:], lambda i: (i, 0, 0, 0)))
    return specs


def attend_args(q, kv_own, kv_other, ids, x8):
    args = [q, kv_own, kv_own, kv_other, kv_other] + list(ids)
    if x8 is not None:
        args.append(x8)
    return args


def attend_cost(q_len, k_len, products):
    return pl.CostEstimate(flops=products, bytes_accessed=q_len, transcendentals=0)


def attend_forward(q, kv_own, kv_other, ids, x8, causal):
    q_len, k_len = q.shape[0], kv_own.shape[0]
    cfg = (256, x8 is not None, causal)
    return pl.pallas_call(
        functools.partial(attend_forward_kernel, cfg),
        grid=(HEADS // 2,),
        in_specs=attend_specs(q_len, k_len, x8 is not None, x8),
        out_specs=pl.BlockSpec((q_len, 128), lambda i: (0, i)),
        out_shape=jax.ShapeDtypeStruct((q_len, D), bf16),
        compiler_params=pltpu.CompilerParams(vmem_limit_bytes=VMEM_LIMIT),
        cost_estimate=attend_cost(q_len, k_len, 2),
    )(*attend_args(q, kv_own, kv_other, ids, x8))


def attend_backward(grad, q, kv_own, kv_other, ids, x8, causal):
    q_len, k_len = q.shape[0], kv_own.shape[0]
    cfg = (256, x8 is not None, causal)
    kv_spec = pl.BlockSpec((2, k_len, 128), lambda i: (0, 0, i))
    out_specs = [pl.BlockSpec((q_len, 128), lambda i: (0, i)), kv_spec, kv_spec]
    out_shape = [
        jax.ShapeDtypeStruct((q_len, D), bf16),
        jax.ShapeDtypeStruct((2, k_len, D), f32),
        jax.ShapeDtypeStruct((2, k_len, D), bf16),
    ]
    if x8 is not None:
        out_specs.append(pl.BlockSpec((2,) + x8.shape[1:], lambda i: (i, 0, 0, 0)))
        out_shape.append(jax.ShapeDtypeStruct(x8.shape, f32))
    return pl.pallas_call(
        functools.partial(attend_backward_kernel, cfg),
        grid=(HEADS // 2,),
        in_specs=attend_specs(q_len, k_len, x8 is not None, x8)
        + [pl.BlockSpec((q_len, 128), lambda i: (0, i))],
        out_specs=out_specs,
        out_shape=out_shape,
        compiler_params=pltpu.CompilerParams(vmem_limit_bytes=VMEM_LIMIT),
        cost_estimate=attend_cost(q_len, k_len, 5),
    )(*attend_args(q, kv_own, kv_other, ids, x8), grad)


def bias_bases(core, q_len, k_len, offset):
    bases = []
    for block in range(q_len // 256):
        for part in range(2):
            k_start = (core if part == 0 else 1 - core) * k_len
            q_start = core * q_len + block * 256
            bases.append(k_start - q_start - 255 + offset)
    return bases


def bias_windows(array, core, q_len, k_len):
    size, width = array.shape[1], k_len + 256
    array = jnp.pad(array, ((0, 0), (0, 16)))
    rows = jnp.stack([array[:, 7 - r : size + 9 - r] for r in range(8)], axis=1)
    bases = bias_bases(core, q_len, k_len, size // 2)
    cut = lambda base: lax.dynamic_slice_in_dim(rows, base, width, axis=2)
    return jnp.stack([cut(base) for base in bases], axis=1)


def bias_lines(table, bucket_row, core, q_len, k_len):
    picks = (bucket_row[None, :] == jnp.arange(BUCKETS, dtype=jnp.int32)[:, None]).astype(bf16)
    per_offset = jnp.einsum("bh,bn->hn", table, picks, preferred_element_type=f32)
    return (
        bias_windows(per_offset, core, q_len, k_len),
        bias_windows(picks.astype(f32), core, q_len, k_len),
    )


def bias_gradient(y8, picks):
    return jnp.einsum("bnrw,hnrw->bh", picks, y8, precision=lax.Precision.HIGHEST)


def head_stats_kernel(count, hid, tab, tgt, lse_out, pick_out):
    logits = dot_nt(tab[...], hid[...].reshape(-1, D))
    row = lax.broadcasted_iota(jnp.int32, logits.shape, 0)
    pick_out[...] = jnp.sum(jnp.where(row == tgt[...], logits, 0.0), axis=0, keepdims=True)
    logits = jnp.where(row < count, logits, masked_out)
    top = jnp.max(logits, axis=0, keepdims=True)
    lse_out[...] = top + jnp.log(jnp.sum(jnp.exp(logits - top), axis=0, keepdims=True))


def head_grad_kernel(count, core, hid, tab, tgt, msk, lse, dhid_a, dhid_b, dtab):
    tokens = hid[...].reshape(-1, D)
    logits = dot_nt(tab[...], tokens)
    row = lax.broadcasted_iota(jnp.int32, logits.shape, 0)
    soft = jnp.exp(jnp.where(row < count, logits, masked_out) - lse[...])
    grad = ((soft - jnp.where(row == tgt[...], 1.0, 0.0)) * msk[...]).astype(bf16)
    dhid = dot_tn(grad, tab[...]).astype(bf16).reshape(hid.shape)
    cut = hid.shape[3] // 2
    dhid_a[...] = dhid[:, 0, :, :cut]
    dhid_b[...] = dhid[:, 0, :, cut:]
    term = dot_nn(grad, tokens)

    @pl.when(pl.program_id(0) == 0)
    def _():
        dtab[...] = term

    @pl.when(pl.program_id(0) != 0)
    def _():
        dtab[...] += term


def head_stats(hidden, table, targets, count):
    places, each = hidden.shape[0], hidden.shape[3]
    tokens, rows = places * 4 * each, table.shape[0]
    steps = places // 2
    line = pl.BlockSpec((1, 2 * each), lambda h, c, i: (0, (h * 2 + c) * steps + i))
    return pl.pallas_call(
        functools.partial(head_stats_kernel, count),
        grid=(2, 2, steps),
        in_specs=[
            pl.BlockSpec((2, 1, 2, each // 2, D), lambda h, c, i: (i, c, 0, h, 0)),
            pl.BlockSpec((rows, D), lambda h, c, i: (0, 0)),
            line,
        ],
        out_specs=[line, line],
        out_shape=[jax.ShapeDtypeStruct((1, tokens), f32)] * 2,
        compiler_params=pltpu.CompilerParams(vmem_limit_bytes=VMEM_LIMIT),
        cost_estimate=pl.CostEstimate(
            flops=2 * tokens * rows * D, bytes_accessed=2 * tokens * D, transcendentals=tokens * rows
        ),
    )(hidden, table, targets)


def head_grad(core, hidden, table, targets, mask, lse, count, half):
    places, each = hidden.shape[0], hidden.shape[3]
    tokens, rows = places * each, table.shape[0]
    steps = places // 2
    line = pl.BlockSpec((1, 2 * each), lambda i, c: (0, (half * 2 + c[0]) * steps + i))
    piece = pl.BlockSpec((2, 2, each // 4, D), lambda i, c: (i, 0, 0, 0))
    return pl.pallas_call(
        functools.partial(head_grad_kernel, count),
        grid_spec=pltpu.PrefetchScalarGridSpec(
            num_scalar_prefetch=1,
            grid=(steps,),
            in_specs=[
                pl.BlockSpec((2, 1, 2, each // 2, D), lambda i, c: (i, c[0], 0, half, 0)),
                pl.BlockSpec((rows, D), lambda i, c: (0, 0)),
                line,
                line,
                line,
            ],
            out_specs=[piece, piece, pl.BlockSpec((rows, D), lambda i, c: (0, 0))],
        ),
        out_shape=[
            jax.ShapeDtypeStruct((places, 2, each // 4, D), bf16),
            jax.ShapeDtypeStruct((places, 2, each // 4, D), bf16),
            jax.ShapeDtypeStruct((rows, D), f32),
        ],
        compiler_params=pltpu.CompilerParams(vmem_limit_bytes=VMEM_LIMIT),
        cost_estimate=pl.CostEstimate(
            flops=6 * tokens * rows * D, bytes_accessed=4 * tokens * D, transcendentals=tokens * rows
        ),
    )(core.reshape(1), hidden, table, targets, mask, lse)


def place_kernel(first, *refs):
    out = refs[-1]
    rows = out.shape[0]
    base = (pl.program_id(0) + first) * rows
    total = None
    for ids, grads in zip(refs[:-1:2], refs[1:-1:2]):
        row = lax.broadcasted_iota(jnp.int32, (rows, ids.shape[1]), 0) + base
        hot = jnp.where(row == ids[...], 1.0, 0.0).astype(bf16)
        term = dot_nn(hot, grads[...])
        total = term if total is None else total + term
    out[...] = total.astype(bf16)


def place_rows(pairs, first, parts, rows):
    specs, args = [], []
    for ids, grads in pairs:
        specs.append(pl.BlockSpec(ids.shape, lambda i: (0, 0)))
        specs.append(pl.BlockSpec(grads.shape, lambda i: (0, 0)))
        args += [ids, grads]
    return pl.pallas_call(
        functools.partial(place_kernel, first),
        grid=(parts,),
        in_specs=specs,
        out_specs=pl.BlockSpec((rows, D), lambda i: (i, 0)),
        out_shape=jax.ShapeDtypeStruct((parts * rows, D), bf16),
        compiler_params=pltpu.CompilerParams(vmem_limit_bytes=VMEM_LIMIT),
        cost_estimate=pl.CostEstimate(flops=1, bytes_accessed=rows, transcendentals=0),
    )(*args)


def gather_axis(value, axis):
    size = lax.axis_size(axis)
    me = lax.axis_index(axis)
    got = [value]
    for step in range(1, size):
        got.append(lax.ppermute(value, axis, [(i, (i + step) % size) for i in range(size)]))
    stacked = jnp.stack(got)
    return jnp.take(stacked, (me - jnp.arange(size, dtype=jnp.int32)) % size, axis=0)


def gather_small(value, axes):
    shape = value.shape
    for axis in reversed(axes):
        value = gather_axis(value, axis)
        value = value.reshape((-1,) + shape)
    return value


def fold_all(value, combine):
    for axis in reversed(ALL):
        size = lax.axis_size(axis)
        hop = 1
        while hop < size:
            other = lax.ppermute(value, axis, [(i, i ^ hop) for i in range(size)])
            value = combine(value, other)
            hop *= 2
    return value


def swap(value, axis):
    return lax.ppermute(value, axis, [(0, 1), (1, 0)])


def swap_core(value):
    return swap(value, "core")


def add16(left, right):
    return (left.astype(f32) + right.astype(f32)).astype(bf16)


def pick(value, index, dim):
    return lax.dynamic_index_in_dim(value, index, dim, keepdims=False)


def scatter_pair(value, axis, dim):
    if lax.axis_size(axis) != 2:
        return lax.psum_scatter(value, axis, scatter_dimension=dim, tiled=False)
    me = lax.axis_index(axis)
    got = swap(pick(value, 1 - me, dim), axis)
    return add16(pick(value, me, dim), got)


def scatter_core(value):
    sizes = tuple(lax.axis_size(axis) for axis in ALL)
    return scatter_pair(value.reshape(sizes + (-1, value.shape[-1])), "core", 2)


def scatter_first(value, seq_first):
    return scatter_pair(value, "seq", 2) if seq_first else scatter_pair(value, "p", 1)


def scatter_second(value, seq_first):
    return scatter_pair(value, "p", 1) if seq_first else scatter_pair(value, "seq", 1)


def scatter_last(value):
    size, me = value.shape[0], lax.axis_index("z")
    total = pick(value, me, 0).astype(f32)
    for hop in range(1, size):
        send = pick(value, (me + hop) % size, 0)
        got = lax.ppermute(send, "z", [(i, (i + hop) % size) for i in range(size)])
        total = total + got.astype(f32)
    return total


def scatter_rest(value, seq_first):
    return scatter_last(scatter_second(scatter_first(value, seq_first), seq_first))


def line_gather(value, axis):
    size = lax.axis_size(axis)
    ups, downs = [value], [value]
    for _ in range(1, size):
        ups.append(lax.ppermute(ups[-1], axis, [(i, i + 1) for i in range(size - 1)]))
        downs.append(lax.ppermute(downs[-1], axis, [(i + 1, i) for i in range(size - 1)]))
    return [value] + [ups[k] + downs[size - k] for k in range(1, size)]


def line_scatter(parts, axis):
    size = lax.axis_size(axis)
    up, down = None, None
    for step in range(1, size):
        far = size - step
        send_up, send_down = parts[size - far], parts[far]
        if up is not None:
            send_up, send_down = send_up + up, send_down + down
        up = lax.ppermute(send_up, axis, [(i, i + 1) for i in range(step)])
        down = lax.ppermute(send_down, axis, [(size - 1 - i, size - 2 - i) for i in range(step)])
    return parts[0].astype(f32) + up.astype(f32) + down.astype(f32)


def plane_gather(table):
    if lax.axis_size("p") != 2:
        return lax.all_gather(table, PLANE, axis=0, tiled=True)
    half = table.shape[0] // 2
    by_seq, by_p = swap(table, "seq"), swap(table, "p")
    far = [swap(by_p[:half], "seq"), swap(by_seq[half:], "p")]
    mine = [table, by_seq, by_p] + far
    return jnp.concatenate(mine + [swap_core(item) for item in mine])


def plane_slot(owner):
    if lax.axis_size("p") != 2:
        return owner
    other = owner ^ lax.axis_index(PLANE)
    return ((other >> 1) & 1) * 4 + (other >> 2) * 2 + (other & 1)


def plane_scatter(pairs, rows, before, after):
    pairs, before = lax.optimization_barrier((pairs, before))
    count = lax.axis_size(PLANE)
    if lax.axis_size("p") != 2:
        placed = place_rows(pairs, 0, count, rows)
        placed = lax.psum_scatter(placed, PLANE, scatter_dimension=0, tiled=True)
        return placed.astype(f32), before, after
    away = swap_core(place_rows(pairs, 4, 4, rows))
    home, after = lax.optimization_barrier((place_rows(pairs, 0, 4, rows), after))
    half = rows // 2
    part = lambda first, last: add16(home[first:last], away[first:last])
    got_low = swap(part(3 * rows, 3 * rows + half), "seq")
    got_high = swap(part(3 * rows + half, 4 * rows), "p")
    seq_high = add16(part(rows + half, 2 * rows), got_high)
    p_low = add16(part(2 * rows, 2 * rows + half), got_low)
    from_seq = swap(jnp.concatenate([part(rows, rows + half), seq_high]), "seq")
    from_p = swap(jnp.concatenate([p_low, part(2 * rows + half, 3 * rows)]), "p")
    return part(0, rows).astype(f32) + from_seq.astype(f32) + from_p.astype(f32), before, after


def add_logs(left, right):
    top = jnp.maximum(left, right)
    return top + jnp.log(jnp.exp(left - top) + jnp.exp(right - top))


def ffn_forward(resid, gain, w_in, w_out):
    normed = rms_scale(resid, gain).astype(bf16)
    both = project(normed, w_in)
    hidden = gate_up(both).astype(bf16)
    return (resid + project(hidden, w_out), (normed, both, hidden))


def ffn_backward(upstream, resid, gain, w_in, w_out, saved):
    normed, both, hidden = saved
    grad_b = upstream.astype(bf16)
    d_out = weight_grad(hidden, grad_b).astype(bf16)
    _, pull = jax.vjp(gate_up, both)
    (d_both,) = pull(input_grad(grad_b, w_out))
    d_both_b = d_both.astype(bf16)
    d_in = weight_grad(normed, d_both_b).astype(bf16)
    d_resid, d_gain = norm_pull(resid, gain, 1.0, input_grad(d_both_b, w_in))
    return (upstream + d_resid, d_gain, d_in, d_out)


def branch_backward(upstream, out_b, w_out):
    grad_b = upstream.astype(bf16)
    return (weight_grad(out_b, grad_b).astype(bf16), input_grad(grad_b, w_out).astype(bf16))


def adamw(weight, grad, first_m, second_m, count, rate, decay):
    first_new = 0.9 * first_m + 0.1 * grad
    second_new = 0.999 * second_m + 0.001 * grad * grad
    first_hat = first_new / (1.0 - 0.9**count)
    second_hat = second_new / (1.0 - 0.999**count)
    return (
        first_new,
        second_new,
        weight - rate * (first_hat / (jnp.sqrt(second_hat) + 1e-08) + decay * weight),
    )


def body(
    enc_ids,
    enc_segs,
    sentinel,
    mode,
    dec_ids,
    dec_segs,
    target_ids,
    target_mask,
    buckets,
    embed,
    attn_in,
    attn_out,
    ffn_in,
    ffn_out,
    rel_table,
    gains,
    m_embed,
    v_embed,
    m_attn_in,
    v_attn_in,
    m_attn_out,
    v_attn_out,
    m_ffn_in,
    v_ffn_in,
    m_ffn_out,
    v_ffn_out,
    m_rel,
    v_rel,
    m_gains,
    v_gains,
):
    core = lax.axis_index("core")
    z_at = lax.axis_index("z")
    z_size = lax.axis_size("z")
    plane_size = lax.axis_size(PLANE)
    device = lax.axis_index(ALL)
    shard = embed.shape[0]
    padded = (shard // 16 + 1) * 16
    enc_count, dec_count = enc_ids.shape[1], dec_ids.shape[1]
    enc_len, dec_len = enc_segs.shape[1], dec_segs.shape[1]

    table_b = jnp.pad(embed.astype(bf16), ((0, padded - shard), (0, 0)))
    misc = jnp.concatenate([gains.T, rel_table.reshape(-1, 1)], axis=1)
    misc = jnp.pad(misc, ((0, 0), (0, 120)))
    shard_in = attn_in.shape[1]
    flat_out = ffn_out.astype(bf16).reshape(2, shard_in, -1)
    enc_cast = jnp.concatenate([attn_in[0], ffn_in[0], attn_out[0], misc], axis=1).astype(bf16)
    enc_pack = lax.all_gather(
        jnp.concatenate([enc_cast, flat_out[0]], axis=1), ALL, axis=0, tiled=True
    )
    dec_cast = jnp.concatenate(
        [attn_in[1], attn_in[2], attn_out[1], attn_out[2]], axis=1
    ).astype(bf16)
    ffn_cast = jnp.concatenate([ffn_in[1].astype(bf16), flat_out[1]], axis=1)
    plane_table = plane_gather(table_b)
    flat = jnp.concatenate(
        [
            enc_ids[0],
            sentinel[0],
            dec_ids[0],
            target_ids[0],
            target_mask[0],
            enc_segs[0],
            dec_segs[0],
            jnp.pad(mode[0], (0, 128 - mode.shape[1])),
        ]
    )
    flat = lax.ppermute(flat, ("core", "seq"), [(0, 0), (1, 2), (2, 1), (3, 3)])
    sizes = [enc_count, enc_count, dec_count, dec_count, dec_count, enc_len, dec_len]
    pieces, start = [], 0
    for size in sizes:
        pieces.append(flat[start : start + size])
        start += size
    enc_id, sent, dec_id, targets, mask_i, enc_seg_all, dec_seg_all = pieces
    mode_row = flat[start : start + mode.shape[1]]
    mask = mask_i.astype(f32)

    enc_seg = lax.dynamic_slice_in_dim(enc_seg_all, core * enc_count, enc_count)
    enc_seg_other = lax.dynamic_slice_in_dim(enc_seg_all, (1 - core) * enc_count, enc_count)
    dec_seg = lax.dynamic_slice_in_dim(dec_seg_all, core * dec_count, dec_count)
    dec_seg_other = lax.dynamic_slice_in_dim(dec_seg_all, (1 - core) * dec_count, dec_count)
    enc_range = jnp.arange(enc_count, dtype=jnp.int32)
    dec_range = jnp.arange(dec_count, dtype=jnp.int32)
    enc_pos, enc_pos_other = core * enc_count + enc_range, (1 - core) * enc_count + enc_range
    dec_pos, dec_pos_other = core * dec_count + dec_range, (1 - core) * dec_count + dec_range
    prior_all = jnp.concatenate([enc_seg_all[:1], enc_seg_all[:-1]])
    prior = lax.dynamic_slice_in_dim(prior_all, core * enc_count, enc_count)
    first = (enc_pos == 0) | (enc_seg != prior)
    mode_of = jnp.sum(
        jnp.where(
            enc_seg[:, None] == jnp.arange(mode.shape[1], dtype=jnp.int32)[None], mode_row[None], 0
        ),
        axis=1,
    )
    enc_tok = jnp.where(sent == 1, V - 1 - enc_seg, enc_id)
    enc_tok = jnp.where(first, V - 101 - mode_of, enc_tok)
    local_ids = jnp.concatenate([enc_tok, dec_id])

    line_ids = line_gather(local_ids, "z")
    plane_rows = plane_size * shard
    places = []
    for ids in line_ids:
        rel_id = ids - z_at * plane_rows
        inside = (rel_id >= 0) & (rel_id < plane_rows)
        places.append(
            jnp.where(inside, plane_slot(rel_id // shard) * padded + rel_id % shard, shard)
        )
    dec_cast, enc_pack, plane_table, places = lax.optimization_barrier(
        (dec_cast, enc_pack, plane_table, places)
    )
    dec_pack = lax.all_gather(dec_cast, ALL, axis=0, tiled=True)
    enc_places = [item[:enc_count] for item in places]
    dec_places = [item[enc_count:] for item in places]

    def look(items):
        got = jnp.take(plane_table, jnp.concatenate(items), axis=0, mode="clip")
        return line_scatter(jnp.split(got, len(items)), "z")

    looked = look(places)
    enc_x0, dec_y0 = looked[:enc_count], looked[enc_count:]

    cut = lambda pack, start, width: lax.slice_in_dim(pack, start, start + width, axis=1)
    enc_wi, enc_fi = cut(enc_pack, 0, 3 * D), cut(enc_pack, 3 * D, 2 * FF)
    enc_wo, misc_all = cut(enc_pack, 3 * D + 2 * FF, D), cut(enc_pack, 4 * D + 2 * FF, 128)
    enc_fo = cut(enc_pack, 4 * D + 2 * FF + 128, FF).reshape(FF, D)
    gain = misc_all[:, :7].T.astype(f32)
    rel_all = jnp.transpose(misc_all[:, 7].reshape(-1, 2, rel_table.shape[1]), (1, 0, 2))
    rel_all = rel_all.reshape(2, BUCKETS, HEADS)

    enc_x8, enc_picks = bias_lines(rel_all[0], buckets[0], core, enc_count, enc_count)
    dec_x8, dec_picks = bias_lines(rel_all[1], buckets[1], core, dec_count, dec_count)
    col, line = (lambda v: v[:, None]), (lambda v: v[None, :])
    enc_info = (
        col(enc_seg), line(enc_seg), line(enc_seg_other),
        col(enc_pos), line(enc_pos), line(enc_pos_other),
    )
    dec_info = (
        col(dec_seg), line(dec_seg), line(dec_seg_other),
        col(dec_pos), line(dec_pos), line(dec_pos_other),
    )
    cross_info = (
        col(dec_seg), line(enc_seg), line(enc_seg_other),
        col(dec_pos), line(enc_pos), line(enc_pos_other),
    )

    enc_n1 = rms_scale(enc_x0, gain[0]).astype(bf16)
    enc_q = project(enc_n1, enc_wi[:, :D]).astype(bf16)
    enc_kv = project(enc_n1, enc_wi[:, D:]).astype(bf16)
    enc_kv2 = swap_core(enc_kv)
    enc_ob = attend_forward(enc_q, enc_kv, enc_kv2, enc_info, enc_x8, False)
    ffn_cast, dec_pack, enc_ob = lax.optimization_barrier((ffn_cast, dec_pack, enc_ob))
    ffn_pack = lax.all_gather(ffn_cast, ALL, axis=0, tiled=True)
    dec_wi, cross_wi = cut(dec_pack, 0, 3 * D), cut(dec_pack, 3 * D, 3 * D)
    dec_wo, cross_wo = cut(dec_pack, 6 * D, D), cut(dec_pack, 7 * D, D)
    dec_fi = cut(ffn_pack, 0, 2 * FF)
    dec_fo = cut(ffn_pack, 2 * FF, FF).reshape(FF, D)
    enc_x1 = enc_x0 + project(enc_ob, enc_wo)
    enc_x2, enc_saved = ffn_forward(enc_x1, gain[1], enc_fi, enc_fo)
    enc_out = rms_scale(enc_x2, gain[2]).astype(bf16)

    dec_n1 = rms_scale(dec_y0, gain[3]).astype(bf16)
    dec_q = project(dec_n1, dec_wi[:, :D]).astype(bf16)
    dec_kv = project(dec_n1, dec_wi[:, D:]).astype(bf16)
    dec_kv2 = swap_core(dec_kv)
    dec_ob = attend_forward(dec_q, dec_kv, dec_kv2, dec_info, dec_x8, True)
    dec_y1 = dec_y0 + project(dec_ob, dec_wo)
    cross_kv = project(enc_out, cross_wi[:, D:]).astype(bf16)
    cross_kv2 = swap_core(cross_kv)
    cross_n = rms_scale(dec_y1, gain[4]).astype(bf16)
    cross_q = project(cross_n, cross_wi[:, :D]).astype(bf16)
    cross_ob = attend_forward(cross_q, cross_kv, cross_kv2, cross_info, None, False)
    dec_y2 = dec_y1 + project(cross_ob, cross_wo)
    dec_y3, dec_saved = ffn_forward(dec_y2, gain[5], dec_fi, dec_fo)
    head_scale = D ** (-0.5)
    hidden_b = (rms_scale(dec_y3, gain[6]) * head_scale).astype(bf16)

    hidden_all = lax.all_gather(hidden_b, ALL, axis=0, tiled=True)
    sizes = tuple(lax.axis_size(axis) for axis in ALL)
    hidden_all = hidden_all.reshape(-1, 2, 2, dec_count, D)
    info = gather_small(jnp.stack([targets, mask_i]), ALL)
    info = info.reshape(-1, 2, 2, 2, 2, dec_count // 2)
    info = jnp.transpose(info, (3, 4, 1, 0, 2, 5)).reshape(2, 1, -1)
    targets_all = info[0] - device * shard
    mask_all = info[1].astype(f32)
    lse_part, picked = head_stats(hidden_all, table_b, targets_all, shard)
    lse = fold_all(lse_part, add_logs)
    d_hidden, head_embed = [], None
    for half in range(2):
        *away, term = head_grad(
            1 - core, hidden_all, table_b, targets_all, mask_all, lse, shard, half
        )
        head_embed = term if head_embed is None else head_embed + term
        away = [swap_core(item) for item in away]
        *home, term = head_grad(
            core, hidden_all, table_b, targets_all, mask_all, lse, shard, half
        )
        head_embed = head_embed + term
        for number in range(2):
            item = add16(home[number], away[number])
            item = item.reshape(sizes[:2] + (2,) + item.shape[2:])
            d_hidden.append(scatter_rest(item, number == 0))
    d_hidden = jnp.concatenate(d_hidden)
    mine = (core * sizes[0] * sizes[1] + device // 4) * 2 + lax.axis_index("seq")
    lse_mine = lax.dynamic_slice_in_dim(
        lse.reshape(2, -1), mine * (dec_count // 2), dec_count // 2, axis=1
    )
    loss_local = jnp.sum(mask * lse_mine.reshape(-1)) - jnp.sum(mask_all * picked)

    d_y3, d_gain_final = norm_pull(dec_y3, gain[6], head_scale, d_hidden)
    d_y2, d_gain_dffn, d_dec_fi, d_dec_fo = ffn_backward(
        d_y3, dec_y2, gain[5], dec_fi, dec_fo, dec_saved
    )
    d_cross_wo, d_cross_ob = branch_backward(d_y2, cross_ob, cross_wo)
    early, d_dec_fo, d_cross_ob = lax.optimization_barrier((d_dec_fi, d_dec_fo, d_cross_ob))
    g_dec_fo = scatter_core(d_dec_fo)
    early = lax.psum_scatter(early, ALL, scatter_dimension=0, tiled=True)
    d_cross_q, own, other = attend_backward(
        d_cross_ob, cross_q, cross_kv, cross_kv2, cross_info, None, False
    )
    got = (own + swap_core(other).astype(f32)).astype(bf16)
    d_cross_kv = jnp.concatenate([got[0], got[1]], axis=1)
    d_cross_wq = weight_grad(cross_n, d_cross_q)
    d_y1_norm, d_gain_cross = norm_pull(
        dec_y1, gain[4], 1.0, input_grad(d_cross_q, cross_wi[:, :D])
    )
    d_y1 = d_y2 + d_y1_norm
    d_cross_wkv = weight_grad(enc_out, d_cross_kv)
    d_dec_wo, d_dec_ob = branch_backward(d_y1, dec_ob, dec_wo)
    g_dec_fo, d_dec_ob = lax.optimization_barrier((g_dec_fo, d_dec_ob))
    g_dec_fo = scatter_first(g_dec_fo, False)
    d_dec_q, own, other, dec_y8 = attend_backward(
        d_dec_ob, dec_q, dec_kv, dec_kv2, dec_info, dec_x8, True
    )
    got = (own + swap_core(other).astype(f32)).astype(bf16)
    d_dec_qkv = jnp.concatenate([d_dec_q, got[0], got[1]], axis=1)
    d_dec_table = bias_gradient(dec_y8, dec_picks)
    d_dec_wi = weight_grad(dec_n1, d_dec_qkv)
    d_y0_norm, d_gain_datt = norm_pull(dec_y0, gain[3], 1.0, input_grad(d_dec_qkv, dec_wi))
    d_y0 = d_y1 + d_y0_norm
    d_dec_rest = jnp.concatenate(
        [
            d_dec_wi.astype(bf16),
            d_cross_wq.astype(bf16),
            d_cross_wkv.astype(bf16),
            d_dec_wo,
            d_cross_wo,
        ],
        axis=1,
    )
    dec_lines = line_gather(d_y0.astype(bf16), "z")

    d_x2, d_gain_efin = norm_pull(
        enc_x2, gain[2], 1.0, input_grad(d_cross_kv, cross_wi[:, D:])
    )
    d_x1, d_gain_effn, d_enc_fi, d_enc_fo = ffn_backward(
        d_x2, enc_x1, gain[1], enc_fi, enc_fo, enc_saved
    )
    early, g_dec_fo, d_x1 = lax.optimization_barrier((early, g_dec_fo, d_x1))
    g_dec_fo = scatter_second(g_dec_fo, False)
    d_enc_wo, d_enc_ob = branch_backward(d_x1, enc_ob, enc_wo)
    d_enc_low, d_enc_high = d_enc_fi[:, :3456], jnp.concatenate([d_enc_fi[:, 3456:], d_enc_wo], 1)
    enc_sums = [scatter_core(item) for item in (d_enc_low, d_enc_high, d_enc_fo)]
    late, dec_lines, enc_sums, g_dec_fo, d_enc_ob = lax.optimization_barrier(
        (d_dec_rest, dec_lines, enc_sums, g_dec_fo, d_enc_ob)
    )
    late = lax.psum_scatter(late, ALL, scatter_dimension=0, tiled=True)
    early = early.astype(f32)
    enc_sums = [scatter_first(item, number == 0) for number, item in enumerate(enc_sums)]
    d_enc_q, own, other, enc_y8 = attend_backward(
        d_enc_ob, enc_q, enc_kv, enc_kv2, enc_info, enc_x8, False
    )
    got = (own + swap_core(other).astype(f32)).astype(bf16)
    d_enc_qkv = jnp.concatenate([d_enc_q, got[0], got[1]], axis=1)
    d_enc_table = bias_gradient(enc_y8, enc_picks)
    d_enc_wi = weight_grad(enc_n1, d_enc_qkv)
    d_x0_norm, d_gain_eatt = norm_pull(enc_x0, gain[0], 1.0, input_grad(d_enc_qkv, enc_wi))
    d_x0 = d_x1 + d_x0_norm

    d_x0, enc_sums = lax.optimization_barrier((d_x0.astype(bf16), enc_sums))
    enc_sums = [scatter_second(item, number == 0) for number, item in enumerate(enc_sums)]
    enc_lines = line_gather(d_x0, "z")
    enc_lines, enc_sums = lax.optimization_barrier((enc_lines, enc_sums))
    g_low, g_high, g_fo, g_dec_fo = [scatter_last(item) for item in (*enc_sums, g_dec_fo)]
    far_place = lambda item: jnp.where(item == shard, -1, item)[None, :]
    pairs = [
        (far_place(item), grads)
        for item, grads in zip(enc_places + dec_places, enc_lines + dec_lines)
    ]
    d_gains = jnp.stack(
        [
            d_gain_eatt,
            d_gain_effn,
            d_gain_efin,
            d_gain_datt,
            d_gain_cross,
            d_gain_dffn,
            d_gain_final,
        ]
    )
    d_rel = jnp.stack([d_enc_table.reshape(-1), d_dec_table.reshape(-1)])
    d_rel = jnp.transpose(d_rel.reshape(2, -1, rel_table.shape[1]), (1, 0, 2)).reshape(D, 1)
    d_misc = jnp.pad(jnp.concatenate([d_gains.T, d_rel], axis=1), ((0, 0), (0, 120)))
    d_last = jnp.concatenate([d_enc_wi.astype(bf16), d_misc.astype(bf16)], axis=1)
    last = [scatter_core(d_last[:, :1152]), scatter_core(d_last[:, 1152:])]
    input_embed, late, last = plane_scatter(pairs, padded, late, last)
    late = late.astype(f32)
    grad_embed = head_embed[:shard] + input_embed[:shard]

    last = [scatter_rest(item, number == 0) for number, item in enumerate(last)]
    squares = sum(
        (jnp.sum(item * item) for item in (grad_embed, early, late, g_low, g_high, g_fo, g_dec_fo, *last))
    )
    sums = fold_all(jnp.stack([jnp.sum(mask), loss_local, squares]), jnp.add)
    last = jnp.concatenate(last, axis=1)
    owned = (
        jnp.stack([cut(last, 0, 3 * D), cut(late, 0, 3 * D), cut(late, 3 * D, 3 * D)]),
        jnp.stack([cut(g_high, 640, D), cut(late, 6 * D, D), cut(late, 7 * D, D)]),
        jnp.stack(
            [jnp.concatenate([g_low, cut(g_high, 0, 640)], axis=1), early]
        ),
        jnp.stack([g_fo, g_dec_fo]),
        last[:, 3 * D + 7].reshape(2, -1),
        last[:, 3 * D : 3 * D + 7].T,
    )
    grads = (grad_embed,) + owned
    count_all, loss_all, squares_all = sums[0], sums[1], sums[2]
    grad_norm = jnp.sqrt(squares_all) / count_all
    factor = jnp.minimum(1.0, clip_limit / grad_norm) / count_all
    weights = (embed, attn_in, attn_out, ffn_in, ffn_out, rel_table, gains)
    moments = [
        (m_embed, v_embed),
        (m_attn_in, v_attn_in),
        (m_attn_out, v_attn_out),
        (m_ffn_in, v_ffn_in),
        (m_ffn_out, v_ffn_out),
        (m_rel, v_rel),
        (m_gains, v_gains),
    ]
    settings = [
        (1.0, 0.01),
        (0.05, 0.01),
        (0.05, 0.01),
        (0.05, 0.01),
        (0.05, 0.01),
        (0.3, 0.0),
        (0.3, 0.0),
    ]
    results = [loss_all / count_all, grad_norm]
    for slot_number, (param, grad, pair, setting) in enumerate(
        zip(weights, grads, moments, settings)
    ):
        clipped = grad * factor
        first_new, second_new, new_param = adamw(
            param, clipped, pair[0], pair[1], float(STEP), setting[0], setting[1]
        )
        results.extend((clipped if slot_number == 0 else first_new, second_new, new_param))
    return tuple(results)


def solution(mesh):
    rows = ("z", "p", "core")
    every = ALL
    inner = Mesh(mesh.devices.reshape(4, -1, 2, mesh.devices.shape[1]), ALL)
    mat = P(None, every, None)
    vec = P(None, every)
    emb = P(every, None)
    in_specs = (
        P(rows, "seq"),
        P(rows, None),
        P(rows, "seq"),
        P(rows, None),
        P(rows, "seq"),
        P(rows, None),
        P(rows, "seq"),
        P(rows, "seq"),
        P(),
        emb,
        mat,
        mat,
        mat,
        mat,
        vec,
        vec,
        emb,
        emb,
    ) + (mat,) * 8 + (vec,) * 4
    out_specs = (P(), P()) + (emb,) * 3 + (mat,) * 12 + (vec,) * 6
    return jax.shard_map(body, mesh=inner, in_specs=in_specs, out_specs=out_specs, check_vma=False)
```

```python
import functools

import jax
import jax.numpy as jnp
from jax import lax
from jax.experimental import pallas as pl
from jax.experimental.pallas import tpu as pltpu
from jax.sharding import Mesh
from jax.sharding import PartitionSpec as P

D = 768
HEADS = 12
HEAD_DIM = 64
FF = 2048
V = 32128
BUCKETS = 32
STEP = 10

masked_out = -1e30
clip_limit = 0.01
ALL = ("z", "p", "core", "seq")
PLANE = ("p", "core", "seq")
bf16 = jnp.bfloat16
f32 = jnp.float32
VMEM_LIMIT = 56 * 1024 * 1024


def rms_scale(values, gain):
    return values * lax.rsqrt(jnp.mean(values * values, axis=-1, keepdims=True) + 1e-06) * gain


def norm_pull(values, gain, factor, upstream):
    _, pull = jax.vjp(lambda left, right: rms_scale(left, right) * factor, values, gain)
    return pull(upstream)


def gate_up(both):
    return jax.nn.gelu(both[:, :FF], approximate=True) * both[:, FF:]


def project(left, right):
    return jnp.dot(left, right, preferred_element_type=f32)


def weight_grad(inputs, grads):
    return jnp.einsum("td,te->de", inputs, grads, preferred_element_type=f32)


def input_grad(grads, weight):
    return jnp.einsum("te,de->td", grads, weight, preferred_element_type=f32)


def dot_nt(a, b):
    return lax.dot_general(a, b, (((1,), (1,)), ((), ())), preferred_element_type=f32)


def dot_tn(a, b):
    return lax.dot_general(a, b, (((0,), (0,)), ((), ())), preferred_element_type=f32)


def dot_nn(a, b):
    return lax.dot_general(a, b, (((1,), (0,)), ((), ())), preferred_element_type=f32)


def spread(eight, rows, width):
    total = eight.shape[-1]
    grid = eight
    have = 8
    while have < rows:
        grid = jnp.concatenate([pltpu.roll(grid, total - have, 1), grid], axis=0)
        have *= 2
    return grid[:, :width]


def collect(grid, total):
    rows, width = grid.shape
    have = jnp.concatenate([grid, jnp.zeros((rows, total - width), f32)], axis=1)
    while rows > 8:
        rows //= 2
        have = pltpu.roll(have[:rows], rows, 1) + have[rows:]
    return have


def probs_of(cfg, refs, block, head):
    bq, has_bias, causal = cfg
    rows = slice(block * bq, (block + 1) * bq)
    cols = slice(head * HEAD_DIM, (head + 1) * HEAD_DIM)
    query = refs["q"][rows, cols]
    scores = []
    for part in range(2):
        keys = refs["k"][part][:, cols]
        s = dot_nt(query, keys) * HEAD_DIM ** (-0.5)
        if has_bias:
            s = s + spread(refs["x8"][head, block * 2 + part], bq, keys.shape[0])
        allowed = refs["qseg"][rows, :] == refs["kseg"][part]
        if causal:
            allowed = allowed & (refs["kpos"][part] <= refs["qpos"][rows, :])
        scores.append(jnp.where(allowed, s, masked_out))
    top = jnp.maximum(
        jnp.max(scores[0], axis=1, keepdims=True), jnp.max(scores[1], axis=1, keepdims=True)
    )
    exps = [jnp.exp(s - top) for s in scores]
    total = jnp.sum(exps[0], axis=1, keepdims=True) + jnp.sum(exps[1], axis=1, keepdims=True)
    scale = 1.0 / total
    return query, [e * scale for e in exps]


def name_refs(cfg, refs):
    bq, has_bias, causal = cfg
    it = iter(refs)
    named = {"q": next(it)}
    k0, v0, k1, v1 = next(it), next(it), next(it), next(it)
    named["k"], named["v"] = (k0, k1), (v0, v1)
    ids = next(it), next(it), next(it), next(it), next(it), next(it)
    named["qseg"], named["kseg"] = ids[0], (ids[1][...], ids[2][...])
    named["qpos"], named["kpos"] = ids[3], (ids[4][...], ids[5][...])
    if has_bias:
        named["x8"] = next(it)
    return named, list(it)


def attend_forward_kernel(cfg, *refs):
    named, (out,) = name_refs(cfg, refs)
    bq = cfg[0]
    for block in range(named["q"].shape[0] // bq):
        for head in range(2):
            cols = slice(head * HEAD_DIM, (head + 1) * HEAD_DIM)
            _, probs = probs_of(cfg, named, block, head)
            acc = dot_nn(probs[0].astype(bf16), named["v"][0][:, cols])
            acc = acc + dot_nn(probs[1].astype(bf16), named["v"][1][:, cols])
            out[block * bq : (block + 1) * bq, cols] = acc.astype(bf16)


def attend_backward_kernel(cfg, *refs):
    named, rest = name_refs(cfg, refs)
    bq, has_bias, causal = cfg
    if has_bias:
        grad, dq, own, other, y8 = rest
    else:
        grad, dq, own, other = rest
    blocks = named["q"].shape[0] // bq
    for head in range(2):
        cols = slice(head * HEAD_DIM, (head + 1) * HEAD_DIM)
        dk, dv = [None, None], [None, None]
        for block in range(blocks):
            rows = slice(block * bq, (block + 1) * bq)
            query, probs = probs_of(cfg, named, block, head)
            do = grad[rows, cols]
            dp = [dot_nt(do, named["v"][part][:, cols]) for part in range(2)]
            delta = jnp.sum(probs[0] * dp[0], axis=1, keepdims=True) + jnp.sum(
                probs[1] * dp[1], axis=1, keepdims=True
            )
            acc = None
            for part in range(2):
                ds = (probs[part] * (dp[part] - delta)).astype(bf16)
                term = dot_nn(ds, named["k"][part][:, cols])
                acc = term if acc is None else acc + term
                k_term = dot_tn(query, ds)
                v_term = dot_tn(do, probs[part].astype(bf16))
                dk[part] = k_term if dk[part] is None else dk[part] + k_term
                dv[part] = v_term if dv[part] is None else dv[part] + v_term
                if has_bias:
                    y8[head, block * 2 + part] = collect(ds.astype(f32), y8.shape[-1])
            dq[rows, cols] = (acc * HEAD_DIM ** (-0.5)).astype(bf16)
        for part, target in enumerate((own, other)):
            target[0, :, cols] = (dk[part] * HEAD_DIM ** (-0.5)).T.astype(target.dtype)
            target[1, :, cols] = dv[part].T.astype(target.dtype)


def attend_specs(q_len, k_len, has_bias, x8):
    whole = lambda shape: pl.BlockSpec(shape, lambda i: (0,) * len(shape))
    kv = [
        pl.BlockSpec((k_len, 128), lambda i: (0, i)),
        pl.BlockSpec((k_len, 128), lambda i: (0, i + 6)),
    ]
    specs = [pl.BlockSpec((q_len, 128), lambda i: (0, i))] + kv + kv
    specs += [whole((q_len, 1)), whole((1, k_len)), whole((1, k_len))] * 2
    if has_bias:
        specs.append(pl.BlockSpec((2,) + x8.shape[1:], lambda i: (i, 0, 0, 0)))
    return specs


def attend_args(q, kv_own, kv_other, ids, x8):
    args = [q, kv_own, kv_own, kv_other, kv_other] + list(ids)
    if x8 is not None:
        args.append(x8)
    return args


def attend_cost(q_len, k_len, products):
    return pl.CostEstimate(flops=products, bytes_accessed=q_len, transcendentals=0)


def attend_forward(q, kv_own, kv_other, ids, x8, causal):
    q_len, k_len = q.shape[0], kv_own.shape[0]
    cfg = (256, x8 is not None, causal)
    return pl.pallas_call(
        functools.partial(attend_forward_kernel, cfg),
        grid=(HEADS // 2,),
        in_specs=attend_specs(q_len, k_len, x8 is not None, x8),
        out_specs=pl.BlockSpec((q_len, 128), lambda i: (0, i)),
        out_shape=jax.ShapeDtypeStruct((q_len, D), bf16),
        compiler_params=pltpu.CompilerParams(vmem_limit_bytes=VMEM_LIMIT),
        cost_estimate=attend_cost(q_len, k_len, 2),
    )(*attend_args(q, kv_own, kv_other, ids, x8))


def attend_backward(grad, q, kv_own, kv_other, ids, x8, causal):
    q_len, k_len = q.shape[0], kv_own.shape[0]
    cfg = (256, x8 is not None, causal)
    kv_spec = pl.BlockSpec((2, k_len, 128), lambda i: (0, 0, i))
    out_specs = [pl.BlockSpec((q_len, 128), lambda i: (0, i)), kv_spec, kv_spec]
    out_shape = [
        jax.ShapeDtypeStruct((q_len, D), bf16),
        jax.ShapeDtypeStruct((2, k_len, D), f32),
        jax.ShapeDtypeStruct((2, k_len, D), bf16),
    ]
    if x8 is not None:
        out_specs.append(pl.BlockSpec((2,) + x8.shape[1:], lambda i: (i, 0, 0, 0)))
        out_shape.append(jax.ShapeDtypeStruct(x8.shape, f32))
    return pl.pallas_call(
        functools.partial(attend_backward_kernel, cfg),
        grid=(HEADS // 2,),
        in_specs=attend_specs(q_len, k_len, x8 is not None, x8)
        + [pl.BlockSpec((q_len, 128), lambda i: (0, i))],
        out_specs=out_specs,
        out_shape=out_shape,
        compiler_params=pltpu.CompilerParams(vmem_limit_bytes=VMEM_LIMIT),
        cost_estimate=attend_cost(q_len, k_len, 5),
    )(*attend_args(q, kv_own, kv_other, ids, x8), grad)


def bias_bases(core, q_len, k_len, offset):
    bases = []
    for block in range(q_len // 256):
        for part in range(2):
            k_start = (core if part == 0 else 1 - core) * k_len
            q_start = core * q_len + block * 256
            bases.append(k_start - q_start - 255 + offset)
    return bases


def bias_windows(array, core, q_len, k_len):
    size, width = array.shape[1], k_len + 256
    array = jnp.pad(array, ((0, 0), (0, 16)))
    rows = jnp.stack([array[:, 7 - r : size + 9 - r] for r in range(8)], axis=1)
    bases = bias_bases(core, q_len, k_len, size // 2)
    cut = lambda base: lax.dynamic_slice_in_dim(rows, base, width, axis=2)
    return jnp.stack([cut(base) for base in bases], axis=1)


def bias_lines(table, bucket_row, core, q_len, k_len):
    picks = (bucket_row[None, :] == jnp.arange(BUCKETS, dtype=jnp.int32)[:, None]).astype(bf16)
    per_offset = jnp.einsum("bh,bn->hn", table, picks, preferred_element_type=f32)
    return (
        bias_windows(per_offset, core, q_len, k_len),
        bias_windows(picks.astype(f32), core, q_len, k_len),
    )


def bias_gradient(y8, picks):
    return jnp.einsum("bnrw,hnrw->bh", picks, y8, precision=lax.Precision.HIGHEST)


def head_stats_kernel(count, hid, tab, tgt, lse_out, pick_out):
    logits = dot_nt(tab[...], hid[...].reshape(-1, D))
    row = lax.broadcasted_iota(jnp.int32, logits.shape, 0)
    pick_out[...] = jnp.sum(jnp.where(row == tgt[...], logits, 0.0), axis=0, keepdims=True)
    logits = jnp.where(row < count, logits, masked_out)
    top = jnp.max(logits, axis=0, keepdims=True)
    lse_out[...] = top + jnp.log(jnp.sum(jnp.exp(logits - top), axis=0, keepdims=True))


def head_grad_kernel(count, core, hid, tab, tgt, msk, lse, dhid_a, dhid_b, dtab):
    tokens = hid[...].reshape(-1, D)
    logits = dot_nt(tab[...], tokens)
    row = lax.broadcasted_iota(jnp.int32, logits.shape, 0)
    soft = jnp.exp(jnp.where(row < count, logits, masked_out) - lse[...])
    grad = ((soft - jnp.where(row == tgt[...], 1.0, 0.0)) * msk[...]).astype(bf16)
    dhid = dot_tn(grad, tab[...]).astype(bf16).reshape(hid.shape)
    cut = hid.shape[3] // 2
    dhid_a[...] = dhid[:, 0, :, :cut]
    dhid_b[...] = dhid[:, 0, :, cut:]
    term = dot_nn(grad, tokens)

    @pl.when(pl.program_id(0) == 0)
    def _():
        dtab[...] = term

    @pl.when(pl.program_id(0) != 0)
    def _():
        dtab[...] += term


def head_stats(hidden, table, targets, count):
    places, each = hidden.shape[0], hidden.shape[3]
    tokens, rows = places * 4 * each, table.shape[0]
    steps = places // 2
    line = pl.BlockSpec((1, 2 * each), lambda h, c, i: (0, (h * 2 + c) * steps + i))
    return pl.pallas_call(
        functools.partial(head_stats_kernel, count),
        grid=(2, 2, steps),
        in_specs=[
            pl.BlockSpec((2, 1, 2, each // 2, D), lambda h, c, i: (i, c, 0, h, 0)),
            pl.BlockSpec((rows, D), lambda h, c, i: (0, 0)),
            line,
        ],
        out_specs=[line, line],
        out_shape=[jax.ShapeDtypeStruct((1, tokens), f32)] * 2,
        compiler_params=pltpu.CompilerParams(vmem_limit_bytes=VMEM_LIMIT),
        cost_estimate=pl.CostEstimate(
            flops=2 * tokens * rows * D, bytes_accessed=2 * tokens * D, transcendentals=tokens * rows
        ),
    )(hidden, table, targets)


def head_grad(core, hidden, table, targets, mask, lse, count, half):
    places, each = hidden.shape[0], hidden.shape[3]
    tokens, rows = places * each, table.shape[0]
    steps = places // 2
    line = pl.BlockSpec((1, 2 * each), lambda i, c: (0, (half * 2 + c[0]) * steps + i))
    piece = pl.BlockSpec((2, 2, each // 4, D), lambda i, c: (i, 0, 0, 0))
    return pl.pallas_call(
        functools.partial(head_grad_kernel, count),
        grid_spec=pltpu.PrefetchScalarGridSpec(
            num_scalar_prefetch=1,
            grid=(steps,),
            in_specs=[
                pl.BlockSpec((2, 1, 2, each // 2, D), lambda i, c: (i, c[0], 0, half, 0)),
                pl.BlockSpec((rows, D), lambda i, c: (0, 0)),
                line,
                line,
                line,
            ],
            out_specs=[piece, piece, pl.BlockSpec((rows, D), lambda i, c: (0, 0))],
        ),
        out_shape=[
            jax.ShapeDtypeStruct((places, 2, each // 4, D), bf16),
            jax.ShapeDtypeStruct((places, 2, each // 4, D), bf16),
            jax.ShapeDtypeStruct((rows, D), f32),
        ],
        compiler_params=pltpu.CompilerParams(vmem_limit_bytes=VMEM_LIMIT),
        cost_estimate=pl.CostEstimate(
            flops=6 * tokens * rows * D, bytes_accessed=4 * tokens * D, transcendentals=tokens * rows
        ),
    )(core.reshape(1), hidden, table, targets, mask, lse)


def place_kernel(first, *refs):
    out = refs[-1]
    rows = out.shape[0]
    base = (pl.program_id(0) + first) * rows
    total = None
    for ids, grads in zip(refs[:-1:2], refs[1:-1:2]):
        row = lax.broadcasted_iota(jnp.int32, (rows, ids.shape[1]), 0) + base
        hot = jnp.where(row == ids[...], 1.0, 0.0).astype(bf16)
        term = dot_nn(hot, grads[...])
        total = term if total is None else total + term
    out[...] = total.astype(bf16)


def place_rows(pairs, first, parts, rows):
    specs, args = [], []
    for ids, grads in pairs:
        specs.append(pl.BlockSpec(ids.shape, lambda i: (0, 0)))
        specs.append(pl.BlockSpec(grads.shape, lambda i: (0, 0)))
        args += [ids, grads]
    return pl.pallas_call(
        functools.partial(place_kernel, first),
        grid=(parts,),
        in_specs=specs,
        out_specs=pl.BlockSpec((rows, D), lambda i: (i, 0)),
        out_shape=jax.ShapeDtypeStruct((parts * rows, D), bf16),
        compiler_params=pltpu.CompilerParams(vmem_limit_bytes=VMEM_LIMIT),
        cost_estimate=pl.CostEstimate(
            flops=2 * sum(grads.shape[0] for _, grads in pairs) * parts * rows * D,
            bytes_accessed=2 * parts * rows * D,
            transcendentals=0,
        ),
    )(*args)


def gather_axis(value, axis):
    size = lax.axis_size(axis)
    me = lax.axis_index(axis)
    got = [value]
    for step in range(1, size):
        got.append(lax.ppermute(value, axis, [(i, (i + step) % size) for i in range(size)]))
    stacked = jnp.stack(got)
    return jnp.take(stacked, (me - jnp.arange(size, dtype=jnp.int32)) % size, axis=0)


def gather_small(value, axes):
    shape = value.shape
    for axis in reversed(axes):
        value = gather_axis(value, axis)
        value = value.reshape((-1,) + shape)
    return value


def fold_all(value, combine):
    for axis in reversed(ALL):
        size = lax.axis_size(axis)
        hop = 1
        while hop < size:
            other = lax.ppermute(value, axis, [(i, i ^ hop) for i in range(size)])
            value = combine(value, other)
            hop *= 2
    return value


def swap(value, axis):
    return lax.ppermute(value, axis, [(0, 1), (1, 0)])


def swap_core(value):
    return swap(value, "core")


def add16(left, right):
    return (left.astype(f32) + right.astype(f32)).astype(bf16)


def pick(value, index, dim):
    return lax.dynamic_index_in_dim(value, index, dim, keepdims=False)


def scatter_pair(value, axis, dim):
    if lax.axis_size(axis) != 2:
        return lax.psum_scatter(value, axis, scatter_dimension=dim, tiled=False)
    me = lax.axis_index(axis)
    got = swap(pick(value, 1 - me, dim), axis)
    return add16(pick(value, me, dim), got)


def scatter_core(value):
    sizes = tuple(lax.axis_size(axis) for axis in ALL)
    return scatter_pair(value.reshape(sizes + (-1, value.shape[-1])), "core", 2)


def scatter_first(value, seq_first):
    return scatter_pair(value, "seq", 2) if seq_first else scatter_pair(value, "p", 1)


def scatter_second(value, seq_first):
    return scatter_pair(value, "p", 1) if seq_first else scatter_pair(value, "seq", 1)


def scatter_last(value):
    size, me = value.shape[0], lax.axis_index("z")
    total = pick(value, me, 0).astype(f32)
    for hop in range(1, size):
        send = pick(value, (me + hop) % size, 0)
        got = lax.ppermute(send, "z", [(i, (i + hop) % size) for i in range(size)])
        total = total + got.astype(f32)
    return total


def scatter_rest(value, seq_first):
    return scatter_last(scatter_second(scatter_first(value, seq_first), seq_first))


def line_gather(value, axis, before=None):
    size = lax.axis_size(axis)
    ups, downs = [value], [value]
    for step in range(1, size):
        if step == 2 and before is not None:
            ups[1], downs[1], before = lax.optimization_barrier((ups[1], downs[1], before))
        ups.append(lax.ppermute(ups[-1], axis, [(i, i + 1) for i in range(size - 1)]))
        downs.append(lax.ppermute(downs[-1], axis, [(i + 1, i) for i in range(size - 1)]))
    got = [value] + [ups[k] + downs[size - k] for k in range(1, size)]
    return got if before is None else (got, before)


def line_scatter(parts, axis, beside=None):
    size = lax.axis_size(axis)
    up, down = None, None
    for step in range(1, size):
        far = size - step
        send_up, send_down = parts[size - far], parts[far]
        if up is not None:
            send_up, send_down = send_up + up, send_down + down
        up = lax.ppermute(send_up, axis, [(i, i + 1) for i in range(step)])
        down = lax.ppermute(send_down, axis, [(size - 1 - i, size - 2 - i) for i in range(step)])
        if beside is not None:
            up, down = beside(step, up, down)
    return parts[0].astype(f32) + up.astype(f32) + down.astype(f32)


def plane_near(table):
    if lax.axis_size("p") != 2:
        return (lax.all_gather(table, PLANE, axis=0, tiled=True),)
    return (swap(table, "seq"), swap(table, "p"))


def plane_gather(table, near):
    if len(near) == 1:
        return near[0]
    by_seq, by_p = near
    half = table.shape[0] // 2
    far = [swap(by_p[:half], "seq"), swap(by_seq[half:], "p")]
    mine = [table, by_seq, by_p] + far
    return jnp.concatenate(mine + [swap_core(item) for item in mine])


def plane_slot(owner):
    if lax.axis_size("p") != 2:
        return owner
    other = owner ^ lax.axis_index(PLANE)
    return ((other >> 1) & 1) * 4 + (other >> 2) * 2 + (other & 1)


def plane_scatter(pairs, rows, after):
    count = lax.axis_size(PLANE)
    if lax.axis_size("p") != 2:
        placed = place_rows(pairs, 0, count, rows)
        placed = lax.psum_scatter(placed, PLANE, scatter_dimension=0, tiled=True)
        return placed.astype(f32), after
    away = swap_core(place_rows(pairs, 4, 4, rows))
    home = place_rows(pairs, 0, 4, rows)
    half = rows // 2
    part = lambda first, last: add16(home[first:last], away[first:last])
    got_low = swap(part(3 * rows, 3 * rows + half), "seq")
    got_high = swap(part(3 * rows + half, 4 * rows), "p")
    got_low, got_high, after = lax.optimization_barrier((got_low, got_high, after))
    seq_high = add16(part(rows + half, 2 * rows), got_high)
    p_low = add16(part(2 * rows, 2 * rows + half), got_low)
    from_seq = swap(jnp.concatenate([part(rows, rows + half), seq_high]), "seq")
    from_p = swap(jnp.concatenate([p_low, part(2 * rows + half, 3 * rows)]), "p")
    return part(0, rows).astype(f32) + from_seq.astype(f32) + from_p.astype(f32), after


def add_logs(left, right):
    top = jnp.maximum(left, right)
    return top + jnp.log(jnp.exp(left - top) + jnp.exp(right - top))


def ffn_forward(resid, gain, w_in, w_out):
    normed = rms_scale(resid, gain).astype(bf16)
    both = project(normed, w_in)
    hidden = gate_up(both).astype(bf16)
    return (resid + project(hidden, w_out), (normed, both, hidden))


def ffn_backward(upstream, resid, gain, w_in, w_out, saved):
    normed, both, hidden = saved
    grad_b = upstream.astype(bf16)
    d_out = weight_grad(hidden, grad_b).astype(bf16)
    _, pull = jax.vjp(gate_up, both)
    (d_both,) = pull(input_grad(grad_b, w_out))
    d_both_b = d_both.astype(bf16)
    d_in = weight_grad(normed, d_both_b).astype(bf16)
    d_resid, d_gain = norm_pull(resid, gain, 1.0, input_grad(d_both_b, w_in))
    return (upstream + d_resid, d_gain, d_in, d_out)


def branch_backward(upstream, out_b, w_out):
    grad_b = upstream.astype(bf16)
    return (weight_grad(out_b, grad_b).astype(bf16), input_grad(grad_b, w_out).astype(bf16))


def adamw(weight, grad, first_m, second_m, count, rate, decay):
    first_new = 0.9 * first_m + 0.1 * grad
    second_new = 0.999 * second_m + 0.001 * grad * grad
    first_hat = first_new / (1.0 - 0.9**count)
    second_hat = second_new / (1.0 - 0.999**count)
    return (
        first_new,
        second_new,
        weight - rate * (first_hat / (jnp.sqrt(second_hat) + 1e-08) + decay * weight),
    )


def body(
    enc_ids,
    enc_segs,
    sentinel,
    mode,
    dec_ids,
    dec_segs,
    target_ids,
    target_mask,
    buckets,
    embed,
    attn_in,
    attn_out,
    ffn_in,
    ffn_out,
    rel_table,
    gains,
    m_embed,
    v_embed,
    m_attn_in,
    v_attn_in,
    m_attn_out,
    v_attn_out,
    m_ffn_in,
    v_ffn_in,
    m_ffn_out,
    v_ffn_out,
    m_rel,
    v_rel,
    m_gains,
    v_gains,
):
    core = lax.axis_index("core")
    z_at = lax.axis_index("z")
    z_size = lax.axis_size("z")
    plane_size = lax.axis_size(PLANE)
    device = lax.axis_index(ALL)
    shard = embed.shape[0]
    padded = (shard // 16 + 1) * 16
    enc_count, dec_count = enc_ids.shape[1], dec_ids.shape[1]
    enc_len, dec_len = enc_segs.shape[1], dec_segs.shape[1]

    table_b = jnp.pad(embed.astype(bf16), ((0, padded - shard), (0, 0)))
    misc = jnp.concatenate([gains.T, rel_table.reshape(-1, 1)], axis=1)
    misc = jnp.pad(misc, ((0, 0), (0, 120)))
    shard_in = attn_in.shape[1]
    flat_out = ffn_out.astype(bf16).reshape(2, shard_in, -1)
    enc_cast = jnp.concatenate([attn_in[0], ffn_in[0], attn_out[0], misc], axis=1).astype(bf16)
    enc_pack = lax.all_gather(
        jnp.concatenate([enc_cast, flat_out[0]], axis=1), ALL, axis=0, tiled=True
    )
    dec_cast = jnp.concatenate(
        [attn_in[1], attn_in[2], attn_out[1], attn_out[2]], axis=1
    ).astype(bf16)
    ffn_cast = jnp.concatenate([ffn_in[1].astype(bf16), flat_out[1]], axis=1)
    flat = jnp.concatenate(
        [
            enc_ids[0],
            sentinel[0],
            dec_ids[0],
            target_ids[0],
            target_mask[0],
            enc_segs[0],
            dec_segs[0],
            jnp.pad(mode[0], (0, 128 - mode.shape[1])),
        ]
    )
    flat = lax.ppermute(flat, ("core", "seq"), [(0, 0), (1, 2), (2, 1), (3, 3)])
    sizes = [enc_count, enc_count, dec_count, dec_count, dec_count, enc_len, dec_len]
    pieces, start = [], 0
    for size in sizes:
        pieces.append(flat[start : start + size])
        start += size
    enc_id, sent, dec_id, targets, mask_i, enc_seg_all, dec_seg_all = pieces
    mode_row = flat[start : start + mode.shape[1]]
    mask = mask_i.astype(f32)

    enc_seg = lax.dynamic_slice_in_dim(enc_seg_all, core * enc_count, enc_count)
    enc_seg_other = lax.dynamic_slice_in_dim(enc_seg_all, (1 - core) * enc_count, enc_count)
    dec_seg = lax.dynamic_slice_in_dim(dec_seg_all, core * dec_count, dec_count)
    dec_seg_other = lax.dynamic_slice_in_dim(dec_seg_all, (1 - core) * dec_count, dec_count)
    enc_range = jnp.arange(enc_count, dtype=jnp.int32)
    dec_range = jnp.arange(dec_count, dtype=jnp.int32)
    enc_pos, enc_pos_other = core * enc_count + enc_range, (1 - core) * enc_count + enc_range
    dec_pos, dec_pos_other = core * dec_count + dec_range, (1 - core) * dec_count + dec_range
    prior_all = jnp.concatenate([enc_seg_all[:1], enc_seg_all[:-1]])
    prior = lax.dynamic_slice_in_dim(prior_all, core * enc_count, enc_count)
    first = (enc_pos == 0) | (enc_seg != prior)
    mode_of = jnp.sum(
        jnp.where(
            enc_seg[:, None] == jnp.arange(mode.shape[1], dtype=jnp.int32)[None], mode_row[None], 0
        ),
        axis=1,
    )
    enc_tok = jnp.where(sent == 1, V - 1 - enc_seg, enc_id)
    enc_tok = jnp.where(first, V - 101 - mode_of, enc_tok)
    local_ids = jnp.concatenate([enc_tok, dec_id])

    line_ids = line_gather(local_ids, "z")
    plane_rows = plane_size * shard
    places = []
    for ids in line_ids:
        rel_id = ids - z_at * plane_rows
        inside = (rel_id >= 0) & (rel_id < plane_rows)
        places.append(
            jnp.where(inside, plane_slot(rel_id // shard) * padded + rel_id % shard, shard)
        )

    def look(table):
        return jnp.take(table, jnp.concatenate(places), axis=0, mode="clip")

    def beside(step, up, down):
        if step == 1:
            up, down, held[0] = lax.optimization_barrier((up, down, plane_gather(high, far)))
        elif step == 2:
            up, down, held[0] = lax.optimization_barrier((up, down, look(held[0])))
        return up, down

    cut_line = lambda got: jnp.split(got, len(places))
    low, high = table_b[:, : D // 2], table_b[:, D // 2 :]
    near = plane_near(low)
    near, high, places = lax.optimization_barrier((near, high, places))
    far = plane_near(high)
    got, far = lax.optimization_barrier((look(plane_gather(low, near)), far))
    held = [None]
    looked_low = line_scatter(cut_line(got), "z", beside)
    looked_high = line_scatter(cut_line(held[0]), "z")
    dec_cast, enc_pack, looked_low = lax.optimization_barrier((dec_cast, enc_pack, looked_low))
    dec_pack = lax.all_gather(dec_cast, ALL, axis=0, tiled=True)
    looked = jnp.concatenate([looked_low, looked_high], axis=1)
    enc_places = [item[:enc_count] for item in places]
    dec_places = [item[enc_count:] for item in places]
    enc_x0, dec_y0 = looked[:enc_count], looked[enc_count:]

    cut = lambda pack, start, width: lax.slice_in_dim(pack, start, start + width, axis=1)
    enc_wi, enc_fi = cut(enc_pack, 0, 3 * D), cut(enc_pack, 3 * D, 2 * FF)
    enc_wo, misc_all = cut(enc_pack, 3 * D + 2 * FF, D), cut(enc_pack, 4 * D + 2 * FF, 128)
    enc_fo = cut(enc_pack, 4 * D + 2 * FF + 128, FF).reshape(FF, D)
    gain = misc_all[:, :7].T.astype(f32)
    rel_all = jnp.transpose(misc_all[:, 7].reshape(-1, 2, rel_table.shape[1]), (1, 0, 2))
    rel_all = rel_all.reshape(2, BUCKETS, HEADS)

    enc_x8, enc_picks = bias_lines(rel_all[0], buckets[0], core, enc_count, enc_count)
    dec_x8, dec_picks = bias_lines(rel_all[1], buckets[1], core, dec_count, dec_count)
    col, line = (lambda v: v[:, None]), (lambda v: v[None, :])
    enc_info = (
        col(enc_seg), line(enc_seg), line(enc_seg_other),
        col(enc_pos), line(enc_pos), line(enc_pos_other),
    )
    dec_info = (
        col(dec_seg), line(dec_seg), line(dec_seg_other),
        col(dec_pos), line(dec_pos), line(dec_pos_other),
    )
    cross_info = (
        col(dec_seg), line(enc_seg), line(enc_seg_other),
        col(dec_pos), line(enc_pos), line(enc_pos_other),
    )

    enc_n1 = rms_scale(enc_x0, gain[0]).astype(bf16)
    enc_q = project(enc_n1, enc_wi[:, :D]).astype(bf16)
    enc_kv = project(enc_n1, enc_wi[:, D:]).astype(bf16)
    enc_kv2 = swap_core(enc_kv)
    enc_ob = attend_forward(enc_q, enc_kv, enc_kv2, enc_info, enc_x8, False)
    ffn_cast, dec_pack, enc_ob = lax.optimization_barrier((ffn_cast, dec_pack, enc_ob))
    ffn_pack = lax.all_gather(ffn_cast, ALL, axis=0, tiled=True)
    dec_wi, cross_wi = cut(dec_pack, 0, 3 * D), cut(dec_pack, 3 * D, 3 * D)
    dec_wo, cross_wo = cut(dec_pack, 6 * D, D), cut(dec_pack, 7 * D, D)
    dec_fi = cut(ffn_pack, 0, 2 * FF)
    dec_fo = cut(ffn_pack, 2 * FF, FF).reshape(FF, D)
    enc_x1 = enc_x0 + project(enc_ob, enc_wo)
    enc_x2, enc_saved = ffn_forward(enc_x1, gain[1], enc_fi, enc_fo)
    enc_out = rms_scale(enc_x2, gain[2]).astype(bf16)

    dec_n1 = rms_scale(dec_y0, gain[3]).astype(bf16)
    dec_q = project(dec_n1, dec_wi[:, :D]).astype(bf16)
    dec_kv = project(dec_n1, dec_wi[:, D:]).astype(bf16)
    dec_kv2 = swap_core(dec_kv)
    dec_ob = attend_forward(dec_q, dec_kv, dec_kv2, dec_info, dec_x8, True)
    dec_y1 = dec_y0 + project(dec_ob, dec_wo)
    cross_kv = project(enc_out, cross_wi[:, D:]).astype(bf16)
    cross_kv2 = swap_core(cross_kv)
    cross_n = rms_scale(dec_y1, gain[4]).astype(bf16)
    cross_q = project(cross_n, cross_wi[:, :D]).astype(bf16)
    cross_ob = attend_forward(cross_q, cross_kv, cross_kv2, cross_info, None, False)
    dec_y2 = dec_y1 + project(cross_ob, cross_wo)
    dec_y3, dec_saved = ffn_forward(dec_y2, gain[5], dec_fi, dec_fo)
    head_scale = D ** (-0.5)
    hidden_b = (rms_scale(dec_y3, gain[6]) * head_scale).astype(bf16)

    hidden_all = lax.all_gather(hidden_b, ALL, axis=0, tiled=True)
    sizes = tuple(lax.axis_size(axis) for axis in ALL)
    hidden_all = hidden_all.reshape(-1, 2, 2, dec_count, D)
    info = gather_small(jnp.stack([targets, mask_i]), ALL)
    info = info.reshape(-1, 2, 2, 2, 2, dec_count // 2)
    info = jnp.transpose(info, (3, 4, 1, 0, 2, 5)).reshape(2, 1, -1)
    targets_all = info[0] - device * shard
    mask_all = info[1].astype(f32)
    lse_part, picked = head_stats(hidden_all, table_b, targets_all, shard)
    lse = fold_all(lse_part, add_logs)
    d_hidden, head_embed = [], None
    for half in range(2):
        *away, term = head_grad(
            1 - core, hidden_all, table_b, targets_all, mask_all, lse, shard, half
        )
        head_embed = term if head_embed is None else head_embed + term
        away = [swap_core(item) for item in away]
        *home, term = head_grad(
            core, hidden_all, table_b, targets_all, mask_all, lse, shard, half
        )
        head_embed = head_embed + term
        for number in range(2):
            item = add16(home[number], away[number])
            item = item.reshape(sizes[:2] + (2,) + item.shape[2:])
            d_hidden.append(scatter_rest(item, number == 0))
    d_hidden = jnp.concatenate(d_hidden)
    mine = (core * sizes[0] * sizes[1] + device // 4) * 2 + lax.axis_index("seq")
    lse_mine = lax.dynamic_slice_in_dim(
        lse.reshape(2, -1), mine * (dec_count // 2), dec_count // 2, axis=1
    )
    loss_local = jnp.sum(mask * lse_mine.reshape(-1)) - jnp.sum(mask_all * picked)

    d_y3, d_gain_final = norm_pull(dec_y3, gain[6], head_scale, d_hidden)
    d_y2, d_gain_dffn, d_dec_fi, d_dec_fo = ffn_backward(
        d_y3, dec_y2, gain[5], dec_fi, dec_fo, dec_saved
    )
    d_cross_wo, d_cross_ob = branch_backward(d_y2, cross_ob, cross_wo)
    early, d_dec_fo, d_cross_ob = lax.optimization_barrier((d_dec_fi, d_dec_fo, d_cross_ob))
    g_dec_fo = scatter_core(d_dec_fo)
    early = lax.psum_scatter(early, ALL, scatter_dimension=0, tiled=True)
    d_cross_q, own, other = attend_backward(
        d_cross_ob, cross_q, cross_kv, cross_kv2, cross_info, None, False
    )
    got = (own + swap_core(other).astype(f32)).astype(bf16)
    d_cross_kv = jnp.concatenate([got[0], got[1]], axis=1)
    d_cross_wq = weight_grad(cross_n, d_cross_q)
    d_y1_norm, d_gain_cross = norm_pull(
        dec_y1, gain[4], 1.0, input_grad(d_cross_q, cross_wi[:, :D])
    )
    d_y1 = d_y2 + d_y1_norm
    d_cross_wkv = weight_grad(enc_out, d_cross_kv)
    d_dec_wo, d_dec_ob = branch_backward(d_y1, dec_ob, dec_wo)
    g_dec_fo, d_dec_ob = lax.optimization_barrier((g_dec_fo, d_dec_ob))
    g_dec_fo = scatter_first(g_dec_fo, False)
    d_dec_q, own, other, dec_y8 = attend_backward(
        d_dec_ob, dec_q, dec_kv, dec_kv2, dec_info, dec_x8, True
    )
    got = (own + swap_core(other).astype(f32)).astype(bf16)
    d_dec_qkv = jnp.concatenate([d_dec_q, got[0], got[1]], axis=1)
    d_dec_table = bias_gradient(dec_y8, dec_picks)
    d_dec_wi = weight_grad(dec_n1, d_dec_qkv)
    d_y0_norm, d_gain_datt = norm_pull(dec_y0, gain[3], 1.0, input_grad(d_dec_qkv, dec_wi))
    d_y0 = d_y1 + d_y0_norm
    d_dec_rest = jnp.concatenate(
        [
            d_dec_wi.astype(bf16),
            d_cross_wq.astype(bf16),
            d_cross_wkv.astype(bf16),
            d_dec_wo,
            d_cross_wo,
        ],
        axis=1,
    )
    dec_lines = line_gather(d_y0.astype(bf16), "z")

    d_x2, d_gain_efin = norm_pull(
        enc_x2, gain[2], 1.0, input_grad(d_cross_kv, cross_wi[:, D:])
    )
    d_x1, d_gain_effn, d_enc_fi, d_enc_fo = ffn_backward(
        d_x2, enc_x1, gain[1], enc_fi, enc_fo, enc_saved
    )
    early, g_dec_fo, d_x1 = lax.optimization_barrier((early, g_dec_fo, d_x1))
    g_dec_fo = scatter_second(g_dec_fo, False)
    d_enc_wo, d_enc_ob = branch_backward(d_x1, enc_ob, enc_wo)
    d_enc_low, d_enc_high = d_enc_fi[:, :3456], jnp.concatenate([d_enc_fi[:, 3456:], d_enc_wo], 1)
    enc_sums = [scatter_core(item) for item in (d_enc_low, d_enc_high, d_enc_fo)]
    late, dec_lines, enc_sums, g_dec_fo, d_enc_ob = lax.optimization_barrier(
        (d_dec_rest, dec_lines, enc_sums, g_dec_fo, d_enc_ob)
    )
    g_dec_fo = scatter_last(g_dec_fo)
    late = lax.psum_scatter(late, ALL, scatter_dimension=0, tiled=True)
    early = early.astype(f32)
    enc_sums = [scatter_first(item, number == 0) for number, item in enumerate(enc_sums)]
    d_enc_q, own, other, enc_y8 = attend_backward(
        d_enc_ob, enc_q, enc_kv, enc_kv2, enc_info, enc_x8, False
    )
    got = (own + swap_core(other).astype(f32)).astype(bf16)
    d_enc_qkv = jnp.concatenate([d_enc_q, got[0], got[1]], axis=1)
    d_enc_table = bias_gradient(enc_y8, enc_picks)
    d_enc_wi = weight_grad(enc_n1, d_enc_qkv)
    d_x0_norm, d_gain_eatt = norm_pull(enc_x0, gain[0], 1.0, input_grad(d_enc_qkv, enc_wi))
    d_x0 = d_x1 + d_x0_norm

    d_gains = jnp.stack(
        [
            d_gain_eatt,
            d_gain_effn,
            d_gain_efin,
            d_gain_datt,
            d_gain_cross,
            d_gain_dffn,
            d_gain_final,
        ]
    )
    d_rel = jnp.stack([d_enc_table.reshape(-1), d_dec_table.reshape(-1)])
    d_rel = jnp.transpose(d_rel.reshape(2, -1, rel_table.shape[1]), (1, 0, 2)).reshape(D, 1)
    d_misc = jnp.pad(jnp.concatenate([d_gains.T, d_rel], axis=1), ((0, 0), (0, 120)))
    d_last = jnp.concatenate([d_enc_wi.astype(bf16), d_misc.astype(bf16)], axis=1)
    d_x0, enc_sums = lax.optimization_barrier((d_x0.astype(bf16), enc_sums))
    enc_sums = [scatter_second(item, number == 0) for number, item in enumerate(enc_sums)]
    last = [scatter_core(d_last[:, :1152]), scatter_core(d_last[:, 1152:])]
    last = [scatter_first(item, number == 0) for number, item in enumerate(last)]
    last = [scatter_second(item, number == 0) for number, item in enumerate(last)]
    enc_lines, late = line_gather(d_x0, "z", late)
    enc_lines, enc_sums, last = lax.optimization_barrier((enc_lines, enc_sums, last))
    far_place = lambda item: jnp.where(item == shard, -1, item)[None, :]
    pairs = [
        (far_place(item), grads)
        for item, grads in zip(enc_places + dec_places, enc_lines + dec_lines)
    ]
    input_embed, (enc_sums, last) = plane_scatter(pairs, padded, (enc_sums, last))
    late = late.astype(f32)
    grad_embed = head_embed[:shard] + input_embed[:shard]
    g_low, g_high, g_fo = [scatter_last(item) for item in enc_sums]
    last = [scatter_last(item) for item in last]
    squares = sum(
        (jnp.sum(item * item) for item in (grad_embed, early, late, g_low, g_high, g_fo, g_dec_fo, *last))
    )
    sums = fold_all(jnp.stack([jnp.sum(mask), loss_local, squares]), jnp.add)
    last = jnp.concatenate(last, axis=1)
    owned = (
        jnp.stack([cut(last, 0, 3 * D), cut(late, 0, 3 * D), cut(late, 3 * D, 3 * D)]),
        jnp.stack([cut(g_high, 640, D), cut(late, 6 * D, D), cut(late, 7 * D, D)]),
        jnp.stack(
            [jnp.concatenate([g_low, cut(g_high, 0, 640)], axis=1), early]
        ),
        jnp.stack([g_fo, g_dec_fo]),
        last[:, 3 * D + 7].reshape(2, -1),
        last[:, 3 * D : 3 * D + 7].T,
    )
    grads = (grad_embed,) + owned
    count_all, loss_all, squares_all = sums[0], sums[1], sums[2]
    grad_norm = jnp.sqrt(squares_all) / count_all
    factor = jnp.minimum(1.0, clip_limit / grad_norm) / count_all
    weights = (embed, attn_in, attn_out, ffn_in, ffn_out, rel_table, gains)
    moments = [
        (m_embed, v_embed),
        (m_attn_in, v_attn_in),
        (m_attn_out, v_attn_out),
        (m_ffn_in, v_ffn_in),
        (m_ffn_out, v_ffn_out),
        (m_rel, v_rel),
        (m_gains, v_gains),
    ]
    settings = [
        (1.0, 0.01),
        (0.05, 0.01),
        (0.05, 0.01),
        (0.05, 0.01),
        (0.05, 0.01),
        (0.3, 0.0),
        (0.3, 0.0),
    ]
    results = [loss_all / count_all, grad_norm]
    for slot_number, (param, grad, pair, setting) in enumerate(
        zip(weights, grads, moments, settings)
    ):
        clipped = grad * factor
        first_new, second_new, new_param = adamw(
            param, clipped, pair[0], pair[1], float(STEP), setting[0], setting[1]
        )
        results.extend((clipped if slot_number == 0 else first_new, second_new, new_param))
    return tuple(results)


def solution(mesh):
    rows = ("z", "p", "core")
    every = ALL
    inner = Mesh(mesh.devices.reshape(4, -1, 2, mesh.devices.shape[1]), ALL)
    mat = P(None, every, None)
    vec = P(None, every)
    emb = P(every, None)
    in_specs = (
        P(rows, "seq"),
        P(rows, None),
        P(rows, "seq"),
        P(rows, None),
        P(rows, "seq"),
        P(rows, None),
        P(rows, "seq"),
        P(rows, "seq"),
        P(),
        emb,
        mat,
        mat,
        mat,
        mat,
        vec,
        vec,
        emb,
        emb,
    ) + (mat,) * 8 + (vec,) * 4
    out_specs = (P(), P()) + (emb,) * 3 + (mat,) * 12 + (vec,) * 6
    return jax.shard_map(body, mesh=inner, in_specs=in_specs, out_specs=out_specs, check_vma=False)
```

```python
import functools

import jax
import jax.numpy as jnp
from jax import lax
from jax.experimental import pallas as pl
from jax.experimental.pallas import tpu as pltpu
from jax.sharding import Mesh
from jax.sharding import PartitionSpec as P

D = 768
HEADS = 12
HEAD_DIM = 64
FF = 2048
V = 32128
BUCKETS = 32
STEP = 10

masked_out = -1e30
clip_limit = 0.01
ALL = ("z", "p", "core", "seq")
PLANE = ("p", "core", "seq")
bf16 = jnp.bfloat16
f32 = jnp.float32
VMEM_LIMIT = 56 * 1024 * 1024


def rms_scale(values, gain):
    return values * lax.rsqrt(jnp.mean(values * values, axis=-1, keepdims=True) + 1e-06) * gain


def norm_pull(values, gain, factor, upstream):
    _, pull = jax.vjp(lambda left, right: rms_scale(left, right) * factor, values, gain)
    return pull(upstream)


def gate_up(both):
    return jax.nn.gelu(both[:, :FF], approximate=True) * both[:, FF:]


def project(left, right):
    return jnp.dot(left, right, preferred_element_type=f32)


def weight_grad(inputs, grads):
    return jnp.einsum("td,te->de", inputs, grads, preferred_element_type=f32)


def input_grad(grads, weight):
    return jnp.einsum("te,de->td", grads, weight, preferred_element_type=f32)


def dot_nt(a, b):
    return lax.dot_general(a, b, (((1,), (1,)), ((), ())), preferred_element_type=f32)


def dot_tn(a, b):
    return lax.dot_general(a, b, (((0,), (0,)), ((), ())), preferred_element_type=f32)


def dot_nn(a, b):
    return lax.dot_general(a, b, (((1,), (0,)), ((), ())), preferred_element_type=f32)


def spread(eight, rows, width):
    total = eight.shape[-1]
    grid = eight
    have = 8
    while have < rows:
        grid = jnp.concatenate([pltpu.roll(grid, total - have, 1), grid], axis=0)
        have *= 2
    return grid[:, :width]


def collect(grid, total):
    rows, width = grid.shape
    have = jnp.concatenate([grid, jnp.zeros((rows, total - width), f32)], axis=1)
    while rows > 8:
        rows //= 2
        have = pltpu.roll(have[:rows], rows, 1) + have[rows:]
    return have


def scores_of(cfg, refs, block, head):
    bq, has_bias, causal = cfg
    rows = slice(block * bq, (block + 1) * bq)
    cols = slice(head * HEAD_DIM, (head + 1) * HEAD_DIM)
    query = refs["q"][rows, cols] * jnp.asarray(HEAD_DIM ** (-0.5), bf16)
    scores = []
    for part in range(2):
        keys = refs["k"][part][:, cols]
        s = dot_nt(query, keys)
        if has_bias:
            s = s + spread(refs["x8"][head, block * 2 + part], bq, keys.shape[0])
        allowed = refs["qseg"][rows, :] == refs["kseg"][part]
        if causal:
            allowed = allowed & (refs["kpos"][part] <= refs["qpos"][rows, :])
        scores.append(jnp.where(allowed, s, masked_out))
    return query, scores


def name_refs(cfg, refs):
    bq, has_bias, causal = cfg
    it = iter(refs)
    named = {"q": next(it)}
    k0, v0, k1, v1 = next(it), next(it), next(it), next(it)
    named["k"], named["v"] = (k0, k1), (v0, v1)
    ids = next(it), next(it), next(it), next(it), next(it), next(it)
    named["qseg"], named["kseg"] = ids[0], (ids[1][...], ids[2][...])
    named["qpos"], named["kpos"] = ids[3], (ids[4][...], ids[5][...])
    if has_bias:
        named["x8"] = next(it)
    return named, list(it)


def attend_forward_kernel(cfg, *refs):
    named, (out, lse) = name_refs(cfg, refs)
    bq = cfg[0]
    for block in range(named["q"].shape[0] // bq):
        rows = slice(block * bq, (block + 1) * bq)
        for head in range(2):
            cols = slice(head * HEAD_DIM, (head + 1) * HEAD_DIM)
            _, scores = scores_of(cfg, named, block, head)
            top = jnp.maximum(
                jnp.max(scores[0], axis=1, keepdims=True), jnp.max(scores[1], axis=1, keepdims=True)
            )
            exps = [jnp.exp(s - top) for s in scores]
            total = jnp.sum(exps[0] + exps[1], axis=1, keepdims=True)
            scale = 1.0 / total
            acc = dot_nn((exps[0] * scale).astype(bf16), named["v"][0][:, cols])
            acc = acc + dot_nn((exps[1] * scale).astype(bf16), named["v"][1][:, cols])
            out[rows, cols] = acc.astype(bf16)
            lse[rows, cols] = jnp.broadcast_to(top + jnp.log(total), (bq, HEAD_DIM))


def attend_backward_kernel(cfg, *refs):
    named, rest = name_refs(cfg, refs)
    bq, has_bias, causal = cfg
    if has_bias:
        grad, lse, dq, own, other, y8 = rest
    else:
        grad, lse, dq, own, other = rest
    blocks = named["q"].shape[0] // bq
    for head in range(2):
        cols = slice(head * HEAD_DIM, (head + 1) * HEAD_DIM)
        dk, dv = [None, None], [None, None]
        for block in range(blocks):
            rows = slice(block * bq, (block + 1) * bq)
            query, scores = scores_of(cfg, named, block, head)
            level = lse[rows, head * HEAD_DIM : head * HEAD_DIM + 1]
            probs = [jnp.exp(s - level) for s in scores]
            do = grad[rows, cols]
            dp = [dot_nt(do, named["v"][part][:, cols]) for part in range(2)]
            delta = jnp.sum(probs[0] * dp[0] + probs[1] * dp[1], axis=1, keepdims=True)
            acc = None
            for part in range(2):
                ds_wide = probs[part] * (dp[part] - delta)
                ds = ds_wide.astype(bf16)
                term = dot_nn(ds, named["k"][part][:, cols])
                acc = term if acc is None else acc + term
                k_term = dot_tn(query, ds)
                v_term = dot_tn(do, probs[part].astype(bf16))
                dk[part] = k_term if dk[part] is None else dk[part] + k_term
                dv[part] = v_term if dv[part] is None else dv[part] + v_term
                if has_bias:
                    y8[head, block * 2 + part] = collect(ds_wide, y8.shape[-1])
            dq[rows, cols] = (acc * HEAD_DIM ** (-0.5)).astype(bf16)
        for part, target in enumerate((own, other)):
            target[0, :, cols] = dk[part].T.astype(target.dtype)
            target[1, :, cols] = dv[part].T.astype(target.dtype)


def attend_specs(q_len, k_len, has_bias, x8):
    whole = lambda shape: pl.BlockSpec(shape, lambda i: (0,) * len(shape))
    kv = [
        pl.BlockSpec((k_len, 128), lambda i: (0, i)),
        pl.BlockSpec((k_len, 128), lambda i: (0, i + 6)),
    ]
    specs = [pl.BlockSpec((q_len, 128), lambda i: (0, i))] + kv + kv
    specs += [whole((q_len, 1)), whole((1, k_len)), whole((1, k_len))] * 2
    if has_bias:
        specs.append(pl.BlockSpec((2,) + x8.shape[1:], lambda i: (i, 0, 0, 0)))
    return specs


def attend_args(q, kv_own, kv_other, ids, x8):
    args = [q, kv_own, kv_own, kv_other, kv_other] + list(ids)
    if x8 is not None:
        args.append(x8)
    return args


def attend_cost(q_len, k_len, products):
    return pl.CostEstimate(flops=products, bytes_accessed=q_len, transcendentals=0)


def attend_forward(q, kv_own, kv_other, ids, x8, causal):
    q_len, k_len = q.shape[0], kv_own.shape[0]
    cfg = (256, x8 is not None, causal)
    return pl.pallas_call(
        functools.partial(attend_forward_kernel, cfg),
        grid=(HEADS // 2,),
        in_specs=attend_specs(q_len, k_len, x8 is not None, x8),
        out_specs=[pl.BlockSpec((q_len, 128), lambda i: (0, i))] * 2,
        out_shape=[
            jax.ShapeDtypeStruct((q_len, D), bf16),
            jax.ShapeDtypeStruct((q_len, D), f32),
        ],
        compiler_params=pltpu.CompilerParams(vmem_limit_bytes=VMEM_LIMIT),
        cost_estimate=attend_cost(q_len, k_len, 2),
    )(*attend_args(q, kv_own, kv_other, ids, x8))


def attend_backward(grad, lse, q, kv_own, kv_other, ids, x8, causal):
    q_len, k_len = q.shape[0], kv_own.shape[0]
    cfg = (256, x8 is not None, causal)
    kv_spec = pl.BlockSpec((2, k_len, 128), lambda i: (0, 0, i))
    out_specs = [pl.BlockSpec((q_len, 128), lambda i: (0, i)), kv_spec, kv_spec]
    out_shape = [
        jax.ShapeDtypeStruct((q_len, D), bf16),
        jax.ShapeDtypeStruct((2, k_len, D), f32),
        jax.ShapeDtypeStruct((2, k_len, D), bf16),
    ]
    if x8 is not None:
        out_specs.append(pl.BlockSpec((2,) + x8.shape[1:], lambda i: (i, 0, 0, 0)))
        out_shape.append(jax.ShapeDtypeStruct(x8.shape, f32))
    return pl.pallas_call(
        functools.partial(attend_backward_kernel, cfg),
        grid=(HEADS // 2,),
        in_specs=attend_specs(q_len, k_len, x8 is not None, x8)
        + [pl.BlockSpec((q_len, 128), lambda i: (0, i))] * 2,
        out_specs=out_specs,
        out_shape=out_shape,
        compiler_params=pltpu.CompilerParams(vmem_limit_bytes=VMEM_LIMIT),
        cost_estimate=attend_cost(q_len, k_len, 5),
    )(*attend_args(q, kv_own, kv_other, ids, x8), grad, lse)


def bias_bases(core, q_len, k_len, offset):
    bases = []
    for block in range(q_len // 256):
        for part in range(2):
            k_start = (core if part == 0 else 1 - core) * k_len
            q_start = core * q_len + block * 256
            bases.append(k_start - q_start - 255 + offset)
    return bases


def bias_windows(array, core, q_len, k_len):
    size, width = array.shape[1], k_len + 256
    array = jnp.pad(array, ((0, 0), (0, 16)))
    rows = jnp.stack([array[:, 7 - r : size + 9 - r] for r in range(8)], axis=1)
    bases = bias_bases(core, q_len, k_len, size // 2)
    cut = lambda base: lax.dynamic_slice_in_dim(rows, base, width, axis=2)
    return jnp.stack([cut(base) for base in bases], axis=1)


def bias_lines(table, bucket_row, core, q_len, k_len):
    picks = (bucket_row[None, :] == jnp.arange(BUCKETS, dtype=jnp.int32)[:, None]).astype(bf16)
    per_offset = jnp.einsum("bh,bn->hn", table, picks, preferred_element_type=f32)
    return (
        bias_windows(per_offset, core, q_len, k_len),
        bias_windows(picks.astype(f32), core, q_len, k_len),
    )


def bias_gradient(y8, picks):
    return jnp.einsum("bnrw,hnrw->bh", picks, y8, precision=lax.Precision.HIGHEST)


def head_stats_kernel(count, hid, tab, tgt, lse_out, pick_out):
    logits = dot_nt(tab[...], hid[...].reshape(-1, D))
    row = lax.broadcasted_iota(jnp.int32, logits.shape, 0)
    pick_out[...] = jnp.sum(jnp.where(row == tgt[...], logits, 0.0), axis=0, keepdims=True)
    logits = jnp.where(row < count, logits, masked_out)
    top = jnp.max(logits, axis=0, keepdims=True)
    lse_out[...] = top + jnp.log(jnp.sum(jnp.exp(logits - top), axis=0, keepdims=True))


def head_grad_kernel(count, core, hid, tab, tgt, msk, lse, dhid_a, dhid_b, dtab):
    tokens = hid[...].reshape(-1, D)
    logits = dot_nt(tab[...], tokens)
    row = lax.broadcasted_iota(jnp.int32, logits.shape, 0)
    soft = jnp.exp(jnp.where(row < count, logits, masked_out) - lse[...])
    grad = ((soft - jnp.where(row == tgt[...], 1.0, 0.0)) * msk[...]).astype(bf16)
    dhid = dot_tn(grad, tab[...]).astype(bf16).reshape(hid.shape)
    cut = hid.shape[3] // 2
    dhid_a[...] = dhid[:, 0, :, :cut]
    dhid_b[...] = dhid[:, 0, :, cut:]
    term = dot_nn(grad, tokens)

    @pl.when(pl.program_id(0) == 0)
    def _():
        dtab[...] = term

    @pl.when(pl.program_id(0) != 0)
    def _():
        dtab[...] += term


def head_stats(hidden, table, targets, count):
    places, each = hidden.shape[0], hidden.shape[3]
    tokens, rows = places * 4 * each, table.shape[0]
    steps = places // 2
    line = pl.BlockSpec((1, 2 * each), lambda h, c, i: (0, (h * 2 + c) * steps + i))
    return pl.pallas_call(
        functools.partial(head_stats_kernel, count),
        grid=(2, 2, steps),
        in_specs=[
            pl.BlockSpec((2, 1, 2, each // 2, D), lambda h, c, i: (i, c, 0, h, 0)),
            pl.BlockSpec((rows, D), lambda h, c, i: (0, 0)),
            line,
        ],
        out_specs=[line, line],
        out_shape=[jax.ShapeDtypeStruct((1, tokens), f32)] * 2,
        compiler_params=pltpu.CompilerParams(vmem_limit_bytes=VMEM_LIMIT),
        cost_estimate=pl.CostEstimate(
            flops=2 * tokens * rows * D, bytes_accessed=2 * tokens * D, transcendentals=tokens * rows
        ),
    )(hidden, table, targets)


def head_grad(core, hidden, table, targets, mask, lse, count, half):
    places, each = hidden.shape[0], hidden.shape[3]
    tokens, rows = places * each, table.shape[0]
    steps = places // 2
    line = pl.BlockSpec((1, 2 * each), lambda i, c: (0, (half * 2 + c[0]) * steps + i))
    piece = pl.BlockSpec((2, 2, each // 4, D), lambda i, c: (i, 0, 0, 0))
    return pl.pallas_call(
        functools.partial(head_grad_kernel, count),
        grid_spec=pltpu.PrefetchScalarGridSpec(
            num_scalar_prefetch=1,
            grid=(steps,),
            in_specs=[
                pl.BlockSpec((2, 1, 2, each // 2, D), lambda i, c: (i, c[0], 0, half, 0)),
                pl.BlockSpec((rows, D), lambda i, c: (0, 0)),
                line,
                line,
                line,
            ],
            out_specs=[piece, piece, pl.BlockSpec((rows, D), lambda i, c: (0, 0))],
        ),
        out_shape=[
            jax.ShapeDtypeStruct((places, 2, each // 4, D), bf16),
            jax.ShapeDtypeStruct((places, 2, each // 4, D), bf16),
            jax.ShapeDtypeStruct((rows, D), f32),
        ],
        compiler_params=pltpu.CompilerParams(vmem_limit_bytes=VMEM_LIMIT),
        cost_estimate=pl.CostEstimate(
            flops=6 * tokens * rows * D, bytes_accessed=4 * tokens * D, transcendentals=tokens * rows
        ),
    )(core.reshape(1), hidden, table, targets, mask, lse)


def place_kernel(first, *refs):
    out = refs[-1]
    rows = out.shape[0]
    base = (pl.program_id(0) + first) * rows
    total = None
    for ids, grads in zip(refs[:-1:2], refs[1:-1:2]):
        row = lax.broadcasted_iota(jnp.int32, (rows, ids.shape[1]), 0) + base
        hot = jnp.where(row == ids[...], 1.0, 0.0).astype(bf16)
        term = dot_nn(hot, grads[...])
        total = term if total is None else total + term
    out[...] = total.astype(bf16)


def place_rows(pairs, first, parts, rows):
    specs, args = [], []
    for ids, grads in pairs:
        specs.append(pl.BlockSpec(ids.shape, lambda i: (0, 0)))
        specs.append(pl.BlockSpec(grads.shape, lambda i: (0, 0)))
        args += [ids, grads]
    return pl.pallas_call(
        functools.partial(place_kernel, first),
        grid=(parts,),
        in_specs=specs,
        out_specs=pl.BlockSpec((rows, D), lambda i: (i, 0)),
        out_shape=jax.ShapeDtypeStruct((parts * rows, D), bf16),
        compiler_params=pltpu.CompilerParams(vmem_limit_bytes=VMEM_LIMIT),
        cost_estimate=pl.CostEstimate(flops=1, bytes_accessed=rows, transcendentals=0),
    )(*args)


def gather_axis(value, axis):
    size = lax.axis_size(axis)
    me = lax.axis_index(axis)
    got = [value]
    for step in range(1, size):
        got.append(lax.ppermute(value, axis, [(i, (i + step) % size) for i in range(size)]))
    stacked = jnp.stack(got)
    return jnp.take(stacked, (me - jnp.arange(size, dtype=jnp.int32)) % size, axis=0)


def gather_small(value, axes):
    shape = value.shape
    for axis in reversed(axes):
        value = gather_axis(value, axis)
        value = value.reshape((-1,) + shape)
    return value


def fold_all(value, combine):
    for axis in reversed(ALL):
        size = lax.axis_size(axis)
        hop = 1
        while hop < size:
            other = lax.ppermute(value, axis, [(i, i ^ hop) for i in range(size)])
            value = combine(value, other)
            hop *= 2
    return value


def swap(value, axis):
    return lax.ppermute(value, axis, [(0, 1), (1, 0)])


def swap_core(value):
    return swap(value, "core")


def add16(left, right):
    return (left.astype(f32) + right.astype(f32)).astype(bf16)


def pick(value, index, dim):
    return lax.dynamic_index_in_dim(value, index, dim, keepdims=False)


def scatter_pair(value, axis, dim):
    if lax.axis_size(axis) != 2:
        return lax.psum_scatter(value, axis, scatter_dimension=dim, tiled=False)
    me = lax.axis_index(axis)
    got = swap(pick(value, 1 - me, dim), axis)
    return add16(pick(value, me, dim), got)


def scatter_core(value):
    sizes = tuple(lax.axis_size(axis) for axis in ALL)
    return scatter_pair(value.reshape(sizes + (-1, value.shape[-1])), "core", 2)


def scatter_first(value, seq_first):
    return scatter_pair(value, "seq", 2) if seq_first else scatter_pair(value, "p", 1)


def scatter_second(value, seq_first):
    return scatter_pair(value, "p", 1) if seq_first else scatter_pair(value, "seq", 1)


def scatter_last(value):
    size, me = value.shape[0], lax.axis_index("z")
    total = pick(value, me, 0).astype(f32)
    for hop in range(1, size):
        send = pick(value, (me + hop) % size, 0)
        got = lax.ppermute(send, "z", [(i, (i + hop) % size) for i in range(size)])
        total = total + got.astype(f32)
    return total


def scatter_rest(value, seq_first):
    return scatter_last(scatter_second(scatter_first(value, seq_first), seq_first))


def line_gather(value, axis):
    size = lax.axis_size(axis)
    ups, downs = [value], [value]
    for _ in range(1, size):
        ups.append(lax.ppermute(ups[-1], axis, [(i, i + 1) for i in range(size - 1)]))
        downs.append(lax.ppermute(downs[-1], axis, [(i + 1, i) for i in range(size - 1)]))
    return [value] + [ups[k] + downs[size - k] for k in range(1, size)]


def line_scatter(parts, axis, beside=None):
    size = lax.axis_size(axis)
    up, down = None, None
    for step in range(1, size):
        far = size - step
        send_up, send_down = parts[size - far], parts[far]
        if up is not None:
            send_up, send_down = send_up + up, send_down + down
        up = lax.ppermute(send_up, axis, [(i, i + 1) for i in range(step)])
        down = lax.ppermute(send_down, axis, [(size - 1 - i, size - 2 - i) for i in range(step)])
        if beside is not None:
            up, down = beside(step, up, down)
    return parts[0].astype(f32) + up.astype(f32) + down.astype(f32)


def plane_gather(table):
    if lax.axis_size("p") != 2:
        return lax.all_gather(table, PLANE, axis=0, tiled=True)
    half = table.shape[0] // 2
    by_seq, by_p = swap(table, "seq"), swap(table, "p")
    far = [swap(by_p[:half], "seq"), swap(by_seq[half:], "p")]
    mine = [table, by_seq, by_p] + far
    return jnp.concatenate(mine + [swap_core(item) for item in mine])


def plane_slot(owner):
    if lax.axis_size("p") != 2:
        return owner
    other = owner ^ lax.axis_index(PLANE)
    return ((other >> 1) & 1) * 4 + (other >> 2) * 2 + (other & 1)


def plane_scatter(pairs, rows, before, after):
    pairs, before = lax.optimization_barrier((pairs, before))
    count = lax.axis_size(PLANE)
    if lax.axis_size("p") != 2:
        placed = place_rows(pairs, 0, count, rows)
        placed = lax.psum_scatter(placed, PLANE, scatter_dimension=0, tiled=True)
        return placed.astype(f32), before, after
    away = swap_core(place_rows(pairs, 4, 4, rows))
    home = place_rows(pairs, 0, 4, rows)
    half = rows // 2
    part = lambda first, last: add16(home[first:last], away[first:last])
    got_low = swap(part(3 * rows, 3 * rows + half), "seq")
    got_high = swap(part(3 * rows + half, 4 * rows), "p")
    got_low, got_high, after = lax.optimization_barrier((got_low, got_high, after))
    seq_high = add16(part(rows + half, 2 * rows), got_high)
    p_low = add16(part(2 * rows, 2 * rows + half), got_low)
    from_seq = swap(jnp.concatenate([part(rows, rows + half), seq_high]), "seq")
    from_p = swap(jnp.concatenate([p_low, part(2 * rows + half, 3 * rows)]), "p")
    return part(0, rows).astype(f32) + from_seq.astype(f32) + from_p.astype(f32), before, after


def add_logs(left, right):
    top = jnp.maximum(left, right)
    return top + jnp.log(jnp.exp(left - top) + jnp.exp(right - top))


def ffn_forward(resid, gain, w_in, w_out):
    normed = rms_scale(resid, gain).astype(bf16)
    both = project(normed, w_in)
    hidden = gate_up(both).astype(bf16)
    return (resid + project(hidden, w_out), (normed, both, hidden))


def ffn_backward(upstream, resid, gain, w_in, w_out, saved):
    normed, both, hidden = saved
    grad_b = upstream.astype(bf16)
    d_out = weight_grad(hidden, grad_b).astype(bf16)
    _, pull = jax.vjp(gate_up, both)
    (d_both,) = pull(input_grad(grad_b, w_out))
    d_both_b = d_both.astype(bf16)
    d_in = weight_grad(normed, d_both_b).astype(bf16)
    d_resid, d_gain = norm_pull(resid, gain, 1.0, input_grad(d_both_b, w_in))
    return (upstream + d_resid, d_gain, d_in, d_out)


def branch_backward(upstream, out_b, w_out):
    grad_b = upstream.astype(bf16)
    return (weight_grad(out_b, grad_b).astype(bf16), input_grad(grad_b, w_out).astype(bf16))


def adamw(weight, grad, first_m, second_m, count, rate, decay):
    first_new = 0.9 * first_m + 0.1 * grad
    second_new = 0.999 * second_m + 0.001 * grad * grad
    first_hat = first_new / (1.0 - 0.9**count)
    second_hat = second_new / (1.0 - 0.999**count)
    return (
        first_new,
        second_new,
        weight - rate * (first_hat / (jnp.sqrt(second_hat) + 1e-08) + decay * weight),
    )


def body(
    enc_ids,
    enc_segs,
    sentinel,
    mode,
    dec_ids,
    dec_segs,
    target_ids,
    target_mask,
    buckets,
    embed,
    attn_in,
    attn_out,
    ffn_in,
    ffn_out,
    rel_table,
    gains,
    m_embed,
    v_embed,
    m_attn_in,
    v_attn_in,
    m_attn_out,
    v_attn_out,
    m_ffn_in,
    v_ffn_in,
    m_ffn_out,
    v_ffn_out,
    m_rel,
    v_rel,
    m_gains,
    v_gains,
):
    core = lax.axis_index("core")
    z_at = lax.axis_index("z")
    z_size = lax.axis_size("z")
    plane_size = lax.axis_size(PLANE)
    device = lax.axis_index(ALL)
    shard = embed.shape[0]
    padded = (shard // 16 + 1) * 16
    enc_count, dec_count = enc_ids.shape[1], dec_ids.shape[1]
    enc_len, dec_len = enc_segs.shape[1], dec_segs.shape[1]

    table_b = jnp.pad(embed.astype(bf16), ((0, padded - shard), (0, 0)))
    misc = jnp.concatenate([gains.T, rel_table.reshape(-1, 1)], axis=1)
    misc = jnp.pad(misc, ((0, 0), (0, 120)))
    shard_in = attn_in.shape[1]
    flat_out = ffn_out.astype(bf16).reshape(2, shard_in, -1)
    enc_cast = jnp.concatenate([attn_in[0], ffn_in[0], attn_out[0], misc], axis=1).astype(bf16)
    enc_pack = lax.all_gather(
        jnp.concatenate([enc_cast, flat_out[0]], axis=1), ALL, axis=0, tiled=True
    )
    dec_cast = jnp.concatenate(
        [attn_in[1], attn_in[2], attn_out[1], attn_out[2]], axis=1
    ).astype(bf16)
    ffn_cast = jnp.concatenate([ffn_in[1].astype(bf16), flat_out[1]], axis=1)
    plane_table = plane_gather(table_b)
    flat = jnp.concatenate(
        [
            enc_ids[0],
            sentinel[0],
            dec_ids[0],
            target_ids[0],
            target_mask[0],
            enc_segs[0],
            dec_segs[0],
            jnp.pad(mode[0], (0, 128 - mode.shape[1])),
        ]
    )
    flat = lax.ppermute(flat, ("core", "seq"), [(0, 0), (1, 2), (2, 1), (3, 3)])
    sizes = [enc_count, enc_count, dec_count, dec_count, dec_count, enc_len, dec_len]
    pieces, start = [], 0
    for size in sizes:
        pieces.append(flat[start : start + size])
        start += size
    enc_id, sent, dec_id, targets, mask_i, enc_seg_all, dec_seg_all = pieces
    mode_row = flat[start : start + mode.shape[1]]
    mask = mask_i.astype(f32)

    enc_seg = lax.dynamic_slice_in_dim(enc_seg_all, core * enc_count, enc_count)
    enc_seg_other = lax.dynamic_slice_in_dim(enc_seg_all, (1 - core) * enc_count, enc_count)
    dec_seg = lax.dynamic_slice_in_dim(dec_seg_all, core * dec_count, dec_count)
    dec_seg_other = lax.dynamic_slice_in_dim(dec_seg_all, (1 - core) * dec_count, dec_count)
    enc_range = jnp.arange(enc_count, dtype=jnp.int32)
    dec_range = jnp.arange(dec_count, dtype=jnp.int32)
    enc_pos, enc_pos_other = core * enc_count + enc_range, (1 - core) * enc_count + enc_range
    dec_pos, dec_pos_other = core * dec_count + dec_range, (1 - core) * dec_count + dec_range
    prior_all = jnp.concatenate([enc_seg_all[:1], enc_seg_all[:-1]])
    prior = lax.dynamic_slice_in_dim(prior_all, core * enc_count, enc_count)
    first = (enc_pos == 0) | (enc_seg != prior)
    mode_of = jnp.sum(
        jnp.where(
            enc_seg[:, None] == jnp.arange(mode.shape[1], dtype=jnp.int32)[None], mode_row[None], 0
        ),
        axis=1,
    )
    enc_tok = jnp.where(sent == 1, V - 1 - enc_seg, enc_id)
    enc_tok = jnp.where(first, V - 101 - mode_of, enc_tok)
    local_ids = jnp.concatenate([enc_tok, dec_id])

    line_ids = line_gather(local_ids, "z")
    plane_rows = plane_size * shard
    places = []
    for ids in line_ids:
        rel_id = ids - z_at * plane_rows
        inside = (rel_id >= 0) & (rel_id < plane_rows)
        places.append(
            jnp.where(inside, plane_slot(rel_id // shard) * padded + rel_id % shard, shard)
        )
    dec_cast, enc_pack, plane_table, places = lax.optimization_barrier(
        (dec_cast, enc_pack, plane_table, places)
    )
    dec_pack = lax.all_gather(dec_cast, ALL, axis=0, tiled=True)
    enc_places = [item[:enc_count] for item in places]
    dec_places = [item[enc_count:] for item in places]


    cut = lambda pack, start, width: lax.slice_in_dim(pack, start, start + width, axis=1)
    enc_wi, enc_fi = cut(enc_pack, 0, 3 * D), cut(enc_pack, 3 * D, 2 * FF)
    enc_wo, misc_all = cut(enc_pack, 3 * D + 2 * FF, D), cut(enc_pack, 4 * D + 2 * FF, 128)
    enc_fo = cut(enc_pack, 4 * D + 2 * FF + 128, FF).reshape(FF, D)
    gain = misc_all[:, :7].T.astype(f32)
    rel_all = jnp.transpose(misc_all[:, 7].reshape(-1, 2, rel_table.shape[1]), (1, 0, 2))
    rel_all = rel_all.reshape(2, BUCKETS, HEADS)

    enc_x8, enc_picks = bias_lines(rel_all[0], buckets[0], core, enc_count, enc_count)
    dec_x8, dec_picks = bias_lines(rel_all[1], buckets[1], core, dec_count, dec_count)
    held = (enc_fo, gain, enc_x8, dec_x8, enc_picks, dec_picks)

    def beside(step, up, down):
        nonlocal held
        if step == 2:
            up, down, held = lax.optimization_barrier((up, down, held))
        return up, down

    got = jnp.take(plane_table, jnp.concatenate(places), axis=0, mode="clip")
    looked = line_scatter(jnp.split(got, len(places)), "z", beside)
    enc_fo, gain, enc_x8, dec_x8, enc_picks, dec_picks = held
    enc_x0, dec_y0 = looked[:enc_count], looked[enc_count:]

    col, line = (lambda v: v[:, None]), (lambda v: v[None, :])
    enc_info = (
        col(enc_seg), line(enc_seg), line(enc_seg_other),
        col(enc_pos), line(enc_pos), line(enc_pos_other),
    )
    dec_info = (
        col(dec_seg), line(dec_seg), line(dec_seg_other),
        col(dec_pos), line(dec_pos), line(dec_pos_other),
    )
    cross_info = (
        col(dec_seg), line(enc_seg), line(enc_seg_other),
        col(dec_pos), line(enc_pos), line(enc_pos_other),
    )

    enc_n1 = rms_scale(enc_x0, gain[0]).astype(bf16)
    enc_q = project(enc_n1, enc_wi[:, :D]).astype(bf16)
    enc_kv = project(enc_n1, enc_wi[:, D:]).astype(bf16)
    enc_kv2 = swap_core(enc_kv)
    enc_ob, enc_lse = attend_forward(enc_q, enc_kv, enc_kv2, enc_info, enc_x8, False)
    ffn_cast, dec_pack, enc_ob = lax.optimization_barrier((ffn_cast, dec_pack, enc_ob))
    ffn_pack = lax.all_gather(ffn_cast, ALL, axis=0, tiled=True)
    dec_wi, cross_wi = cut(dec_pack, 0, 3 * D), cut(dec_pack, 3 * D, 3 * D)
    dec_wo, cross_wo = cut(dec_pack, 6 * D, D), cut(dec_pack, 7 * D, D)
    dec_fi = cut(ffn_pack, 0, 2 * FF)
    dec_fo = cut(ffn_pack, 2 * FF, FF).reshape(FF, D)
    enc_x1 = enc_x0 + project(enc_ob, enc_wo)
    enc_x2, enc_saved = ffn_forward(enc_x1, gain[1], enc_fi, enc_fo)
    enc_out = rms_scale(enc_x2, gain[2]).astype(bf16)

    dec_n1 = rms_scale(dec_y0, gain[3]).astype(bf16)
    dec_q = project(dec_n1, dec_wi[:, :D]).astype(bf16)
    dec_kv = project(dec_n1, dec_wi[:, D:]).astype(bf16)
    dec_kv2 = swap_core(dec_kv)
    dec_ob, dec_lse = attend_forward(dec_q, dec_kv, dec_kv2, dec_info, dec_x8, True)
    dec_y1 = dec_y0 + project(dec_ob, dec_wo)
    cross_kv = project(enc_out, cross_wi[:, D:]).astype(bf16)
    cross_kv2 = swap_core(cross_kv)
    cross_n = rms_scale(dec_y1, gain[4]).astype(bf16)
    cross_q = project(cross_n, cross_wi[:, :D]).astype(bf16)
    cross_ob, cross_lse = attend_forward(cross_q, cross_kv, cross_kv2, cross_info, None, False)
    dec_y2 = dec_y1 + project(cross_ob, cross_wo)
    dec_y3, dec_saved = ffn_forward(dec_y2, gain[5], dec_fi, dec_fo)
    head_scale = D ** (-0.5)
    hidden_b = (rms_scale(dec_y3, gain[6]) * head_scale).astype(bf16)

    hidden_all = lax.all_gather(hidden_b, ALL, axis=0, tiled=True)
    sizes = tuple(lax.axis_size(axis) for axis in ALL)
    hidden_all = hidden_all.reshape(-1, 2, 2, dec_count, D)
    info = gather_small(jnp.stack([targets, mask_i]), ALL)
    info = info.reshape(-1, 2, 2, 2, 2, dec_count // 2)
    info = jnp.transpose(info, (3, 4, 1, 0, 2, 5)).reshape(2, 1, -1)
    targets_all = info[0] - device * shard
    mask_all = info[1].astype(f32)
    lse_part, picked = head_stats(hidden_all, table_b, targets_all, shard)
    lse = fold_all(lse_part, add_logs)
    d_hidden, head_embed = [], None
    for half in range(2):
        *away, term = head_grad(
            1 - core, hidden_all, table_b, targets_all, mask_all, lse, shard, half
        )
        head_embed = term if head_embed is None else head_embed + term
        away = [swap_core(item) for item in away]
        *home, term = head_grad(
            core, hidden_all, table_b, targets_all, mask_all, lse, shard, half
        )
        head_embed = head_embed + term
        for number in range(2):
            item = add16(home[number], away[number])
            item = item.reshape(sizes[:2] + (2,) + item.shape[2:])
            d_hidden.append(scatter_rest(item, number == 0))
    d_hidden = jnp.concatenate(d_hidden)
    mine = (core * sizes[0] * sizes[1] + device // 4) * 2 + lax.axis_index("seq")
    lse_mine = lax.dynamic_slice_in_dim(
        lse.reshape(2, -1), mine * (dec_count // 2), dec_count // 2, axis=1
    )
    loss_local = jnp.sum(mask * lse_mine.reshape(-1)) - jnp.sum(mask_all * picked)

    d_y3, d_gain_final = norm_pull(dec_y3, gain[6], head_scale, d_hidden)
    d_y2, d_gain_dffn, d_dec_fi, d_dec_fo = ffn_backward(
        d_y3, dec_y2, gain[5], dec_fi, dec_fo, dec_saved
    )
    d_cross_wo, d_cross_ob = branch_backward(d_y2, cross_ob, cross_wo)
    early, d_dec_fo, d_cross_ob = lax.optimization_barrier((d_dec_fi, d_dec_fo, d_cross_ob))
    g_dec_fo = scatter_core(d_dec_fo)
    early = lax.psum_scatter(early, ALL, scatter_dimension=0, tiled=True)
    d_cross_q, own, other = attend_backward(
        d_cross_ob, cross_lse, cross_q, cross_kv, cross_kv2, cross_info, None, False
    )
    got = (own + swap_core(other).astype(f32)).astype(bf16)
    d_cross_kv = jnp.concatenate([got[0], got[1]], axis=1)
    d_cross_wq = weight_grad(cross_n, d_cross_q)
    d_y1_norm, d_gain_cross = norm_pull(
        dec_y1, gain[4], 1.0, input_grad(d_cross_q, cross_wi[:, :D])
    )
    d_y1 = d_y2 + d_y1_norm
    d_cross_wkv = weight_grad(enc_out, d_cross_kv)
    d_dec_wo, d_dec_ob = branch_backward(d_y1, dec_ob, dec_wo)
    g_dec_fo, d_dec_ob = lax.optimization_barrier((g_dec_fo, d_dec_ob))
    g_dec_fo = scatter_first(g_dec_fo, False)
    d_dec_q, own, other, dec_y8 = attend_backward(
        d_dec_ob, dec_lse, dec_q, dec_kv, dec_kv2, dec_info, dec_x8, True
    )
    got = (own + swap_core(other).astype(f32)).astype(bf16)
    d_dec_qkv = jnp.concatenate([d_dec_q, got[0], got[1]], axis=1)
    d_dec_table = bias_gradient(dec_y8, dec_picks)
    d_dec_wi = weight_grad(dec_n1, d_dec_qkv)
    d_y0_norm, d_gain_datt = norm_pull(dec_y0, gain[3], 1.0, input_grad(d_dec_qkv, dec_wi))
    d_y0 = d_y1 + d_y0_norm
    d_dec_rest = jnp.concatenate(
        [
            d_dec_wi.astype(bf16),
            d_cross_wq.astype(bf16),
            d_cross_wkv.astype(bf16),
            d_dec_wo,
            d_cross_wo,
        ],
        axis=1,
    )
    dec_lines = line_gather(d_y0.astype(bf16), "z")

    d_x2, d_gain_efin = norm_pull(
        enc_x2, gain[2], 1.0, input_grad(d_cross_kv, cross_wi[:, D:])
    )
    d_x1, d_gain_effn, d_enc_fi, d_enc_fo = ffn_backward(
        d_x2, enc_x1, gain[1], enc_fi, enc_fo, enc_saved
    )
    early, g_dec_fo, d_x1 = lax.optimization_barrier((early, g_dec_fo, d_x1))
    g_dec_fo = scatter_second(g_dec_fo, False)
    d_enc_wo, d_enc_ob = branch_backward(d_x1, enc_ob, enc_wo)
    d_enc_low, d_enc_high = d_enc_fi[:, :3456], jnp.concatenate([d_enc_fi[:, 3456:], d_enc_wo], 1)
    enc_sums = [scatter_core(item) for item in (d_enc_low, d_enc_high, d_enc_fo)]
    late, dec_lines, enc_sums, g_dec_fo, d_enc_ob = lax.optimization_barrier(
        (d_dec_rest, dec_lines, enc_sums, g_dec_fo, d_enc_ob)
    )
    late = lax.psum_scatter(late, ALL, scatter_dimension=0, tiled=True)
    early = early.astype(f32)
    enc_sums = [scatter_first(item, number == 0) for number, item in enumerate(enc_sums)]
    d_enc_q, own, other, enc_y8 = attend_backward(
        d_enc_ob, enc_lse, enc_q, enc_kv, enc_kv2, enc_info, enc_x8, False
    )
    got = (own + swap_core(other).astype(f32)).astype(bf16)
    d_enc_qkv = jnp.concatenate([d_enc_q, got[0], got[1]], axis=1)
    d_enc_table = bias_gradient(enc_y8, enc_picks)
    d_enc_wi = weight_grad(enc_n1, d_enc_qkv)
    d_x0_norm, d_gain_eatt = norm_pull(enc_x0, gain[0], 1.0, input_grad(d_enc_qkv, enc_wi))
    d_x0 = d_x1 + d_x0_norm

    d_x0, enc_sums, g_dec_fo = lax.optimization_barrier(
        (d_x0.astype(bf16), enc_sums, scatter_last(g_dec_fo))
    )
    enc_sums = [scatter_second(item, number == 0) for number, item in enumerate(enc_sums)]
    enc_lines = line_gather(d_x0, "z")
    enc_lines, enc_sums = lax.optimization_barrier((enc_lines, enc_sums))
    far_place = lambda item: jnp.where(item == shard, -1, item)[None, :]
    pairs = [
        (far_place(item), grads)
        for item, grads in zip(enc_places + dec_places, enc_lines + dec_lines)
    ]
    d_gains = jnp.stack(
        [
            d_gain_eatt,
            d_gain_effn,
            d_gain_efin,
            d_gain_datt,
            d_gain_cross,
            d_gain_dffn,
            d_gain_final,
        ]
    )
    d_rel = jnp.stack([d_enc_table.reshape(-1), d_dec_table.reshape(-1)])
    d_rel = jnp.transpose(d_rel.reshape(2, -1, rel_table.shape[1]), (1, 0, 2)).reshape(D, 1)
    d_misc = jnp.pad(jnp.concatenate([d_gains.T, d_rel], axis=1), ((0, 0), (0, 120)))
    d_last = jnp.concatenate([d_enc_wi.astype(bf16), d_misc.astype(bf16)], axis=1)
    last = [scatter_core(d_last[:, :1152]), scatter_core(d_last[:, 1152:])]
    input_embed, late, (last, enc_sums) = plane_scatter(pairs, padded, late, (last, enc_sums))
    late = late.astype(f32)
    grad_embed = head_embed[:shard] + input_embed[:shard]

    last = [scatter_rest(item, number == 0) for number, item in enumerate(last)]
    g_low, g_high, g_fo = [scatter_last(item) for item in enc_sums]
    squares = sum(
        (jnp.sum(item * item) for item in (grad_embed, early, late, g_low, g_high, g_fo, g_dec_fo, *last))
    )
    sums = fold_all(jnp.stack([jnp.sum(mask), loss_local, squares]), jnp.add)
    last = jnp.concatenate(last, axis=1)
    owned = (
        jnp.stack([cut(last, 0, 3 * D), cut(late, 0, 3 * D), cut(late, 3 * D, 3 * D)]),
        jnp.stack([cut(g_high, 640, D), cut(late, 6 * D, D), cut(late, 7 * D, D)]),
        jnp.stack(
            [jnp.concatenate([g_low, cut(g_high, 0, 640)], axis=1), early]
        ),
        jnp.stack([g_fo, g_dec_fo]),
        last[:, 3 * D + 7].reshape(2, -1),
        last[:, 3 * D : 3 * D + 7].T,
    )
    grads = (grad_embed,) + owned
    count_all, loss_all, squares_all = sums[0], sums[1], sums[2]
    grad_norm = jnp.sqrt(squares_all) / count_all
    factor = jnp.minimum(1.0, clip_limit / grad_norm) / count_all
    weights = (embed, attn_in, attn_out, ffn_in, ffn_out, rel_table, gains)
    moments = [
        (m_embed, v_embed),
        (m_attn_in, v_attn_in),
        (m_attn_out, v_attn_out),
        (m_ffn_in, v_ffn_in),
        (m_ffn_out, v_ffn_out),
        (m_rel, v_rel),
        (m_gains, v_gains),
    ]
    settings = [
        (1.0, 0.01),
        (0.05, 0.01),
        (0.05, 0.01),
        (0.05, 0.01),
        (0.05, 0.01),
        (0.3, 0.0),
        (0.3, 0.0),
    ]
    results = [loss_all / count_all, grad_norm]
    for slot_number, (param, grad, pair, setting) in enumerate(
        zip(weights, grads, moments, settings)
    ):
        clipped = grad * factor
        first_new, second_new, new_param = adamw(
            param, clipped, pair[0], pair[1], float(STEP), setting[0], setting[1]
        )
        results.extend((clipped if slot_number == 0 else first_new, second_new, new_param))
    return tuple(results)


def solution(mesh):
    rows = ("z", "p", "core")
    every = ALL
    inner = Mesh(mesh.devices.reshape(4, -1, 2, mesh.devices.shape[1]), ALL)
    mat = P(None, every, None)
    vec = P(None, every)
    emb = P(every, None)
    in_specs = (
        P(rows, "seq"),
        P(rows, None),
        P(rows, "seq"),
        P(rows, None),
        P(rows, "seq"),
        P(rows, None),
        P(rows, "seq"),
        P(rows, "seq"),
        P(),
        emb,
        mat,
        mat,
        mat,
        mat,
        vec,
        vec,
        emb,
        emb,
    ) + (mat,) * 8 + (vec,) * 4
    out_specs = (P(), P()) + (emb,) * 3 + (mat,) * 12 + (vec,) * 6
    return jax.shard_map(body, mesh=inner, in_specs=in_specs, out_specs=out_specs, check_vma=False)
```

```python
import functools

import jax
import jax.numpy as jnp
from jax import lax
from jax.experimental import pallas as pl
from jax.experimental.pallas import tpu as pltpu
from jax.sharding import Mesh
from jax.sharding import PartitionSpec as P

D = 768
HEADS = 12
HEAD_DIM = 64
FF = 2048
V = 32128
BUCKETS = 32
STEP = 10

masked_out = -1e30
clip_limit = 0.01
ALL = ("z", "p", "core", "seq")
PLANE = ("p", "core", "seq")
bf16 = jnp.bfloat16
f32 = jnp.float32
VMEM_LIMIT = 56 * 1024 * 1024


def rms_scale(values, gain):
    return values * lax.rsqrt(jnp.mean(values * values, axis=-1, keepdims=True) + 1e-06) * gain


def norm_pull(values, gain, factor, upstream):
    _, pull = jax.vjp(lambda left, right: rms_scale(left, right) * factor, values, gain)
    return pull(upstream)


def gate_up(both):
    return jax.nn.gelu(both[:, :FF], approximate=True) * both[:, FF:]


def project(left, right):
    return jnp.dot(left, right, preferred_element_type=f32)


def weight_grad(inputs, grads):
    return jnp.einsum("td,te->de", inputs, grads, preferred_element_type=f32)


def input_grad(grads, weight):
    return jnp.einsum("te,de->td", grads, weight, preferred_element_type=f32)


def dot_nt(a, b):
    return lax.dot_general(a, b, (((1,), (1,)), ((), ())), preferred_element_type=f32)


def dot_tn(a, b):
    return lax.dot_general(a, b, (((0,), (0,)), ((), ())), preferred_element_type=f32)


def dot_nn(a, b):
    return lax.dot_general(a, b, (((1,), (0,)), ((), ())), preferred_element_type=f32)


def spread(eight, rows, width):
    total = eight.shape[-1]
    grid = eight
    have = 8
    while have < rows:
        grid = jnp.concatenate([pltpu.roll(grid, total - have, 1), grid], axis=0)
        have *= 2
    return grid[:, :width]


def collect(grid, total):
    rows, width = grid.shape
    have = jnp.concatenate([grid, jnp.zeros((rows, total - width), f32)], axis=1)
    while rows > 8:
        rows //= 2
        have = pltpu.roll(have[:rows], rows, 1) + have[rows:]
    return have


def scores_of(cfg, refs, block, head):
    bq, has_bias, causal = cfg
    rows = slice(block * bq, (block + 1) * bq)
    cols = slice(head * HEAD_DIM, (head + 1) * HEAD_DIM)
    query = refs["q"][rows, cols] * jnp.asarray(HEAD_DIM ** (-0.5), bf16)
    scores = []
    for part in range(2):
        keys = refs["k"][part][:, cols]
        s = dot_nt(query, keys)
        if has_bias:
            s = s + spread(refs["x8"][head, block * 2 + part], bq, keys.shape[0])
        allowed = refs["qseg"][rows, :] == refs["kseg"][part]
        if causal:
            allowed = allowed & (refs["kpos"][part] <= refs["qpos"][rows, :])
        scores.append(jnp.where(allowed, s, masked_out))
    return query, scores


def name_refs(cfg, refs):
    bq, has_bias, causal = cfg
    it = iter(refs)
    named = {"q": next(it)}
    k0, v0, k1, v1 = next(it), next(it), next(it), next(it)
    named["k"], named["v"] = (k0, k1), (v0, v1)
    ids = next(it), next(it), next(it), next(it), next(it), next(it)
    named["qseg"], named["kseg"] = ids[0], (ids[1][...], ids[2][...])
    named["qpos"], named["kpos"] = ids[3], (ids[4][...], ids[5][...])
    if has_bias:
        named["x8"] = next(it)
    return named, list(it)


def attend_forward_kernel(cfg, *refs):
    named, (out, lse) = name_refs(cfg, refs)
    bq = cfg[0]
    for block in range(named["q"].shape[0] // bq):
        rows = slice(block * bq, (block + 1) * bq)
        for head in range(2):
            cols = slice(head * HEAD_DIM, (head + 1) * HEAD_DIM)
            _, scores = scores_of(cfg, named, block, head)
            top = jnp.maximum(
                jnp.max(scores[0], axis=1, keepdims=True), jnp.max(scores[1], axis=1, keepdims=True)
            )
            exps = [jnp.exp(s - top) for s in scores]
            total = jnp.sum(exps[0] + exps[1], axis=1, keepdims=True)
            scale = 1.0 / total
            acc = dot_nn((exps[0] * scale).astype(bf16), named["v"][0][:, cols])
            acc = acc + dot_nn((exps[1] * scale).astype(bf16), named["v"][1][:, cols])
            out[rows, cols] = acc.astype(bf16)
            lse[rows, cols] = jnp.broadcast_to(top + jnp.log(total), (bq, HEAD_DIM))


def attend_backward_kernel(cfg, *refs):
    named, rest = name_refs(cfg, refs)
    bq, has_bias, causal = cfg
    if has_bias:
        grad, lse, dq, own, other, y8 = rest
    else:
        grad, lse, dq, own, other = rest
    blocks = named["q"].shape[0] // bq
    for head in range(2):
        cols = slice(head * HEAD_DIM, (head + 1) * HEAD_DIM)
        dk, dv = [None, None], [None, None]
        for block in range(blocks):
            rows = slice(block * bq, (block + 1) * bq)
            query, scores = scores_of(cfg, named, block, head)
            level = lse[rows, head * HEAD_DIM : head * HEAD_DIM + 1]
            probs = [jnp.exp(s - level) for s in scores]
            do = grad[rows, cols]
            dp = [dot_nt(do, named["v"][part][:, cols]) for part in range(2)]
            delta = jnp.sum(probs[0] * dp[0] + probs[1] * dp[1], axis=1, keepdims=True)
            acc = None
            for part in range(2):
                ds_wide = probs[part] * (dp[part] - delta)
                ds = ds_wide.astype(bf16)
                term = dot_nn(ds, named["k"][part][:, cols])
                acc = term if acc is None else acc + term
                k_term = dot_tn(query, ds)
                v_term = dot_tn(do, probs[part].astype(bf16))
                dk[part] = k_term if dk[part] is None else dk[part] + k_term
                dv[part] = v_term if dv[part] is None else dv[part] + v_term
                if has_bias:
                    y8[head, block * 2 + part] = collect(ds_wide, y8.shape[-1])
            dq[rows, cols] = (acc * HEAD_DIM ** (-0.5)).astype(bf16)
        for part, target in enumerate((own, other)):
            target[0, :, cols] = dk[part].T.astype(target.dtype)
            target[1, :, cols] = dv[part].T.astype(target.dtype)


def attend_specs(q_len, k_len, has_bias, x8):
    whole = lambda shape: pl.BlockSpec(shape, lambda i: (0,) * len(shape))
    kv = [
        pl.BlockSpec((k_len, 128), lambda i: (0, i)),
        pl.BlockSpec((k_len, 128), lambda i: (0, i + 6)),
    ]
    specs = [pl.BlockSpec((q_len, 128), lambda i: (0, i))] + kv + kv
    specs += [whole((q_len, 1)), whole((1, k_len)), whole((1, k_len))] * 2
    if has_bias:
        specs.append(pl.BlockSpec((2,) + x8.shape[1:], lambda i: (i, 0, 0, 0)))
    return specs


def attend_args(q, kv_own, kv_other, ids, x8):
    args = [q, kv_own, kv_own, kv_other, kv_other] + list(ids)
    if x8 is not None:
        args.append(x8)
    return args


def attend_cost(q_len, k_len, products):
    return pl.CostEstimate(flops=products, bytes_accessed=q_len, transcendentals=0)


def attend_forward(q, kv_own, kv_other, ids, x8, causal):
    q_len, k_len = q.shape[0], kv_own.shape[0]
    cfg = (256, x8 is not None, causal)
    return pl.pallas_call(
        functools.partial(attend_forward_kernel, cfg),
        grid=(HEADS // 2,),
        in_specs=attend_specs(q_len, k_len, x8 is not None, x8),
        out_specs=[pl.BlockSpec((q_len, 128), lambda i: (0, i))] * 2,
        out_shape=[
            jax.ShapeDtypeStruct((q_len, D), bf16),
            jax.ShapeDtypeStruct((q_len, D), f32),
        ],
        compiler_params=pltpu.CompilerParams(vmem_limit_bytes=VMEM_LIMIT),
        cost_estimate=attend_cost(q_len, k_len, 2),
    )(*attend_args(q, kv_own, kv_other, ids, x8))


def attend_backward(grad, lse, q, kv_own, kv_other, ids, x8, causal):
    q_len, k_len = q.shape[0], kv_own.shape[0]
    cfg = (256, x8 is not None, causal)
    kv_spec = pl.BlockSpec((2, k_len, 128), lambda i: (0, 0, i))
    out_specs = [pl.BlockSpec((q_len, 128), lambda i: (0, i)), kv_spec, kv_spec]
    out_shape = [
        jax.ShapeDtypeStruct((q_len, D), bf16),
        jax.ShapeDtypeStruct((2, k_len, D), f32),
        jax.ShapeDtypeStruct((2, k_len, D), bf16),
    ]
    if x8 is not None:
        out_specs.append(pl.BlockSpec((2,) + x8.shape[1:], lambda i: (i, 0, 0, 0)))
        out_shape.append(jax.ShapeDtypeStruct(x8.shape, f32))
    return pl.pallas_call(
        functools.partial(attend_backward_kernel, cfg),
        grid=(HEADS // 2,),
        in_specs=attend_specs(q_len, k_len, x8 is not None, x8)
        + [pl.BlockSpec((q_len, 128), lambda i: (0, i))] * 2,
        out_specs=out_specs,
        out_shape=out_shape,
        compiler_params=pltpu.CompilerParams(vmem_limit_bytes=VMEM_LIMIT),
        cost_estimate=attend_cost(q_len, k_len, 5),
    )(*attend_args(q, kv_own, kv_other, ids, x8), grad, lse)


def bias_bases(core, q_len, k_len, offset):
    bases = []
    for block in range(q_len // 256):
        for part in range(2):
            k_start = (core if part == 0 else 1 - core) * k_len
            q_start = core * q_len + block * 256
            bases.append(k_start - q_start - 255 + offset)
    return bases


def bias_windows(array, core, q_len, k_len):
    size, width = array.shape[1], k_len + 256
    array = jnp.pad(array, ((0, 0), (0, 16)))
    rows = jnp.stack([array[:, 7 - r : size + 9 - r] for r in range(8)], axis=1)
    bases = bias_bases(core, q_len, k_len, size // 2)
    cut = lambda base: lax.dynamic_slice_in_dim(rows, base, width, axis=2)
    return jnp.stack([cut(base) for base in bases], axis=1)


def bias_lines(table, bucket_row, core, q_len, k_len):
    picks = (bucket_row[None, :] == jnp.arange(BUCKETS, dtype=jnp.int32)[:, None]).astype(bf16)
    per_offset = jnp.einsum("bh,bn->hn", table, picks, preferred_element_type=f32)
    return (
        bias_windows(per_offset, core, q_len, k_len),
        bias_windows(picks.astype(f32), core, q_len, k_len),
    )


def bias_gradient(y8, picks):
    return jnp.einsum("bnrw,hnrw->bh", picks, y8, precision=lax.Precision.HIGHEST)


def head_stats_kernel(count, hid, tab, tgt, lse_out, pick_out):
    logits = dot_nt(tab[...], hid[...].reshape(-1, D))
    row = lax.broadcasted_iota(jnp.int32, logits.shape, 0)
    pick_out[...] = jnp.sum(jnp.where(row == tgt[...], logits, 0.0), axis=0, keepdims=True)
    logits = jnp.where(row < count, logits, masked_out)
    top = jnp.max(logits, axis=0, keepdims=True)
    lse_out[...] = top + jnp.log(jnp.sum(jnp.exp(logits - top), axis=0, keepdims=True))


def head_grad_kernel(count, core, hid, tab, tgt, msk, lse, dhid_a, dhid_b, dtab):
    tokens = hid[...].reshape(-1, D)
    logits = dot_nt(tab[...], tokens)
    row = lax.broadcasted_iota(jnp.int32, logits.shape, 0)
    soft = jnp.exp(jnp.where(row < count, logits, masked_out) - lse[...])
    grad = ((soft - jnp.where(row == tgt[...], 1.0, 0.0)) * msk[...]).astype(bf16)
    dhid = dot_tn(grad, tab[...]).astype(bf16).reshape(hid.shape)
    cut = hid.shape[3] // 2
    dhid_a[...] = dhid[:, 0, :, :cut]
    dhid_b[...] = dhid[:, 0, :, cut:]
    term = dot_nn(grad, tokens)

    @pl.when(pl.program_id(0) == 0)
    def _():
        dtab[...] = term

    @pl.when(pl.program_id(0) != 0)
    def _():
        dtab[...] += term


def head_stats(hidden, table, targets, count):
    places, each = hidden.shape[0], hidden.shape[3]
    tokens, rows = places * 4 * each, table.shape[0]
    steps = places // 2
    line = pl.BlockSpec((1, 2 * each), lambda h, c, i: (0, (h * 2 + c) * steps + i))
    return pl.pallas_call(
        functools.partial(head_stats_kernel, count),
        grid=(2, 2, steps),
        in_specs=[
            pl.BlockSpec((2, 1, 2, each // 2, D), lambda h, c, i: (i, c, 0, h, 0)),
            pl.BlockSpec((rows, D), lambda h, c, i: (0, 0)),
            line,
        ],
        out_specs=[line, line],
        out_shape=[jax.ShapeDtypeStruct((1, tokens), f32)] * 2,
        compiler_params=pltpu.CompilerParams(vmem_limit_bytes=VMEM_LIMIT),
        cost_estimate=pl.CostEstimate(
            flops=2 * tokens * rows * D, bytes_accessed=2 * tokens * D, transcendentals=tokens * rows
        ),
    )(hidden, table, targets)


def head_grad(core, hidden, table, targets, mask, lse, count, half):
    places, each = hidden.shape[0], hidden.shape[3]
    tokens, rows = places * each, table.shape[0]
    steps = places // 2
    line = pl.BlockSpec((1, 2 * each), lambda i, c: (0, (half * 2 + c[0]) * steps + i))
    piece = pl.BlockSpec((2, 2, each // 4, D), lambda i, c: (i, 0, 0, 0))
    return pl.pallas_call(
        functools.partial(head_grad_kernel, count),
        grid_spec=pltpu.PrefetchScalarGridSpec(
            num_scalar_prefetch=1,
            grid=(steps,),
            in_specs=[
                pl.BlockSpec((2, 1, 2, each // 2, D), lambda i, c: (i, c[0], 0, half, 0)),
                pl.BlockSpec((rows, D), lambda i, c: (0, 0)),
                line,
                line,
                line,
            ],
            out_specs=[piece, piece, pl.BlockSpec((rows, D), lambda i, c: (0, 0))],
        ),
        out_shape=[
            jax.ShapeDtypeStruct((places, 2, each // 4, D), bf16),
            jax.ShapeDtypeStruct((places, 2, each // 4, D), bf16),
            jax.ShapeDtypeStruct((rows, D), f32),
        ],
        compiler_params=pltpu.CompilerParams(vmem_limit_bytes=VMEM_LIMIT),
        cost_estimate=pl.CostEstimate(
            flops=6 * tokens * rows * D, bytes_accessed=4 * tokens * D, transcendentals=tokens * rows
        ),
    )(core.reshape(1), hidden, table, targets, mask, lse)


def place_kernel(first, *refs):
    out = refs[-1]
    rows = out.shape[0]
    base = (pl.program_id(0) + first) * rows
    total = None
    for ids, grads in zip(refs[:-1:2], refs[1:-1:2]):
        row = lax.broadcasted_iota(jnp.int32, (rows, ids.shape[1]), 0) + base
        hot = jnp.where(row == ids[...], 1.0, 0.0).astype(bf16)
        term = dot_nn(hot, grads[...])
        total = term if total is None else total + term
    out[...] = total.astype(bf16)


def place_rows(pairs, first, parts, rows):
    specs, args = [], []
    for ids, grads in pairs:
        specs.append(pl.BlockSpec(ids.shape, lambda i: (0, 0)))
        specs.append(pl.BlockSpec(grads.shape, lambda i: (0, 0)))
        args += [ids, grads]
    return pl.pallas_call(
        functools.partial(place_kernel, first),
        grid=(parts,),
        in_specs=specs,
        out_specs=pl.BlockSpec((rows, D), lambda i: (i, 0)),
        out_shape=jax.ShapeDtypeStruct((parts * rows, D), bf16),
        compiler_params=pltpu.CompilerParams(vmem_limit_bytes=VMEM_LIMIT),
        cost_estimate=pl.CostEstimate(flops=1, bytes_accessed=rows, transcendentals=0),
    )(*args)


def gather_axis(value, axis):
    size = lax.axis_size(axis)
    me = lax.axis_index(axis)
    got = [value]
    for step in range(1, size):
        got.append(lax.ppermute(value, axis, [(i, (i + step) % size) for i in range(size)]))
    stacked = jnp.stack(got)
    return jnp.take(stacked, (me - jnp.arange(size, dtype=jnp.int32)) % size, axis=0)


def gather_small(value, axes):
    shape = value.shape
    for axis in reversed(axes):
        value = gather_axis(value, axis)
        value = value.reshape((-1,) + shape)
    return value


def fold_all(value, combine):
    for axis in reversed(ALL):
        size = lax.axis_size(axis)
        hop = 1
        while hop < size:
            other = lax.ppermute(value, axis, [(i, i ^ hop) for i in range(size)])
            value = combine(value, other)
            hop *= 2
    return value


def swap(value, axis):
    return lax.ppermute(value, axis, [(0, 1), (1, 0)])


def swap_core(value):
    return swap(value, "core")


def add16(left, right):
    return (left.astype(f32) + right.astype(f32)).astype(bf16)


def pick(value, index, dim):
    return lax.dynamic_index_in_dim(value, index, dim, keepdims=False)


def scatter_pair(value, axis, dim):
    if lax.axis_size(axis) != 2:
        return lax.psum_scatter(value, axis, scatter_dimension=dim, tiled=False)
    me = lax.axis_index(axis)
    got = swap(pick(value, 1 - me, dim), axis)
    return add16(pick(value, me, dim), got)


def scatter_core(value):
    sizes = tuple(lax.axis_size(axis) for axis in ALL)
    return scatter_pair(value.reshape(sizes + (-1, value.shape[-1])), "core", 2)


def scatter_first(value, seq_first):
    return scatter_pair(value, "seq", 2) if seq_first else scatter_pair(value, "p", 1)


def scatter_second(value, seq_first):
    return scatter_pair(value, "p", 1) if seq_first else scatter_pair(value, "seq", 1)


def scatter_last(value):
    size, me = value.shape[0], lax.axis_index("z")
    total = pick(value, me, 0).astype(f32)
    for hop in range(1, size):
        send = pick(value, (me + hop) % size, 0)
        got = lax.ppermute(send, "z", [(i, (i + hop) % size) for i in range(size)])
        total = total + got.astype(f32)
    return total


def scatter_rest(value, seq_first):
    return scatter_last(scatter_second(scatter_first(value, seq_first), seq_first))


def line_gather(value, axis):
    size = lax.axis_size(axis)
    ups, downs = [value], [value]
    for _ in range(1, size):
        ups.append(lax.ppermute(ups[-1], axis, [(i, i + 1) for i in range(size - 1)]))
        downs.append(lax.ppermute(downs[-1], axis, [(i + 1, i) for i in range(size - 1)]))
    return [value] + [ups[k] + downs[size - k] for k in range(1, size)]


def line_scatter(parts, axis, beside=None):
    size = lax.axis_size(axis)
    up, down = None, None
    for step in range(1, size):
        far = size - step
        send_up, send_down = parts[size - far], parts[far]
        if up is not None:
            send_up, send_down = send_up + up, send_down + down
        up = lax.ppermute(send_up, axis, [(i, i + 1) for i in range(step)])
        down = lax.ppermute(send_down, axis, [(size - 1 - i, size - 2 - i) for i in range(step)])
        if beside is not None:
            up, down = beside(step, up, down)
    return parts[0].astype(f32) + up.astype(f32) + down.astype(f32)


def plane_gather(table):
    if lax.axis_size("p") != 2:
        return lax.all_gather(table, PLANE, axis=0, tiled=True)
    half = table.shape[0] // 2
    by_seq, by_p = swap(table, "seq"), swap(table, "p")
    far = [swap(by_p[:half], "seq"), swap(by_seq[half:], "p")]
    mine = [table, by_seq, by_p] + far
    return jnp.concatenate(mine + [swap_core(item) for item in mine])


def plane_slot(owner):
    if lax.axis_size("p") != 2:
        return owner
    other = owner ^ lax.axis_index(PLANE)
    return ((other >> 1) & 1) * 4 + (other >> 2) * 2 + (other & 1)


def plane_scatter(pairs, rows, before, after):
    count = lax.axis_size(PLANE)
    if lax.axis_size("p") != 2:
        placed = place_rows(pairs, 0, count, rows)
        placed = lax.psum_scatter(placed, PLANE, scatter_dimension=0, tiled=True)
        return placed.astype(f32), after(after(before))
    pairs, before = lax.optimization_barrier((pairs, before))
    away = swap_core(place_rows(pairs, 4, 4, rows))
    pairs, sums = lax.optimization_barrier((pairs, after(before)))
    home = place_rows(pairs, 0, 4, rows)
    half = rows // 2
    part = lambda first, last: add16(home[first:last], away[first:last])
    far_low, far_high = part(3 * rows, 3 * rows + half), part(3 * rows + half, 4 * rows)
    far_low, far_high, sums = lax.optimization_barrier((far_low, far_high, after(sums)))
    got_low, got_high = swap(far_low, "seq"), swap(far_high, "p")
    seq_high = add16(part(rows + half, 2 * rows), got_high)
    p_low = add16(part(2 * rows, 2 * rows + half), got_low)
    from_seq = swap(jnp.concatenate([part(rows, rows + half), seq_high]), "seq")
    from_p = swap(jnp.concatenate([p_low, part(2 * rows + half, 3 * rows)]), "p")
    return part(0, rows).astype(f32) + from_seq.astype(f32) + from_p.astype(f32), sums


def add_logs(left, right):
    top = jnp.maximum(left, right)
    return top + jnp.log(jnp.exp(left - top) + jnp.exp(right - top))


def ffn_forward(resid, gain, w_in, w_out):
    normed = rms_scale(resid, gain).astype(bf16)
    both = project(normed, w_in)
    hidden = gate_up(both).astype(bf16)
    return (resid + project(hidden, w_out), (normed, both, hidden))


def ffn_backward(upstream, resid, gain, w_in, w_out, saved):
    normed, both, hidden = saved
    grad_b = upstream.astype(bf16)
    d_out = weight_grad(hidden, grad_b).astype(bf16)
    _, pull = jax.vjp(gate_up, both)
    (d_both,) = pull(input_grad(grad_b, w_out))
    d_both_b = d_both.astype(bf16)
    d_in = weight_grad(normed, d_both_b).astype(bf16)
    d_resid, d_gain = norm_pull(resid, gain, 1.0, input_grad(d_both_b, w_in))
    return (upstream + d_resid, d_gain, d_in, d_out)


def branch_backward(upstream, out_b, w_out):
    grad_b = upstream.astype(bf16)
    return (weight_grad(out_b, grad_b).astype(bf16), input_grad(grad_b, w_out).astype(bf16))


def adamw(weight, grad, first_m, second_m, count, rate, decay):
    first_new = 0.9 * first_m + 0.1 * grad
    second_new = 0.999 * second_m + 0.001 * grad * grad
    first_hat = first_new / (1.0 - 0.9**count)
    second_hat = second_new / (1.0 - 0.999**count)
    return (
        first_new,
        second_new,
        weight - rate * (first_hat / (jnp.sqrt(second_hat) + 1e-08) + decay * weight),
    )


def body(
    enc_ids,
    enc_segs,
    sentinel,
    mode,
    dec_ids,
    dec_segs,
    target_ids,
    target_mask,
    buckets,
    embed,
    attn_in,
    attn_out,
    ffn_in,
    ffn_out,
    rel_table,
    gains,
    m_embed,
    v_embed,
    m_attn_in,
    v_attn_in,
    m_attn_out,
    v_attn_out,
    m_ffn_in,
    v_ffn_in,
    m_ffn_out,
    v_ffn_out,
    m_rel,
    v_rel,
    m_gains,
    v_gains,
):
    core = lax.axis_index("core")
    z_at = lax.axis_index("z")
    z_size = lax.axis_size("z")
    plane_size = lax.axis_size(PLANE)
    device = lax.axis_index(ALL)
    shard = embed.shape[0]
    padded = (shard // 16 + 1) * 16
    enc_count, dec_count = enc_ids.shape[1], dec_ids.shape[1]
    enc_len, dec_len = enc_segs.shape[1], dec_segs.shape[1]

    table_b = jnp.pad(embed.astype(bf16), ((0, padded - shard), (0, 0)))
    misc = jnp.concatenate([gains.T, rel_table.reshape(-1, 1)], axis=1)
    misc = jnp.pad(misc, ((0, 0), (0, 120)))
    shard_in = attn_in.shape[1]
    flat_out = ffn_out.astype(bf16).reshape(2, shard_in, -1)
    enc_cast = jnp.concatenate([attn_in[0], ffn_in[0], attn_out[0], misc], axis=1).astype(bf16)
    enc_pack = lax.all_gather(
        jnp.concatenate([enc_cast, flat_out[0]], axis=1), ALL, axis=0, tiled=True
    )
    dec_cast = jnp.concatenate(
        [attn_in[1], attn_in[2], attn_out[1], attn_out[2]], axis=1
    ).astype(bf16)
    ffn_cast = jnp.concatenate([ffn_in[1].astype(bf16), flat_out[1]], axis=1)
    plane_table = plane_gather(table_b)
    flat = jnp.concatenate(
        [
            enc_ids[0],
            sentinel[0],
            dec_ids[0],
            target_ids[0],
            target_mask[0],
            enc_segs[0],
            dec_segs[0],
            jnp.pad(mode[0], (0, 128 - mode.shape[1])),
        ]
    )
    flat = lax.ppermute(flat, ("core", "seq"), [(0, 0), (1, 2), (2, 1), (3, 3)])
    sizes = [enc_count, enc_count, dec_count, dec_count, dec_count, enc_len, dec_len]
    pieces, start = [], 0
    for size in sizes:
        pieces.append(flat[start : start + size])
        start += size
    enc_id, sent, dec_id, targets, mask_i, enc_seg_all, dec_seg_all = pieces
    mode_row = flat[start : start + mode.shape[1]]
    mask = mask_i.astype(f32)

    enc_seg = lax.dynamic_slice_in_dim(enc_seg_all, core * enc_count, enc_count)
    enc_seg_other = lax.dynamic_slice_in_dim(enc_seg_all, (1 - core) * enc_count, enc_count)
    dec_seg = lax.dynamic_slice_in_dim(dec_seg_all, core * dec_count, dec_count)
    dec_seg_other = lax.dynamic_slice_in_dim(dec_seg_all, (1 - core) * dec_count, dec_count)
    enc_range = jnp.arange(enc_count, dtype=jnp.int32)
    dec_range = jnp.arange(dec_count, dtype=jnp.int32)
    enc_pos, enc_pos_other = core * enc_count + enc_range, (1 - core) * enc_count + enc_range
    dec_pos, dec_pos_other = core * dec_count + dec_range, (1 - core) * dec_count + dec_range
    prior_all = jnp.concatenate([enc_seg_all[:1], enc_seg_all[:-1]])
    prior = lax.dynamic_slice_in_dim(prior_all, core * enc_count, enc_count)
    first = (enc_pos == 0) | (enc_seg != prior)
    mode_of = jnp.sum(
        jnp.where(
            enc_seg[:, None] == jnp.arange(mode.shape[1], dtype=jnp.int32)[None], mode_row[None], 0
        ),
        axis=1,
    )
    enc_tok = jnp.where(sent == 1, V - 1 - enc_seg, enc_id)
    enc_tok = jnp.where(first, V - 101 - mode_of, enc_tok)
    local_ids = jnp.concatenate([enc_tok, dec_id])

    line_ids = line_gather(local_ids, "z")
    plane_rows = plane_size * shard
    places = []
    for ids in line_ids:
        rel_id = ids - z_at * plane_rows
        inside = (rel_id >= 0) & (rel_id < plane_rows)
        places.append(
            jnp.where(inside, plane_slot(rel_id // shard) * padded + rel_id % shard, shard)
        )
    dec_cast, enc_pack, plane_table, places = lax.optimization_barrier(
        (dec_cast, enc_pack, plane_table, places)
    )
    dec_pack = lax.all_gather(dec_cast, ALL, axis=0, tiled=True)
    enc_places = [item[:enc_count] for item in places]
    dec_places = [item[enc_count:] for item in places]


    cut = lambda pack, start, width: lax.slice_in_dim(pack, start, start + width, axis=1)
    enc_wi, enc_fi = cut(enc_pack, 0, 3 * D), cut(enc_pack, 3 * D, 2 * FF)
    enc_wo, misc_all = cut(enc_pack, 3 * D + 2 * FF, D), cut(enc_pack, 4 * D + 2 * FF, 128)
    enc_fo = cut(enc_pack, 4 * D + 2 * FF + 128, FF).reshape(FF, D)
    gain = misc_all[:, :7].T.astype(f32)
    rel_all = jnp.transpose(misc_all[:, 7].reshape(-1, 2, rel_table.shape[1]), (1, 0, 2))
    rel_all = rel_all.reshape(2, BUCKETS, HEADS)

    enc_x8, enc_picks = bias_lines(rel_all[0], buckets[0], core, enc_count, enc_count)
    dec_x8, dec_picks = bias_lines(rel_all[1], buckets[1], core, dec_count, dec_count)
    held = (enc_fo, gain, enc_x8, dec_x8, enc_picks, dec_picks)

    def beside(step, up, down):
        nonlocal held
        if step == 2:
            up, down, held = lax.optimization_barrier((up, down, held))
        return up, down

    got = jnp.take(plane_table, jnp.concatenate(places), axis=0, mode="clip")
    looked = line_scatter(jnp.split(got, len(places)), "z", beside)
    enc_fo, gain, enc_x8, dec_x8, enc_picks, dec_picks = held
    ffn_cast, dec_pack, looked = lax.optimization_barrier((ffn_cast, dec_pack, looked))
    ffn_pack = lax.all_gather(ffn_cast, ALL, axis=0, tiled=True)
    dec_wi, cross_wi = cut(dec_pack, 0, 3 * D), cut(dec_pack, 3 * D, 3 * D)
    dec_wo, cross_wo = cut(dec_pack, 6 * D, D), cut(dec_pack, 7 * D, D)
    dec_fi = cut(ffn_pack, 0, 2 * FF)
    dec_fo = cut(ffn_pack, 2 * FF, FF).reshape(FF, D)
    enc_x0, dec_y0 = looked[:enc_count], looked[enc_count:]

    col, line = (lambda v: v[:, None]), (lambda v: v[None, :])
    enc_info = (
        col(enc_seg), line(enc_seg), line(enc_seg_other),
        col(enc_pos), line(enc_pos), line(enc_pos_other),
    )
    dec_info = (
        col(dec_seg), line(dec_seg), line(dec_seg_other),
        col(dec_pos), line(dec_pos), line(dec_pos_other),
    )
    cross_info = (
        col(dec_seg), line(enc_seg), line(enc_seg_other),
        col(dec_pos), line(enc_pos), line(enc_pos_other),
    )

    enc_n1 = rms_scale(enc_x0, gain[0]).astype(bf16)
    enc_q = project(enc_n1, enc_wi[:, :D]).astype(bf16)
    enc_kv = project(enc_n1, enc_wi[:, D:]).astype(bf16)
    enc_kv2 = swap_core(enc_kv)
    enc_ob, enc_lse = attend_forward(enc_q, enc_kv, enc_kv2, enc_info, enc_x8, False)
    enc_x1 = enc_x0 + project(enc_ob, enc_wo)
    enc_x2, enc_saved = ffn_forward(enc_x1, gain[1], enc_fi, enc_fo)
    enc_out = rms_scale(enc_x2, gain[2]).astype(bf16)

    dec_n1 = rms_scale(dec_y0, gain[3]).astype(bf16)
    dec_q = project(dec_n1, dec_wi[:, :D]).astype(bf16)
    dec_kv = project(dec_n1, dec_wi[:, D:]).astype(bf16)
    dec_kv2 = swap_core(dec_kv)
    dec_ob, dec_lse = attend_forward(dec_q, dec_kv, dec_kv2, dec_info, dec_x8, True)
    dec_y1 = dec_y0 + project(dec_ob, dec_wo)
    cross_kv = project(enc_out, cross_wi[:, D:]).astype(bf16)
    cross_kv2 = swap_core(cross_kv)
    cross_n = rms_scale(dec_y1, gain[4]).astype(bf16)
    cross_q = project(cross_n, cross_wi[:, :D]).astype(bf16)
    cross_ob, cross_lse = attend_forward(cross_q, cross_kv, cross_kv2, cross_info, None, False)
    dec_y2 = dec_y1 + project(cross_ob, cross_wo)
    dec_y3, dec_saved = ffn_forward(dec_y2, gain[5], dec_fi, dec_fo)
    head_scale = D ** (-0.5)
    hidden_b = (rms_scale(dec_y3, gain[6]) * head_scale).astype(bf16)

    hidden_all = lax.all_gather(hidden_b, ALL, axis=0, tiled=True)
    sizes = tuple(lax.axis_size(axis) for axis in ALL)
    hidden_all = hidden_all.reshape(-1, 2, 2, dec_count, D)
    info = gather_small(jnp.stack([targets, mask_i]), ALL)
    info = info.reshape(-1, 2, 2, 2, 2, dec_count // 2)
    info = jnp.transpose(info, (3, 4, 1, 0, 2, 5)).reshape(2, 1, -1)
    targets_all = info[0] - device * shard
    mask_all = info[1].astype(f32)
    lse_part, picked = head_stats(hidden_all, table_b, targets_all, shard)
    lse = fold_all(lse_part, add_logs)
    d_hidden, head_embed = [], None
    for half in range(2):
        *away, term = head_grad(
            1 - core, hidden_all, table_b, targets_all, mask_all, lse, shard, half
        )
        head_embed = term if head_embed is None else head_embed + term
        away = [swap_core(item) for item in away]
        *home, term = head_grad(
            core, hidden_all, table_b, targets_all, mask_all, lse, shard, half
        )
        head_embed = head_embed + term
        for number in range(2):
            item = add16(home[number], away[number])
            item = item.reshape(sizes[:2] + (2,) + item.shape[2:])
            d_hidden.append(scatter_rest(item, number == 0))
    d_hidden = jnp.concatenate(d_hidden)
    mine = (core * sizes[0] * sizes[1] + device // 4) * 2 + lax.axis_index("seq")
    lse_mine = lax.dynamic_slice_in_dim(
        lse.reshape(2, -1), mine * (dec_count // 2), dec_count // 2, axis=1
    )
    loss_local = jnp.sum(mask * lse_mine.reshape(-1)) - jnp.sum(mask_all * picked)

    d_y3, d_gain_final = norm_pull(dec_y3, gain[6], head_scale, d_hidden)
    d_y2, d_gain_dffn, d_dec_fi, d_dec_fo = ffn_backward(
        d_y3, dec_y2, gain[5], dec_fi, dec_fo, dec_saved
    )
    d_cross_wo, d_cross_ob = branch_backward(d_y2, cross_ob, cross_wo)
    early, d_dec_fo, d_cross_ob = lax.optimization_barrier((d_dec_fi, d_dec_fo, d_cross_ob))
    g_dec_fo = scatter_core(d_dec_fo)
    early = lax.psum_scatter(early, ALL, scatter_dimension=0, tiled=True)
    d_cross_q, own, other = attend_backward(
        d_cross_ob, cross_lse, cross_q, cross_kv, cross_kv2, cross_info, None, False
    )
    got = (own + swap_core(other).astype(f32)).astype(bf16)
    d_cross_kv = jnp.concatenate([got[0], got[1]], axis=1)
    d_cross_wq = weight_grad(cross_n, d_cross_q)
    d_y1_norm, d_gain_cross = norm_pull(
        dec_y1, gain[4], 1.0, input_grad(d_cross_q, cross_wi[:, :D])
    )
    d_y1 = d_y2 + d_y1_norm
    d_cross_wkv = weight_grad(enc_out, d_cross_kv)
    d_dec_wo, d_dec_ob = branch_backward(d_y1, dec_ob, dec_wo)
    g_dec_fo, d_dec_ob = lax.optimization_barrier((g_dec_fo, d_dec_ob))
    g_dec_fo = scatter_first(g_dec_fo, False)
    d_dec_q, own, other, dec_y8 = attend_backward(
        d_dec_ob, dec_lse, dec_q, dec_kv, dec_kv2, dec_info, dec_x8, True
    )
    got = (own + swap_core(other).astype(f32)).astype(bf16)
    d_dec_qkv = jnp.concatenate([d_dec_q, got[0], got[1]], axis=1)
    d_dec_table = bias_gradient(dec_y8, dec_picks)
    d_dec_wi = weight_grad(dec_n1, d_dec_qkv)
    d_y0_norm, d_gain_datt = norm_pull(dec_y0, gain[3], 1.0, input_grad(d_dec_qkv, dec_wi))
    d_y0 = d_y1 + d_y0_norm
    d_dec_rest = jnp.concatenate(
        [
            d_dec_wi.astype(bf16),
            d_cross_wq.astype(bf16),
            d_cross_wkv.astype(bf16),
            d_dec_wo,
            d_cross_wo,
        ],
        axis=1,
    )
    dec_lines = line_gather(d_y0.astype(bf16), "z")

    d_x2, d_gain_efin = norm_pull(
        enc_x2, gain[2], 1.0, input_grad(d_cross_kv, cross_wi[:, D:])
    )
    d_x1, d_gain_effn, d_enc_fi, d_enc_fo = ffn_backward(
        d_x2, enc_x1, gain[1], enc_fi, enc_fo, enc_saved
    )
    early, g_dec_fo, d_x1 = lax.optimization_barrier((early, g_dec_fo, d_x1))
    g_dec_fo = scatter_second(g_dec_fo, False)
    d_enc_wo, d_enc_ob = branch_backward(d_x1, enc_ob, enc_wo)
    d_enc_low, d_enc_high = d_enc_fi[:, :3456], jnp.concatenate([d_enc_fi[:, 3456:], d_enc_wo], 1)
    enc_sums = [scatter_core(item) for item in (d_enc_low, d_enc_high, d_enc_fo)]
    late, dec_lines, enc_sums, g_dec_fo, d_enc_ob = lax.optimization_barrier(
        (d_dec_rest, dec_lines, enc_sums, g_dec_fo, d_enc_ob)
    )
    late = lax.psum_scatter(late, ALL, scatter_dimension=0, tiled=True)
    early = early.astype(f32)
    enc_sums = [scatter_first(item, number == 0) for number, item in enumerate(enc_sums)]
    d_enc_q, own, other, enc_y8 = attend_backward(
        d_enc_ob, enc_lse, enc_q, enc_kv, enc_kv2, enc_info, enc_x8, False
    )
    got = (own + swap_core(other).astype(f32)).astype(bf16)
    d_enc_qkv = jnp.concatenate([d_enc_q, got[0], got[1]], axis=1)
    d_enc_table = bias_gradient(enc_y8, enc_picks)
    d_enc_wi = weight_grad(enc_n1, d_enc_qkv)
    d_x0_norm, d_gain_eatt = norm_pull(enc_x0, gain[0], 1.0, input_grad(d_enc_qkv, enc_wi))
    d_x0 = d_x1 + d_x0_norm

    d_x0, enc_sums, g_dec_fo = lax.optimization_barrier(
        (d_x0.astype(bf16), enc_sums, scatter_last(g_dec_fo))
    )
    enc_sums = [scatter_second(item, number == 0) for number, item in enumerate(enc_sums)]
    enc_lines = line_gather(d_x0, "z")
    enc_lines, enc_sums = lax.optimization_barrier((enc_lines, enc_sums))
    far_place = lambda item: jnp.where(item == shard, -1, item)[None, :]
    pairs = [
        (far_place(item), grads)
        for item, grads in zip(enc_places + dec_places, enc_lines + dec_lines)
    ]
    d_gains = jnp.stack(
        [
            d_gain_eatt,
            d_gain_effn,
            d_gain_efin,
            d_gain_datt,
            d_gain_cross,
            d_gain_dffn,
            d_gain_final,
        ]
    )
    d_rel = jnp.stack([d_enc_table.reshape(-1), d_dec_table.reshape(-1)])
    d_rel = jnp.transpose(d_rel.reshape(2, -1, rel_table.shape[1]), (1, 0, 2)).reshape(D, 1)
    d_misc = jnp.pad(jnp.concatenate([d_gains.T, d_rel], axis=1), ((0, 0), (0, 120)))
    d_last = jnp.concatenate([d_enc_wi.astype(bf16), d_misc.astype(bf16)], axis=1)
    last = [scatter_core(d_last[:, :1152]), scatter_core(d_last[:, 1152:])]

    def beside_place(sums):
        if len(sums) == 3:
            late, last, enc_sums = sums
            last = [scatter_first(item, number == 0) for number, item in enumerate(last)]
            wide = jnp.concatenate(enc_sums[:2], axis=2)
            return late, last, [scatter_last(wide), scatter_last(enc_sums[2])], None
        late, last, enc_sums, _ = sums
        return late, [scatter_second(item, not number) for number, item in enumerate(last)], enc_sums

    input_embed, (late, last, (g_wide, g_fo)) = plane_scatter(
        pairs, padded, (late, last, enc_sums), beside_place
    )
    late = late.astype(f32)
    grad_embed = head_embed[:shard] + input_embed[:shard]

    last = [scatter_last(item) for item in last]
    squares = sum(
        (jnp.sum(item * item) for item in (grad_embed, early, late, g_wide, g_fo, g_dec_fo, *last))
    )
    sums = fold_all(jnp.stack([jnp.sum(mask), loss_local, squares]), jnp.add)
    last = jnp.concatenate(last, axis=1)
    owned = (
        jnp.stack([cut(last, 0, 3 * D), cut(late, 0, 3 * D), cut(late, 3 * D, 3 * D)]),
        jnp.stack([cut(g_wide, 2 * FF, D), cut(late, 6 * D, D), cut(late, 7 * D, D)]),
        jnp.stack([cut(g_wide, 0, 2 * FF), early]),
        jnp.stack([g_fo, g_dec_fo]),
        last[:, 3 * D + 7].reshape(2, -1),
        last[:, 3 * D : 3 * D + 7].T,
    )
    grads = (grad_embed,) + owned
    count_all, loss_all, squares_all = sums[0], sums[1], sums[2]
    grad_norm = jnp.sqrt(squares_all) / count_all
    factor = jnp.minimum(1.0, clip_limit / grad_norm) / count_all
    weights = (embed, attn_in, attn_out, ffn_in, ffn_out, rel_table, gains)
    moments = [
        (m_embed, v_embed),
        (m_attn_in, v_attn_in),
        (m_attn_out, v_attn_out),
        (m_ffn_in, v_ffn_in),
        (m_ffn_out, v_ffn_out),
        (m_rel, v_rel),
        (m_gains, v_gains),
    ]
    settings = [
        (1.0, 0.01),
        (0.05, 0.01),
        (0.05, 0.01),
        (0.05, 0.01),
        (0.05, 0.01),
        (0.3, 0.0),
        (0.3, 0.0),
    ]
    results = [loss_all / count_all, grad_norm]
    for slot_number, (param, grad, pair, setting) in enumerate(
        zip(weights, grads, moments, settings)
    ):
        clipped = grad * factor
        first_new, second_new, new_param = adamw(
            param, clipped, pair[0], pair[1], float(STEP), setting[0], setting[1]
        )
        results.extend((clipped if slot_number == 0 else first_new, second_new, new_param))
    return tuple(results)


def solution(mesh):
    rows = ("z", "p", "core")
    every = ALL
    inner = Mesh(mesh.devices.reshape(4, -1, 2, mesh.devices.shape[1]), ALL)
    mat = P(None, every, None)
    vec = P(None, every)
    emb = P(every, None)
    in_specs = (
        P(rows, "seq"),
        P(rows, None),
        P(rows, "seq"),
        P(rows, None),
        P(rows, "seq"),
        P(rows, None),
        P(rows, "seq"),
        P(rows, "seq"),
        P(),
        emb,
        mat,
        mat,
        mat,
        mat,
        vec,
        vec,
        emb,
        emb,
    ) + (mat,) * 8 + (vec,) * 4
    out_specs = (P(), P()) + (emb,) * 3 + (mat,) * 12 + (vec,) * 6
    return jax.shard_map(body, mesh=inner, in_specs=in_specs, out_specs=out_specs, check_vma=False)
```

```python
import functools

import jax
import jax.numpy as jnp
from jax import lax
from jax.experimental import pallas as pl
from jax.experimental.pallas import tpu as pltpu
from jax.sharding import Mesh
from jax.sharding import PartitionSpec as P

D = 768
HEADS = 12
HEAD_DIM = 64
FF = 2048
V = 32128
BUCKETS = 32
STEP = 10

masked_out = -1e30
clip_limit = 0.01
ALL = ("z", "p", "core", "seq")
PLANE = ("p", "core", "seq")
bf16 = jnp.bfloat16
f32 = jnp.float32
VMEM_LIMIT = 56 * 1024 * 1024


def rms_scale(values, gain):
    return values * lax.rsqrt(jnp.mean(values * values, axis=-1, keepdims=True) + 1e-06) * gain


def norm_pull(values, gain, factor, upstream):
    _, pull = jax.vjp(lambda left, right: rms_scale(left, right) * factor, values, gain)
    return pull(upstream)


def gate_up(both):
    return jax.nn.gelu(both[:, :FF], approximate=True) * both[:, FF:]


def project(left, right):
    return jnp.dot(left, right, preferred_element_type=f32)


def weight_grad(inputs, grads):
    return jnp.einsum("td,te->de", inputs, grads, preferred_element_type=f32)


def input_grad(grads, weight):
    return jnp.einsum("te,de->td", grads, weight, preferred_element_type=f32)


def dot_nt(a, b):
    return lax.dot_general(a, b, (((1,), (1,)), ((), ())), preferred_element_type=f32)


def dot_tn(a, b):
    return lax.dot_general(a, b, (((0,), (0,)), ((), ())), preferred_element_type=f32)


def dot_nn(a, b):
    return lax.dot_general(a, b, (((1,), (0,)), ((), ())), preferred_element_type=f32)


def spread(eight, rows, width):
    total = eight.shape[-1]
    grid = eight
    have = 8
    while have < rows:
        grid = jnp.concatenate([pltpu.roll(grid, total - have, 1), grid], axis=0)
        have *= 2
    return grid[:, :width]


def collect(grid, total):
    rows, width = grid.shape
    have = jnp.concatenate([grid, jnp.zeros((rows, total - width), f32)], axis=1)
    while rows > 8:
        rows //= 2
        have = pltpu.roll(have[:rows], rows, 1) + have[rows:]
    return have


def scores_of(cfg, refs, block, head):
    bq, has_bias, causal = cfg
    rows = slice(block * bq, (block + 1) * bq)
    cols = slice(head * HEAD_DIM, (head + 1) * HEAD_DIM)
    query = refs["q"][rows, cols] * jnp.asarray(HEAD_DIM ** (-0.5), bf16)
    scores = []
    for part in range(2):
        keys = refs["k"][part][:, cols]
        s = dot_nt(query, keys)
        if has_bias:
            s = s + spread(refs["x8"][head, block * 2 + part], bq, keys.shape[0])
        allowed = refs["qseg"][rows, :] == refs["kseg"][part]
        if causal:
            allowed = allowed & (refs["kpos"][part] <= refs["qpos"][rows, :])
        scores.append(jnp.where(allowed, s, masked_out))
    return query, scores


def name_refs(cfg, refs):
    bq, has_bias, causal = cfg
    it = iter(refs)
    named = {"q": next(it)}
    k0, v0, k1, v1 = next(it), next(it), next(it), next(it)
    named["k"], named["v"] = (k0, k1), (v0, v1)
    ids = next(it), next(it), next(it), next(it), next(it), next(it)
    named["qseg"], named["kseg"] = ids[0], (ids[1][...], ids[2][...])
    named["qpos"], named["kpos"] = ids[3], (ids[4][...], ids[5][...])
    if has_bias:
        named["x8"] = next(it)
    return named, list(it)


def attend_forward_kernel(cfg, *refs):
    named, (out, lse) = name_refs(cfg, refs)
    bq = cfg[0]
    for block in range(named["q"].shape[0] // bq):
        rows = slice(block * bq, (block + 1) * bq)
        for head in range(2):
            cols = slice(head * HEAD_DIM, (head + 1) * HEAD_DIM)
            _, scores = scores_of(cfg, named, block, head)
            top = jnp.maximum(
                jnp.max(scores[0], axis=1, keepdims=True), jnp.max(scores[1], axis=1, keepdims=True)
            )
            exps = [jnp.exp(s - top) for s in scores]
            total = jnp.sum(exps[0] + exps[1], axis=1, keepdims=True)
            scale = 1.0 / total
            acc = dot_nn((exps[0] * scale).astype(bf16), named["v"][0][:, cols])
            acc = acc + dot_nn((exps[1] * scale).astype(bf16), named["v"][1][:, cols])
            out[rows, cols] = acc.astype(bf16)
            lse[rows, cols] = jnp.broadcast_to(top + jnp.log(total), (bq, HEAD_DIM))


def attend_backward_kernel(cfg, *refs):
    named, rest = name_refs(cfg, refs)
    bq, has_bias, causal = cfg
    if has_bias:
        grad, lse, dq, own, other, y8 = rest
    else:
        grad, lse, dq, own, other = rest
    blocks = named["q"].shape[0] // bq
    for head in range(2):
        cols = slice(head * HEAD_DIM, (head + 1) * HEAD_DIM)
        dk, dv = [None, None], [None, None]
        for block in range(blocks):
            rows = slice(block * bq, (block + 1) * bq)
            query, scores = scores_of(cfg, named, block, head)
            level = lse[rows, head * HEAD_DIM : head * HEAD_DIM + 1]
            probs = [jnp.exp(s - level) for s in scores]
            do = grad[rows, cols]
            dp = [dot_nt(do, named["v"][part][:, cols]) for part in range(2)]
            delta = jnp.sum(probs[0] * dp[0] + probs[1] * dp[1], axis=1, keepdims=True)
            acc = None
            for part in range(2):
                ds_wide = probs[part] * (dp[part] - delta)
                ds = ds_wide.astype(bf16)
                term = dot_nn(ds, named["k"][part][:, cols])
                acc = term if acc is None else acc + term
                k_term = dot_tn(query, ds)
                v_term = dot_tn(do, probs[part].astype(bf16))
                dk[part] = k_term if dk[part] is None else dk[part] + k_term
                dv[part] = v_term if dv[part] is None else dv[part] + v_term
                if has_bias:
                    y8[head, block * 2 + part] = collect(ds_wide, y8.shape[-1])
            dq[rows, cols] = (acc * HEAD_DIM ** (-0.5)).astype(bf16)
        for part, target in enumerate((own, other)):
            target[0, :, cols] = dk[part].T.astype(target.dtype)
            target[1, :, cols] = dv[part].T.astype(target.dtype)


def attend_specs(q_len, k_len, has_bias, x8):
    whole = lambda shape: pl.BlockSpec(shape, lambda i: (0,) * len(shape))
    kv = [
        pl.BlockSpec((k_len, 128), lambda i: (0, i)),
        pl.BlockSpec((k_len, 128), lambda i: (0, i + 6)),
    ]
    specs = [pl.BlockSpec((q_len, 128), lambda i: (0, i))] + kv + kv
    specs += [whole((q_len, 1)), whole((1, k_len)), whole((1, k_len))] * 2
    if has_bias:
        specs.append(pl.BlockSpec((2,) + x8.shape[1:], lambda i: (i, 0, 0, 0)))
    return specs


def attend_args(q, kv_own, kv_other, ids, x8):
    args = [q, kv_own, kv_own, kv_other, kv_other] + list(ids)
    if x8 is not None:
        args.append(x8)
    return args


def attend_cost(q_len, k_len, products):
    return pl.CostEstimate(flops=products, bytes_accessed=q_len, transcendentals=0)


def attend_forward(q, kv_own, kv_other, ids, x8, causal):
    q_len, k_len = q.shape[0], kv_own.shape[0]
    cfg = (256, x8 is not None, causal)
    return pl.pallas_call(
        functools.partial(attend_forward_kernel, cfg),
        grid=(HEADS // 2,),
        in_specs=attend_specs(q_len, k_len, x8 is not None, x8),
        out_specs=[pl.BlockSpec((q_len, 128), lambda i: (0, i))] * 2,
        out_shape=[
            jax.ShapeDtypeStruct((q_len, D), bf16),
            jax.ShapeDtypeStruct((q_len, D), f32),
        ],
        compiler_params=pltpu.CompilerParams(vmem_limit_bytes=VMEM_LIMIT),
        cost_estimate=attend_cost(q_len, k_len, 2),
    )(*attend_args(q, kv_own, kv_other, ids, x8))


def attend_backward(grad, lse, q, kv_own, kv_other, ids, x8, causal):
    q_len, k_len = q.shape[0], kv_own.shape[0]
    cfg = (256, x8 is not None, causal)
    kv_spec = pl.BlockSpec((2, k_len, 128), lambda i: (0, 0, i))
    out_specs = [pl.BlockSpec((q_len, 128), lambda i: (0, i)), kv_spec, kv_spec]
    out_shape = [
        jax.ShapeDtypeStruct((q_len, D), bf16),
        jax.ShapeDtypeStruct((2, k_len, D), f32),
        jax.ShapeDtypeStruct((2, k_len, D), bf16),
    ]
    if x8 is not None:
        out_specs.append(pl.BlockSpec((2,) + x8.shape[1:], lambda i: (i, 0, 0, 0)))
        out_shape.append(jax.ShapeDtypeStruct(x8.shape, f32))
    return pl.pallas_call(
        functools.partial(attend_backward_kernel, cfg),
        grid=(HEADS // 2,),
        in_specs=attend_specs(q_len, k_len, x8 is not None, x8)
        + [pl.BlockSpec((q_len, 128), lambda i: (0, i))] * 2,
        out_specs=out_specs,
        out_shape=out_shape,
        compiler_params=pltpu.CompilerParams(vmem_limit_bytes=VMEM_LIMIT),
        cost_estimate=attend_cost(q_len, k_len, 5),
    )(*attend_args(q, kv_own, kv_other, ids, x8), grad, lse)


def bias_bases(core, q_len, k_len, offset):
    bases = []
    for block in range(q_len // 256):
        for part in range(2):
            k_start = (core if part == 0 else 1 - core) * k_len
            q_start = core * q_len + block * 256
            bases.append(k_start - q_start - 255 + offset)
    return bases


def bias_windows(array, core, q_len, k_len):
    size, width = array.shape[1], k_len + 256
    array = jnp.pad(array, ((0, 0), (0, 16)))
    rows = jnp.stack([array[:, 7 - r : size + 9 - r] for r in range(8)], axis=1)
    bases = bias_bases(core, q_len, k_len, size // 2)
    cut = lambda base: lax.dynamic_slice_in_dim(rows, base, width, axis=2)
    return jnp.stack([cut(base) for base in bases], axis=1)


def bias_lines(table, bucket_row, core, q_len, k_len):
    picks = (bucket_row[None, :] == jnp.arange(BUCKETS, dtype=jnp.int32)[:, None]).astype(bf16)
    per_offset = jnp.einsum("bh,bn->hn", table, picks, preferred_element_type=f32)
    return (
        bias_windows(per_offset, core, q_len, k_len),
        bias_windows(picks.astype(f32), core, q_len, k_len),
    )


def bias_gradient(y8, picks):
    return jnp.einsum("bnrw,hnrw->bh", picks, y8, precision=lax.Precision.HIGHEST)


def head_stats_kernel(count, hid, tab, tgt, lse_out, pick_out):
    logits = dot_nt(tab[...], hid[...].reshape(-1, D))
    row = lax.broadcasted_iota(jnp.int32, logits.shape, 0)
    pick_out[...] = jnp.sum(jnp.where(row == tgt[...], logits, 0.0), axis=0, keepdims=True)
    logits = jnp.where(row < count, logits, masked_out)
    top = jnp.max(logits, axis=0, keepdims=True)
    lse_out[...] = top + jnp.log(jnp.sum(jnp.exp(logits - top), axis=0, keepdims=True))


def head_grad_kernel(count, core, hid, tab, tgt, msk, lse, dhid_a, dhid_b, dtab):
    tokens = hid[...].reshape(-1, D)
    logits = dot_nt(tab[...], tokens)
    row = lax.broadcasted_iota(jnp.int32, logits.shape, 0)
    soft = jnp.exp(jnp.where(row < count, logits, masked_out) - lse[...])
    grad = ((soft - jnp.where(row == tgt[...], 1.0, 0.0)) * msk[...]).astype(bf16)
    dhid = dot_tn(grad, tab[...]).astype(bf16).reshape(hid.shape)
    cut = hid.shape[3] // 2
    dhid_a[...] = dhid[:, 0, :, :cut]
    dhid_b[...] = dhid[:, 0, :, cut:]
    term = dot_nn(grad, tokens)

    @pl.when(pl.program_id(0) == 0)
    def _():
        dtab[...] = term

    @pl.when(pl.program_id(0) != 0)
    def _():
        dtab[...] += term


def head_stats(hidden, table, targets, count):
    places, each = hidden.shape[0], hidden.shape[3]
    tokens, rows = places * 4 * each, table.shape[0]
    steps = places // 2
    line = pl.BlockSpec((1, 2 * each), lambda h, c, i: (0, (h * 2 + c) * steps + i))
    return pl.pallas_call(
        functools.partial(head_stats_kernel, count),
        grid=(2, 2, steps),
        in_specs=[
            pl.BlockSpec((2, 1, 2, each // 2, D), lambda h, c, i: (i, c, 0, h, 0)),
            pl.BlockSpec((rows, D), lambda h, c, i: (0, 0)),
            line,
        ],
        out_specs=[line, line],
        out_shape=[jax.ShapeDtypeStruct((1, tokens), f32)] * 2,
        compiler_params=pltpu.CompilerParams(vmem_limit_bytes=VMEM_LIMIT),
        cost_estimate=pl.CostEstimate(
            flops=2 * tokens * rows * D, bytes_accessed=2 * tokens * D, transcendentals=tokens * rows
        ),
    )(hidden, table, targets)


def head_grad(core, hidden, table, targets, mask, lse, count, half):
    places, each = hidden.shape[0], hidden.shape[3]
    tokens, rows = places * each, table.shape[0]
    steps = places // 2
    line = pl.BlockSpec((1, 2 * each), lambda i, c: (0, (half * 2 + c[0]) * steps + i))
    piece = pl.BlockSpec((2, 2, each // 4, D), lambda i, c: (i, 0, 0, 0))
    return pl.pallas_call(
        functools.partial(head_grad_kernel, count),
        grid_spec=pltpu.PrefetchScalarGridSpec(
            num_scalar_prefetch=1,
            grid=(steps,),
            in_specs=[
                pl.BlockSpec((2, 1, 2, each // 2, D), lambda i, c: (i, c[0], 0, half, 0)),
                pl.BlockSpec((rows, D), lambda i, c: (0, 0)),
                line,
                line,
                line,
            ],
            out_specs=[piece, piece, pl.BlockSpec((rows, D), lambda i, c: (0, 0))],
        ),
        out_shape=[
            jax.ShapeDtypeStruct((places, 2, each // 4, D), bf16),
            jax.ShapeDtypeStruct((places, 2, each // 4, D), bf16),
            jax.ShapeDtypeStruct((rows, D), f32),
        ],
        compiler_params=pltpu.CompilerParams(vmem_limit_bytes=VMEM_LIMIT),
        cost_estimate=pl.CostEstimate(
            flops=6 * tokens * rows * D, bytes_accessed=4 * tokens * D, transcendentals=tokens * rows
        ),
    )(core.reshape(1), hidden, table, targets, mask, lse)


def place_kernel(first, *refs):
    out = refs[-1]
    rows = out.shape[0]
    base = (pl.program_id(0) + first) * rows
    total = None
    for ids, grads in zip(refs[:-1:2], refs[1:-1:2]):
        row = lax.broadcasted_iota(jnp.int32, (rows, ids.shape[1]), 0) + base
        hot = jnp.where(row == ids[...], 1.0, 0.0).astype(bf16)
        term = dot_nn(hot, grads[...])
        total = term if total is None else total + term
    out[...] = total.astype(bf16)


def place_rows(pairs, first, parts, rows):
    specs, args = [], []
    for ids, grads in pairs:
        specs.append(pl.BlockSpec(ids.shape, lambda i: (0, 0)))
        specs.append(pl.BlockSpec(grads.shape, lambda i: (0, 0)))
        args += [ids, grads]
    return pl.pallas_call(
        functools.partial(place_kernel, first),
        grid=(parts,),
        in_specs=specs,
        out_specs=pl.BlockSpec((rows, D), lambda i: (i, 0)),
        out_shape=jax.ShapeDtypeStruct((parts * rows, D), bf16),
        compiler_params=pltpu.CompilerParams(vmem_limit_bytes=VMEM_LIMIT),
        cost_estimate=pl.CostEstimate(flops=1, bytes_accessed=rows, transcendentals=0),
    )(*args)


def gather_axis(value, axis):
    size = lax.axis_size(axis)
    me = lax.axis_index(axis)
    got = [value]
    for step in range(1, size):
        got.append(lax.ppermute(value, axis, [(i, (i + step) % size) for i in range(size)]))
    stacked = jnp.stack(got)
    return jnp.take(stacked, (me - jnp.arange(size, dtype=jnp.int32)) % size, axis=0)


def gather_small(value, axes):
    shape = value.shape
    for axis in reversed(axes):
        value = gather_axis(value, axis)
        value = value.reshape((-1,) + shape)
    return value


def fold_all(value, combine):
    for axis in reversed(ALL):
        size = lax.axis_size(axis)
        hop = 1
        while hop < size:
            other = lax.ppermute(value, axis, [(i, i ^ hop) for i in range(size)])
            value = combine(value, other)
            hop *= 2
    return value


def swap(value, axis):
    return lax.ppermute(value, axis, [(0, 1), (1, 0)])


def swap_core(value):
    return swap(value, "core")


def add16(left, right):
    return (left.astype(f32) + right.astype(f32)).astype(bf16)


def pick(value, index, dim):
    return lax.dynamic_index_in_dim(value, index, dim, keepdims=False)


def scatter_pair(value, axis, dim):
    if lax.axis_size(axis) != 2:
        return lax.psum_scatter(value, axis, scatter_dimension=dim, tiled=False)
    me = lax.axis_index(axis)
    got = swap(pick(value, 1 - me, dim), axis)
    return add16(pick(value, me, dim), got)


def scatter_core(value):
    sizes = tuple(lax.axis_size(axis) for axis in ALL)
    return scatter_pair(value.reshape(sizes + (-1, value.shape[-1])), "core", 2)


def scatter_first(value, seq_first):
    return scatter_pair(value, "seq", 2) if seq_first else scatter_pair(value, "p", 1)


def scatter_second(value, seq_first):
    return scatter_pair(value, "p", 1) if seq_first else scatter_pair(value, "seq", 1)


def scatter_last(value):
    size, me = value.shape[0], lax.axis_index("z")
    total = pick(value, me, 0).astype(f32)
    for hop in range(1, size):
        send = pick(value, (me + hop) % size, 0)
        got = lax.ppermute(send, "z", [(i, (i + hop) % size) for i in range(size)])
        total = total + got.astype(f32)
    return total


def scatter_rest(value, seq_first):
    return scatter_last(scatter_second(scatter_first(value, seq_first), seq_first))


def line_gather(value, axis):
    size = lax.axis_size(axis)
    ups, downs = [value], [value]
    for _ in range(1, size):
        ups.append(lax.ppermute(ups[-1], axis, [(i, i + 1) for i in range(size - 1)]))
        downs.append(lax.ppermute(downs[-1], axis, [(i + 1, i) for i in range(size - 1)]))
    return [value] + [ups[k] + downs[size - k] for k in range(1, size)]


def line_scatter(parts, axis, beside=None):
    size = lax.axis_size(axis)
    up, down = None, None
    for step in range(1, size):
        far = size - step
        send_up, send_down = parts[size - far], parts[far]
        if up is not None:
            send_up, send_down = send_up + up, send_down + down
        up = lax.ppermute(send_up, axis, [(i, i + 1) for i in range(step)])
        down = lax.ppermute(send_down, axis, [(size - 1 - i, size - 2 - i) for i in range(step)])
        if beside is not None:
            up, down = beside(step, up, down)
    return parts[0].astype(f32) + up.astype(f32) + down.astype(f32)


def plane_gather(table):
    if lax.axis_size("p") != 2:
        return lax.all_gather(table, PLANE, axis=0, tiled=True)
    half = table.shape[0] // 2
    by_seq, by_p = swap(table, "seq"), swap(table, "p")
    far = [swap(by_p[:half], "seq"), swap(by_seq[half:], "p")]
    mine = [table, by_seq, by_p] + far
    return jnp.concatenate(mine + [swap_core(item) for item in mine])


def plane_slot(owner):
    if lax.axis_size("p") != 2:
        return owner
    other = owner ^ lax.axis_index(PLANE)
    return ((other >> 1) & 1) * 4 + (other >> 2) * 2 + (other & 1)


def plane_scatter(pairs, rows, before, after):
    count = lax.axis_size(PLANE)
    if lax.axis_size("p") != 2:
        placed = place_rows(pairs, 0, count, rows)
        placed = lax.psum_scatter(placed, PLANE, scatter_dimension=0, tiled=True)
        return placed.astype(f32), after(after(before))
    pairs, before = lax.optimization_barrier((pairs, before))
    away = swap_core(place_rows(pairs, 4, 4, rows))
    pairs, sums = lax.optimization_barrier((pairs, after(before)))
    home = place_rows(pairs, 0, 4, rows)
    half = rows // 2
    part = lambda first, last: add16(home[first:last], away[first:last])
    far_low, far_high = part(3 * rows, 3 * rows + half), part(3 * rows + half, 4 * rows)
    far_low, far_high, sums = lax.optimization_barrier((far_low, far_high, after(sums)))
    got_low, got_high = swap(far_low, "seq"), swap(far_high, "p")
    seq_high = add16(part(rows + half, 2 * rows), got_high)
    p_low = add16(part(2 * rows, 2 * rows + half), got_low)
    from_seq = swap(jnp.concatenate([part(rows, rows + half), seq_high]), "seq")
    from_p = swap(jnp.concatenate([p_low, part(2 * rows + half, 3 * rows)]), "p")
    return part(0, rows).astype(f32) + from_seq.astype(f32) + from_p.astype(f32), sums


def add_logs(left, right):
    top = jnp.maximum(left, right)
    return top + jnp.log(jnp.exp(left - top) + jnp.exp(right - top))


def ffn_forward(resid, gain, w_in, w_out):
    normed = rms_scale(resid, gain).astype(bf16)
    both = project(normed, w_in)
    hidden = gate_up(both).astype(bf16)
    return (resid + project(hidden, w_out), (normed, both, hidden))


def ffn_backward(upstream, resid, gain, w_in, w_out, saved):
    normed, both, hidden = saved
    grad_b = upstream.astype(bf16)
    d_out = weight_grad(hidden, grad_b).astype(bf16)
    _, pull = jax.vjp(gate_up, both)
    (d_both,) = pull(input_grad(grad_b, w_out))
    d_both_b = d_both.astype(bf16)
    d_in = weight_grad(normed, d_both_b).astype(bf16)
    d_resid, d_gain = norm_pull(resid, gain, 1.0, input_grad(d_both_b, w_in))
    return (upstream + d_resid, d_gain, d_in, d_out)


def branch_backward(upstream, out_b, w_out):
    grad_b = upstream.astype(bf16)
    return (weight_grad(out_b, grad_b).astype(bf16), input_grad(grad_b, w_out).astype(bf16))


def adamw(weight, grad, first_m, second_m, count, rate, decay):
    first_new = 0.9 * first_m + 0.1 * grad
    second_new = 0.999 * second_m + 0.001 * grad * grad
    first_hat = first_new / (1.0 - 0.9**count)
    second_hat = second_new / (1.0 - 0.999**count)
    return (
        first_new,
        second_new,
        weight - rate * (first_hat / (jnp.sqrt(second_hat) + 1e-08) + decay * weight),
    )


def body(
    enc_ids,
    enc_segs,
    sentinel,
    mode,
    dec_ids,
    dec_segs,
    target_ids,
    target_mask,
    buckets,
    embed,
    attn_in,
    attn_out,
    ffn_in,
    ffn_out,
    rel_table,
    gains,
    m_embed,
    v_embed,
    m_attn_in,
    v_attn_in,
    m_attn_out,
    v_attn_out,
    m_ffn_in,
    v_ffn_in,
    m_ffn_out,
    v_ffn_out,
    m_rel,
    v_rel,
    m_gains,
    v_gains,
):
    core = lax.axis_index("core")
    z_at = lax.axis_index("z")
    z_size = lax.axis_size("z")
    plane_size = lax.axis_size(PLANE)
    device = lax.axis_index(ALL)
    shard = embed.shape[0]
    padded = (shard // 16 + 1) * 16
    enc_count, dec_count = enc_ids.shape[1], dec_ids.shape[1]
    enc_len, dec_len = enc_segs.shape[1], dec_segs.shape[1]

    table_b = jnp.pad(embed.astype(bf16), ((0, padded - shard), (0, 0)))
    misc = jnp.concatenate([gains.T, rel_table.reshape(-1, 1)], axis=1)
    misc = jnp.pad(misc, ((0, 0), (0, 120)))
    shard_in = attn_in.shape[1]
    flat_out = ffn_out.astype(bf16).reshape(2, shard_in, -1)
    enc_cast = jnp.concatenate([attn_in[0], ffn_in[0], attn_out[0], misc], axis=1).astype(bf16)
    enc_pack = lax.all_gather(
        jnp.concatenate([enc_cast, flat_out[0]], axis=1), ALL, axis=0, tiled=True
    )
    dec_cast = jnp.concatenate(
        [attn_in[1], attn_in[2], attn_out[1], attn_out[2]], axis=1
    ).astype(bf16)
    ffn_cast = jnp.concatenate([ffn_in[1].astype(bf16), flat_out[1]], axis=1)
    plane_table = plane_gather(table_b)
    flat = jnp.concatenate(
        [
            enc_ids[0],
            sentinel[0],
            dec_ids[0],
            target_ids[0],
            target_mask[0],
            enc_segs[0],
            dec_segs[0],
            jnp.pad(mode[0], (0, 128 - mode.shape[1])),
        ]
    )
    flat = lax.ppermute(flat, ("core", "seq"), [(0, 0), (1, 2), (2, 1), (3, 3)])
    sizes = [enc_count, enc_count, dec_count, dec_count, dec_count, enc_len, dec_len]
    pieces, start = [], 0
    for size in sizes:
        pieces.append(flat[start : start + size])
        start += size
    enc_id, sent, dec_id, targets, mask_i, enc_seg_all, dec_seg_all = pieces
    mode_row = flat[start : start + mode.shape[1]]
    mask = mask_i.astype(f32)

    enc_seg = lax.dynamic_slice_in_dim(enc_seg_all, core * enc_count, enc_count)
    enc_seg_other = lax.dynamic_slice_in_dim(enc_seg_all, (1 - core) * enc_count, enc_count)
    dec_seg = lax.dynamic_slice_in_dim(dec_seg_all, core * dec_count, dec_count)
    dec_seg_other = lax.dynamic_slice_in_dim(dec_seg_all, (1 - core) * dec_count, dec_count)
    enc_range = jnp.arange(enc_count, dtype=jnp.int32)
    dec_range = jnp.arange(dec_count, dtype=jnp.int32)
    enc_pos, enc_pos_other = core * enc_count + enc_range, (1 - core) * enc_count + enc_range
    dec_pos, dec_pos_other = core * dec_count + dec_range, (1 - core) * dec_count + dec_range
    prior_all = jnp.concatenate([enc_seg_all[:1], enc_seg_all[:-1]])
    prior = lax.dynamic_slice_in_dim(prior_all, core * enc_count, enc_count)
    first = (enc_pos == 0) | (enc_seg != prior)
    mode_of = jnp.sum(
        jnp.where(
            enc_seg[:, None] == jnp.arange(mode.shape[1], dtype=jnp.int32)[None], mode_row[None], 0
        ),
        axis=1,
    )
    enc_tok = jnp.where(sent == 1, V - 1 - enc_seg, enc_id)
    enc_tok = jnp.where(first, V - 101 - mode_of, enc_tok)
    local_ids = jnp.concatenate([enc_tok, dec_id])

    line_ids = line_gather(local_ids, "z")
    plane_rows = plane_size * shard
    places = []
    for ids in line_ids:
        rel_id = ids - z_at * plane_rows
        inside = (rel_id >= 0) & (rel_id < plane_rows)
        places.append(
            jnp.where(inside, plane_slot(rel_id // shard) * padded + rel_id % shard, shard)
        )
    got = jnp.take(plane_table, jnp.concatenate(places), axis=0, mode="clip")
    dec_cast, enc_pack, got = lax.optimization_barrier((dec_cast, enc_pack, got))
    dec_pack = lax.all_gather(dec_cast, ALL, axis=0, tiled=True)
    enc_places = [item[:enc_count] for item in places]
    dec_places = [item[enc_count:] for item in places]


    cut = lambda pack, start, width: lax.slice_in_dim(pack, start, start + width, axis=1)
    enc_wi, enc_fi = cut(enc_pack, 0, 3 * D), cut(enc_pack, 3 * D, 2 * FF)
    enc_wo, misc_all = cut(enc_pack, 3 * D + 2 * FF, D), cut(enc_pack, 4 * D + 2 * FF, 128)
    enc_fo = cut(enc_pack, 4 * D + 2 * FF + 128, FF).reshape(FF, D)
    gain = misc_all[:, :7].T.astype(f32)
    rel_all = jnp.transpose(misc_all[:, 7].reshape(-1, 2, rel_table.shape[1]), (1, 0, 2))
    rel_all = rel_all.reshape(2, BUCKETS, HEADS)

    enc_x8, enc_picks = bias_lines(rel_all[0], buckets[0], core, enc_count, enc_count)
    dec_x8, dec_picks = bias_lines(rel_all[1], buckets[1], core, dec_count, dec_count)
    held = (enc_fo, gain, enc_x8, dec_x8, enc_picks, dec_picks)

    def beside(step, up, down):
        nonlocal held
        if step == 2:
            up, down, held = lax.optimization_barrier((up, down, held))
        return up, down

    looked = line_scatter(jnp.split(got, len(places)), "z", beside)
    enc_fo, gain, enc_x8, dec_x8, enc_picks, dec_picks = held
    ffn_cast, dec_pack, looked = lax.optimization_barrier((ffn_cast, dec_pack, looked))
    ffn_pack = lax.all_gather(ffn_cast, ALL, axis=0, tiled=True)
    dec_wi, cross_wi = cut(dec_pack, 0, 3 * D), cut(dec_pack, 3 * D, 3 * D)
    dec_wo, cross_wo = cut(dec_pack, 6 * D, D), cut(dec_pack, 7 * D, D)
    dec_fi = cut(ffn_pack, 0, 2 * FF)
    dec_fo = cut(ffn_pack, 2 * FF, FF).reshape(FF, D)
    enc_x0, dec_y0 = looked[:enc_count], looked[enc_count:]

    col, line = (lambda v: v[:, None]), (lambda v: v[None, :])
    enc_info = (
        col(enc_seg), line(enc_seg), line(enc_seg_other),
        col(enc_pos), line(enc_pos), line(enc_pos_other),
    )
    dec_info = (
        col(dec_seg), line(dec_seg), line(dec_seg_other),
        col(dec_pos), line(dec_pos), line(dec_pos_other),
    )
    cross_info = (
        col(dec_seg), line(enc_seg), line(enc_seg_other),
        col(dec_pos), line(enc_pos), line(enc_pos_other),
    )

    enc_n1 = rms_scale(enc_x0, gain[0]).astype(bf16)
    enc_q = project(enc_n1, enc_wi[:, :D]).astype(bf16)
    enc_kv = project(enc_n1, enc_wi[:, D:]).astype(bf16)
    enc_kv2 = swap_core(enc_kv)
    enc_ob, enc_lse = attend_forward(enc_q, enc_kv, enc_kv2, enc_info, enc_x8, False)
    enc_x1 = enc_x0 + project(enc_ob, enc_wo)
    enc_x2, enc_saved = ffn_forward(enc_x1, gain[1], enc_fi, enc_fo)
    enc_out = rms_scale(enc_x2, gain[2]).astype(bf16)

    dec_n1 = rms_scale(dec_y0, gain[3]).astype(bf16)
    dec_q = project(dec_n1, dec_wi[:, :D]).astype(bf16)
    dec_kv = project(dec_n1, dec_wi[:, D:]).astype(bf16)
    dec_kv2 = swap_core(dec_kv)
    dec_ob, dec_lse = attend_forward(dec_q, dec_kv, dec_kv2, dec_info, dec_x8, True)
    dec_y1 = dec_y0 + project(dec_ob, dec_wo)
    cross_kv = project(enc_out, cross_wi[:, D:]).astype(bf16)
    cross_kv2 = swap_core(cross_kv)
    cross_n = rms_scale(dec_y1, gain[4]).astype(bf16)
    cross_q = project(cross_n, cross_wi[:, :D]).astype(bf16)
    cross_ob, cross_lse = attend_forward(cross_q, cross_kv, cross_kv2, cross_info, None, False)
    dec_y2 = dec_y1 + project(cross_ob, cross_wo)
    dec_y3, dec_saved = ffn_forward(dec_y2, gain[5], dec_fi, dec_fo)
    head_scale = D ** (-0.5)
    hidden_b = (rms_scale(dec_y3, gain[6]) * head_scale).astype(bf16)

    hidden_all = lax.all_gather(hidden_b, ALL, axis=0, tiled=True)
    sizes = tuple(lax.axis_size(axis) for axis in ALL)
    hidden_all = hidden_all.reshape(-1, 2, 2, dec_count, D)
    info = gather_small(jnp.stack([targets, mask_i]), ALL)
    info = info.reshape(-1, 2, 2, 2, 2, dec_count // 2)
    info = jnp.transpose(info, (3, 4, 1, 0, 2, 5)).reshape(2, 1, -1)
    targets_all = info[0] - device * shard
    mask_all = info[1].astype(f32)
    lse_part, picked = head_stats(hidden_all, table_b, targets_all, shard)
    lse = fold_all(lse_part, add_logs)
    d_hidden, head_embed = [], None
    for half in range(2):
        *away, term = head_grad(
            1 - core, hidden_all, table_b, targets_all, mask_all, lse, shard, half
        )
        head_embed = term if head_embed is None else head_embed + term
        away = [swap_core(item) for item in away]
        *home, term = head_grad(
            core, hidden_all, table_b, targets_all, mask_all, lse, shard, half
        )
        head_embed = head_embed + term
        for number in range(2):
            item = add16(home[number], away[number])
            item = item.reshape(sizes[:2] + (2,) + item.shape[2:])
            d_hidden.append(scatter_rest(item, number == 0))
    d_hidden = jnp.concatenate(d_hidden)
    mine = (core * sizes[0] * sizes[1] + device // 4) * 2 + lax.axis_index("seq")
    lse_mine = lax.dynamic_slice_in_dim(
        lse.reshape(2, -1), mine * (dec_count // 2), dec_count // 2, axis=1
    )
    loss_local = jnp.sum(mask * lse_mine.reshape(-1)) - jnp.sum(mask_all * picked)

    d_y3, d_gain_final = norm_pull(dec_y3, gain[6], head_scale, d_hidden)
    d_y2, d_gain_dffn, d_dec_fi, d_dec_fo = ffn_backward(
        d_y3, dec_y2, gain[5], dec_fi, dec_fo, dec_saved
    )
    d_cross_wo, d_cross_ob = branch_backward(d_y2, cross_ob, cross_wo)
    early, d_dec_fo, d_cross_ob = lax.optimization_barrier((d_dec_fi, d_dec_fo, d_cross_ob))
    g_dec_fo = scatter_core(d_dec_fo)
    early = lax.psum_scatter(early, ALL, scatter_dimension=0, tiled=True)
    d_cross_q, own, other = attend_backward(
        d_cross_ob, cross_lse, cross_q, cross_kv, cross_kv2, cross_info, None, False
    )
    got = (own + swap_core(other).astype(f32)).astype(bf16)
    d_cross_kv = jnp.concatenate([got[0], got[1]], axis=1)
    d_cross_wq = weight_grad(cross_n, d_cross_q)
    d_y1_norm, d_gain_cross = norm_pull(
        dec_y1, gain[4], 1.0, input_grad(d_cross_q, cross_wi[:, :D])
    )
    d_y1 = d_y2 + d_y1_norm
    d_cross_wkv = weight_grad(enc_out, d_cross_kv)
    d_dec_wo, d_dec_ob = branch_backward(d_y1, dec_ob, dec_wo)
    g_dec_fo, d_dec_ob = lax.optimization_barrier((g_dec_fo, d_dec_ob))
    g_dec_fo = scatter_first(g_dec_fo, False)
    d_dec_q, own, other, dec_y8 = attend_backward(
        d_dec_ob, dec_lse, dec_q, dec_kv, dec_kv2, dec_info, dec_x8, True
    )
    got = (own + swap_core(other).astype(f32)).astype(bf16)
    d_dec_qkv = jnp.concatenate([d_dec_q, got[0], got[1]], axis=1)
    d_dec_table = bias_gradient(dec_y8, dec_picks)
    d_dec_wi = weight_grad(dec_n1, d_dec_qkv)
    d_y0_norm, d_gain_datt = norm_pull(dec_y0, gain[3], 1.0, input_grad(d_dec_qkv, dec_wi))
    d_y0 = d_y1 + d_y0_norm
    d_dec_rest = jnp.concatenate(
        [
            d_dec_wi.astype(bf16),
            d_cross_wq.astype(bf16),
            d_cross_wkv.astype(bf16),
            d_dec_wo,
            d_cross_wo,
        ],
        axis=1,
    )
    dec_lines = line_gather(d_y0.astype(bf16), "z")

    d_x2, d_gain_efin = norm_pull(
        enc_x2, gain[2], 1.0, input_grad(d_cross_kv, cross_wi[:, D:])
    )
    d_x1, d_gain_effn, d_enc_fi, d_enc_fo = ffn_backward(
        d_x2, enc_x1, gain[1], enc_fi, enc_fo, enc_saved
    )
    early, g_dec_fo, d_x1 = lax.optimization_barrier((early, g_dec_fo, d_x1))
    g_dec_fo = scatter_second(g_dec_fo, False)
    d_enc_wo, d_enc_ob = branch_backward(d_x1, enc_ob, enc_wo)
    d_enc_low, d_enc_high = d_enc_fi[:, :3456], jnp.concatenate([d_enc_fi[:, 3456:], d_enc_wo], 1)
    enc_sums = [scatter_core(item) for item in (d_enc_low, d_enc_high, d_enc_fo)]
    late, dec_lines, enc_sums, g_dec_fo, d_enc_ob = lax.optimization_barrier(
        (d_dec_rest, dec_lines, enc_sums, g_dec_fo, d_enc_ob)
    )
    late = lax.psum_scatter(late, ALL, scatter_dimension=0, tiled=True)
    early = early.astype(f32)
    enc_sums = [scatter_first(item, number == 0) for number, item in enumerate(enc_sums)]
    d_enc_q, own, other, enc_y8 = attend_backward(
        d_enc_ob, enc_lse, enc_q, enc_kv, enc_kv2, enc_info, enc_x8, False
    )
    got = (own + swap_core(other).astype(f32)).astype(bf16)
    d_enc_qkv = jnp.concatenate([d_enc_q, got[0], got[1]], axis=1)
    d_enc_table = bias_gradient(enc_y8, enc_picks)
    d_enc_wi = weight_grad(enc_n1, d_enc_qkv)
    d_x0_norm, d_gain_eatt = norm_pull(enc_x0, gain[0], 1.0, input_grad(d_enc_qkv, enc_wi))
    d_x0 = d_x1 + d_x0_norm

    d_x0, wides = lax.optimization_barrier((d_x0.astype(bf16), enc_sums[:2]))
    enc_sums = wides + enc_sums[2:]
    enc_sums = [scatter_second(item, number == 0) for number, item in enumerate(enc_sums)]
    enc_lines = line_gather(d_x0, "z")
    enc_lines, enc_sums = lax.optimization_barrier((enc_lines, enc_sums))
    far_place = lambda item: jnp.where(item == shard, -1, item)[None, :]
    pairs = [
        (far_place(item), grads)
        for item, grads in zip(enc_places + dec_places, enc_lines + dec_lines)
    ]
    d_gains = jnp.stack(
        [
            d_gain_eatt,
            d_gain_effn,
            d_gain_efin,
            d_gain_datt,
            d_gain_cross,
            d_gain_dffn,
            d_gain_final,
        ]
    )
    d_rel = jnp.stack([d_enc_table.reshape(-1), d_dec_table.reshape(-1)])
    d_rel = jnp.transpose(d_rel.reshape(2, -1, rel_table.shape[1]), (1, 0, 2)).reshape(D, 1)
    d_misc = jnp.pad(jnp.concatenate([d_gains.T, d_rel], axis=1), ((0, 0), (0, 120)))
    d_last = jnp.concatenate([d_enc_wi.astype(bf16), d_misc.astype(bf16)], axis=1)
    last = [scatter_core(d_last[:, :1152]), scatter_core(d_last[:, 1152:])]

    def beside_place(sums):
        if len(sums) == 3:
            late, last, enc_sums = sums
            last = [scatter_first(item, number == 0) for number, item in enumerate(last)]
            wide = jnp.concatenate(enc_sums[:2], axis=2)
            both = jnp.concatenate([enc_sums[2], g_dec_fo], axis=1)
            return late, last, [scatter_last(wide), scatter_last(both)], None
        late, last, enc_sums, _ = sums
        last = [scatter_second(item, number == 0) for number, item in enumerate(last)]
        return late, jnp.concatenate(last, axis=2), enc_sums

    input_embed, (late, last, (g_wide, g_out)) = plane_scatter(
        pairs, padded, (late, last, enc_sums), beside_place
    )
    late = late.astype(f32)
    grad_embed = head_embed[:shard] + input_embed[:shard]

    last = scatter_last(last)
    squares = sum(
        (jnp.sum(item * item) for item in (grad_embed, early, late, g_wide, g_out, last))
    )
    sums = fold_all(jnp.stack([jnp.sum(mask), loss_local, squares]), jnp.add)
    owned = (
        jnp.stack([cut(last, 0, 3 * D), cut(late, 0, 3 * D), cut(late, 3 * D, 3 * D)]),
        jnp.stack([cut(g_wide, 2 * FF, D), cut(late, 6 * D, D), cut(late, 7 * D, D)]),
        jnp.stack([cut(g_wide, 0, 2 * FF), early]),
        g_out.reshape(2, -1, D),
        last[:, 3 * D + 7].reshape(2, -1),
        last[:, 3 * D : 3 * D + 7].T,
    )
    grads = (grad_embed,) + owned
    count_all, loss_all, squares_all = sums[0], sums[1], sums[2]
    grad_norm = jnp.sqrt(squares_all) / count_all
    factor = jnp.minimum(1.0, clip_limit / grad_norm) / count_all
    weights = (embed, attn_in, attn_out, ffn_in, ffn_out, rel_table, gains)
    moments = [
        (m_embed, v_embed),
        (m_attn_in, v_attn_in),
        (m_attn_out, v_attn_out),
        (m_ffn_in, v_ffn_in),
        (m_ffn_out, v_ffn_out),
        (m_rel, v_rel),
        (m_gains, v_gains),
    ]
    settings = [
        (1.0, 0.01),
        (0.05, 0.01),
        (0.05, 0.01),
        (0.05, 0.01),
        (0.05, 0.01),
        (0.3, 0.0),
        (0.3, 0.0),
    ]
    results = [loss_all / count_all, grad_norm]
    for slot_number, (param, grad, pair, setting) in enumerate(
        zip(weights, grads, moments, settings)
    ):
        clipped = grad * factor
        first_new, second_new, new_param = adamw(
            param, clipped, pair[0], pair[1], float(STEP), setting[0], setting[1]
        )
        results.extend((clipped if slot_number == 0 else first_new, second_new, new_param))
    return tuple(results)


def solution(mesh):
    rows = ("z", "p", "core")
    every = ALL
    inner = Mesh(mesh.devices.reshape(4, -1, 2, mesh.devices.shape[1]), ALL)
    mat = P(None, every, None)
    vec = P(None, every)
    emb = P(every, None)
    in_specs = (
        P(rows, "seq"),
        P(rows, None),
        P(rows, "seq"),
        P(rows, None),
        P(rows, "seq"),
        P(rows, None),
        P(rows, "seq"),
        P(rows, "seq"),
        P(),
        emb,
        mat,
        mat,
        mat,
        mat,
        vec,
        vec,
        emb,
        emb,
    ) + (mat,) * 8 + (vec,) * 4
    out_specs = (P(), P()) + (emb,) * 3 + (mat,) * 12 + (vec,) * 6
    return jax.shard_map(body, mesh=inner, in_specs=in_specs, out_specs=out_specs, check_vma=False)
```

```python
import functools

import jax
import jax.numpy as jnp
from jax import lax
from jax.experimental import pallas as pl
from jax.experimental.pallas import tpu as pltpu
from jax.sharding import Mesh
from jax.sharding import PartitionSpec as P

D = 768
HEADS = 12
HEAD_DIM = 64
FF = 2048
V = 32128
BUCKETS = 32
STEP = 10

masked_out = -1e30
clip_limit = 0.01
ALL = ("z", "p", "core", "seq")
PLANE = ("p", "core", "seq")
bf16 = jnp.bfloat16
f32 = jnp.float32
VMEM_LIMIT = 56 * 1024 * 1024


def rms_scale(values, gain):
    return values * lax.rsqrt(jnp.mean(values * values, axis=-1, keepdims=True) + 1e-06) * gain


def norm_pull(values, gain, factor, upstream):
    _, pull = jax.vjp(lambda left, right: rms_scale(left, right) * factor, values, gain)
    return pull(upstream)


def gate_up(both):
    return jax.nn.gelu(both[:, :FF], approximate=True) * both[:, FF:]


def project(left, right):
    return jnp.dot(left, right, preferred_element_type=f32)


def weight_grad(inputs, grads):
    return jnp.einsum("td,te->de", inputs, grads, preferred_element_type=f32)


def input_grad(grads, weight):
    return jnp.einsum("te,de->td", grads, weight, preferred_element_type=f32)


def dot_nt(a, b):
    return lax.dot_general(a, b, (((1,), (1,)), ((), ())), preferred_element_type=f32)


def dot_tn(a, b):
    return lax.dot_general(a, b, (((0,), (0,)), ((), ())), preferred_element_type=f32)


def dot_nn(a, b):
    return lax.dot_general(a, b, (((1,), (0,)), ((), ())), preferred_element_type=f32)


def spread(eight, rows, width):
    total = eight.shape[-1]
    grid = eight
    have = 8
    while have < rows:
        grid = jnp.concatenate([pltpu.roll(grid, total - have, 1), grid], axis=0)
        have *= 2
    return grid[:, :width]


def collect(grid, total):
    rows, width = grid.shape
    have = jnp.concatenate([grid, jnp.zeros((rows, total - width), f32)], axis=1)
    while rows > 8:
        rows //= 2
        have = pltpu.roll(have[:rows], rows, 1) + have[rows:]
    return have


def scores_of(cfg, refs, block, head):
    bq, has_bias, causal = cfg
    rows = slice(block * bq, (block + 1) * bq)
    cols = slice(head * HEAD_DIM, (head + 1) * HEAD_DIM)
    query = refs["q"][rows, cols] * jnp.asarray(HEAD_DIM ** (-0.5), bf16)
    scores = []
    for part in range(2):
        keys = refs["k"][part][:, cols]
        s = dot_nt(query, keys)
        if has_bias:
            s = s + spread(refs["x8"][head, block * 2 + part], bq, keys.shape[0])
        allowed = refs["qseg"][rows, :] == refs["kseg"][part]
        if causal:
            allowed = allowed & (refs["kpos"][part] <= refs["qpos"][rows, :])
        scores.append(jnp.where(allowed, s, masked_out))
    return query, scores


def name_refs(cfg, refs):
    bq, has_bias, causal = cfg
    it = iter(refs)
    named = {"q": next(it)}
    k0, v0, k1, v1 = next(it), next(it), next(it), next(it)
    named["k"], named["v"] = (k0, k1), (v0, v1)
    ids = next(it), next(it), next(it), next(it), next(it), next(it)
    named["qseg"], named["kseg"] = ids[0], (ids[1][...], ids[2][...])
    named["qpos"], named["kpos"] = ids[3], (ids[4][...], ids[5][...])
    if has_bias:
        named["x8"] = next(it)
    return named, list(it)


def attend_forward_kernel(cfg, *refs):
    named, (out, lse) = name_refs(cfg, refs)
    bq = cfg[0]
    for block in range(named["q"].shape[0] // bq):
        rows = slice(block * bq, (block + 1) * bq)
        for head in range(2):
            cols = slice(head * HEAD_DIM, (head + 1) * HEAD_DIM)
            _, scores = scores_of(cfg, named, block, head)
            top = jnp.maximum(
                jnp.max(scores[0], axis=1, keepdims=True), jnp.max(scores[1], axis=1, keepdims=True)
            )
            exps = [jnp.exp(s - top) for s in scores]
            total = jnp.sum(exps[0] + exps[1], axis=1, keepdims=True)
            scale = 1.0 / total
            acc = dot_nn((exps[0] * scale).astype(bf16), named["v"][0][:, cols])
            acc = acc + dot_nn((exps[1] * scale).astype(bf16), named["v"][1][:, cols])
            out[rows, cols] = acc.astype(bf16)
            lse[rows, cols] = jnp.broadcast_to(top + jnp.log(total), (bq, HEAD_DIM))


def attend_backward_kernel(cfg, *refs):
    named, rest = name_refs(cfg, refs)
    bq, has_bias, causal = cfg
    if has_bias:
        grad, lse, dq, own, other, y8 = rest
    else:
        grad, lse, dq, own, other = rest
    blocks = named["q"].shape[0] // bq
    for head in range(2):
        cols = slice(head * HEAD_DIM, (head + 1) * HEAD_DIM)
        dk, dv = [None, None], [None, None]
        for block in range(blocks):
            rows = slice(block * bq, (block + 1) * bq)
            query, scores = scores_of(cfg, named, block, head)
            level = lse[rows, head * HEAD_DIM : head * HEAD_DIM + 1]
            probs = [jnp.exp(s - level) for s in scores]
            do = grad[rows, cols]
            dp = [dot_nt(do, named["v"][part][:, cols]) for part in range(2)]
            delta = jnp.sum(probs[0] * dp[0] + probs[1] * dp[1], axis=1, keepdims=True)
            acc = None
            for part in range(2):
                ds_wide = probs[part] * (dp[part] - delta)
                ds = ds_wide.astype(bf16)
                term = dot_nn(ds, named["k"][part][:, cols])
                acc = term if acc is None else acc + term
                k_term = dot_tn(query, ds)
                v_term = dot_tn(do, probs[part].astype(bf16))
                dk[part] = k_term if dk[part] is None else dk[part] + k_term
                dv[part] = v_term if dv[part] is None else dv[part] + v_term
                if has_bias:
                    y8[head, block * 2 + part] = collect(ds_wide, y8.shape[-1])
            dq[rows, cols] = (acc * HEAD_DIM ** (-0.5)).astype(bf16)
        for part, target in enumerate((own, other)):
            target[0, :, cols] = dk[part].T.astype(target.dtype)
            target[1, :, cols] = dv[part].T.astype(target.dtype)


def attend_specs(q_len, k_len, has_bias, x8):
    whole = lambda shape: pl.BlockSpec(shape, lambda i: (0,) * len(shape))
    kv = [
        pl.BlockSpec((k_len, 128), lambda i: (0, i)),
        pl.BlockSpec((k_len, 128), lambda i: (0, i + 6)),
    ]
    specs = [pl.BlockSpec((q_len, 128), lambda i: (0, i))] + kv + kv
    specs += [whole((q_len, 1)), whole((1, k_len)), whole((1, k_len))] * 2
    if has_bias:
        specs.append(pl.BlockSpec((2,) + x8.shape[1:], lambda i: (i, 0, 0, 0)))
    return specs


def attend_args(q, kv_own, kv_other, ids, x8):
    args = [q, kv_own, kv_own, kv_other, kv_other] + list(ids)
    if x8 is not None:
        args.append(x8)
    return args


def attend_cost(q_len, k_len, products):
    return pl.CostEstimate(flops=products, bytes_accessed=q_len, transcendentals=0)


def attend_forward(q, kv_own, kv_other, ids, x8, causal):
    q_len, k_len = q.shape[0], kv_own.shape[0]
    cfg = (256, x8 is not None, causal)
    return pl.pallas_call(
        functools.partial(attend_forward_kernel, cfg),
        grid=(HEADS // 2,),
        in_specs=attend_specs(q_len, k_len, x8 is not None, x8),
        out_specs=[pl.BlockSpec((q_len, 128), lambda i: (0, i))] * 2,
        out_shape=[
            jax.ShapeDtypeStruct((q_len, D), bf16),
            jax.ShapeDtypeStruct((q_len, D), f32),
        ],
        compiler_params=pltpu.CompilerParams(vmem_limit_bytes=VMEM_LIMIT),
        cost_estimate=attend_cost(q_len, k_len, 2),
    )(*attend_args(q, kv_own, kv_other, ids, x8))


def attend_backward(grad, lse, q, kv_own, kv_other, ids, x8, causal):
    q_len, k_len = q.shape[0], kv_own.shape[0]
    cfg = (256, x8 is not None, causal)
    kv_spec = pl.BlockSpec((2, k_len, 128), lambda i: (0, 0, i))
    out_specs = [pl.BlockSpec((q_len, 128), lambda i: (0, i)), kv_spec, kv_spec]
    out_shape = [
        jax.ShapeDtypeStruct((q_len, D), bf16),
        jax.ShapeDtypeStruct((2, k_len, D), f32),
        jax.ShapeDtypeStruct((2, k_len, D), bf16),
    ]
    if x8 is not None:
        out_specs.append(pl.BlockSpec((2,) + x8.shape[1:], lambda i: (i, 0, 0, 0)))
        out_shape.append(jax.ShapeDtypeStruct(x8.shape, f32))
    return pl.pallas_call(
        functools.partial(attend_backward_kernel, cfg),
        grid=(HEADS // 2,),
        in_specs=attend_specs(q_len, k_len, x8 is not None, x8)
        + [pl.BlockSpec((q_len, 128), lambda i: (0, i))] * 2,
        out_specs=out_specs,
        out_shape=out_shape,
        compiler_params=pltpu.CompilerParams(vmem_limit_bytes=VMEM_LIMIT),
        cost_estimate=attend_cost(q_len, k_len, 5),
    )(*attend_args(q, kv_own, kv_other, ids, x8), grad, lse)


def bias_bases(core, q_len, k_len, offset):
    bases = []
    for block in range(q_len // 256):
        for part in range(2):
            k_start = (core if part == 0 else 1 - core) * k_len
            q_start = core * q_len + block * 256
            bases.append(k_start - q_start - 255 + offset)
    return bases


def bias_windows(array, core, q_len, k_len):
    size, width = array.shape[1], k_len + 256
    array = jnp.pad(array, ((0, 0), (0, 16)))
    rows = jnp.stack([array[:, 7 - r : size + 9 - r] for r in range(8)], axis=1)
    bases = bias_bases(core, q_len, k_len, size // 2)
    cut = lambda base: lax.dynamic_slice_in_dim(rows, base, width, axis=2)
    return jnp.stack([cut(base) for base in bases], axis=1)


def bias_lines(table, bucket_row, core, q_len, k_len):
    picks = (bucket_row[None, :] == jnp.arange(BUCKETS, dtype=jnp.int32)[:, None]).astype(bf16)
    per_offset = jnp.einsum("bh,bn->hn", table, picks, preferred_element_type=f32)
    return (
        bias_windows(per_offset, core, q_len, k_len),
        bias_windows(picks.astype(f32), core, q_len, k_len),
    )


def bias_gradient(y8, picks):
    return jnp.einsum("bnrw,hnrw->bh", picks, y8, precision=lax.Precision.HIGHEST)


def head_stats_kernel(count, hid, tab, tgt, lse_out, pick_out):
    logits = dot_nt(tab[...], hid[...].reshape(-1, D))
    row = lax.broadcasted_iota(jnp.int32, logits.shape, 0)
    pick_out[...] = jnp.sum(jnp.where(row == tgt[...], logits, 0.0), axis=0, keepdims=True)
    logits = jnp.where(row < count, logits, masked_out)
    top = jnp.max(logits, axis=0, keepdims=True)
    lse_out[...] = top + jnp.log(jnp.sum(jnp.exp(logits - top), axis=0, keepdims=True))


def head_grad_kernel(count, core, hid, tab, tgt, msk, lse, dhid_a, dhid_b, dtab):
    tokens = hid[...].reshape(-1, D)
    logits = dot_nt(tab[...], tokens)
    row = lax.broadcasted_iota(jnp.int32, logits.shape, 0)
    soft = jnp.exp(jnp.where(row < count, logits, masked_out) - lse[...])
    grad = ((soft - jnp.where(row == tgt[...], 1.0, 0.0)) * msk[...]).astype(bf16)
    dhid = dot_tn(grad, tab[...]).astype(bf16).reshape(hid.shape)
    cut = hid.shape[3] // 2
    dhid_a[...] = dhid[:, 0, :, :cut]
    dhid_b[...] = dhid[:, 0, :, cut:]
    term = dot_nn(grad, tokens)

    @pl.when(pl.program_id(0) == 0)
    def _():
        dtab[...] = term

    @pl.when(pl.program_id(0) != 0)
    def _():
        dtab[...] += term


def head_stats(hidden, table, targets, count):
    places, each = hidden.shape[0], hidden.shape[3]
    tokens, rows = places * 4 * each, table.shape[0]
    steps = places // 2
    line = pl.BlockSpec((1, 2 * each), lambda h, c, i: (0, (h * 2 + c) * steps + i))
    return pl.pallas_call(
        functools.partial(head_stats_kernel, count),
        grid=(2, 2, steps),
        in_specs=[
            pl.BlockSpec((2, 1, 2, each // 2, D), lambda h, c, i: (i, c, 0, h, 0)),
            pl.BlockSpec((rows, D), lambda h, c, i: (0, 0)),
            line,
        ],
        out_specs=[line, line],
        out_shape=[jax.ShapeDtypeStruct((1, tokens), f32)] * 2,
        compiler_params=pltpu.CompilerParams(vmem_limit_bytes=VMEM_LIMIT),
        cost_estimate=pl.CostEstimate(
            flops=2 * tokens * rows * D, bytes_accessed=2 * tokens * D, transcendentals=tokens * rows
        ),
    )(hidden, table, targets)


def head_grad(core, hidden, table, targets, mask, lse, count, half):
    places, each = hidden.shape[0], hidden.shape[3]
    tokens, rows = places * each, table.shape[0]
    steps = places // 2
    line = pl.BlockSpec((1, 2 * each), lambda i, c: (0, (half * 2 + c[0]) * steps + i))
    piece = pl.BlockSpec((2, 2, each // 4, D), lambda i, c: (i, 0, 0, 0))
    return pl.pallas_call(
        functools.partial(head_grad_kernel, count),
        grid_spec=pltpu.PrefetchScalarGridSpec(
            num_scalar_prefetch=1,
            grid=(steps,),
            in_specs=[
                pl.BlockSpec((2, 1, 2, each // 2, D), lambda i, c: (i, c[0], 0, half, 0)),
                pl.BlockSpec((rows, D), lambda i, c: (0, 0)),
                line,
                line,
                line,
            ],
            out_specs=[piece, piece, pl.BlockSpec((rows, D), lambda i, c: (0, 0))],
        ),
        out_shape=[
            jax.ShapeDtypeStruct((places, 2, each // 4, D), bf16),
            jax.ShapeDtypeStruct((places, 2, each // 4, D), bf16),
            jax.ShapeDtypeStruct((rows, D), f32),
        ],
        compiler_params=pltpu.CompilerParams(vmem_limit_bytes=VMEM_LIMIT),
        cost_estimate=pl.CostEstimate(
            flops=6 * tokens * rows * D, bytes_accessed=4 * tokens * D, transcendentals=tokens * rows
        ),
    )(core.reshape(1), hidden, table, targets, mask, lse)


def place_kernel(first, *refs):
    out = refs[-1]
    rows = out.shape[0]
    base = (pl.program_id(0) + first) * rows
    total = None
    for ids, grads in zip(refs[:-1:2], refs[1:-1:2]):
        row = lax.broadcasted_iota(jnp.int32, (rows, ids.shape[1]), 0) + base
        hot = jnp.where(row == ids[...], 1.0, 0.0).astype(bf16)
        term = dot_nn(hot, grads[...])
        total = term if total is None else total + term
    out[...] = total.astype(bf16)


def place_rows(pairs, first, parts, rows):
    specs, args = [], []
    for ids, grads in pairs:
        specs.append(pl.BlockSpec(ids.shape, lambda i: (0, 0)))
        specs.append(pl.BlockSpec(grads.shape, lambda i: (0, 0)))
        args += [ids, grads]
    return pl.pallas_call(
        functools.partial(place_kernel, first),
        grid=(parts,),
        in_specs=specs,
        out_specs=pl.BlockSpec((rows, D), lambda i: (i, 0)),
        out_shape=jax.ShapeDtypeStruct((parts * rows, D), bf16),
        compiler_params=pltpu.CompilerParams(vmem_limit_bytes=VMEM_LIMIT),
        cost_estimate=pl.CostEstimate(flops=1, bytes_accessed=rows, transcendentals=0),
    )(*args)


def gather_axis(value, axis):
    size = lax.axis_size(axis)
    me = lax.axis_index(axis)
    got = [value]
    for step in range(1, size):
        got.append(lax.ppermute(value, axis, [(i, (i + step) % size) for i in range(size)]))
    stacked = jnp.stack(got)
    return jnp.take(stacked, (me - jnp.arange(size, dtype=jnp.int32)) % size, axis=0)


def gather_small(value, axes):
    shape = value.shape
    for axis in reversed(axes):
        value = gather_axis(value, axis)
        value = value.reshape((-1,) + shape)
    return value


def fold_all(value, combine):
    for axis in reversed(ALL):
        size = lax.axis_size(axis)
        hop = 1
        while hop < size:
            other = lax.ppermute(value, axis, [(i, i ^ hop) for i in range(size)])
            value = combine(value, other)
            hop *= 2
    return value


def swap(value, axis):
    return lax.ppermute(value, axis, [(0, 1), (1, 0)])


def swap_core(value):
    return swap(value, "core")


def add16(left, right):
    return (left.astype(f32) + right.astype(f32)).astype(bf16)


def pick(value, index, dim):
    return lax.dynamic_index_in_dim(value, index, dim, keepdims=False)


def scatter_pair(value, axis, dim):
    if lax.axis_size(axis) != 2:
        return lax.psum_scatter(value, axis, scatter_dimension=dim, tiled=False)
    me = lax.axis_index(axis)
    got = swap(pick(value, 1 - me, dim), axis)
    return add16(pick(value, me, dim), got)


def scatter_core(value):
    sizes = tuple(lax.axis_size(axis) for axis in ALL)
    return scatter_pair(value.reshape(sizes + (-1, value.shape[-1])), "core", 2)


def scatter_first(value, seq_first):
    return scatter_pair(value, "seq", 2) if seq_first else scatter_pair(value, "p", 1)


def scatter_second(value, seq_first):
    return scatter_pair(value, "p", 1) if seq_first else scatter_pair(value, "seq", 1)


def scatter_last(value):
    size, me = value.shape[0], lax.axis_index("z")
    total = pick(value, me, 0).astype(f32)
    for hop in range(1, size):
        send = pick(value, (me + hop) % size, 0)
        got = lax.ppermute(send, "z", [(i, (i + hop) % size) for i in range(size)])
        total = total + got.astype(f32)
    return total


def scatter_rest(value, seq_first):
    return scatter_last(scatter_second(scatter_first(value, seq_first), seq_first))


def line_gather(value, axis):
    size = lax.axis_size(axis)
    ups, downs = [value], [value]
    for _ in range(1, size):
        ups.append(lax.ppermute(ups[-1], axis, [(i, i + 1) for i in range(size - 1)]))
        downs.append(lax.ppermute(downs[-1], axis, [(i + 1, i) for i in range(size - 1)]))
    return [value] + [ups[k] + downs[size - k] for k in range(1, size)]


def line_scatter(parts, axis, beside=None):
    size = lax.axis_size(axis)
    up, down = None, None
    for step in range(1, size):
        far = size - step
        send_up, send_down = parts[size - far], parts[far]
        if up is not None:
            send_up, send_down = send_up + up, send_down + down
        up = lax.ppermute(send_up, axis, [(i, i + 1) for i in range(step)])
        down = lax.ppermute(send_down, axis, [(size - 1 - i, size - 2 - i) for i in range(step)])
        if beside is not None:
            up, down = beside(step, up, down)
    return parts[0].astype(f32) + up.astype(f32) + down.astype(f32)


def plane_gather(table):
    if lax.axis_size("p") != 2:
        return lax.all_gather(table, PLANE, axis=0, tiled=True)
    half = table.shape[0] // 2
    by_seq, by_p = swap(table, "seq"), swap(table, "p")
    far = [swap(by_p[:half], "seq"), swap(by_seq[half:], "p")]
    mine = [table, by_seq, by_p] + far
    return jnp.concatenate(mine + [swap_core(item) for item in mine])


def plane_slot(owner):
    if lax.axis_size("p") != 2:
        return owner
    other = owner ^ lax.axis_index(PLANE)
    return ((other >> 1) & 1) * 4 + (other >> 2) * 2 + (other & 1)


def plane_scatter(pairs, rows, before, after):
    count = lax.axis_size(PLANE)
    if lax.axis_size("p") != 2:
        placed = place_rows(pairs, 0, count, rows)
        placed = lax.psum_scatter(placed, PLANE, scatter_dimension=0, tiled=True)
        return placed.astype(f32), after(after(before))
    pairs, before = lax.optimization_barrier((pairs, before))
    away = swap_core(place_rows(pairs, 4, 4, rows))
    pairs, sums = lax.optimization_barrier((pairs, after(before)))
    home = place_rows(pairs, 0, 4, rows)
    half = rows // 2
    part = lambda first, last: add16(home[first:last], away[first:last])
    far_low, far_high = part(3 * rows, 3 * rows + half), part(3 * rows + half, 4 * rows)
    far_low, far_high, sums = lax.optimization_barrier((far_low, far_high, after(sums)))
    got_low, got_high = swap(far_low, "seq"), swap(far_high, "p")
    seq_high = add16(part(rows + half, 2 * rows), got_high)
    p_low = add16(part(2 * rows, 2 * rows + half), got_low)
    from_seq = swap(jnp.concatenate([part(rows, rows + half), seq_high]), "seq")
    from_p = swap(jnp.concatenate([p_low, part(2 * rows + half, 3 * rows)]), "p")
    return part(0, rows).astype(f32) + from_seq.astype(f32) + from_p.astype(f32), sums


def add_logs(left, right):
    top = jnp.maximum(left, right)
    return top + jnp.log(jnp.exp(left - top) + jnp.exp(right - top))


def ffn_forward(resid, gain, w_in, w_out):
    normed = rms_scale(resid, gain).astype(bf16)
    both = project(normed, w_in)
    hidden = gate_up(both).astype(bf16)
    return (resid + project(hidden, w_out), (normed, both, hidden))


def ffn_backward(upstream, resid, gain, w_in, w_out, saved):
    normed, both, hidden = saved
    grad_b = upstream.astype(bf16)
    d_out = weight_grad(hidden, grad_b).astype(bf16)
    _, pull = jax.vjp(gate_up, both)
    (d_both,) = pull(input_grad(grad_b, w_out))
    d_both_b = d_both.astype(bf16)
    d_in = weight_grad(normed, d_both_b).astype(bf16)
    d_resid, d_gain = norm_pull(resid, gain, 1.0, input_grad(d_both_b, w_in))
    return (upstream + d_resid, d_gain, d_in, d_out)


def branch_backward(upstream, out_b, w_out):
    grad_b = upstream.astype(bf16)
    return (weight_grad(out_b, grad_b).astype(bf16), input_grad(grad_b, w_out).astype(bf16))


def adamw(weight, grad, first_m, second_m, count, rate, decay):
    first_new = 0.9 * first_m + 0.1 * grad
    second_new = 0.999 * second_m + 0.001 * grad * grad
    first_hat = first_new / (1.0 - 0.9**count)
    second_hat = second_new / (1.0 - 0.999**count)
    return (
        first_new,
        second_new,
        weight - rate * (first_hat / (jnp.sqrt(second_hat) + 1e-08) + decay * weight),
    )


def body(
    enc_ids,
    enc_segs,
    sentinel,
    mode,
    dec_ids,
    dec_segs,
    target_ids,
    target_mask,
    buckets,
    embed,
    attn_in,
    attn_out,
    ffn_in,
    ffn_out,
    rel_table,
    gains,
    m_embed,
    v_embed,
    m_attn_in,
    v_attn_in,
    m_attn_out,
    v_attn_out,
    m_ffn_in,
    v_ffn_in,
    m_ffn_out,
    v_ffn_out,
    m_rel,
    v_rel,
    m_gains,
    v_gains,
):
    core = lax.axis_index("core")
    z_at = lax.axis_index("z")
    z_size = lax.axis_size("z")
    plane_size = lax.axis_size(PLANE)
    device = lax.axis_index(ALL)
    shard = embed.shape[0]
    padded = (shard // 16 + 1) * 16
    enc_count, dec_count = enc_ids.shape[1], dec_ids.shape[1]
    enc_len, dec_len = enc_segs.shape[1], dec_segs.shape[1]

    table_b = jnp.pad(embed.astype(bf16), ((0, padded - shard), (0, 0)))
    misc = jnp.concatenate([gains.T, rel_table.reshape(-1, 1)], axis=1)
    misc = jnp.pad(misc, ((0, 0), (0, 120)))
    shard_in = attn_in.shape[1]
    flat_out = ffn_out.astype(bf16).reshape(2, shard_in, -1)
    enc_cast = jnp.concatenate([attn_in[0], ffn_in[0], attn_out[0], misc], axis=1).astype(bf16)
    enc_pack = lax.all_gather(
        jnp.concatenate([enc_cast, flat_out[0]], axis=1), ALL, axis=0, tiled=True
    )
    dec_cast = jnp.concatenate(
        [attn_in[1], attn_in[2], attn_out[1], attn_out[2]], axis=1
    ).astype(bf16)
    ffn_cast = jnp.concatenate([ffn_in[1].astype(bf16), flat_out[1]], axis=1)
    plane_table = plane_gather(table_b)
    flat = jnp.concatenate(
        [
            enc_ids[0],
            sentinel[0],
            dec_ids[0],
            target_ids[0],
            target_mask[0],
            enc_segs[0],
            dec_segs[0],
            jnp.pad(mode[0], (0, 128 - mode.shape[1])),
        ]
    )
    flat = lax.ppermute(flat, ("core", "seq"), [(0, 0), (1, 2), (2, 1), (3, 3)])
    sizes = [enc_count, enc_count, dec_count, dec_count, dec_count, enc_len, dec_len]
    pieces, start = [], 0
    for size in sizes:
        pieces.append(flat[start : start + size])
        start += size
    enc_id, sent, dec_id, targets, mask_i, enc_seg_all, dec_seg_all = pieces
    mode_row = flat[start : start + mode.shape[1]]
    mask = mask_i.astype(f32)

    enc_seg = lax.dynamic_slice_in_dim(enc_seg_all, core * enc_count, enc_count)
    enc_seg_other = lax.dynamic_slice_in_dim(enc_seg_all, (1 - core) * enc_count, enc_count)
    dec_seg = lax.dynamic_slice_in_dim(dec_seg_all, core * dec_count, dec_count)
    dec_seg_other = lax.dynamic_slice_in_dim(dec_seg_all, (1 - core) * dec_count, dec_count)
    enc_range = jnp.arange(enc_count, dtype=jnp.int32)
    dec_range = jnp.arange(dec_count, dtype=jnp.int32)
    enc_pos, enc_pos_other = core * enc_count + enc_range, (1 - core) * enc_count + enc_range
    dec_pos, dec_pos_other = core * dec_count + dec_range, (1 - core) * dec_count + dec_range
    prior_all = jnp.concatenate([enc_seg_all[:1], enc_seg_all[:-1]])
    prior = lax.dynamic_slice_in_dim(prior_all, core * enc_count, enc_count)
    first = (enc_pos == 0) | (enc_seg != prior)
    mode_of = jnp.sum(
        jnp.where(
            enc_seg[:, None] == jnp.arange(mode.shape[1], dtype=jnp.int32)[None], mode_row[None], 0
        ),
        axis=1,
    )
    enc_tok = jnp.where(sent == 1, V - 1 - enc_seg, enc_id)
    enc_tok = jnp.where(first, V - 101 - mode_of, enc_tok)
    local_ids = jnp.concatenate([enc_tok, dec_id])

    line_ids = line_gather(local_ids, "z")
    plane_rows = plane_size * shard
    places = []
    for ids in line_ids:
        rel_id = ids - z_at * plane_rows
        inside = (rel_id >= 0) & (rel_id < plane_rows)
        places.append(
            jnp.where(inside, plane_slot(rel_id // shard) * padded + rel_id % shard, shard)
        )
    got = jnp.take(plane_table, jnp.concatenate(places), axis=0, mode="clip")
    dec_cast, enc_pack, got = lax.optimization_barrier((dec_cast, enc_pack, got))
    dec_pack = lax.all_gather(dec_cast, ALL, axis=0, tiled=True)
    enc_places = [item[:enc_count] for item in places]
    dec_places = [item[enc_count:] for item in places]


    cut = lambda pack, start, width: lax.slice_in_dim(pack, start, start + width, axis=1)
    enc_wi, enc_fi = cut(enc_pack, 0, 3 * D), cut(enc_pack, 3 * D, 2 * FF)
    enc_wo, misc_all = cut(enc_pack, 3 * D + 2 * FF, D), cut(enc_pack, 4 * D + 2 * FF, 128)
    enc_fo = cut(enc_pack, 4 * D + 2 * FF + 128, FF).reshape(FF, D)
    gain = misc_all[:, :7].T.astype(f32)
    rel_all = jnp.transpose(misc_all[:, 7].reshape(-1, 2, rel_table.shape[1]), (1, 0, 2))
    rel_all = rel_all.reshape(2, BUCKETS, HEADS)

    enc_x8, enc_picks = bias_lines(rel_all[0], buckets[0], core, enc_count, enc_count)
    dec_x8, dec_picks = bias_lines(rel_all[1], buckets[1], core, dec_count, dec_count)
    held = (enc_fo, gain, enc_x8, dec_x8, enc_picks, dec_picks)

    def beside(step, up, down):
        nonlocal held
        if step == 2:
            up, down, held = lax.optimization_barrier((up, down, held))
        return up, down

    looked = line_scatter(jnp.split(got, len(places)), "z", beside)
    enc_fo, gain, enc_x8, dec_x8, enc_picks, dec_picks = held
    ffn_cast, dec_pack, looked = lax.optimization_barrier((ffn_cast, dec_pack, looked))
    ffn_pack = lax.all_gather(ffn_cast, ALL, axis=0, tiled=True)
    dec_wi, cross_wi = cut(dec_pack, 0, 3 * D), cut(dec_pack, 3 * D, 3 * D)
    dec_wo, cross_wo = cut(dec_pack, 6 * D, D), cut(dec_pack, 7 * D, D)
    dec_fi = cut(ffn_pack, 0, 2 * FF)
    dec_fo = cut(ffn_pack, 2 * FF, FF).reshape(FF, D)
    enc_x0, dec_y0 = looked[:enc_count], looked[enc_count:]

    col, line = (lambda v: v[:, None]), (lambda v: v[None, :])
    enc_info = (
        col(enc_seg), line(enc_seg), line(enc_seg_other),
        col(enc_pos), line(enc_pos), line(enc_pos_other),
    )
    dec_info = (
        col(dec_seg), line(dec_seg), line(dec_seg_other),
        col(dec_pos), line(dec_pos), line(dec_pos_other),
    )
    cross_info = (
        col(dec_seg), line(enc_seg), line(enc_seg_other),
        col(dec_pos), line(enc_pos), line(enc_pos_other),
    )

    enc_n1 = rms_scale(enc_x0, gain[0]).astype(bf16)
    enc_q = project(enc_n1, enc_wi[:, :D]).astype(bf16)
    enc_kv = project(enc_n1, enc_wi[:, D:]).astype(bf16)
    enc_kv2 = swap_core(enc_kv)
    enc_ob, enc_lse = attend_forward(enc_q, enc_kv, enc_kv2, enc_info, enc_x8, False)
    enc_x1 = enc_x0 + project(enc_ob, enc_wo)
    enc_x2, enc_saved = ffn_forward(enc_x1, gain[1], enc_fi, enc_fo)
    enc_out = rms_scale(enc_x2, gain[2]).astype(bf16)

    dec_n1 = rms_scale(dec_y0, gain[3]).astype(bf16)
    dec_q = project(dec_n1, dec_wi[:, :D]).astype(bf16)
    dec_kv = project(dec_n1, dec_wi[:, D:]).astype(bf16)
    dec_kv2 = swap_core(dec_kv)
    dec_ob, dec_lse = attend_forward(dec_q, dec_kv, dec_kv2, dec_info, dec_x8, True)
    dec_y1 = dec_y0 + project(dec_ob, dec_wo)
    cross_kv = project(enc_out, cross_wi[:, D:]).astype(bf16)
    cross_kv2 = swap_core(cross_kv)
    cross_n = rms_scale(dec_y1, gain[4]).astype(bf16)
    cross_q = project(cross_n, cross_wi[:, :D]).astype(bf16)
    cross_ob, cross_lse = attend_forward(cross_q, cross_kv, cross_kv2, cross_info, None, False)
    dec_y2 = dec_y1 + project(cross_ob, cross_wo)
    dec_y3, dec_saved = ffn_forward(dec_y2, gain[5], dec_fi, dec_fo)
    head_scale = D ** (-0.5)
    hidden_b = (rms_scale(dec_y3, gain[6]) * head_scale).astype(bf16)

    hidden_all = lax.all_gather(hidden_b, ALL, axis=0, tiled=True)
    sizes = tuple(lax.axis_size(axis) for axis in ALL)
    hidden_all = hidden_all.reshape(-1, 2, 2, dec_count, D)
    info = gather_small(jnp.stack([targets, mask_i]), ALL)
    info = info.reshape(-1, 2, 2, 2, 2, dec_count // 2)
    info = jnp.transpose(info, (3, 4, 1, 0, 2, 5)).reshape(2, 1, -1)
    targets_all = info[0] - device * shard
    mask_all = info[1].astype(f32)
    lse_part, picked = head_stats(hidden_all, table_b, targets_all, shard)
    lse = fold_all(lse_part, add_logs)
    d_hidden, head_embed = [], None
    for half in range(2):
        *away, term = head_grad(
            1 - core, hidden_all, table_b, targets_all, mask_all, lse, shard, half
        )
        head_embed = term if head_embed is None else head_embed + term
        away = [swap_core(item) for item in away]
        *home, term = head_grad(
            core, hidden_all, table_b, targets_all, mask_all, lse, shard, half
        )
        head_embed = head_embed + term
        for number in range(2):
            item = add16(home[number], away[number])
            item = item.reshape(sizes[:2] + (2,) + item.shape[2:])
            d_hidden.append(scatter_rest(item, number == 0))
    d_hidden = jnp.concatenate(d_hidden)
    mine = (core * sizes[0] * sizes[1] + device // 4) * 2 + lax.axis_index("seq")
    lse_mine = lax.dynamic_slice_in_dim(
        lse.reshape(2, -1), mine * (dec_count // 2), dec_count // 2, axis=1
    )
    loss_local = jnp.sum(mask * lse_mine.reshape(-1)) - jnp.sum(mask_all * picked)

    d_y3, d_gain_final = norm_pull(dec_y3, gain[6], head_scale, d_hidden)
    d_y2, d_gain_dffn, d_dec_fi, d_dec_fo = ffn_backward(
        d_y3, dec_y2, gain[5], dec_fi, dec_fo, dec_saved
    )
    d_cross_wo, d_cross_ob = branch_backward(d_y2, cross_ob, cross_wo)
    early, d_dec_fo, d_cross_ob = lax.optimization_barrier((d_dec_fi, d_dec_fo, d_cross_ob))
    g_dec_fo = scatter_core(d_dec_fo)
    early = lax.psum_scatter(early, ALL, scatter_dimension=0, tiled=True)
    d_cross_q, own, other = attend_backward(
        d_cross_ob, cross_lse, cross_q, cross_kv, cross_kv2, cross_info, None, False
    )
    got = (own + swap_core(other).astype(f32)).astype(bf16)
    d_cross_kv = jnp.concatenate([got[0], got[1]], axis=1)
    d_cross_wq = weight_grad(cross_n, d_cross_q)
    d_y1_norm, d_gain_cross = norm_pull(
        dec_y1, gain[4], 1.0, input_grad(d_cross_q, cross_wi[:, :D])
    )
    d_y1 = d_y2 + d_y1_norm
    d_cross_wkv = weight_grad(enc_out, d_cross_kv)
    d_dec_wo, d_dec_ob = branch_backward(d_y1, dec_ob, dec_wo)
    g_dec_fo, d_dec_ob = lax.optimization_barrier((g_dec_fo, d_dec_ob))
    g_dec_fo = scatter_first(g_dec_fo, False)
    d_dec_q, own, other, dec_y8 = attend_backward(
        d_dec_ob, dec_lse, dec_q, dec_kv, dec_kv2, dec_info, dec_x8, True
    )
    got = (own + swap_core(other).astype(f32)).astype(bf16)
    d_dec_qkv = jnp.concatenate([d_dec_q, got[0], got[1]], axis=1)
    d_dec_table = bias_gradient(dec_y8, dec_picks)
    d_dec_wi = weight_grad(dec_n1, d_dec_qkv)
    d_y0_norm, d_gain_datt = norm_pull(dec_y0, gain[3], 1.0, input_grad(d_dec_qkv, dec_wi))
    d_y0 = d_y1 + d_y0_norm
    d_dec_rest = jnp.concatenate(
        [
            d_dec_wi.astype(bf16),
            d_cross_wq.astype(bf16),
            d_cross_wkv.astype(bf16),
            d_dec_wo,
            d_cross_wo,
        ],
        axis=1,
    )
    dec_lines = line_gather(d_y0.astype(bf16), "z")

    d_x2, d_gain_efin = norm_pull(
        enc_x2, gain[2], 1.0, input_grad(d_cross_kv, cross_wi[:, D:])
    )
    d_x1, d_gain_effn, d_enc_fi, d_enc_fo = ffn_backward(
        d_x2, enc_x1, gain[1], enc_fi, enc_fo, enc_saved
    )
    early, g_dec_fo, d_x1 = lax.optimization_barrier((early, g_dec_fo, d_x1))
    g_dec_fo = scatter_second(g_dec_fo, False)
    d_enc_wo, d_enc_ob = branch_backward(d_x1, enc_ob, enc_wo)
    d_enc_low, d_enc_high = d_enc_fi[:, :3456], jnp.concatenate([d_enc_fi[:, 3456:], d_enc_wo], 1)
    enc_sums = [scatter_core(item) for item in (d_enc_low, d_enc_high, d_enc_fo)]
    late, dec_lines, enc_sums, g_dec_fo, d_enc_ob = lax.optimization_barrier(
        (d_dec_rest, dec_lines, enc_sums, g_dec_fo, d_enc_ob)
    )
    late = lax.psum_scatter(late, ALL, scatter_dimension=0, tiled=True)
    early = early.astype(f32)
    enc_sums = [scatter_first(enc_sums[0], True), scatter_first(enc_sums[1], False), enc_sums[2]]
    d_enc_q, own, other, enc_y8 = attend_backward(
        d_enc_ob, enc_lse, enc_q, enc_kv, enc_kv2, enc_info, enc_x8, False
    )
    got = (own + swap_core(other).astype(f32)).astype(bf16)
    d_enc_qkv = jnp.concatenate([d_enc_q, got[0], got[1]], axis=1)
    d_enc_table = bias_gradient(enc_y8, enc_picks)
    d_enc_wi = weight_grad(enc_n1, d_enc_qkv)
    d_x0_norm, d_gain_eatt = norm_pull(enc_x0, gain[0], 1.0, input_grad(d_enc_qkv, enc_wi))
    d_x0 = d_x1 + d_x0_norm

    d_x0, enc_sums = lax.optimization_barrier((d_x0.astype(bf16), enc_sums))
    enc_sums[2] = scatter_first(enc_sums[2], False)
    enc_sums = [scatter_second(item, number == 0) for number, item in enumerate(enc_sums)]
    enc_lines = line_gather(d_x0, "z")
    enc_lines, enc_sums = lax.optimization_barrier((enc_lines, enc_sums))
    far_place = lambda item: jnp.where(item == shard, -1, item)[None, :]
    pairs = [
        (far_place(item), grads)
        for item, grads in zip(enc_places + dec_places, enc_lines + dec_lines)
    ]
    d_gains = jnp.stack(
        [
            d_gain_eatt,
            d_gain_effn,
            d_gain_efin,
            d_gain_datt,
            d_gain_cross,
            d_gain_dffn,
            d_gain_final,
        ]
    )
    d_rel = jnp.stack([d_enc_table.reshape(-1), d_dec_table.reshape(-1)])
    d_rel = jnp.transpose(d_rel.reshape(2, -1, rel_table.shape[1]), (1, 0, 2)).reshape(D, 1)
    d_misc = jnp.pad(jnp.concatenate([d_gains.T, d_rel], axis=1), ((0, 0), (0, 120)))
    d_last = jnp.concatenate([d_enc_wi.astype(bf16), d_misc.astype(bf16)], axis=1)
    last = [scatter_core(d_last[:, :1152]), scatter_core(d_last[:, 1152:])]

    def beside_place(sums):
        if len(sums) == 3:
            late, last, enc_sums = sums
            last = [scatter_first(item, number == 0) for number, item in enumerate(last)]
            wide = jnp.concatenate(enc_sums[:2], axis=2)
            both = jnp.concatenate([enc_sums[2], g_dec_fo], axis=1)
            return late, last, [scatter_last(wide), scatter_last(both)], None
        late, last, enc_sums, _ = sums
        last = [scatter_second(item, number == 0) for number, item in enumerate(last)]
        return late, jnp.concatenate(last, axis=2), enc_sums

    input_embed, (late, last, (g_wide, g_out)) = plane_scatter(
        pairs, padded, (late, last, enc_sums), beside_place
    )
    late = late.astype(f32)
    grad_embed = head_embed[:shard] + input_embed[:shard]

    last = scatter_last(last)
    squares = sum(
        (jnp.sum(item * item) for item in (grad_embed, early, late, g_wide, g_out, last))
    )
    sums = fold_all(jnp.stack([jnp.sum(mask), loss_local, squares]), jnp.add)
    owned = (
        jnp.stack([cut(last, 0, 3 * D), cut(late, 0, 3 * D), cut(late, 3 * D, 3 * D)]),
        jnp.stack([cut(g_wide, 2 * FF, D), cut(late, 6 * D, D), cut(late, 7 * D, D)]),
        jnp.stack([cut(g_wide, 0, 2 * FF), early]),
        g_out.reshape(2, -1, D),
        last[:, 3 * D + 7].reshape(2, -1),
        last[:, 3 * D : 3 * D + 7].T,
    )
    grads = (grad_embed,) + owned
    count_all, loss_all, squares_all = sums[0], sums[1], sums[2]
    grad_norm = jnp.sqrt(squares_all) / count_all
    factor = jnp.minimum(1.0, clip_limit / grad_norm) / count_all
    weights = (embed, attn_in, attn_out, ffn_in, ffn_out, rel_table, gains)
    moments = [
        (m_embed, v_embed),
        (m_attn_in, v_attn_in),
        (m_attn_out, v_attn_out),
        (m_ffn_in, v_ffn_in),
        (m_ffn_out, v_ffn_out),
        (m_rel, v_rel),
        (m_gains, v_gains),
    ]
    settings = [
        (1.0, 0.01),
        (0.05, 0.01),
        (0.05, 0.01),
        (0.05, 0.01),
        (0.05, 0.01),
        (0.3, 0.0),
        (0.3, 0.0),
    ]
    results = [loss_all / count_all, grad_norm]
    for slot_number, (param, grad, pair, setting) in enumerate(
        zip(weights, grads, moments, settings)
    ):
        clipped = grad * factor
        first_new, second_new, new_param = adamw(
            param, clipped, pair[0], pair[1], float(STEP), setting[0], setting[1]
        )
        results.extend((clipped if slot_number == 0 else first_new, second_new, new_param))
    return tuple(results)


def solution(mesh):
    rows = ("z", "p", "core")
    every = ALL
    inner = Mesh(mesh.devices.reshape(4, -1, 2, mesh.devices.shape[1]), ALL)
    mat = P(None, every, None)
    vec = P(None, every)
    emb = P(every, None)
    in_specs = (
        P(rows, "seq"),
        P(rows, None),
        P(rows, "seq"),
        P(rows, None),
        P(rows, "seq"),
        P(rows, None),
        P(rows, "seq"),
        P(rows, "seq"),
        P(),
        emb,
        mat,
        mat,
        mat,
        mat,
        vec,
        vec,
        emb,
        emb,
    ) + (mat,) * 8 + (vec,) * 4
    out_specs = (P(), P()) + (emb,) * 3 + (mat,) * 12 + (vec,) * 6
    return jax.shard_map(body, mesh=inner, in_specs=in_specs, out_specs=out_specs, check_vma=False)
```
